32 devices in a mesh: rep: 8 (over z, x), shard: 4 (over y, core).
Axes of the slice: x: 2, y: 2, z: 4, core: 2. Of those that a mesh axis runs over, the one named last changes fastest.
Arguments:
- tokens: bfloat16 [32768, 1024], P(('rep', 'shard')), may hold values from -6 to 6
- segment_ids: int32 [32, 1024], P(('rep', 'shard')), may hold values from 0 to 3, never falling along the last dimension, each value on 1 to 800 neighbouring positions
- norm_gain_one: bfloat16 [1024], P('shard'), may hold values from 0.5 to 1.5
- w_query: bfloat16 [1024, 256], P('shard'), may hold values from -0.1875 to 0.1875
- w_key: bfloat16 [1024, 256], P('shard'), may hold values from -0.1875 to 0.1875
- w_value: bfloat16 [1024, 1024], P('shard'), may hold values from -0.1875 to 0.1875
- w_convgate: bfloat16 [1024, 1024], P('shard'), may hold values from -0.1875 to 0.1875
- w_output: bfloat16 [1024, 1024], P('shard'), may hold values from -0.375 to 0.375
- conv_filter: bfloat16 [3, 1024], P(None, 'shard'), may hold values from -2.390625 to 2.390625
- norm_gain_two: bfloat16 [1024], P('shard'), may hold values from 0.5 to 1.5
- w_gate: bfloat16 [1024, 4096], P('shard'), may hold values from -0.1875 to 0.1875
- w_up: bfloat16 [1024, 4096], P('shard'), may hold values from -0.1875 to 0.1875
- w_down: bfloat16 [4096, 1024], P('shard'), may hold values from -0.1875 to 0.1875
- cotangent: bfloat16 [32768, 1024], P(('rep', 'shard')), may hold values from -6 to 6
Outputs:
- out: bfloat16 [32768, 1024], P(('rep', 'shard'))
- grad_tokens: float32 [32768, 1024], P(('rep', 'shard'))
- grad_gain_one: float32 [1024], P('shard')
- grad_query: float32 [1024, 256], P('shard')
- grad_key: float32 [1024, 256], P('shard')
- grad_value: float32 [1024, 1024], P('shard')
- grad_convgate: float32 [1024, 1024], P('shard')
- grad_output: float32 [1024, 1024], P('shard')
- grad_filter: float32 [3, 1024], P(None, 'shard')
- grad_gain_two: float32 [1024], P('shard')
- grad_gate: float32 [1024, 4096], P('shard')
- grad_up: float32 [1024, 4096], P('shard')
- grad_down: float32 [4096, 1024], P('shard')
The draws below stay inside these ranges and needn't reach their ends.
Inputs may be any that keep to these rules, and one draw needn't show every extreme that they name: `segment_ids`: along each sequence the document numbers never fall; a document holds at most 800 tokens.
All inputs are finite; a program needn't handle non-finite values.
Results may differ from the reference program's by a relative error of at most 0.02.
Values may be sent and summed in bfloat16 or wider, within the bound.
No kernel may reach another device: no remote copies, remote signals or barrier semaphores. Data moves between devices by JAX's collectives and lax.ppermute only.
A program may use at most 256 MiB of HBM per device.

```python
import math
import jax
import jax.numpy as jnp
import numpy as np
from jax import lax

D = 1024
FF = 4096
HEADS = 16
FEAT = 16
KW = 3
SEQ = 1024
SEQS = 32
TOKENS = 32768


def shard_levels(own_key, extent, cuts, smallest, high):
    factor_of, own = 1.0, jax.random.fold_in(own_key, 6)
    for position, blocks in cuts:
        heights = jnp.exp(jax.random.uniform(jax.random.fold_in(own, position), (blocks,), jnp.float32, smallest / len(cuts), high / len(cuts)))
        factor_of = factor_of * jnp.repeat(heights, extent[position] // blocks).reshape([-1 if axis == position else 1 for axis in range(len(extent))])
    return factor_of


def split_up(count, total, most, lean):
    weights = [(1 << 20) // math.isqrt(standing ** lean) + 1 for standing in range(2, count + 1)]
    surplus, holding = total - most - (count - 1), [1] * (count - 1)
    while surplus > 0:
        free = [i for i in range(count - 1) if holding[i] < most]
        mass, left = sum([weights[i] for i in free]), surplus
        for i in free:
            addition = min(most - holding[i], max(1, left * weights[i] // mass), surplus)
            holding[i] = holding[i] + addition
            surplus = surplus - addition
    return np.array([most] + holding)


def uneven_parts(rng, number_of, total, limit, slope):
    if number_of == 2:
        one = jax.random.randint(rng, (), max(1, total - limit), min(limit, total - 1) + 1)
        return jnp.stack([one, total - one])
    lengths = jnp.asarray(split_up(number_of, total, limit, slope), jnp.int32)
    couples = (number_of - 1) // 2
    donor, sink = lengths[1:1 + 2 * couples:2], lengths[2:2 + 2 * couples:2]
    room = jnp.minimum(donor - 1, limit - sink)
    passed = jax.random.randint(jax.random.fold_in(rng, 1), (couples,), 0, 1 << 20) % (room + 1)
    lengths = lengths.at[1:1 + 2 * couples:2].set(donor - passed).at[2:2 + 2 * couples:2].set(sink + passed)
    return lengths[jax.random.permutation(jax.random.fold_in(rng, 2), number_of)]


def centred(rng, extent, deviation, most, split=(), kind=jnp.bfloat16):
    entries = jax.random.normal(rng, extent, jnp.float32) * deviation
    if len(split) > 0:
        entries = shard_levels(rng, extent, split, -0.22, 0.18) * entries
    return jnp.clip(entries, min=-most, max=most).astype(kind)


def setup_inputs(seed: int = 0) -> dict:
    streams_of = jax.random.split(jax.random.key(seed), 15)
    return {
        "tokens": centred(streams_of[0], (TOKENS, D), 1.0, 6.0, ((0, 32),)),
        "segment_ids": jax.vmap(lambda own: jnp.searchsorted(jnp.cumsum(uneven_parts(own, 4, SEQ, SEQ * 25 // 32, 1)), jnp.arange(SEQ), side="right"))(jax.random.split(streams_of[1], SEQS)).reshape((SEQS, SEQ)).astype(jnp.int32),
        "norm_gain_one": jnp.clip(1.0 + 0.1 * jax.random.normal(streams_of[2], (D,), jnp.float32), 0.5, 1.5).astype(jnp.bfloat16),
        "w_query": centred(streams_of[3], (D, HEADS * FEAT), D ** -0.5, 0.1875, ((0, 4),)),
        "w_key": centred(streams_of[4], (D, HEADS * FEAT), D ** -0.5, 0.1875, ((0, 4),)),
        "w_value": centred(streams_of[5], (D, D), D ** -0.5, 0.1875, ((0, 4),)),
        "w_convgate": centred(streams_of[6], (D, D), D ** -0.5, 0.1875, ((0, 4),)),
        "w_output": centred(streams_of[7], (D, D), (D // 4) ** -0.5, 0.375, ((0, 4),)),
        "conv_filter": centred(streams_of[8], (KW, D), 0.4, 2.390625, ((1, 4),)),
        "norm_gain_two": jnp.clip(1.0 + 0.1 * jax.random.normal(streams_of[9], (D,), jnp.float32), 0.5, 1.5).astype(jnp.bfloat16),
        "w_gate": centred(streams_of[10], (D, FF), D ** -0.5, 0.1875, ((0, 4),)),
        "w_up": centred(streams_of[11], (D, FF), D ** -0.5, 0.1875, ((0, 4),)),
        "w_down": centred(streams_of[12], (FF, D), (FF // 4) ** -0.5, 0.1875, ((0, 4),)),
        "cotangent": centred(streams_of[13], (TOKENS, D), 1.0, 6.0, ((0, 32),)),
    }


eps_norm = 1e-06
highest = lax.Precision.HIGHEST

@jax.custom_vjp
def low(v):
    return lax.optimization_barrier(v.astype(jnp.bfloat16)).astype(jnp.float32)

@jax.custom_vjp
def low_back(v):
    return v

def low_keep(v):
    return (low(v), None)

def low_pass(kept, grad):
    return (grad,)

def back_keep(v):
    return (v, None)

def back_low(kept, grad):
    return (low(grad),)
low.defvjp(low_keep, low_pass)
low_back.defvjp(back_keep, back_low)

def matmul(operand_one, operand_two):
    return jnp.dot(operand_one, operand_two, precision=highest)

def rms_norm(inputs, gain_vector):
    inverse = lax.rsqrt(lax.optimization_barrier(jnp.mean(inputs * inputs, axis=-1, keepdims=True)) + eps_norm)
    return inputs * inverse * gain_vector

def shifted(values, segments, offset):
    moved_rows = jnp.concatenate([jnp.zeros((offset, values.shape[1]), values.dtype), values[:-offset]], axis=0)
    moved_segments = jnp.concatenate([jnp.full((offset,), -1, jnp.int32), segments[:-offset].astype(jnp.int32)])
    keep_rows = moved_segments == segments.astype(jnp.int32)
    return jnp.where(keep_rows[:, None], moved_rows, 0.0)

def layer(inputs, segments, weights):
    gain_one, w_query, w_key, w_value, w_convgate, w_output, conv_filter, gain_two, w_gate, w_up, w_down = weights
    length = inputs.shape[0]
    hidden = low(rms_norm(inputs, gain_one))
    queries = low(low_back(matmul(hidden, w_query)))
    key_rows = low(low_back(matmul(hidden, w_key)))
    values = low(low_back(matmul(hidden, w_value)))
    conv_gate = low_back(matmul(hidden, w_convgate))
    places = jnp.arange(length)
    visible = (places[:, None] >= places[None, :]) & (segments[:, None] == segments[None, :])
    head_query = queries.reshape(length, HEADS, FEAT).transpose(1, 0, 2)
    head_key = key_rows.reshape(length, HEADS, FEAT).transpose(1, 0, 2)
    head_value = values.reshape(length, HEADS, D // HEADS).transpose(1, 0, 2)
    scores = low_back(jnp.einsum('htf,hsf->hts', head_query, head_key, precision=highest) * FEAT ** (-0.5))
    kernel = jnp.where(visible[None], 1.0 + scores + 0.5 * scores * scores, 0.0)
    totals = lax.optimization_barrier(jnp.sum(kernel, axis=-1, keepdims=True))
    numerators = low_back(jnp.einsum('hts,hse->hte', low(kernel), head_value, precision=highest))
    attention = (numerators / totals).transpose(1, 0, 2).reshape(length, D)
    conv_value = conv_filter[0] * values
    for offset in range(1, KW):
        conv_value = conv_value + conv_filter[offset] * shifted(values, segments, offset)
    mixed_low = low(low_back(attention + conv_gate * conv_value))
    middle = inputs + low_back(matmul(mixed_low, w_output))
    hidden_two = low(rms_norm(middle, gain_two))
    gate_pre = low_back(matmul(hidden_two, w_gate))
    up_pre = low_back(matmul(hidden_two, w_up))
    activation = low(jax.nn.silu(gate_pre) * up_pre)
    return middle + low_back(matmul(activation, w_down))

def reference(tokens, segment_ids, norm_gain_one, w_query, w_key, w_value, w_convgate, w_output, conv_filter, norm_gain_two, w_gate, w_up, w_down, cotangent):
    weights = tuple((weight.astype(jnp.float32) for weight in (norm_gain_one, w_query, w_key, w_value, w_convgate, w_output, conv_filter, norm_gain_two, w_gate, w_up, w_down)))
    inputs = tokens.astype(jnp.float32).reshape(SEQS, SEQ, D)

    def forward(inputs, weights):

        def advance(carried, sequence):
            return (carried, jax.checkpoint(layer)(sequence[0], sequence[1], weights))
        unused, outputs = lax.scan(advance, jnp.zeros((), jnp.float32), (inputs, segment_ids))
        return outputs
    outputs, pullback = jax.vjp(forward, inputs, weights)
    grad_inputs, grad_weights = pullback(cotangent.astype(jnp.float32).reshape(SEQS, SEQ, D))
    return (outputs.reshape(TOKENS, D).astype(jnp.bfloat16), grad_inputs.reshape(TOKENS, D), grad_weights[0], grad_weights[1], grad_weights[2], grad_weights[3], grad_weights[4], grad_weights[5], grad_weights[6], grad_weights[7], grad_weights[8], grad_weights[9], grad_weights[10])
```

```python
import functools

import jax
import jax.numpy as jnp
import numpy as np
from jax import lax
from jax.experimental import pallas as pl
from jax.experimental.pallas import tpu as pltpu
from jax.sharding import Mesh
from jax.sharding import PartitionSpec as P

HEADS = 16
FEAT = 16
KW = 3
EPS = 1e-06
TILE = 256
SHARD_ROWS = 256
LANES = 128
COST = 0.6
X_AT, MIXER_AT, FEED_AT, DOWN_AT, PACK_AT, COLS_AT, GRAD_AT, OWNER_AT, ACT_AT = 0, 2, 8, 12, 16, 24, 32, 36, 40

low = jnp.bfloat16
wide = jnp.float32


def dot(a, b):
    return jnp.dot(a, b, preferred_element_type=wide)


def dot_nt(a, b):
    return lax.dot_general(a, b, (((1,), (1,)), ((), ())), preferred_element_type=wide)


def dot_tn(a, b):
    return lax.dot_general(a, b, (((0,), (0,)), ((), ())), preferred_element_type=wide)


class Order:
    last = None


def launch(kernel, deps=(), onto=(), *, scalars=0, grid, in_specs, out_specs, out_shape, scratch_shapes=(), **rest):
    taken = scalars + len(in_specs)
    deps = list(onto) + [d for d in deps if d is not None] + ([] if Order.last is None else [Order.last])

    def body(*refs):
        kernel(*refs[:taken], *refs[taken + len(deps) :])

    spec = pltpu.PrefetchScalarGridSpec(
        num_scalar_prefetch=scalars,
        grid=grid,
        in_specs=list(in_specs) + [pl.BlockSpec(memory_space=pl.ANY)] * len(deps),
        out_specs=out_specs,
        scratch_shapes=list(scratch_shapes),
    )
    aliases = {taken + n: n for n in range(len(onto))}
    run = pl.pallas_call(body, grid_spec=spec, out_shape=out_shape, input_output_aliases=aliases, **rest)

    def call(*operands):
        result = run(*operands, *deps)
        Order.last = result[0] if isinstance(result, (list, tuple)) else result
        return result

    return call


def params(mib):
    return pltpu.CompilerParams(vmem_limit_bytes=max(mib, 60) << 20)


def cost(gigaflops, mebibytes):
    return pl.CostEstimate(
        flops=int(gigaflops * COST * 1e9), bytes_accessed=int(mebibytes * COST * (1 << 20)), transcendentals=0
    )


def fixed(shape):
    return pl.BlockSpec(shape, lambda *_: (0,) * len(shape), pipeline_mode=pl.Buffered(1))


def rows(height, width):
    return pl.BlockSpec((height, width), lambda i, *_: (i, 0))


def place(offs_ref, base, pieces, full_ref):
    for n, piece in enumerate(pieces):
        at = pl.multiple_of(offs_ref[base + n], 128)
        full_ref[pl.ds(at, piece.shape[0]), :] = piece[...]


def project_kernel(offs_ref, x_ref, *refs):
    pieces, (hidden_ref, q_ref, k_ref, v_ref, gate_ref, full_ref, vec_ref) = refs[:6], refs[6:]
    heads = HEADS * FEAT
    width = x_ref.shape[1]

    @pl.when(pl.program_id(0) == 0)
    def _():
        place(offs_ref, MIXER_AT, pieces, full_ref)
        small = full_ref[:, 2 * heads + 2 * width :].astype(wide)
        vec_ref[...] = small.T[:8, :]

    x = x_ref[...].astype(wide)
    inverse = lax.rsqrt(jnp.mean(x * x, axis=-1, keepdims=True) + EPS)
    hidden = (x * inverse * vec_ref[0:1, :]).astype(low)
    hidden_ref[...] = hidden
    q_ref[...] = (dot(hidden, full_ref[:, :heads]) * FEAT ** (-0.5)).astype(low)
    k_ref[...] = dot(hidden, full_ref[:, heads : 2 * heads]).astype(low)
    v_ref[...] = dot(hidden, full_ref[:, 2 * heads : 2 * heads + width]).astype(low)
    gate_ref[...] = dot(hidden, full_ref[:, 2 * heads + width : 2 * heads + 2 * width]).astype(low)


def project(offs, x, pieces, deps=()):
    length, width = x.shape
    heads = HEADS * FEAT
    columns = pieces[0].shape[1]
    shapes = [
        jax.ShapeDtypeStruct((length, width), low),
        jax.ShapeDtypeStruct((length, heads), low),
        jax.ShapeDtypeStruct((length, heads), low),
        jax.ShapeDtypeStruct((length, width), low),
        jax.ShapeDtypeStruct((length, width), low),
        jax.ShapeDtypeStruct((width, columns), low),
        jax.ShapeDtypeStruct((8, width), wide),
    ]
    return launch(
        project_kernel,
        deps,
        scalars=1,
        grid=(length // TILE,),
        in_specs=[rows(TILE, width)] + [fixed(p.shape) for p in pieces],
        out_specs=[
            rows(TILE, width),
            rows(TILE, heads),
            rows(TILE, heads),
            rows(TILE, width),
            rows(TILE, width),
            fixed((width, columns)),
            fixed((8, width)),
        ],
        out_shape=shapes,
        compiler_params=params(40),
        cost_estimate=cost(7, 22),
        name="project",
    )(offs, x, *pieces)


def shift_rows(v, seg, by, up):
    zeros = jnp.zeros((by, v.shape[1]), v.dtype)
    none = jnp.full((by, 1), -1, seg.dtype)
    if up:
        moved, moved_seg = jnp.concatenate([v[by:], zeros], 0), jnp.concatenate([seg[by:], none], 0)
    else:
        moved = jnp.concatenate([zeros, v[:-by]], 0)
        moved_seg = jnp.concatenate([none, seg[:-by]], 0)
    return jnp.where(moved_seg == seg, moved, 0.0)


def lane_pick(width, start, stop):
    i = lax.broadcasted_iota(jnp.int32, (1, width), 1)
    return (i >= start) & (i < stop)


def attend_kernel(
    first, q_ref, k_ref, v_ref, gate_ref, vec_ref, segr_ref, segc_ref, mixed_ref, att_ref, recip_ref, mask_ref
):
    length = q_ref.shape[0]
    pair = pl.program_id(0) + first
    zero = jnp.zeros((), low)

    @pl.when(pair == first)
    def _():
        for tb in range(0, length, TILE):
            t = lax.broadcasted_iota(jnp.int32, (TILE, length), 0) + tb
            s = lax.broadcasted_iota(jnp.int32, (TILE, length), 1)
            seen = (s <= t) & (segc_ref[tb : tb + TILE, :] == segr_ref[...])
            mask_ref[tb : tb + TILE, :] = jnp.where(seen, 1.0, 0.0).astype(low)

    v = v_ref[...]
    keys, sides = [], []
    for i in range(2):
        head = 2 * pair + i
        keys.append(jnp.where(lane_pick(HEADS * FEAT, head * FEAT, (head + 1) * FEAT), k_ref[...], zero))
        lanes = lane_pick(128, 64 * i, 64 * i + 64)
        ones = jnp.broadcast_to(jnp.where(lanes, 1.0, 0.0).astype(low), (length, 128))
        sides.append(jnp.concatenate([jnp.where(lanes, v, zero), ones], 1))
    for tb in range(0, length, TILE):
        n = tb + TILE
        total = None
        for i in range(2):
            one_plus = dot_nt(q_ref[tb:n, :], keys[i][:n]) + 1.0
            kernel = (one_plus * one_plus + 1.0).astype(low) * mask_ref[tb:n, :n]
            part = dot(kernel, sides[i][:n])
            total = part if total is None else total + part
        recip = 1.0 / total[:, 128:]
        att_ref[tb:n, :] = (total[:, :128] * recip).astype(low)
        recip_ref[tb:n, :] = (2.0 * recip).astype(low)
    v_wide = v.astype(wide)
    seg = segc_ref[...]
    conv = vec_ref[2:3, :] * v_wide
    for j in range(1, KW):
        conv = conv + vec_ref[2 + j : 3 + j, :] * shift_rows(v_wide, seg, j, False)
    mixed_ref[...] = (att_ref[...].astype(wide) + gate_ref[...].astype(wide) * conv).astype(low)


def whole(a):
    return pl.BlockSpec(a.shape, lambda p: (0, 0))


def attend(q, k, v, gate, vec, seg, first, count, onto=(), deps=()):
    length, width = v.shape
    column = pl.BlockSpec((length, 128), lambda p: (0, p + first))
    seg_row, seg_col = seg.reshape(1, length), seg.reshape(length, 1)
    return launch(
        functools.partial(attend_kernel, first),
        deps,
        onto,
        grid=(count,),
        in_specs=[
            whole(q), whole(k), column, column, pl.BlockSpec((8, 128), lambda p: (0, p + first)), whole(seg_row), whole(seg_col)
        ],
        out_specs=[column] * 3,
        out_shape=[jax.ShapeDtypeStruct((length, width), low)] * 3,
        scratch_shapes=[pltpu.VMEM((length, length), low)],
        compiler_params=params(40),
        cost_estimate=cost(18 * count * 128 / width, 14),
        name="attention_forward",
    )(q, k, v, gate, vec, seg_row, seg_col)


def attend_back_kernel(
    first, q_ref, k_ref, v_ref, gm_ref, att_ref, recip_ref, gconv_ref, segr_ref, segc_ref,
    gqk_ref, gv_ref, mask_ref, gq_acc, gk_acc,
):
    length, heads = q_ref.shape
    pair = pl.program_id(0) + first
    zero = jnp.zeros((), low)

    @pl.when(pair == first)
    def _():
        for sb in range(0, length, TILE):
            s = lax.broadcasted_iota(jnp.int32, (TILE, length), 0) + sb
            t = lax.broadcasted_iota(jnp.int32, (TILE, length), 1)
            seen = (s <= t) & (segc_ref[sb : sb + TILE, :] == segr_ref[...])
            mask_ref[sb : sb + TILE, :] = jnp.where(seen, 1.0, 0.0).astype(low)
        gk_acc[...] = jnp.zeros_like(gk_acc)
        gq_acc[...] = jnp.zeros_like(gq_acc)

    v = v_ref[...]
    gm = gm_ref[...].astype(wide)
    gnum_wide = gm * recip_ref[...].astype(wide)
    gnum = gnum_wide.astype(low)
    product = gnum_wide * att_ref[...].astype(wide)
    high = product.astype(low)
    rest = (product - high.astype(wide)).astype(low)
    r = lax.broadcasted_iota(jnp.int32, (256, 128), 0)
    c = lax.broadcasted_iota(jnp.int32, (256, 128), 1)
    same_head = jnp.where(((r % 128) // 64) == (c // 64), 1.0, 0.0).astype(low)
    gtot = -dot(jnp.concatenate([high, rest], 1), same_head)
    gtot_high = gtot.astype(low)
    gtot_rest = (gtot - gtot_high.astype(wide)).astype(low)
    lane = lax.broadcasted_iota(jnp.int32, (1, 128), 1)
    left = jnp.concatenate([gnum, jnp.where(lane % 64 == 0, gtot_high, gtot_rest)], 1)
    gnum_half = gnum * jnp.asarray(0.5, low)
    queries, sides, gnums, keys = [], [], [], []
    for i in range(2):
        head = 2 * pair + i
        mine = lane_pick(heads, head * FEAT, (head + 1) * FEAT)
        queries.append(jnp.where(mine, q_ref[...], zero))
        keys.append(jnp.where(mine, k_ref[...], zero))
        lanes = lane_pick(128, 64 * i, 64 * i + 64)
        ones = jnp.where(lane_pick(128, 64 * i, 64 * i + 2), 1.0, 0.0).astype(low)
        sides.append(jnp.concatenate([jnp.where(lanes, v, zero), jnp.broadcast_to(ones, (length, 128))], 1))
        gnums.append(jnp.where(lanes, gnum_half, zero))
    for sb in range(0, length, TILE):
        n = sb + TILE
        gv = gconv_ref[sb:n, :].astype(wide)
        gk = None
        for i in range(2):
            one_plus = dot_nt(k_ref[sb:n, :], queries[i][sb:]) + 1.0
            mask = mask_ref[sb:n, sb:]
            kernel = (one_plus * one_plus + 1.0).astype(low) * mask
            gv = gv + dot(kernel, gnums[i][sb:])
            gkernel = dot_nt(sides[i][sb:n], left[sb:])
            gscores = (gkernel * one_plus).astype(low) * mask
            part = dot(gscores, queries[i][sb:])
            gk = part if gk is None else gk + part
            gq_acc[sb:, :] += dot_tn(gscores, keys[i][sb:n])
        gv_ref[sb:n, :] = gv.astype(low)
        gk_acc[sb:n, :] += gk

    @pl.when(pl.program_id(0) == pl.num_programs(0) - 1)
    def _():
        mine = slice(2 * FEAT * first, 2 * FEAT * first + gqk_ref.shape[1] // 2)
        gqk_ref[:, : gqk_ref.shape[1] // 2] = (gq_acc[:, mine] * FEAT ** (-0.5)).astype(low)
        gqk_ref[:, gqk_ref.shape[1] // 2 :] = gk_acc[:, mine].astype(low)


def attend_back(q, k, v, gm, att, recip, gconv, seg, first, count, onto=(), deps=()):
    length, width = v.shape
    heads = q.shape[1]
    column = pl.BlockSpec((length, 128), lambda p: (0, p + first))
    seg_row, seg_col = seg.reshape(1, length), seg.reshape(length, 1)
    return launch(
        functools.partial(attend_back_kernel, first),
        deps,
        onto,
        grid=(count,),
        in_specs=[whole(q), whole(k)] + [column] * 5 + [whole(seg_row), whole(seg_col)],
        out_specs=[pl.BlockSpec((length, 4 * FEAT * count), lambda p: (0, first // count)), column],
        out_shape=[jax.ShapeDtypeStruct((length, 2 * heads), low), jax.ShapeDtypeStruct((length, width), low)],
        scratch_shapes=[
            pltpu.VMEM((length, length), low),
            pltpu.VMEM((length, heads), wide),
            pltpu.VMEM((length, heads), wide),
        ],
        compiler_params=params(48),
        cost_estimate=cost(40 * count * 128 / width, 18),
        name="attention_backward",
    )(q, k, v, gm, att, recip, gconv, seg_row, seg_col)


def conv_back_kernel(v_ref, gm_ref, gate_ref, vec_ref, segc_ref, ggate_ref, gconv_ref, gfilt_ref):
    v_wide = v_ref[...].astype(wide)
    gm = gm_ref[...].astype(wide)
    seg = segc_ref[...]
    taps = [vec_ref[2 + j : 3 + j, :] for j in range(KW)]
    grad = gm * gate_ref[...].astype(wide)
    conv = taps[0] * v_wide
    gv_conv = taps[0] * grad
    lines = [jnp.sum(grad * v_wide, 0, keepdims=True)]
    for j in range(1, KW):
        moved = shift_rows(v_wide, seg, j, False)
        conv = conv + taps[j] * moved
        lines.append(jnp.sum(grad * moved, 0, keepdims=True))
        gv_conv = gv_conv + taps[j] * shift_rows(grad, seg, j, True)
    lines.append(jnp.zeros((LANES - KW, 128), wide))
    gfilt_ref[...] = jnp.concatenate(lines, 0).T.astype(low)
    ggate_ref[...] = (gm * conv).astype(low)
    gconv_ref[...] = gv_conv.astype(low)


def conv_back(v, gm, gate, vec, seg, deps=()):
    length, width = v.shape
    column = pl.BlockSpec((length, 128), lambda p: (0, p))
    small = pl.BlockSpec((8, 128), lambda p: (0, p))
    seg_col = seg.reshape(length, 1)
    return launch(
        conv_back_kernel,
        deps,
        grid=(width // 128,),
        in_specs=[column, column, column, small, whole(seg_col)],
        out_specs=[column, column, pl.BlockSpec((128, LANES), lambda p: (p, 0))],
        out_shape=[jax.ShapeDtypeStruct((length, width), low)] * 2 + [jax.ShapeDtypeStruct((width, LANES), low)],
        compiler_params=params(48),
        cost_estimate=cost(1, 10),
        name="convolution_backward",
    )(v, gm, gate, vec, seg_col)


def mix_kernel(offs_ref, x_ref, mixed_ref, vec_ref, *refs):
    pieces, (middle_ref, hidden_ref, full_ref) = refs[:6], refs[6:]

    @pl.when(pl.program_id(0) == 0)
    def _():
        place(offs_ref, MIXER_AT, pieces, full_ref)

    middle = x_ref[...].astype(wide) + dot(mixed_ref[...], full_ref[...])
    inverse = lax.rsqrt(jnp.mean(middle * middle, axis=-1, keepdims=True) + EPS)
    middle_ref[...] = middle
    hidden_ref[...] = (middle * inverse * vec_ref[1:2, :]).astype(low)


def mix(offs, x, mixed, vec, pieces, deps=()):
    length, width = x.shape
    return launch(
        mix_kernel,
        deps,
        scalars=1,
        grid=(length // TILE,),
        in_specs=[rows(TILE, width), rows(TILE, width), fixed(vec.shape)] + [fixed(p.shape) for p in pieces],
        out_specs=[rows(TILE, width), rows(TILE, width), fixed((width, width))],
        out_shape=[
            jax.ShapeDtypeStruct((length, width), wide),
            jax.ShapeDtypeStruct((length, width), low),
            jax.ShapeDtypeStruct((width, width), low),
        ],
        compiler_params=params(32),
        cost_estimate=cost(3, 16),
        name="mix",
    )(offs, x, mixed, vec, *pieces)


def first_half(n):
    return lambda i, *_: (jnp.minimum(i, n - 1), 0)


def second_half(n):
    return lambda i, *_: (jnp.maximum(i - n, 0), 0)


def feed_kernel(n, offs_ref, ha_ref, hb_ref, ca_ref, cb_ref, *refs):
    pieces, downs, (act_ref, both_ref, full_ref, down_ref) = refs[:4], refs[4:7], refs[7:]
    step = pl.program_id(0)
    half = full_ref.shape[1] // 2

    @pl.when(step == 0)
    def _():
        place(offs_ref, FEED_AT, pieces, full_ref)
        place(offs_ref, DOWN_AT, downs, down_ref)

    def work(hidden, cotangent):
        for at in range(0, half, 256):
            gate = dot(hidden, full_ref[:, at : at + 256])
            up = dot(hidden, full_ref[:, half + at : half + at + 256])
            gact = dot_nt(cotangent, down_ref[at : at + 256, :])
            sig = jax.nn.sigmoid(gate)
            silu = gate * sig
            act_ref[:, at : at + 256] = (silu * up).astype(low)
            both_ref[:, at : at + 256] = (gact * up * (sig + silu * (1.0 - sig))).astype(low)
            both_ref[:, half + at : half + at + 256] = (gact * silu).astype(low)

    @pl.when(step < n)
    def _():
        work(ha_ref[...], ca_ref[...])

    @pl.when(step >= n)
    def _():
        work(hb_ref[...], cb_ref[...])


def feed(offs, hidden, cotangent, j, w_down, pieces, down_pieces, deps=()):
    length, width = hidden[0].shape
    n = length // TILE
    half = w_down.shape[0]
    first = pl.BlockSpec((TILE, width), first_half(n))
    second = pl.BlockSpec((TILE, width), second_half(n))
    own_down = pl.BlockSpec((half // 2, width), lambda *_: (j, 0), pipeline_mode=pl.Buffered(1))
    given_rows = pl.BlockSpec(pieces[0].shape, lambda *_: (j, 0), pipeline_mode=pl.Buffered(1))
    return launch(
        functools.partial(feed_kernel, n),
        deps,
        scalars=1,
        grid=(2 * n,),
        in_specs=[first, second, first, second]
        + [fixed(pieces[0].shape), given_rows]
        + [fixed(p.shape) for p in pieces[2:]]
        + [own_down]
        + [fixed(p.shape) for p in down_pieces],
        out_specs=[rows(TILE, half), rows(TILE, 2 * half), fixed((width, 2 * half)), fixed((half, width))],
        out_shape=[
            jax.ShapeDtypeStruct((2 * length, half), low),
            jax.ShapeDtypeStruct((2 * length, 2 * half), low),
            jax.ShapeDtypeStruct((width, 2 * half), low),
            jax.ShapeDtypeStruct((half, width), low),
        ],
        compiler_params=params(48),
        cost_estimate=cost(16, 34),
        name="feed_in",
    )(offs, *hidden, *cotangent, *pieces, w_down, *down_pieces)


def weight_grad_kernel(parts, counts, outs, length, offs_ref, *refs):
    blocks = sum(outs)
    lefts = [refs[b * parts : (b + 1) * parts] for b in range(blocks)]
    rights = refs[blocks * parts : -len(outs)]
    targets = [(ref, row * TILE) for ref, height in zip(refs[-len(outs) :], outs) for row in range(height)]
    terms = max(parts, len(rights) // len(counts))
    step = pl.program_id(0)

    def part_of(group, t):
        return group[t][...] if len(group) == terms else group[0][t * length : (t + 1) * length, :]

    def work(group):
        for b in range(blocks):
            value = None
            for t in range(terms):
                product = dot_tn(part_of(lefts[b], t), part_of(group, t))
                value = product if value is None else value + product
            ref, row = targets[b]
            ref[row : row + TILE, :] = value.astype(low)

    each = len(rights) // len(counts)
    start = 0
    for n, count in enumerate(counts):
        group = rights[n * each : (n + 1) * each]
        if len(counts) == 1:
            work(group)
        else:
            pl.when((step >= start) & (step < start + count))(functools.partial(work, group))
        start += count


def weight_grad(offs, base, lefts, rights, outs, name, tile=512, deps=()):
    blocks = sum(outs)
    counts = [group[0].shape[1] // tile for group in rights]
    columns = sum(counts) * tile
    in_specs, operands = [], []
    for b in range(blocks):
        for a in lefts:
            in_specs.append(pl.BlockSpec((a.shape[0], TILE), lambda j, offs, b=b: (0, offs[base + b])))
            operands.append(a)
    start = 0
    for group, count in zip(rights, counts):
        for a in group:
            def where_to(j, offs, start=start, count=count):
                return (0, jnp.clip(j - start, 0, count - 1))
            in_specs.append(pl.BlockSpec((a.shape[0], tile), where_to))
            operands.append(a)
        start += count
    tokens = sum(a.shape[0] for a in lefts)
    terms = max(len(lefts), len(rights[0]))
    result = launch(
        functools.partial(weight_grad_kernel, len(lefts), counts, outs, tokens // terms),
        deps,
        scalars=1,
        grid=(sum(counts),),
        in_specs=in_specs,
        out_specs=[pl.BlockSpec((height * TILE, tile), lambda j, offs: (0, j)) for height in outs],
        out_shape=[jax.ShapeDtypeStruct((height * TILE, columns), low) for height in outs],
        compiler_params=params(48),
        cost_estimate=cost(2.5e-9 * tokens * 1024 * columns, (tokens * (1024 + columns) * 2 + 2048 * columns) / 2**20),
        name=name,
    )(offs, *operands)
    return result


def feed_back_kernel(a_ref, b_ref, wa_ref, wb_ref, out_ref):
    out_ref[...] = (dot_nt(a_ref[...], wa_ref[...]) + dot_nt(b_ref[...], wb_ref[...])).astype(low)


def feed_back(first, second, full_first, full_second, deps=()):
    length = first.shape[0] // 2
    width = full_first.shape[0]
    n = length // TILE
    tile = pl.BlockSpec((TILE, first.shape[1]), lambda i: (i + n, 0))
    return launch(
        feed_back_kernel,
        deps,
        grid=(n,),
        in_specs=[tile, tile, fixed(full_first.shape), fixed(full_second.shape)],
        out_specs=rows(TILE, width),
        out_shape=jax.ShapeDtypeStruct((length, width), low),
        compiler_params=params(32),
        cost_estimate=cost(10, 18),
        name="feed_back_partner",
    )(first, second, full_first, full_second)


def middle_back_kernel(
    a_ref, b_ref, other_ref, middle_ref, cot_ref, vec_ref, wa_ref, wb_ref, wo_ref,
    gmiddle_ref, gbranch_ref, gmixed_ref, ggain_ref,
):
    ghidden = dot_nt(a_ref[...], wa_ref[...]) + dot_nt(b_ref[...], wb_ref[...]) + other_ref[...].astype(wide)
    middle = middle_ref[...]
    inverse = lax.rsqrt(jnp.mean(middle * middle, axis=-1, keepdims=True) + EPS)
    normed = middle * inverse
    gain = jnp.sum(ghidden * normed, axis=0, keepdims=True)

    @pl.when(pl.program_id(0) == 0)
    def _():
        ggain_ref[...] = jnp.zeros_like(ggain_ref)

    ggain_ref[0:1, :] += gain
    scaled = ghidden * vec_ref[1:2, :]
    gmiddle = cot_ref[...].astype(wide) + inverse * (
        scaled - normed * jnp.mean(scaled * normed, axis=-1, keepdims=True)
    )
    gmiddle_ref[...] = gmiddle
    gbranch = gmiddle.astype(low)
    gbranch_ref[...] = gbranch
    gmixed_ref[...] = dot_nt(gbranch, wo_ref[...]).astype(low)


def middle_back(first, second, other, middle, cotangent, vec, full_first, full_second, w_output, deps=()):
    length, width = middle.shape
    tile = rows(TILE, first.shape[1])
    line = rows(TILE, width)
    return launch(
        middle_back_kernel,
        deps,
        grid=(length // TILE,),
        in_specs=[
            tile, tile, line, line, line, fixed(vec.shape), fixed(full_first.shape), fixed(full_second.shape), fixed(w_output.shape)
        ],
        out_specs=[line, line, line, fixed((8, width))],
        out_shape=[
            jax.ShapeDtypeStruct((length, width), wide),
            jax.ShapeDtypeStruct((length, width), low),
            jax.ShapeDtypeStruct((length, width), low),
            jax.ShapeDtypeStruct((8, width), wide),
        ],
        compiler_params=params(48),
        cost_estimate=cost(13, 40),
        name="middle_back",
    )(first, second, other, middle, cotangent, vec, full_first, full_second, w_output)


def feed_out_kernel(add, *refs):
    out_ref = refs[-1]
    value = dot(refs[0][...], refs[2][...]) + dot(refs[1][...], refs[3][...])
    for ref in refs[4:-1]:
        value = value + ref[...].astype(wide)
    out_ref[...] = value.astype(low)


def feed_out(first, second, down_first, down_second, shift, extras, name, deps=()):
    length = first.shape[0] // 2
    width = down_first.shape[1]
    n = length // TILE
    tile = pl.BlockSpec((TILE, first.shape[1]), lambda i: (i + shift * n, 0))
    return launch(
        functools.partial(feed_out_kernel, len(extras)),
        deps,
        grid=(n,),
        in_specs=[tile, tile, fixed(down_first.shape), fixed(down_second.shape)] + [rows(TILE, width)] * len(extras),
        out_specs=rows(TILE, width),
        out_shape=jax.ShapeDtypeStruct((length, width), low),
        compiler_params=params(32),
        cost_estimate=cost(5, 16),
        name=name,
    )(first, second, down_first, down_second, *extras)


def tokens_back_kernel(gqk_ref, gv_ref, ggate_ref, x_ref, gmiddle_ref, vec_ref, full_ref, gtokens_ref, ggain_ref):
    two = gqk_ref.shape[1]
    width = x_ref.shape[1]
    quarter = two // 4
    ghidden = None
    for n, col in enumerate((0, 2, 1, 3)):
        term = dot_nt(gqk_ref[:, n * quarter : (n + 1) * quarter], full_ref[:, col * quarter : (col + 1) * quarter])
        ghidden = term if ghidden is None else ghidden + term
    ghidden = (
        ghidden
        + dot_nt(gv_ref[...], full_ref[:, two : two + width])
        + dot_nt(ggate_ref[...], full_ref[:, two + width : two + 2 * width])
    )
    x = x_ref[...].astype(wide)
    inverse = lax.rsqrt(jnp.mean(x * x, axis=-1, keepdims=True) + EPS)
    normed = x * inverse

    @pl.when(pl.program_id(0) == 0)
    def _():
        ggain_ref[...] = jnp.zeros_like(ggain_ref)

    ggain_ref[0:1, :] += jnp.sum(ghidden * normed, axis=0, keepdims=True)
    scaled = ghidden * vec_ref[0:1, :]
    gtokens_ref[...] = gmiddle_ref[...] + inverse * (
        scaled - normed * jnp.mean(scaled * normed, axis=-1, keepdims=True)
    )


def tokens_back(gqk, gv, ggate, x, gmiddle, vec, full, deps=()):
    length, width = x.shape
    line = rows(TILE, width)
    return launch(
        tokens_back_kernel,
        deps,
        grid=(length // TILE,),
        in_specs=[rows(TILE, gqk.shape[1]), line, line, line, line, fixed(vec.shape), fixed(full.shape)],
        out_specs=[line, fixed((8, width))],
        out_shape=[jax.ShapeDtypeStruct((length, width), wide), jax.ShapeDtypeStruct((8, width), wide)],
        compiler_params=params(40),
        cost_estimate=cost(7, 24),
        name="tokens_back",
    )(gqk, gv, ggate, x, gmiddle, vec, full)


def spread_kernel(cols_ref, gain_ref, wg_ref, wu_ref, a_ref, b_ref, c_ref, d_ref, gate_ref, up_ref, ggain_ref):
    total = None
    for n, ref in enumerate((a_ref, b_ref, c_ref, d_ref)):
        quarter = ref.shape[1] // 4
        for part_y in range(2):
            at = pl.ds(pl.multiple_of(cols_ref[COLS_AT + 2 * n + part_y], 512), quarter)
            gate = ref[:, part_y * quarter : (part_y + 1) * quarter].astype(wide)
            up = ref[:, (2 + part_y) * quarter : (3 + part_y) * quarter].astype(wide)
            gate_ref[:, at] = gate
            up_ref[:, at] = up
            term = gate * wg_ref[:, at].astype(wide) + up * wu_ref[:, at].astype(wide)
            line = jnp.sum(term, axis=1, keepdims=True)
            total = line if total is None else total + line
    ggain_ref[...] = total / gain_ref[...]


def spread(cols, gain, w_gate, w_up, blocks, deps=()):
    height, width = blocks[0].shape
    shape = jax.ShapeDtypeStruct((height, 2 * width), wide)
    return launch(
        spread_kernel,
        deps,
        scalars=1,
        grid=(1,),
        in_specs=[fixed(gain.shape), fixed(w_gate.shape), fixed(w_up.shape)] + [fixed(b.shape) for b in blocks],
        out_specs=[fixed(shape.shape)] * 2 + [fixed(gain.shape)],
        out_shape=[shape, shape, jax.ShapeDtypeStruct(gain.shape, wide)],
        compiler_params=params(24),
        cost_estimate=cost(0.001, 16),
        name="spread",
    )(cols, gain, w_gate, w_up, *blocks)


def pack_kernel(at_ref, g1_ref, g2_ref, taps_ref, q_ref, k_ref, v_ref, c_ref, o_ref, pack_ref, half_ref, ohalf_ref):
    height = q_ref.shape[0]
    col = 0
    for ref in (q_ref, k_ref, v_ref, c_ref):
        pack_ref[:, col : col + ref.shape[1]] = ref[...]
        col += ref.shape[1]
    small = jnp.concatenate([g1_ref[...].astype(wide), g2_ref[...].astype(wide), taps_ref[...].astype(wide)], 0)
    small = jnp.concatenate([small, jnp.zeros((LANES - small.shape[0], height), wide)], 0)
    pack_ref[:, col : col + LANES] = small.T.astype(low)
    at = pl.multiple_of(at_ref[X_AT] * (height // 2), 128)
    half_ref[...] = pack_ref[pl.ds(at, height // 2), :]
    ohalf_ref[...] = o_ref[pl.ds(at, height // 2), :]


def pack_mixer(at, gain_one, gain_two, taps, w_query, w_key, w_value, w_convgate, w_output):
    operands = (gain_one, gain_two, taps, w_query, w_key, w_value, w_convgate, w_output)
    height = w_query.shape[0]
    columns = w_query.shape[1] + w_key.shape[1] + w_value.shape[1] + w_convgate.shape[1] + LANES
    shapes = [(height, columns), (height // 2, columns), (height // 2, w_output.shape[1])]
    return launch(
        pack_kernel,
        scalars=1,
        grid=(1,),
        in_specs=[fixed(a.shape) for a in operands],
        out_specs=[fixed(a) for a in shapes],
        out_shape=[jax.ShapeDtypeStruct(a, low) for a in shapes],
        compiler_params=params(24),
        cost_estimate=cost(0.001, 4),
        name="pack_mixer",
    )(at, *operands)


def pack_feed_kernel(offs_ref, gate_ref, up_ref, down_ref, first_ref, second_ref, give_ref, low_ref, high_ref):
    height = gate_ref.shape[0]
    targets = ((first_ref, 0), (second_ref, 0), (give_ref, 0), (give_ref, height))
    for n, (ref, row) in enumerate(targets):
        quarter = ref.shape[1] // 4
        for part_y in range(2):
            at = pl.ds(pl.multiple_of(offs_ref[PACK_AT + 2 * n + part_y], 512), quarter)
            ref[row : row + height, part_y * quarter : (part_y + 1) * quarter] = gate_ref[:, at]
            ref[row : row + height, (2 + part_y) * quarter : (3 + part_y) * quarter] = up_ref[:, at]
    size = low_ref.shape[0]
    for turn, ref in enumerate((low_ref, high_ref)):
        at = pl.multiple_of(offs_ref[X_AT] * size + turn * 2 * size, 128)
        ref[...] = down_ref[pl.ds(at, size), :]


def pack_feed(offs, w_gate, w_up, w_down, deps=()):
    height, columns = w_gate.shape
    shapes = [(height, columns // 2)] * 2 + [(2 * height, columns // 2)] + [(w_down.shape[0] // 4, w_down.shape[1])] * 2
    return launch(
        pack_feed_kernel,
        deps,
        scalars=1,
        grid=(1,),
        in_specs=[fixed(w_gate.shape), fixed(w_up.shape), fixed(w_down.shape)],
        out_specs=[fixed(a) for a in shapes],
        out_shape=[jax.ShapeDtypeStruct(a, low) for a in shapes],
        compiler_params=params(24),
        cost_estimate=cost(0.001, 8),
        name="pack_feed",
    )(offs, w_gate, w_up, w_down)


def step(kernel, offs, operands, shapes, name, deps=()):
    return launch(
        kernel,
        deps,
        scalars=1,
        grid=(1,),
        in_specs=[fixed(a.shape) for a in operands],
        out_specs=[fixed(a) for a in shapes],
        out_shape=[jax.ShapeDtypeStruct(a, low) for a in shapes],
        compiler_params=params(24),
        cost_estimate=cost(0.001, 8),
        name=name,
    )(offs, *operands)


def pick_kernel(offs_ref, first_ref, second_ref, given_ref, a_ref, b_ref):
    height = first_ref.shape[0]

    @pl.when(offs_ref[X_AT] == 0)
    def _():
        a_ref[...] = first_ref[...]
        b_ref[...] = second_ref[...]

    @pl.when(offs_ref[X_AT] != 0)
    def _():
        a_ref[...] = given_ref[:height, :]
        b_ref[...] = given_ref[height:, :]


def add(*refs):
    total = refs[0].astype(wide)
    for other in refs[1:]:
        total = total + other.astype(wide)
    return total.astype(low)


def top_kernel(offs_ref, keep_ref, came_ref, give_ref):
    size = give_ref.shape[0]
    give_ref[...] = add(keep_ref[:size, :], came_ref[:size, :])


def top_sum(offs, keep, came, deps=()):
    return step(top_kernel, offs, [keep, came], [(keep.shape[0] // 2, keep.shape[1])], "top_sum", deps)[0]


def rest_kernel(offs_ref, *refs):
    out_ref = refs[-1]
    col = 0
    for n in range(0, len(refs) - 1, 3):
        keep_ref, came_ref, passed_ref = refs[n : n + 3]
        size, width = passed_ref.shape
        skip = came_ref.shape[0] - size
        out_ref[:, col : col + width] = add(keep_ref[size:, :], came_ref[skip:, :], passed_ref[...])
        col += width


def rest_sum(offs, triples, deps=()):
    operands = [a for triple in triples for a in triple]
    shape = (triples[0][2].shape[0], sum(t[2].shape[1] for t in triples))
    return step(rest_kernel, offs, operands, [shape], "rest_sum", deps)[0]


def halves_kernel(filters, offs_ref, *refs):
    top_ref, rest_ref = refs[-2:]
    size = top_ref.shape[0]
    col = 0
    for n in range(0, len(refs) - 2, 2):
        keep_ref, came_ref = refs[n : n + 2]
        at = slice(col, col + keep_ref.shape[1])
        col += keep_ref.shape[1]
        if filters and n == len(refs) - 4:
            for ref, line in ((top_ref, offs_ref[OWNER_AT + 2]), (rest_ref, offs_ref[OWNER_AT + 3])):
                rows_at = pl.ds(pl.multiple_of(line * size, 128), size)
                ref[:, at] = add(keep_ref[rows_at, :], came_ref[rows_at, :])
        else:
            top_ref[:, at] = add(keep_ref[:size, :], came_ref[:size, :])
            rest_ref[:, at] = add(keep_ref[size:, :], came_ref[size:, :])


def halves_sum(offs, pairs, filters=False, deps=()):
    operands = [a for pair in pairs for a in pair]
    shape = (pairs[0][0].shape[0] // 2, sum(pair[0].shape[1] for pair in pairs))
    return step(functools.partial(halves_kernel, filters), offs, operands, [shape] * 2, "halves_sum", deps)


def near_kernel(offs_ref, keep_ref, came_ref, own_ref, other_ref):
    size = own_ref.shape[0]
    for ref, side in ((own_ref, offs_ref[X_AT]), (other_ref, 1 - offs_ref[X_AT])):
        at = pl.ds(pl.multiple_of(side * size, 128), size)
        ref[...] = add(keep_ref[at, :], came_ref[at, :])


def near_split(offs, keep, came, deps=()):
    return step(near_kernel, offs, [keep, came], [(keep.shape[0] // 2, keep.shape[1])] * 2, "near_split", deps)


def pair_kernel(offs_ref, a_ref, b_ref, out_ref):
    out_ref[...] = add(a_ref[...], b_ref[...])


def pair_sum(offs, a, b, deps=()):
    return step(pair_kernel, offs, [a, b], [a.shape], "pair_sum", deps)[0]


def sort_kernel(offs_ref, total_ref, other_ref, own_ref, give_ref):
    @pl.when(offs_ref[X_AT + 1] == 0)
    def _():
        own_ref[...] = total_ref[...]
        give_ref[...] = other_ref[...]

    @pl.when(offs_ref[X_AT + 1] != 0)
    def _():
        own_ref[...] = other_ref[...]
        give_ref[...] = total_ref[...]


def sort_rows(offs, total, other, deps=()):
    return step(sort_kernel, offs, [total, other], [total.shape] * 2, "sort_rows", deps)


def swap(value, axis):
    return lax.ppermute(value, axis, [(0, 1), (1, 0)])


def part(value, index, count, axis=0):
    size = value.shape[axis] // count
    return lax.dynamic_slice_in_dim(value, index * size, size, axis)


def in_order(index, mine, other):
    return jnp.where(
        index == 0, jnp.concatenate([mine, other], 0), jnp.concatenate([other, mine], 0)
    )


def per_device(
    tokens, segment_ids, gain_one, w_query, w_key, w_value, w_convgate, w_output, conv_filter,
    gain_two, w_gate, w_up, w_down, cotangent,
):
    Order.last = None
    x = lax.axis_index("near")
    y = lax.axis_index("row")
    c = lax.axis_index("core")
    s = 2 * y + c
    width = tokens.shape[1]
    seg = segment_ids[0]
    block = w_down.shape[0]

    def flip(bits):
        return jnp.bitwise_xor(s, bits)

    small_block = block // 2
    half = SHARD_ROWS // 2

    def feed_cols(core, j):
        return [((2 * row + core) * 2 + j) * small_block for row in range(2)]

    feed_rows = [s, flip(1), jnp.bitwise_xor(flip(2), x), jnp.bitwise_xor(flip(3), x)]
    offs = [
        x,
        jnp.bitwise_xor(x, c),
        s * SHARD_ROWS,
        flip(1) * SHARD_ROWS,
        flip(2) * SHARD_ROWS + x * half,
        flip(2) * SHARD_ROWS + (1 - x) * half,
        flip(3) * SHARD_ROWS + x * half,
        flip(3) * SHARD_ROWS + (1 - x) * half,
        *(a * SHARD_ROWS for a in feed_rows),
        y * small_block,
        (1 - y) * small_block + x * (small_block // 2),
        (1 - y) * small_block + (1 - x) * (small_block // 2),
        0,
        *feed_cols(c, 0), *feed_cols(c, 1), *feed_cols(1 - c, 0), *feed_cols(1 - c, 1),
        *feed_cols(c, 0), *feed_cols(1 - c, 0), *feed_cols(c, 1), *feed_cols(1 - c, 1),
        2 * (1 - y) + 1 - x, 2 * (1 - y) + x, 2 * y + 1 - x, 2 * y + x,
        flip(3), flip(1), flip(2), s,
        2 * (1 - y) + 1 - x, 2 * y + 1 - x, 2 * (1 - y) + x, 2 * y + x,
    ]
    offs = jnp.stack([jnp.asarray(a, jnp.int32) for a in offs])

    pack, pack_half, output_half = pack_mixer(
        offs, gain_one[None], gain_two[None], conv_filter, w_query, w_key, w_value, w_convgate, w_output
    )

    def fetch(own, own_half):
        near_core = swap(own, "core")
        direct = swap(own_half, "row")
        relayed = swap(direct, "near")
        return [own, near_core, direct, relayed, swap(direct, "core"), swap(relayed, "core")]

    pack_pieces = fetch(pack, pack_half)
    output_pieces = fetch(w_output, output_half)
    cot_other = swap(cotangent, "core")

    mine_first, mine_second, give, *down_halves = pack_feed(offs, w_gate, w_up, w_down)
    given = swap(give, "core")
    sends = step(pick_kernel, offs, [mine_first, mine_second, given], [mine_first.shape] * 2, "pick")
    feed_pieces, down_pieces = [], []
    for j, own in enumerate((mine_first, mine_second)):
        direct = swap(sends[j], "row")
        feed_pieces.append([own, given, direct, swap(direct, "near")])
        direct = swap(down_halves[j], "row")
        down_pieces.append([direct, swap(direct, "near")])

    hidden_one, queries, keys, values, gates, full_one, vec = project(
        offs, tokens, pack_pieces, deps=[cot_other, output_pieces[1], output_pieces[2]]
    )
    pairs = width // 256
    attended = attend(
        queries, keys, values, gates, vec, seg, 0, pairs, deps=[output_pieces[3], output_pieces[4]]
    )
    mixed, attention, recips = attend(
        queries, keys, values, gates, vec, seg, pairs, pairs, onto=attended, deps=[feed_pieces[0][2], output_pieces[5]]
    )
    middle, hidden_two, full_output = mix(offs, tokens, mixed, vec, output_pieces, deps=[down_pieces[0][0]])
    hiddens = [hidden_two, swap(hidden_two, "core")]
    cots = [cotangent, cot_other]

    def after(value, other):
        return value if other is None else lax.optimization_barrier((value, other))[0]

    def far_sum(part, previous):
        return lax.psum(after(part, previous), "far")

    def far_swap(value, bit):
        count = lax.axis_size("far")
        if bit >= count:
            return None
        return lax.ppermute(value, "far", [(i, i ^ bit) for i in range(count)])

    def far_rest(value, came):
        value = pair_sum(offs, value, came)
        bit = 4
        while bit < lax.axis_size("far"):
            value = pair_sum(offs, value, far_swap(value, bit))
            bit *= 2
        return value

    first_feed = feed(offs, hiddens, cots, 0, w_down, feed_pieces[0], down_pieces[0], deps=[feed_pieces[1][2]])
    down_send, down_keep = weight_grad(
        offs, ACT_AT, [first_feed[0]], [cots], (2, 2), "grad_down", deps=[down_pieces[1][0]]
    )
    down_came = swap(down_send, "near")
    gate_send, gate_send_own, gate_keep = weight_grad(
        offs, GRAD_AT, hiddens, [[first_feed[1]]], (1, 1, 2), "grad_gate_up"
    )
    gate_came, gate_came_own = swap(gate_send, "row"), swap(gate_send_own, "row")
    second_feed = feed(offs, hiddens, cots, 1, w_down, feed_pieces[1], down_pieces[1])
    gate_passed = swap(top_sum(offs, gate_keep, gate_came), "near")
    down_passed = swap(top_sum(offs, down_keep, down_came), "row")
    down_send_2, down_keep_2 = weight_grad(offs, ACT_AT, [second_feed[0]], [cots], (2, 2), "grad_down")
    down_came_2 = swap(down_send_2, "near")
    gate_send_2, gate_send_own_2, gate_keep_2 = weight_grad(
        offs, GRAD_AT, hiddens, [[second_feed[1]]], (1, 1, 2), "grad_gate_up"
    )
    gate_came_2, gate_came_own_2 = swap(gate_send_2, "row"), swap(gate_send_own_2, "row")
    acts, boths, fulls, downs = zip(first_feed, second_feed)
    gate_total = far_sum(rest_sum(offs, [(gate_keep, gate_came_own, gate_passed)]), None)
    ghidden_part = feed_back(boths[0], boths[1], fulls[0], fulls[1])
    ghidden_other = swap(ghidden_part, "core")
    down_sum = rest_sum(offs, [(down_keep, down_came, down_passed)])
    down_far = far_swap(down_sum, 1)
    gmiddle, gbranch, gmixed, _ = middle_back(
        boths[0], boths[1], ghidden_other, middle, cotangent, vec, fulls[0], fulls[1], full_output
    )
    gate_passed_2 = swap(top_sum(offs, gate_keep_2, gate_came_2), "near")
    down_passed_2 = swap(top_sum(offs, down_keep_2, down_came_2), "row")
    down_sum = pair_sum(offs, down_sum, down_far)
    down_far = far_swap(down_sum, 2)

    output_send, output_keep = weight_grad(offs, OWNER_AT, [mixed], [[gbranch]], (2, 2), "grad_output")
    output_came = swap(output_send, "core")
    ggate, gconv, gfilter = conv_back(values, gmixed, gates, vec, seg)
    filter_came = swap(gfilter, "core")
    convgate_send, convgate_keep = weight_grad(
        offs, OWNER_AT, [hidden_one], [[ggate]], (2, 2), "grad_convgate", deps=[output_came]
    )
    convgate_came = swap(convgate_send, "core")
    gate_total_2 = far_sum(rest_sum(offs, [(gate_keep_2, gate_came_own_2, gate_passed_2)]), gate_total)
    attended = attend_back(
        queries, keys, values, gmixed, attention, recips, gconv, seg, 0, pairs, deps=[filter_came]
    )
    early_give, early_held = halves_sum(
        offs, [(output_keep, output_came), (convgate_keep, convgate_came), (gfilter, filter_came)], True
    )
    early_came = swap(early_give, "row")
    down_sum_2 = rest_sum(offs, [(down_keep_2, down_came_2, down_passed_2)])
    down_far_2 = far_swap(down_sum_2, 1)
    down_sum = far_rest(down_sum, down_far)
    down_other = swap(down_sum, "near")
    gqk, gv = attend_back(
        queries, keys, values, gmixed, attention, recips, gconv, seg, pairs, pairs, onto=attended
    )
    down_sum_2 = pair_sum(offs, down_sum_2, down_far_2)
    down_far_2 = far_swap(down_sum_2, 2)
    early_own, early_other = near_split(offs, early_held, early_came)
    early_passed = swap(early_other, "near")
    late_send, late_keep = weight_grad(offs, OWNER_AT, [hidden_one], [[gqk], [gv]], (2, 2), "grad_query_key_value")
    late_came = swap(late_send, "core")
    grad_tokens, _ = tokens_back(gqk, gv, ggate, tokens, gmiddle, vec, full_one)
    late_give, late_held = halves_sum(offs, [(late_keep, late_came)])
    late_came = swap(late_give, "row")
    early = pair_sum(offs, early_own, early_passed)
    early_far = far_swap(early, 1)
    out_part = feed_out(acts[0], acts[1], downs[0], downs[1], 1, [], "feed_out_partner")
    out_came = swap(out_part, "core")
    down_sum_2 = far_rest(down_sum_2, down_far_2)
    down_other_2 = swap(down_sum_2, "near")
    gate_other = swap(gate_total, "near")
    early = pair_sum(offs, early, early_far)
    early_far = far_swap(early, 2)
    late_own, late_other = near_split(offs, late_held, late_came)
    late_passed = swap(late_other, "near")
    result = feed_out(acts[0], acts[1], downs[0], downs[1], 0, [middle, out_came], "feed_out")
    own_rows, theirs = sort_rows(offs, gate_total, gate_other)
    spreads = [own_rows, swap(theirs, "core")]
    late = pair_sum(offs, late_own, late_passed)
    late_far = far_swap(late, 1)
    gate_other = swap(gate_total_2, "near")
    early = far_rest(early, early_far)
    early_other = swap(early, "near")
    late = pair_sum(offs, late, late_far)
    late_far = far_swap(late, 2)
    own_rows, theirs = sort_rows(offs, gate_total_2, gate_other)
    spreads += [own_rows, swap(theirs, "core")]
    late = far_rest(late, late_far)
    late_other = swap(late, "near")
    grad_gate, grad_up, ggain_two = spread(offs, gain_two[:, None].astype(wide), w_gate, w_up, spreads)

    grad_down = jnp.concatenate(
        [in_order(x, down_sum, down_other), in_order(x, down_sum_2, down_other_2)], 0
    ).astype(wide)
    early = in_order(x, early, early_other).astype(wide)
    late = in_order(x, late, late_other).astype(wide)
    heads = HEADS * FEAT
    quarters = [late[:, n * heads // 2 : (n + 1) * heads // 2] for n in range(4)]
    grads = (
        jnp.concatenate([quarters[0], quarters[2]], 1),
        jnp.concatenate([quarters[1], quarters[3]], 1),
        late[:, 2 * heads :],
        early[:, width : 2 * width],
    )
    ggain_one = sum(
        jnp.sum(g * w.astype(wide), axis=1) for g, w in zip(grads, (w_query, w_key, w_value, w_convgate))
    ) / gain_one.astype(wide)
    return (
        result,
        grad_tokens,
        ggain_one,
        *grads,
        early[:, :width],
        early[:, 2 * width : 2 * width + KW].T,
        ggain_two[:, 0],
        grad_gate,
        grad_up,
        grad_down,
    )


def solution(mesh):
    replicas, shards = mesh.shape["rep"], mesh.shape["shard"]
    devices = np.asarray(mesh.devices).reshape(replicas // 2, 2, shards // 2, 2)
    fine = Mesh(devices, ("far", "near", "row", "core"))
    token = P(("far", "near", "row", "core"), None)
    line = P(("row", "core"))
    weight = P(("row", "core"), None)
    taps = P(None, ("row", "core"))
    return jax.shard_map(
        per_device,
        mesh=fine,
        in_specs=(
            token, token, line, weight, weight, weight, weight, weight, taps, line, weight, weight, weight, token
        ),
        out_specs=(
            token, token, line, weight, weight, weight, weight, weight, taps, line, weight, weight, weight
        ),
        check_vma=False,
    )
```

```python
import functools

import jax
import jax.numpy as jnp
import numpy as np
from jax import lax
from jax.experimental import pallas as pl
from jax.experimental.pallas import tpu as pltpu
from jax.sharding import Mesh
from jax.sharding import PartitionSpec as P

HEADS = 16
FEAT = 16
KW = 3
EPS = 1e-06
TILE = 256
SHARD_ROWS = 256
LANES = 128
TICK = 1e5
X_AT, MIXER_AT, FEED_AT, DOWN_AT, PACK_AT, COLS_AT, GRAD_AT, OWNER_AT, ACT_AT = 0, 2, 8, 12, 16, 24, 32, 36, 40

low = jnp.bfloat16
wide = jnp.float32


def dot(a, b):
    return jnp.dot(a, b, preferred_element_type=wide)


def dot_nt(a, b):
    return lax.dot_general(a, b, (((1,), (1,)), ((), ())), preferred_element_type=wide)


def dot_tn(a, b):
    return lax.dot_general(a, b, (((0,), (0,)), ((), ())), preferred_element_type=wide)


class Order:
    last = None
    scale = 1.0


def launch(kernel, deps=(), onto=(), *, scalars=0, grid, in_specs, out_specs, out_shape, scratch_shapes=(), **rest):
    taken = scalars + len(in_specs)
    deps = list(onto) + [d for d in deps if d is not None] + ([] if Order.last is None else [Order.last])

    def body(*refs):
        kernel(*refs[:taken], *refs[taken + len(deps) :])

    spec = pltpu.PrefetchScalarGridSpec(
        num_scalar_prefetch=scalars,
        grid=grid,
        in_specs=list(in_specs) + [pl.BlockSpec(memory_space=pl.ANY)] * len(deps),
        out_specs=out_specs,
        scratch_shapes=list(scratch_shapes),
    )
    aliases = {taken + n: n for n in range(len(onto))}
    run = pl.pallas_call(body, grid_spec=spec, out_shape=out_shape, input_output_aliases=aliases, **rest)

    def call(*operands):
        result = run(*operands, *deps)
        Order.last = result[0] if isinstance(result, (list, tuple)) else result
        return result

    return call


def params(mib):
    return pltpu.CompilerParams(vmem_limit_bytes=max(mib, 60) << 20)


def cost(gigaflops, mebibytes):
    return pl.CostEstimate(
        flops=int(gigaflops * Order.scale * 1e9), bytes_accessed=int(mebibytes * Order.scale * (1 << 20)), transcendentals=0
    )


def fixed(shape):
    return pl.BlockSpec(shape, lambda *_: (0,) * len(shape), pipeline_mode=pl.Buffered(1))


def rows(height, width):
    return pl.BlockSpec((height, width), lambda i, *_: (i, 0))


def place(offs_ref, base, pieces, full_ref):
    for n, piece in enumerate(pieces):
        at = pl.multiple_of(offs_ref[base + n], 128)
        full_ref[pl.ds(at, piece.shape[0]), :] = piece[...]


def project_kernel(offs_ref, x_ref, *refs):
    pieces, (hidden_ref, q_ref, k_ref, v_ref, gate_ref, full_ref, vec_ref) = refs[:6], refs[6:]
    heads = HEADS * FEAT
    width = x_ref.shape[1]

    @pl.when(pl.program_id(0) == 0)
    def _():
        place(offs_ref, MIXER_AT, pieces, full_ref)
        small = full_ref[:, 2 * heads + 3 * width :].astype(wide)
        vec_ref[...] = small.T[:8, :]

    x = x_ref[...].astype(wide)
    inverse = lax.rsqrt(jnp.mean(x * x, axis=-1, keepdims=True) + EPS)
    hidden = (x * inverse * vec_ref[0:1, :]).astype(low)
    hidden_ref[...] = hidden
    at = width
    q_ref[...] = (dot(hidden, full_ref[:, at : at + heads]) * FEAT ** (-0.5)).astype(low)
    k_ref[...] = dot(hidden, full_ref[:, at + heads : at + 2 * heads]).astype(low)
    at = at + 2 * heads
    v_ref[...] = dot(hidden, full_ref[:, at : at + width]).astype(low)
    gate_ref[...] = dot(hidden, full_ref[:, at + width : at + 2 * width]).astype(low)


def project(offs, x, pieces, deps=()):
    length, width = x.shape
    heads = HEADS * FEAT
    columns = pieces[0].shape[1]
    shapes = [
        jax.ShapeDtypeStruct((length, width), low),
        jax.ShapeDtypeStruct((length, heads), low),
        jax.ShapeDtypeStruct((length, heads), low),
        jax.ShapeDtypeStruct((length, width), low),
        jax.ShapeDtypeStruct((length, width), low),
        jax.ShapeDtypeStruct((width, columns), low),
        jax.ShapeDtypeStruct((8, width), wide),
    ]
    return launch(
        project_kernel,
        deps,
        scalars=1,
        grid=(length // TILE,),
        in_specs=[rows(TILE, width)] + [fixed(p.shape) for p in pieces],
        out_specs=[
            rows(TILE, width),
            rows(TILE, heads),
            rows(TILE, heads),
            rows(TILE, width),
            rows(TILE, width),
            fixed((width, columns)),
            fixed((8, width)),
        ],
        out_shape=shapes,
        compiler_params=params(40),
        cost_estimate=cost(7, 22),
        name="project",
    )(offs, x, *pieces)


def shift_rows(v, seg, by, up):
    zeros = jnp.zeros((by, v.shape[1]), v.dtype)
    none = jnp.full((by, 1), -1, seg.dtype)
    if up:
        moved, moved_seg = jnp.concatenate([v[by:], zeros], 0), jnp.concatenate([seg[by:], none], 0)
    else:
        moved = jnp.concatenate([zeros, v[:-by]], 0)
        moved_seg = jnp.concatenate([none, seg[:-by]], 0)
    return jnp.where(moved_seg == seg, moved, 0.0)


def lane_pick(width, start, stop):
    i = lax.broadcasted_iota(jnp.int32, (1, width), 1)
    return (i >= start) & (i < stop)


def attend_kernel(
    first, q_ref, k_ref, v_ref, gate_ref, vec_ref, segr_ref, segc_ref, mixed_ref, att_ref, recip_ref, mask_ref
):
    length = q_ref.shape[0]
    pair = pl.program_id(0) + first
    zero = jnp.zeros((), low)

    @pl.when(pair == first)
    def _():
        for tb in range(0, length, TILE):
            t = lax.broadcasted_iota(jnp.int32, (TILE, length), 0) + tb
            s = lax.broadcasted_iota(jnp.int32, (TILE, length), 1)
            seen = (s <= t) & (segc_ref[tb : tb + TILE, :] == segr_ref[...])
            mask_ref[tb : tb + TILE, :] = jnp.where(seen, 1.0, 0.0).astype(low)

    v = v_ref[...]
    keys, sides = [], []
    for i in range(2):
        head = 2 * pair + i
        keys.append(jnp.where(lane_pick(HEADS * FEAT, head * FEAT, (head + 1) * FEAT), k_ref[...], zero))
        lanes = lane_pick(128, 64 * i, 64 * i + 64)
        ones = jnp.broadcast_to(jnp.where(lanes, 1.0, 0.0).astype(low), (length, 128))
        sides.append(jnp.concatenate([jnp.where(lanes, v, zero), ones], 1))
    for tb in range(0, length, TILE):
        n = tb + TILE
        total = None
        for i in range(2):
            one_plus = dot_nt(q_ref[tb:n, :], keys[i][:n]) + 1.0
            kernel = (one_plus * one_plus + 1.0).astype(low) * mask_ref[tb:n, :n]
            part = dot(kernel, sides[i][:n])
            total = part if total is None else total + part
        recip = 1.0 / total[:, 128:]
        att_ref[tb:n, :] = (total[:, :128] * recip).astype(low)
        recip_ref[tb:n, :] = (2.0 * recip).astype(low)
    v_wide = v.astype(wide)
    seg = segc_ref[...]
    conv = vec_ref[2:3, :] * v_wide
    for j in range(1, KW):
        conv = conv + vec_ref[2 + j : 3 + j, :] * shift_rows(v_wide, seg, j, False)
    mixed_ref[...] = (att_ref[...].astype(wide) + gate_ref[...].astype(wide) * conv).astype(low)


def whole(a):
    return pl.BlockSpec(a.shape, lambda p: (0, 0))


def attend(q, k, v, gate, vec, seg, first, count, onto=(), deps=()):
    length, width = v.shape
    column = pl.BlockSpec((length, 128), lambda p: (0, p + first))
    seg_row, seg_col = seg.reshape(1, length), seg.reshape(length, 1)
    return launch(
        functools.partial(attend_kernel, first),
        deps,
        onto,
        grid=(count,),
        in_specs=[
            whole(q), whole(k), column, column, pl.BlockSpec((8, 128), lambda p: (0, p + first)), whole(seg_row), whole(seg_col)
        ],
        out_specs=[column] * 3,
        out_shape=[jax.ShapeDtypeStruct((length, width), low)] * 3,
        scratch_shapes=[pltpu.VMEM((length, length), low)],
        compiler_params=params(40),
        cost_estimate=cost(18 * count * 128 / width, 14),
        name="attention_forward",
    )(q, k, v, gate, vec, seg_row, seg_col)


def attend_back_kernel(
    first, q_ref, k_ref, v_ref, gm_ref, att_ref, recip_ref, gconv_ref, segr_ref, segc_ref,
    gqk_ref, gv_ref, mask_ref, gq_acc, gk_acc,
):
    length, heads = q_ref.shape
    pair = pl.program_id(0) + first
    zero = jnp.zeros((), low)

    @pl.when(pair == first)
    def _():
        for sb in range(0, length, TILE):
            s = lax.broadcasted_iota(jnp.int32, (TILE, length), 0) + sb
            t = lax.broadcasted_iota(jnp.int32, (TILE, length), 1)
            seen = (s <= t) & (segc_ref[sb : sb + TILE, :] == segr_ref[...])
            mask_ref[sb : sb + TILE, :] = jnp.where(seen, 1.0, 0.0).astype(low)
        gk_acc[...] = jnp.zeros_like(gk_acc)
        gq_acc[...] = jnp.zeros_like(gq_acc)

    v = v_ref[...]
    gm = gm_ref[...].astype(wide)
    gnum_wide = gm * recip_ref[...].astype(wide)
    gnum = gnum_wide.astype(low)
    product = gnum_wide * att_ref[...].astype(wide)
    high = product.astype(low)
    rest = (product - high.astype(wide)).astype(low)
    r = lax.broadcasted_iota(jnp.int32, (256, 128), 0)
    c = lax.broadcasted_iota(jnp.int32, (256, 128), 1)
    same_head = jnp.where(((r % 128) // 64) == (c // 64), 1.0, 0.0).astype(low)
    gtot = -dot(jnp.concatenate([high, rest], 1), same_head)
    gtot_high = gtot.astype(low)
    gtot_rest = (gtot - gtot_high.astype(wide)).astype(low)
    lane = lax.broadcasted_iota(jnp.int32, (1, 128), 1)
    left = jnp.concatenate([gnum, jnp.where(lane % 64 == 0, gtot_high, gtot_rest)], 1)
    gnum_half = gnum * jnp.asarray(0.5, low)
    queries, sides, gnums, keys = [], [], [], []
    for i in range(2):
        head = 2 * pair + i
        mine = lane_pick(heads, head * FEAT, (head + 1) * FEAT)
        queries.append(jnp.where(mine, q_ref[...], zero))
        keys.append(jnp.where(mine, k_ref[...], zero))
        lanes = lane_pick(128, 64 * i, 64 * i + 64)
        ones = jnp.where(lane_pick(128, 64 * i, 64 * i + 2), 1.0, 0.0).astype(low)
        sides.append(jnp.concatenate([jnp.where(lanes, v, zero), jnp.broadcast_to(ones, (length, 128))], 1))
        gnums.append(jnp.where(lanes, gnum_half, zero))
    for sb in range(0, length, TILE):
        n = sb + TILE
        gv = gconv_ref[sb:n, :].astype(wide)
        gk = None
        for i in range(2):
            one_plus = dot_nt(k_ref[sb:n, :], queries[i][sb:]) + 1.0
            mask = mask_ref[sb:n, sb:]
            kernel = (one_plus * one_plus + 1.0).astype(low) * mask
            gv = gv + dot(kernel, gnums[i][sb:])
            gkernel = dot_nt(sides[i][sb:n], left[sb:])
            gscores = (gkernel * one_plus).astype(low) * mask
            part = dot(gscores, queries[i][sb:])
            gk = part if gk is None else gk + part
            gq_acc[sb:, :] += dot_tn(gscores, keys[i][sb:n])
        gv_ref[sb:n, :] = gv.astype(low)
        gk_acc[sb:n, :] += gk

    @pl.when(pl.program_id(0) == pl.num_programs(0) - 1)
    def _():
        mine = slice(2 * FEAT * first, 2 * FEAT * first + gqk_ref.shape[1] // 2)
        gqk_ref[:, : gqk_ref.shape[1] // 2] = (gq_acc[:, mine] * FEAT ** (-0.5)).astype(low)
        gqk_ref[:, gqk_ref.shape[1] // 2 :] = gk_acc[:, mine].astype(low)


def attend_back(q, k, v, gm, att, recip, gconv, seg, first, count, onto=(), deps=()):
    length, width = v.shape
    heads = q.shape[1]
    column = pl.BlockSpec((length, 128), lambda p: (0, p + first))
    seg_row, seg_col = seg.reshape(1, length), seg.reshape(length, 1)
    return launch(
        functools.partial(attend_back_kernel, first),
        deps,
        onto,
        grid=(count,),
        in_specs=[whole(q), whole(k)] + [column] * 5 + [whole(seg_row), whole(seg_col)],
        out_specs=[pl.BlockSpec((length, 4 * FEAT * count), lambda p: (0, first // count)), column],
        out_shape=[jax.ShapeDtypeStruct((length, 2 * heads), low), jax.ShapeDtypeStruct((length, width), low)],
        scratch_shapes=[
            pltpu.VMEM((length, length), low),
            pltpu.VMEM((length, heads), wide),
            pltpu.VMEM((length, heads), wide),
        ],
        compiler_params=params(48),
        cost_estimate=cost(40 * count * 128 / width, 18),
        name="attention_backward",
    )(q, k, v, gm, att, recip, gconv, seg_row, seg_col)


def conv_back_kernel(v_ref, gm_ref, gate_ref, vec_ref, segc_ref, ggate_ref, gconv_ref, gfilt_ref):
    v_wide = v_ref[...].astype(wide)
    gm = gm_ref[...].astype(wide)
    seg = segc_ref[...]
    taps = [vec_ref[2 + j : 3 + j, :] for j in range(KW)]
    grad = gm * gate_ref[...].astype(wide)
    conv = taps[0] * v_wide
    gv_conv = taps[0] * grad
    lines = [jnp.sum(grad * v_wide, 0, keepdims=True)]
    for j in range(1, KW):
        moved = shift_rows(v_wide, seg, j, False)
        conv = conv + taps[j] * moved
        lines.append(jnp.sum(grad * moved, 0, keepdims=True))
        gv_conv = gv_conv + taps[j] * shift_rows(grad, seg, j, True)
    lines.append(jnp.zeros((LANES - KW, 128), wide))
    gfilt_ref[...] = jnp.concatenate(lines, 0).T.astype(low)
    ggate_ref[...] = (gm * conv).astype(low)
    gconv_ref[...] = gv_conv.astype(low)


def conv_back(v, gm, gate, vec, seg, deps=()):
    length, width = v.shape
    column = pl.BlockSpec((length, 128), lambda p: (0, p))
    small = pl.BlockSpec((8, 128), lambda p: (0, p))
    seg_col = seg.reshape(length, 1)
    return launch(
        conv_back_kernel,
        deps,
        grid=(width // 128,),
        in_specs=[column, column, column, small, whole(seg_col)],
        out_specs=[column, column, pl.BlockSpec((128, LANES), lambda p: (p, 0))],
        out_shape=[jax.ShapeDtypeStruct((length, width), low)] * 2 + [jax.ShapeDtypeStruct((width, LANES), low)],
        compiler_params=params(48),
        cost_estimate=cost(1, 10),
        name="convolution_backward",
    )(v, gm, gate, vec, seg_col)


def mix_kernel(x_ref, mixed_ref, vec_ref, weight_ref, middle_ref, hidden_ref):
    middle = x_ref[...].astype(wide) + dot(mixed_ref[...], weight_ref[...])
    inverse = lax.rsqrt(jnp.mean(middle * middle, axis=-1, keepdims=True) + EPS)
    middle_ref[...] = middle
    hidden_ref[...] = (middle * inverse * vec_ref[1:2, :]).astype(low)


def mix(x, mixed, vec, full, deps=()):
    length, width = x.shape
    return launch(
        mix_kernel,
        deps,
        grid=(length // TILE,),
        in_specs=[rows(TILE, width), rows(TILE, width), fixed(vec.shape), fixed((width, width))],
        out_specs=[rows(TILE, width), rows(TILE, width)],
        out_shape=[jax.ShapeDtypeStruct((length, width), wide), jax.ShapeDtypeStruct((length, width), low)],
        compiler_params=params(32),
        cost_estimate=cost(3, 16),
        name="mix",
    )(x, mixed, vec, full)


def first_half(n):
    return lambda i, *_: (jnp.minimum(i, n - 1), 0)


def second_half(n):
    return lambda i, *_: (jnp.maximum(i - n, 0), 0)


def feed_kernel(n, offs_ref, ha_ref, hb_ref, ca_ref, cb_ref, *refs):
    pieces, downs, (act_ref, both_ref, full_ref, down_ref) = refs[:4], refs[4:6], refs[6:]
    step = pl.program_id(0)
    half = full_ref.shape[1] // 2

    @pl.when(step == 0)
    def _():
        place(offs_ref, FEED_AT, pieces, full_ref)
        place(offs_ref, DOWN_AT, downs, down_ref)

    def work(hidden, cotangent):
        for at in range(0, half, 256):
            gate = dot(hidden, full_ref[:, at : at + 256])
            up = dot(hidden, full_ref[:, half + at : half + at + 256])
            gact = dot_nt(cotangent, down_ref[at : at + 256, :])
            sig = jax.nn.sigmoid(gate)
            silu = gate * sig
            act_ref[:, at : at + 256] = (silu * up).astype(low)
            both_ref[:, at : at + 256] = (gact * up * (sig + silu * (1.0 - sig))).astype(low)
            both_ref[:, half + at : half + at + 256] = (gact * silu).astype(low)

    @pl.when(step < n)
    def _():
        work(ha_ref[...], ca_ref[...])

    @pl.when(step >= n)
    def _():
        work(hb_ref[...], cb_ref[...])


def feed(offs, hidden, cotangent, j, w_down, pieces, down_pieces, deps=()):
    length, width = hidden[0].shape
    n = length // TILE
    half = w_down.shape[0]
    first = pl.BlockSpec((TILE, width), first_half(n))
    second = pl.BlockSpec((TILE, width), second_half(n))
    own_down = pl.BlockSpec((half // 2, width), lambda *_: (j, 0), pipeline_mode=pl.Buffered(1))
    given_rows = pl.BlockSpec(pieces[0].shape, lambda *_: (j, 0), pipeline_mode=pl.Buffered(1))
    return launch(
        functools.partial(feed_kernel, n),
        deps,
        scalars=1,
        grid=(2 * n,),
        in_specs=[first, second, first, second]
        + [fixed(pieces[0].shape), given_rows]
        + [fixed(p.shape) for p in pieces[2:]]
        + [own_down]
        + [fixed(p.shape) for p in down_pieces],
        out_specs=[rows(TILE, half), rows(TILE, 2 * half), fixed((width, 2 * half)), fixed((half, width))],
        out_shape=[
            jax.ShapeDtypeStruct((2 * length, half), low),
            jax.ShapeDtypeStruct((2 * length, 2 * half), low),
            jax.ShapeDtypeStruct((width, 2 * half), low),
            jax.ShapeDtypeStruct((half, width), low),
        ],
        compiler_params=params(48),
        cost_estimate=cost(16, 34),
        name="feed_in",
    )(offs, *hidden, *cotangent, *pieces, w_down, *down_pieces)


def weight_grad_kernel(shape_of, counts, outs, length, offs_ref, *refs):
    targets = [(ref, row * TILE) for ref, height in zip(refs[-len(outs) :], outs) for row in range(height)]
    step = pl.program_id(0)

    def work(lefts, rights):
        terms = max(len(lefts[0]), len(rights))

        def part_of(group, t):
            return group[t][...] if len(group) == terms else group[0][t * length : (t + 1) * length, :]

        for b, (ref, row) in enumerate(targets):
            value = None
            for t in range(terms):
                product = dot_tn(part_of(lefts[b], t), part_of(rights, t))
                value = product if value is None else value + product
            ref[row : row + TILE, :] = value.astype(low)

    start = 0
    for (left_at, right_at), count in zip(shape_of, counts):
        lefts = [[refs[n] for n in block] for block in left_at]
        rights = [refs[n] for n in right_at]
        if len(counts) == 1:
            work(lefts, rights)
        else:
            pl.when((step >= start) & (step < start + count))(functools.partial(work, lefts, rights))
        start += count


def weight_grad(offs, base, groups, outs, name, tile=512, deps=()):
    blocks = sum(outs)
    counts = [rights[0].shape[1] // tile for _, rights in groups]
    columns = sum(counts) * tile
    in_specs, operands, shape_of, known = [], [], [], {}
    start = 0
    for (lefts, rights), count in zip(groups, counts):
        key = tuple(id(a) for a in lefts)
        if key not in known:
            known[key] = []
            for b in range(blocks):
                known[key].append([len(operands) + n for n in range(len(lefts))])
                for a in lefts:
                    in_specs.append(pl.BlockSpec((a.shape[0], TILE), lambda j, offs, b=b: (0, offs[base + b])))
                    operands.append(a)
        shape_of.append((known[key], [len(operands) + n for n in range(len(rights))]))
        for a in rights:

            def where_to(j, offs, start=start, count=count):
                return (0, jnp.clip(j - start, 0, count - 1))

            in_specs.append(pl.BlockSpec((a.shape[0], tile), where_to))
            operands.append(a)
        start += count
    tokens = sum(a.shape[0] for a in groups[0][0])
    terms = max(len(groups[0][0]), len(groups[0][1]))
    return launch(
        functools.partial(weight_grad_kernel, shape_of, counts, outs, tokens // terms),
        deps,
        scalars=1,
        grid=(sum(counts),),
        in_specs=in_specs,
        out_specs=[pl.BlockSpec((height * TILE, tile), lambda j, offs: (0, j)) for height in outs],
        out_shape=[jax.ShapeDtypeStruct((height * TILE, columns), low) for height in outs],
        compiler_params=params(48),
        cost_estimate=cost(2.5e-9 * tokens * 1024 * columns, (tokens * (1024 + columns) * 2 + 2048 * columns) / 2**20),
        name=name,
    )(offs, *operands)


def feed_back_kernel(a_ref, b_ref, wa_ref, wb_ref, out_ref):
    out_ref[...] = (dot_nt(a_ref[...], wa_ref[...]) + dot_nt(b_ref[...], wb_ref[...])).astype(low)


def feed_back(first, second, full_first, full_second, deps=()):
    length = first.shape[0] // 2
    width = full_first.shape[0]
    n = length // TILE
    tile = pl.BlockSpec((TILE, first.shape[1]), lambda i: (i + n, 0))
    return launch(
        feed_back_kernel,
        deps,
        grid=(n,),
        in_specs=[tile, tile, fixed(full_first.shape), fixed(full_second.shape)],
        out_specs=rows(TILE, width),
        out_shape=jax.ShapeDtypeStruct((length, width), low),
        compiler_params=params(32),
        cost_estimate=cost(10, 18),
        name="feed_back_partner",
    )(first, second, full_first, full_second)


def middle_back_kernel(
    a_ref, b_ref, other_ref, middle_ref, cot_ref, vec_ref, wa_ref, wb_ref, wo_ref,
    gmiddle_ref, gbranch_ref, gmixed_ref, ggain_ref,
):
    ghidden = dot_nt(a_ref[...], wa_ref[...]) + dot_nt(b_ref[...], wb_ref[...]) + other_ref[...].astype(wide)
    middle = middle_ref[...]
    inverse = lax.rsqrt(jnp.mean(middle * middle, axis=-1, keepdims=True) + EPS)
    normed = middle * inverse
    gain = jnp.sum(ghidden * normed, axis=0, keepdims=True)

    @pl.when(pl.program_id(0) == 0)
    def _():
        ggain_ref[...] = jnp.zeros_like(ggain_ref)

    ggain_ref[0:1, :] += gain
    scaled = ghidden * vec_ref[1:2, :]
    gmiddle = cot_ref[...].astype(wide) + inverse * (
        scaled - normed * jnp.mean(scaled * normed, axis=-1, keepdims=True)
    )
    gmiddle_ref[...] = gmiddle
    gbranch = gmiddle.astype(low)
    gbranch_ref[...] = gbranch
    gmixed_ref[...] = dot_nt(gbranch, wo_ref[...]).astype(low)


def middle_back(first, second, other, middle, cotangent, vec, full_first, full_second, w_output, deps=()):
    length, width = middle.shape
    tile = rows(TILE, first.shape[1])
    line = rows(TILE, width)
    return launch(
        middle_back_kernel,
        deps,
        grid=(length // TILE,),
        in_specs=[
            tile, tile, line, line, line, fixed(vec.shape), fixed(full_first.shape), fixed(full_second.shape), fixed((width, width))
        ],
        out_specs=[line, line, line, fixed((8, width))],
        out_shape=[
            jax.ShapeDtypeStruct((length, width), wide),
            jax.ShapeDtypeStruct((length, width), low),
            jax.ShapeDtypeStruct((length, width), low),
            jax.ShapeDtypeStruct((8, width), wide),
        ],
        compiler_params=params(48),
        cost_estimate=cost(13, 40),
        name="middle_back",
    )(first, second, other, middle, cotangent, vec, full_first, full_second, w_output)


def feed_out_kernel(add, *refs):
    out_ref = refs[-1]
    value = dot(refs[0][...], refs[2][...]) + dot(refs[1][...], refs[3][...])
    for ref in refs[4:-1]:
        value = value + ref[...].astype(wide)
    out_ref[...] = value.astype(low)


def feed_out(first, second, down_first, down_second, shift, extras, name, deps=()):
    length = first.shape[0] // 2
    width = down_first.shape[1]
    n = length // TILE
    tile = pl.BlockSpec((TILE, first.shape[1]), lambda i: (i + shift * n, 0))
    return launch(
        functools.partial(feed_out_kernel, len(extras)),
        deps,
        grid=(n,),
        in_specs=[tile, tile, fixed(down_first.shape), fixed(down_second.shape)] + [rows(TILE, width)] * len(extras),
        out_specs=rows(TILE, width),
        out_shape=jax.ShapeDtypeStruct((length, width), low),
        compiler_params=params(32),
        cost_estimate=cost(5, 16),
        name=name,
    )(first, second, down_first, down_second, *extras)


def tokens_back_kernel(gqk_ref, gv_ref, ggate_ref, x_ref, gmiddle_ref, vec_ref, full_ref, gtokens_ref, ggain_ref):
    two = gqk_ref.shape[1]
    width = x_ref.shape[1]
    quarter = two // 4
    ghidden = None
    for n, col in enumerate((0, 2, 1, 3)):
        at = width + col * quarter
        term = dot_nt(gqk_ref[:, n * quarter : (n + 1) * quarter], full_ref[:, at : at + quarter])
        ghidden = term if ghidden is None else ghidden + term
    ghidden = (
        ghidden
        + dot_nt(gv_ref[...], full_ref[:, width + two : 2 * width + two])
        + dot_nt(ggate_ref[...], full_ref[:, two + 2 * width : two + 3 * width])
    )
    x = x_ref[...].astype(wide)
    inverse = lax.rsqrt(jnp.mean(x * x, axis=-1, keepdims=True) + EPS)
    normed = x * inverse

    @pl.when(pl.program_id(0) == 0)
    def _():
        ggain_ref[...] = jnp.zeros_like(ggain_ref)

    ggain_ref[0:1, :] += jnp.sum(ghidden * normed, axis=0, keepdims=True)
    scaled = ghidden * vec_ref[0:1, :]
    gtokens_ref[...] = gmiddle_ref[...] + inverse * (
        scaled - normed * jnp.mean(scaled * normed, axis=-1, keepdims=True)
    )


def tokens_back(gqk, gv, ggate, x, gmiddle, vec, full, deps=()):
    length, width = x.shape
    line = rows(TILE, width)
    return launch(
        tokens_back_kernel,
        deps,
        grid=(length // TILE,),
        in_specs=[rows(TILE, gqk.shape[1]), line, line, line, line, fixed(vec.shape), fixed(full.shape)],
        out_specs=[line, fixed((8, width))],
        out_shape=[jax.ShapeDtypeStruct((length, width), wide), jax.ShapeDtypeStruct((8, width), wide)],
        compiler_params=params(40),
        cost_estimate=cost(7, 24),
        name="tokens_back",
    )(gqk, gv, ggate, x, gmiddle, vec, full)


def spread_kernel(cols_ref, gain_ref, wg_ref, wu_ref, a_ref, b_ref, c_ref, d_ref, gate_ref, up_ref, ggain_ref):
    total = None
    for n, ref in enumerate((a_ref, b_ref, c_ref, d_ref)):
        quarter = ref.shape[1] // 4
        for part_y in range(2):
            at = pl.ds(pl.multiple_of(cols_ref[COLS_AT + 2 * n + part_y], 512), quarter)
            gate = ref[:, part_y * quarter : (part_y + 1) * quarter].astype(wide)
            up = ref[:, (2 + part_y) * quarter : (3 + part_y) * quarter].astype(wide)
            gate_ref[:, at] = gate
            up_ref[:, at] = up
            term = gate * wg_ref[:, at].astype(wide) + up * wu_ref[:, at].astype(wide)
            line = jnp.sum(term, axis=1, keepdims=True)
            total = line if total is None else total + line
    ggain_ref[...] = total / gain_ref[...]


def spread(cols, gain, w_gate, w_up, blocks, deps=()):
    height, width = blocks[0].shape
    shape = jax.ShapeDtypeStruct((height, 2 * width), wide)
    return launch(
        spread_kernel,
        deps,
        scalars=1,
        grid=(1,),
        in_specs=[fixed(gain.shape), fixed(w_gate.shape), fixed(w_up.shape)] + [fixed(b.shape) for b in blocks],
        out_specs=[fixed(shape.shape)] * 2 + [fixed(gain.shape)],
        out_shape=[shape, shape, jax.ShapeDtypeStruct(gain.shape, wide)],
        compiler_params=params(24),
        cost_estimate=cost(0.001, 16),
        name="spread",
    )(cols, gain, w_gate, w_up, *blocks)


def pack_kernel(at_ref, g1_ref, g2_ref, taps_ref, q_ref, k_ref, v_ref, c_ref, o_ref, pack_ref, half_ref):
    height = q_ref.shape[0]
    col = 0
    for ref in (o_ref, q_ref, k_ref, v_ref, c_ref):
        pack_ref[:, col : col + ref.shape[1]] = ref[...]
        col += ref.shape[1]
    small = jnp.concatenate([g1_ref[...].astype(wide), g2_ref[...].astype(wide), taps_ref[...].astype(wide)], 0)
    small = jnp.concatenate([small, jnp.zeros((LANES - small.shape[0], height), wide)], 0)
    pack_ref[:, col : col + LANES] = small.T.astype(low)
    at = pl.multiple_of(at_ref[X_AT] * (height // 2), 128)
    half_ref[...] = pack_ref[pl.ds(at, height // 2), :]


def pack_mixer(at, gain_one, gain_two, taps, w_query, w_key, w_value, w_convgate, w_output):
    operands = (gain_one, gain_two, taps, w_query, w_key, w_value, w_convgate, w_output)
    height = w_query.shape[0]
    columns = sum(a.shape[1] for a in operands[3:]) + LANES
    shapes = [(height, columns), (height // 2, columns)]
    return launch(
        pack_kernel,
        scalars=1,
        grid=(1,),
        in_specs=[fixed(a.shape) for a in operands],
        out_specs=[fixed(a) for a in shapes],
        out_shape=[jax.ShapeDtypeStruct(a, low) for a in shapes],
        compiler_params=params(24),
        cost_estimate=cost(0.001, 4),
        name="pack_mixer",
    )(at, *operands)


def pack_feed_kernel(offs_ref, gate_ref, up_ref, down_ref, first_ref, second_ref, give_ref, low_ref, high_ref):
    height = gate_ref.shape[0]
    targets = ((first_ref, 0), (second_ref, 0), (give_ref, 0), (give_ref, height))
    for n, (ref, row) in enumerate(targets):
        quarter = ref.shape[1] // 4
        for part_y in range(2):
            at = pl.ds(pl.multiple_of(offs_ref[PACK_AT + 2 * n + part_y], 512), quarter)
            ref[row : row + height, part_y * quarter : (part_y + 1) * quarter] = gate_ref[:, at]
            ref[row : row + height, (2 + part_y) * quarter : (3 + part_y) * quarter] = up_ref[:, at]
    size = low_ref.shape[0]
    low_ref[...] = down_ref[:size, :]
    high_ref[...] = down_ref[size:, :]


def pack_feed(offs, w_gate, w_up, w_down, deps=()):
    height, columns = w_gate.shape
    shapes = [(height, columns // 2)] * 2 + [(2 * height, columns // 2)] + [(w_down.shape[0] // 2, w_down.shape[1])] * 2
    return launch(
        pack_feed_kernel,
        deps,
        scalars=1,
        grid=(1,),
        in_specs=[fixed(w_gate.shape), fixed(w_up.shape), fixed(w_down.shape)],
        out_specs=[fixed(a) for a in shapes],
        out_shape=[jax.ShapeDtypeStruct(a, low) for a in shapes],
        compiler_params=params(24),
        cost_estimate=cost(0.001, 8),
        name="pack_feed",
    )(offs, w_gate, w_up, w_down)


def step(kernel, offs, operands, shapes, name, deps=(), giga=0.001):
    return launch(
        kernel,
        deps,
        scalars=1,
        grid=(1,),
        in_specs=[fixed(a.shape) for a in operands],
        out_specs=[fixed(a) for a in shapes],
        out_shape=[jax.ShapeDtypeStruct(a, low) for a in shapes],
        compiler_params=params(24),
        cost_estimate=cost(giga, 8),
        name=name,
    )(offs, *operands)


def pick_kernel(offs_ref, first_ref, second_ref, given_ref, a_ref, b_ref):
    height = first_ref.shape[0]

    @pl.when(offs_ref[X_AT] == 0)
    def _():
        a_ref[...] = first_ref[...]
        b_ref[...] = second_ref[...]

    @pl.when(offs_ref[X_AT] != 0)
    def _():
        a_ref[...] = given_ref[:height, :]
        b_ref[...] = given_ref[height:, :]


def add(*refs):
    total = refs[0].astype(wide)
    for other in refs[1:]:
        total = total + other.astype(wide)
    return total.astype(low)


def top_kernel(offs_ref, keep_ref, came_ref, give_ref):
    size = give_ref.shape[0]
    give_ref[...] = add(keep_ref[:size, :], came_ref[:size, :])


def top_sum(offs, keep, came, deps=()):
    return step(top_kernel, offs, [keep, came], [(keep.shape[0] // 2, keep.shape[1])], "top_sum", deps)[0]


def rest_kernel(offs_ref, *refs):
    out_ref = refs[-1]
    col = 0
    for n in range(0, len(refs) - 1, 3):
        keep_ref, came_ref, passed_ref = refs[n : n + 3]
        size, width = passed_ref.shape
        skip = came_ref.shape[0] - size
        out_ref[:, col : col + width] = add(keep_ref[size:, :], came_ref[skip:, :], passed_ref[...])
        col += width


def rest_sum(offs, triples, deps=()):
    operands = [a for triple in triples for a in triple]
    shape = (triples[0][2].shape[0], sum(t[2].shape[1] for t in triples))
    return step(rest_kernel, offs, operands, [shape], "rest_sum", deps)[0]


def halves_kernel(filters, offs_ref, *refs):
    top_ref, rest_ref = refs[-2:]
    size = top_ref.shape[0]
    col = 0
    for n in range(0, len(refs) - 2, 2):
        keep_ref, came_ref = refs[n : n + 2]
        at = slice(col, col + keep_ref.shape[1])
        col += keep_ref.shape[1]
        if filters and n == len(refs) - 4:
            for ref, line in ((top_ref, offs_ref[OWNER_AT + 2]), (rest_ref, offs_ref[OWNER_AT + 3])):
                rows_at = pl.ds(pl.multiple_of(line * size, 128), size)
                ref[:, at] = add(keep_ref[rows_at, :], came_ref[rows_at, :])
        else:
            top_ref[:, at] = add(keep_ref[:size, :], came_ref[:size, :])
            rest_ref[:, at] = add(keep_ref[size:, :], came_ref[size:, :])


def halves_sum(offs, pairs, filters=False, deps=()):
    operands = [a for pair in pairs for a in pair]
    shape = (pairs[0][0].shape[0] // 2, sum(pair[0].shape[1] for pair in pairs))
    return step(functools.partial(halves_kernel, filters), offs, operands, [shape] * 2, "halves_sum", deps)


def near_kernel(offs_ref, keep_ref, came_ref, own_ref, other_ref):
    size = own_ref.shape[0]
    for ref, side in ((own_ref, offs_ref[X_AT]), (other_ref, 1 - offs_ref[X_AT])):
        at = pl.ds(pl.multiple_of(side * size, 128), size)
        ref[...] = add(keep_ref[at, :], came_ref[at, :])


def near_split(offs, keep, came, deps=()):
    return step(near_kernel, offs, [keep, came], [(keep.shape[0] // 2, keep.shape[1])] * 2, "near_split", deps)


def pair_kernel(offs_ref, a_ref, b_ref, out_ref):
    out_ref[...] = add(a_ref[...], b_ref[...])


def pair_sum(offs, a, b, deps=()):
    return step(pair_kernel, offs, [a, b], [a.shape], "pair_sum", deps)[0]


def sort_kernel(offs_ref, total_ref, other_ref, own_ref, give_ref):
    skip = total_ref.shape[1] - own_ref.shape[1]

    @pl.when(offs_ref[X_AT + 1] == 0)
    def _():
        own_ref[...] = total_ref[:, skip:]
        give_ref[...] = other_ref[:, skip:]

    @pl.when(offs_ref[X_AT + 1] != 0)
    def _():
        own_ref[...] = other_ref[:, skip:]
        give_ref[...] = total_ref[:, skip:]


def sort_rows(offs, total, other, skip, deps=()):
    shape = (total.shape[0], total.shape[1] - skip)
    return step(sort_kernel, offs, [total, other], [shape, shape], "sort_rows", deps)


def pairs_kernel(offs_ref, *refs):
    col = 0
    for n in range(0, len(refs) - 1, 2):
        width = refs[n].shape[1]
        refs[-1][:, col : col + width] = add(refs[n][...], refs[n + 1][...])
        col += width


def pairs_sum(offs, pairs, deps=()):
    shape = (pairs[0][0].shape[0], sum(a.shape[1] for a, _ in pairs))
    return step(pairs_kernel, offs, [a for pair in pairs for a in pair], [shape], "pairs_sum", deps)[0]


def settle_down_kernel(offs_ref, *refs):
    out_ref = refs[-1]
    size = out_ref.shape[0] // 4
    width = out_ref.shape[1]
    for n in range(4):
        side = offs_ref[X_AT] if n % 2 == 0 else 1 - offs_ref[X_AT]
        at = pl.ds(pl.multiple_of((n // 2) * 2 * size + side * size, 128), size)
        out_ref[at, :] = refs[n][:, :width].astype(wide)


def settle_down(offs, pairs, width, deps=()):
    operands = [a for pair in pairs for a in pair]
    size = operands[0].shape[0]
    column = pl.BlockSpec((size, width), lambda *_: (0, 0), pipeline_mode=pl.Buffered(1))
    return launch(
        settle_down_kernel,
        deps,
        scalars=1,
        grid=(1,),
        in_specs=[column] * 4,
        out_specs=fixed((4 * size, width)),
        out_shape=jax.ShapeDtypeStruct((4 * size, width), wide),
        compiler_params=params(24),
        cost_estimate=cost(0.001, 6),
        name="settle_down",
    )(offs, *operands)


def settle_mixer_kernel(
    offs_ref, gain_ref, mine_ref, other_ref, wq_ref, wk_ref, wv_ref, wc_ref,
    gq_ref, gk_ref, gv_ref, gc_ref, go_ref, gf_ref, ggain_ref, all_ref,
):
    size = mine_ref.shape[0]
    for ref, side in ((mine_ref, offs_ref[X_AT]), (other_ref, 1 - offs_ref[X_AT])):
        all_ref[pl.ds(pl.multiple_of(side * size, 128), size), :] = ref[...].astype(wide)
    width = wv_ref.shape[1]
    half = wq_ref.shape[1] // 2
    go_ref[...] = all_ref[:, :width]
    gc = all_ref[:, width : 2 * width]
    gc_ref[...] = gc
    gf_ref[...] = all_ref[:, 2 * width : 2 * width + LANES].T
    at = 2 * width + LANES
    gv = all_ref[:, at + 4 * half :]
    gv_ref[...] = gv
    total = jnp.sum(gc * wc_ref[...].astype(wide), axis=1, keepdims=True)
    total = total + jnp.sum(gv * wv_ref[...].astype(wide), axis=1, keepdims=True)
    for n, (ref, weight_ref, cols) in enumerate(
        (
            (gq_ref, wq_ref, slice(0, half)),
            (gk_ref, wk_ref, slice(0, half)),
            (gq_ref, wq_ref, slice(half, 2 * half)),
            (gk_ref, wk_ref, slice(half, 2 * half)),
        )
    ):
        value = all_ref[:, at + n * half : at + (n + 1) * half]
        ref[:, cols] = value
        total = total + jnp.sum(value * weight_ref[:, cols].astype(wide), axis=1, keepdims=True)
    ggain_ref[...] = total / gain_ref[...]


def settle_mixer(offs, gain, mine, other, w_query, w_key, w_value, w_convgate, deps=()):
    operands = (gain, mine, other, w_query, w_key, w_value, w_convgate)
    height, width = w_value.shape
    shapes = [w_query.shape, w_key.shape, w_value.shape, w_convgate.shape, (height, width), (LANES, height), gain.shape]
    return launch(
        settle_mixer_kernel,
        deps,
        scalars=1,
        grid=(1,),
        in_specs=[fixed(a.shape) for a in operands],
        out_specs=[fixed(a) for a in shapes],
        out_shape=[jax.ShapeDtypeStruct(a, wide) for a in shapes],
        scratch_shapes=[pltpu.VMEM((height, mine.shape[1]), wide)],
        compiler_params=params(24),
        cost_estimate=cost(0.001, 8),
        name="settle_mixer",
    )(offs, *operands)


def tick_kernel(offs_ref, out_ref):
    out_ref[...] = jnp.zeros_like(out_ref)


def tick(offs, deps=()):
    return step(tick_kernel, offs, [], [(16, 128)], "arrived", deps, TICK)[0]


def swap(value, axis):
    return lax.ppermute(value, axis, [(0, 1), (1, 0)])


def later(value, other):
    return lax.optimization_barrier((value, other))[0]


def part(value, index, count, axis=0):
    size = value.shape[axis] // count
    return lax.dynamic_slice_in_dim(value, index * size, size, axis)


def in_order(index, mine, other):
    return jnp.where(
        index == 0, jnp.concatenate([mine, other], 0), jnp.concatenate([other, mine], 0)
    )


def per_device(
    tokens, segment_ids, gain_one, w_query, w_key, w_value, w_convgate, w_output, conv_filter,
    gain_two, w_gate, w_up, w_down, cotangent,
):
    Order.last = None
    Order.scale = 0.05
    x = lax.axis_index("near")
    y = lax.axis_index("row")
    c = lax.axis_index("core")
    s = 2 * y + c
    width = tokens.shape[1]
    seg = segment_ids[0]
    block = w_down.shape[0]

    def flip(bits):
        return jnp.bitwise_xor(s, bits)

    small_block = block // 2
    half = SHARD_ROWS // 2

    def feed_cols(core, j):
        return [((2 * row + core) * 2 + j) * small_block for row in range(2)]

    feed_rows = [s, flip(1), jnp.bitwise_xor(flip(2), x), jnp.bitwise_xor(flip(3), x)]
    offs = [
        x,
        jnp.bitwise_xor(x, c),
        s * SHARD_ROWS,
        flip(1) * SHARD_ROWS,
        flip(2) * SHARD_ROWS + x * half,
        flip(2) * SHARD_ROWS + (1 - x) * half,
        flip(3) * SHARD_ROWS + x * half,
        flip(3) * SHARD_ROWS + (1 - x) * half,
        *(a * SHARD_ROWS for a in feed_rows),
        y * small_block,
        (1 - y) * small_block,
        0,
        0,
        *feed_cols(c, 0), *feed_cols(c, 1), *feed_cols(1 - c, 0), *feed_cols(1 - c, 1),
        *feed_cols(c, 0), *feed_cols(1 - c, 0), *feed_cols(c, 1), *feed_cols(1 - c, 1),
        2 * (1 - y) + 1 - x, 2 * (1 - y) + x, 2 * y + 1 - x, 2 * y + x,
        flip(3), flip(1), flip(2), s,
        2 * (1 - y) + 1 - x, 2 * y + 1 - x, 2 * (1 - y) + x, 2 * y + x,
    ]
    offs = jnp.stack([jnp.asarray(a, jnp.int32) for a in offs])

    pack, pack_half = pack_mixer(
        offs, gain_one[None], gain_two[None], conv_filter, w_query, w_key, w_value, w_convgate, w_output
    )
    direct = swap(pack_half, "row")
    near_core = swap(pack, "core")
    relayed = swap(direct, "near")
    pack_pieces = [pack, near_core, direct, relayed, swap(direct, "core"), swap(relayed, "core")]
    cot_other = swap(later(cotangent, direct), "core")

    mine_first, mine_second, give, *down_halves = pack_feed(offs, w_gate, w_up, w_down)
    given = swap(later(give, direct), "core")
    sends = step(pick_kernel, offs, [mine_first, mine_second, given], [mine_first.shape] * 2, "pick")
    feed_pieces = [[own, given] for own in (mine_first, mine_second)]

    feed_pieces[0].append(swap(sends[0], "row"))
    hidden_one, queries, keys, values, gates, full_one, vec = project(offs, tokens, pack_pieces, deps=[cot_other])
    down_pieces = [[swap(later(down_halves[0], queries), "row")]]
    pairs = width // 256
    attended = attend(queries, keys, values, gates, vec, seg, 0, pairs)
    token = tick(offs)
    feed_pieces[0].append(swap(later(feed_pieces[0][2], token), "near"))
    feed_pieces[1].append(swap(later(sends[1], token), "row"))
    mixed, attention, recips = attend(
        queries, keys, values, gates, vec, seg, pairs, pairs, onto=attended, deps=[feed_pieces[0][2]]
    )
    middle, hidden_two = mix(tokens, mixed, vec, full_one, deps=[down_pieces[0][0]])
    down_pieces.append([swap(later(down_halves[1], middle), "row")])
    tick(offs, [feed_pieces[0][3]])
    hiddens = [hidden_two, swap(hidden_two, "core")]
    cots = [cotangent, cot_other]

    Order.scale = 20.0

    def down_grad(act, deps=()):
        return weight_grad(offs, ACT_AT, [([act], cots)], (2, 2), "grad_down", deps=deps)

    def gate_grad(both):
        return weight_grad(offs, GRAD_AT, [(hiddens, [both])], (1, 1, 2), "grad_gate_up")

    first_feed = feed(offs, hiddens, cots, 0, w_down, feed_pieces[0], down_pieces[0])
    feed_pieces[1].append(swap(later(feed_pieces[1][2], first_feed[0]), "near"))
    down_send, down_keep = down_grad(first_feed[0], deps=[feed_pieces[1][2]])
    down_came = swap(down_send, "near")
    gate_send, gate_send_own, gate_keep = gate_grad(first_feed[1])
    gate_came, gate_came_own = swap(gate_send, "row"), swap(gate_send_own, "row")
    second_feed = feed(offs, hiddens, cots, 1, w_down, feed_pieces[1], down_pieces[1])
    acts, boths, fulls, downs = zip(first_feed, second_feed)
    down_passed = swap(top_sum(offs, down_keep, down_came), "row")
    gate_passed = swap(top_sum(offs, gate_keep, gate_came), "near")
    ghidden_part = feed_back(boths[0], boths[1], fulls[0], fulls[1])
    ghidden_other = swap(ghidden_part, "core")
    down_send_2, down_keep_2 = down_grad(second_feed[0])
    down_came_2 = swap(down_send_2, "near")
    gate_send_2, gate_send_own_2, gate_keep_2 = gate_grad(second_feed[1])
    gate_came_2, gate_came_own_2 = swap(gate_send_2, "row"), swap(gate_send_own_2, "row")
    feed_sum = lax.psum(
        rest_sum(offs, [(down_keep, down_came, down_passed), (gate_keep, gate_came_own, gate_passed)]), "far"
    )
    tick(offs)
    gmiddle, gbranch, gmixed, _ = middle_back(
        boths[0], boths[1], ghidden_other, middle, cotangent, vec, fulls[0], fulls[1], full_one
    )
    down_passed_2 = swap(top_sum(offs, down_keep_2, down_came_2), "row")
    gate_passed_2 = swap(top_sum(offs, gate_keep_2, gate_came_2), "near")

    ggate, gconv, gfilter = conv_back(values, gmixed, gates, vec, seg)
    filter_came = swap(gfilter, "core")
    early_send, early_keep = weight_grad(
        offs, OWNER_AT, [([mixed], [gbranch]), ([hidden_one], [ggate])], (2, 2), "grad_output_convgate"
    )
    early_came = swap(early_send, "core")
    attended = attend_back(queries, keys, values, gmixed, attention, recips, gconv, seg, 0, pairs)
    early_give, early_held = halves_sum(offs, [(early_keep, early_came), (gfilter, filter_came)], True)
    early_came = swap(early_give, "row")
    tick(offs, [feed_sum])
    feed_near = rest_sum(
        offs, [(down_keep_2, down_came_2, down_passed_2), (gate_keep_2, gate_came_own_2, gate_passed_2)]
    )
    feed_other = swap(later(feed_sum, feed_near), "near")
    feed_sum_2 = lax.psum(feed_near, "far")
    tick(offs)
    gqk, gv = attend_back(
        queries, keys, values, gmixed, attention, recips, gconv, seg, pairs, pairs, onto=attended
    )
    early_own, early_other = near_split(offs, early_held, early_came)
    early_passed = swap(early_other, "near")
    late_send, late_keep = weight_grad(
        offs, OWNER_AT, [([hidden_one], [gqk]), ([hidden_one], [gv])], (2, 2), "grad_query_key_value"
    )
    late_came = swap(late_send, "core")
    own_rows, theirs = sort_rows(offs, feed_sum, feed_other, width)
    spreads = [own_rows, swap(theirs, "core")]
    late_give, late_held = halves_sum(offs, [(late_keep, late_came)])
    late_came = swap(late_give, "row")
    grad_tokens, _ = tokens_back(gqk, gv, ggate, tokens, gmiddle, vec, full_one)
    late_own, late_other = near_split(offs, late_held, late_came)
    late_passed = swap(late_other, "near")
    out_part = feed_out(acts[0], acts[1], downs[0], downs[1], 1, [], "feed_out_partner")
    out_came = swap(out_part, "core")
    tick(offs, [feed_sum_2])
    mixer_near = pairs_sum(offs, [(early_own, early_passed), (late_own, late_passed)])
    feed_other_2 = swap(later(feed_sum_2, mixer_near), "near")
    mixer_sum = lax.psum(mixer_near, "far")
    tick(offs)
    result = feed_out(acts[0], acts[1], downs[0], downs[1], 0, [middle, out_came], "feed_out")
    own_rows, theirs = sort_rows(offs, feed_sum_2, feed_other_2, width)
    spreads += [own_rows, swap(theirs, "core")]
    grad_down = settle_down(offs, [(feed_sum, feed_other), (feed_sum_2, feed_other_2)], width)
    grad_gate, grad_up, ggain_two = spread(offs, gain_two[:, None].astype(wide), w_gate, w_up, spreads)
    mixer_other = swap(mixer_sum, "near")
    *grads, grad_output, grad_filter, ggain_one = settle_mixer(
        offs, gain_one[:, None].astype(wide), mixer_sum, mixer_other, w_query, w_key, w_value, w_convgate
    )
    return (
        result,
        grad_tokens,
        ggain_one[:, 0],
        *grads,
        grad_output,
        grad_filter[:KW],
        ggain_two[:, 0],
        grad_gate,
        grad_up,
        grad_down,
    )


def solution(mesh):
    replicas, shards = mesh.shape["rep"], mesh.shape["shard"]
    devices = np.asarray(mesh.devices).reshape(replicas // 2, 2, shards // 2, 2)
    fine = Mesh(devices, ("far", "near", "row", "core"))
    token = P(("far", "near", "row", "core"), None)
    line = P(("row", "core"))
    weight = P(("row", "core"), None)
    taps = P(None, ("row", "core"))
    return jax.shard_map(
        per_device,
        mesh=fine,
        in_specs=(
            token, token, line, weight, weight, weight, weight, weight, taps, line, weight, weight, weight, token
        ),
        out_specs=(
            token, token, line, weight, weight, weight, weight, weight, taps, line, weight, weight, weight
        ),
        check_vma=False,
    )
```

```python
import functools

import jax
import jax.numpy as jnp
import numpy as np
from jax import lax
from jax.experimental import pallas as pl
from jax.experimental.pallas import tpu as pltpu
from jax.sharding import Mesh
from jax.sharding import PartitionSpec as P

HEADS = 16
FEAT = 16
KW = 3
EPS = 1e-06
TILE = 256
SHARD_ROWS = 256
LANES = 128
TICK = 1e5
X_AT, MIXER_AT, FEED_AT, DOWN_AT, PACK_AT, COLS_AT, GRAD_AT, OWNER_AT, ACT_AT = 0, 2, 8, 12, 16, 24, 32, 36, 40

low = jnp.bfloat16
wide = jnp.float32


def dot(a, b):
    return jnp.dot(a, b, preferred_element_type=wide)


def dot_nt(a, b):
    return lax.dot_general(a, b, (((1,), (1,)), ((), ())), preferred_element_type=wide)


def dot_tn(a, b):
    return lax.dot_general(a, b, (((0,), (0,)), ((), ())), preferred_element_type=wide)


class Order:
    last = None
    scale = 1.0


def launch(kernel, deps=(), onto=(), *, scalars=0, grid, in_specs, out_specs, out_shape, scratch_shapes=(), **rest):
    taken = scalars + len(in_specs)
    deps = list(onto) + [d for d in deps if d is not None] + ([] if Order.last is None else [Order.last])

    def body(*refs):
        kernel(*refs[:taken], *refs[taken + len(deps) :])

    spec = pltpu.PrefetchScalarGridSpec(
        num_scalar_prefetch=scalars,
        grid=grid,
        in_specs=list(in_specs) + [pl.BlockSpec(memory_space=pl.ANY)] * len(deps),
        out_specs=out_specs,
        scratch_shapes=list(scratch_shapes),
    )
    aliases = {taken + n: n for n in range(len(onto))}
    run = pl.pallas_call(body, grid_spec=spec, out_shape=out_shape, input_output_aliases=aliases, **rest)

    def call(*operands):
        result = run(*operands, *deps)
        Order.last = result[0] if isinstance(result, (list, tuple)) else result
        return result

    return call


def params(mib):
    return pltpu.CompilerParams(vmem_limit_bytes=max(mib, 60) << 20)


def cost(gigaflops, mebibytes):
    return pl.CostEstimate(
        flops=int(gigaflops * Order.scale * 1e9), bytes_accessed=int(mebibytes * Order.scale * (1 << 20)), transcendentals=0
    )


def fixed(shape):
    return pl.BlockSpec(shape, lambda *_: (0,) * len(shape), pipeline_mode=pl.Buffered(1))


def rows(height, width):
    return pl.BlockSpec((height, width), lambda i, *_: (i, 0))


def place(offs_ref, base, pieces, full_ref):
    for n, piece in enumerate(pieces):
        at = pl.multiple_of(offs_ref[base + n], 128)
        full_ref[pl.ds(at, piece.shape[0]), :] = piece[...]


def project_kernel(offs_ref, x_ref, *refs):
    pieces, (hidden_ref, q_ref, k_ref, v_ref, gate_ref, vec_ref, out_ref, full_ref, sem) = refs[:6], refs[6:]
    copy = pltpu.make_async_copy(full_ref, out_ref, sem)
    heads = HEADS * FEAT
    width = x_ref.shape[1]

    @pl.when(pl.program_id(0) == 0)
    def _():
        place(offs_ref, MIXER_AT, pieces, full_ref)
        copy.start()
        small = full_ref[:, 2 * heads + 3 * width :].astype(wide)
        vec_ref[...] = small.T[:8, :]

    x = x_ref[...].astype(wide)
    inverse = lax.rsqrt(jnp.mean(x * x, axis=-1, keepdims=True) + EPS)
    hidden = (x * inverse * vec_ref[0:1, :]).astype(low)
    hidden_ref[...] = hidden
    at = width
    q_ref[...] = (dot(hidden, full_ref[:, at : at + heads]) * FEAT ** (-0.5)).astype(low)
    k_ref[...] = dot(hidden, full_ref[:, at + heads : at + 2 * heads]).astype(low)
    at = at + 2 * heads
    v_ref[...] = dot(hidden, full_ref[:, at : at + width]).astype(low)
    gate_ref[...] = dot(hidden, full_ref[:, at + width : at + 2 * width]).astype(low)

    @pl.when(pl.program_id(0) == pl.num_programs(0) - 1)
    def _():
        copy.wait()


def project(offs, x, pieces, deps=()):
    length, width = x.shape
    heads = HEADS * FEAT
    columns = pieces[0].shape[1]
    shapes = [
        jax.ShapeDtypeStruct((length, width), low),
        jax.ShapeDtypeStruct((length, heads), low),
        jax.ShapeDtypeStruct((length, heads), low),
        jax.ShapeDtypeStruct((length, width), low),
        jax.ShapeDtypeStruct((length, width), low),
        jax.ShapeDtypeStruct((8, width), wide),
        jax.ShapeDtypeStruct((width, columns), low),
    ]
    return launch(
        project_kernel,
        deps,
        scalars=1,
        grid=(length // TILE,),
        in_specs=[rows(TILE, width)] + [fixed(p.shape) for p in pieces],
        out_specs=[
            rows(TILE, width),
            rows(TILE, heads),
            rows(TILE, heads),
            rows(TILE, width),
            rows(TILE, width),
            fixed((8, width)),
            pl.BlockSpec(memory_space=pl.ANY),
        ],
        scratch_shapes=[pltpu.VMEM((width, columns), low), pltpu.SemaphoreType.DMA],
        out_shape=shapes,
        compiler_params=params(40),
        cost_estimate=cost(7, 22),
        name="project",
    )(offs, x, *pieces)


def shift_rows(v, seg, by, up):
    zeros = jnp.zeros((by, v.shape[1]), v.dtype)
    none = jnp.full((by, 1), -1, seg.dtype)
    if up:
        moved, moved_seg = jnp.concatenate([v[by:], zeros], 0), jnp.concatenate([seg[by:], none], 0)
    else:
        moved = jnp.concatenate([zeros, v[:-by]], 0)
        moved_seg = jnp.concatenate([none, seg[:-by]], 0)
    return jnp.where(moved_seg == seg, moved, 0.0)


def lane_pick(width, start, stop):
    i = lax.broadcasted_iota(jnp.int32, (1, width), 1)
    return (i >= start) & (i < stop)


def attend_kernel(
    first, q_ref, k_ref, v_ref, gate_ref, vec_ref, segr_ref, segc_ref, mixed_ref, att_ref, recip_ref, mask_ref
):
    length = q_ref.shape[0]
    pair = pl.program_id(0) + first
    zero = jnp.zeros((), low)

    @pl.when(pair == first)
    def _():
        for tb in range(0, length, TILE):
            t = lax.broadcasted_iota(jnp.int32, (TILE, length), 0) + tb
            s = lax.broadcasted_iota(jnp.int32, (TILE, length), 1)
            seen = (s <= t) & (segc_ref[tb : tb + TILE, :] == segr_ref[...])
            mask_ref[tb : tb + TILE, :] = jnp.where(seen, 1.0, 0.0).astype(low)

    v = v_ref[...]
    keys, sides = [], []
    for i in range(2):
        head = 2 * pair + i
        keys.append(jnp.where(lane_pick(HEADS * FEAT, head * FEAT, (head + 1) * FEAT), k_ref[...], zero))
        lanes = lane_pick(128, 64 * i, 64 * i + 64)
        ones = jnp.broadcast_to(jnp.where(lanes, 1.0, 0.0).astype(low), (length, 128))
        sides.append(jnp.concatenate([jnp.where(lanes, v, zero), ones], 1))
    for tb in range(0, length, TILE):
        n = tb + TILE
        total = None
        for i in range(2):
            one_plus = dot_nt(q_ref[tb:n, :], keys[i][:n]) + 1.0
            kernel = (one_plus * one_plus + 1.0).astype(low) * mask_ref[tb:n, :n]
            part = dot(kernel, sides[i][:n])
            total = part if total is None else total + part
        recip = 1.0 / total[:, 128:]
        att_ref[tb:n, :] = (total[:, :128] * recip).astype(low)
        recip_ref[tb:n, :] = (2.0 * recip).astype(low)
    v_wide = v.astype(wide)
    seg = segc_ref[...]
    conv = vec_ref[2:3, :] * v_wide
    for j in range(1, KW):
        conv = conv + vec_ref[2 + j : 3 + j, :] * shift_rows(v_wide, seg, j, False)
    mixed_ref[...] = (att_ref[...].astype(wide) + gate_ref[...].astype(wide) * conv).astype(low)


def whole(a):
    return pl.BlockSpec(a.shape, lambda p: (0, 0))


def attend(q, k, v, gate, vec, seg, first, count, onto=(), deps=()):
    length, width = v.shape
    column = pl.BlockSpec((length, 128), lambda p: (0, p + first))
    seg_row, seg_col = seg.reshape(1, length), seg.reshape(length, 1)
    return launch(
        functools.partial(attend_kernel, first),
        deps,
        onto,
        grid=(count,),
        in_specs=[
            whole(q), whole(k), column, column, pl.BlockSpec((8, 128), lambda p: (0, p + first)), whole(seg_row), whole(seg_col)
        ],
        out_specs=[column] * 3,
        out_shape=[jax.ShapeDtypeStruct((length, width), low)] * 3,
        scratch_shapes=[pltpu.VMEM((length, length), low)],
        compiler_params=params(40),
        cost_estimate=cost(18 * count * 128 / width, 14),
        name="attention_forward",
    )(q, k, v, gate, vec, seg_row, seg_col)


def attend_back_kernel(
    first, q_ref, k_ref, v_ref, gm_ref, att_ref, recip_ref, gconv_ref, segr_ref, segc_ref,
    gqk_ref, gv_ref, mask_ref, gq_acc, gk_acc,
):
    length, heads = q_ref.shape
    pair = pl.program_id(0) + first
    zero = jnp.zeros((), low)

    @pl.when(pair == first)
    def _():
        for sb in range(0, length, TILE):
            s = lax.broadcasted_iota(jnp.int32, (TILE, length), 0) + sb
            t = lax.broadcasted_iota(jnp.int32, (TILE, length), 1)
            seen = (s <= t) & (segc_ref[sb : sb + TILE, :] == segr_ref[...])
            mask_ref[sb : sb + TILE, :] = jnp.where(seen, 1.0, 0.0).astype(low)
        gk_acc[...] = jnp.zeros_like(gk_acc)
        gq_acc[...] = jnp.zeros_like(gq_acc)

    v = v_ref[...]
    gm = gm_ref[...].astype(wide)
    gnum_wide = gm * recip_ref[...].astype(wide)
    gnum = gnum_wide.astype(low)
    product = gnum_wide * att_ref[...].astype(wide)
    high = product.astype(low)
    rest = (product - high.astype(wide)).astype(low)
    r = lax.broadcasted_iota(jnp.int32, (256, 128), 0)
    c = lax.broadcasted_iota(jnp.int32, (256, 128), 1)
    same_head = jnp.where(((r % 128) // 64) == (c // 64), 1.0, 0.0).astype(low)
    gtot = -dot(jnp.concatenate([high, rest], 1), same_head)
    gtot_high = gtot.astype(low)
    gtot_rest = (gtot - gtot_high.astype(wide)).astype(low)
    lane = lax.broadcasted_iota(jnp.int32, (1, 128), 1)
    left = jnp.concatenate([gnum, jnp.where(lane % 64 == 0, gtot_high, gtot_rest)], 1)
    gnum_half = gnum * jnp.asarray(0.5, low)
    queries, sides, gnums, keys = [], [], [], []
    for i in range(2):
        head = 2 * pair + i
        mine = lane_pick(heads, head * FEAT, (head + 1) * FEAT)
        queries.append(jnp.where(mine, q_ref[...], zero))
        keys.append(jnp.where(mine, k_ref[...], zero))
        lanes = lane_pick(128, 64 * i, 64 * i + 64)
        ones = jnp.where(lane_pick(128, 64 * i, 64 * i + 2), 1.0, 0.0).astype(low)
        sides.append(jnp.concatenate([jnp.where(lanes, v, zero), jnp.broadcast_to(ones, (length, 128))], 1))
        gnums.append(jnp.where(lanes, gnum_half, zero))
    for sb in range(0, length, TILE):
        n = sb + TILE
        gv = gconv_ref[sb:n, :].astype(wide)
        gk = None
        for i in range(2):
            one_plus = dot_nt(k_ref[sb:n, :], queries[i][sb:]) + 1.0
            mask = mask_ref[sb:n, sb:]
            kernel = (one_plus * one_plus + 1.0).astype(low) * mask
            gv = gv + dot(kernel, gnums[i][sb:])
            gkernel = dot_nt(sides[i][sb:n], left[sb:])
            gscores = (gkernel * one_plus).astype(low) * mask
            part = dot(gscores, queries[i][sb:])
            gk = part if gk is None else gk + part
            gq_acc[sb:, :] += dot_tn(gscores, keys[i][sb:n])
        gv_ref[sb:n, :] = gv.astype(low)
        gk_acc[sb:n, :] += gk

    @pl.when(pl.program_id(0) == pl.num_programs(0) - 1)
    def _():
        mine = slice(2 * FEAT * first, 2 * FEAT * first + gqk_ref.shape[1] // 2)
        gqk_ref[:, : gqk_ref.shape[1] // 2] = (gq_acc[:, mine] * FEAT ** (-0.5)).astype(low)
        gqk_ref[:, gqk_ref.shape[1] // 2 :] = gk_acc[:, mine].astype(low)


def attend_back(q, k, v, gm, att, recip, gconv, seg, first, count, onto=(), deps=()):
    length, width = v.shape
    heads = q.shape[1]
    column = pl.BlockSpec((length, 128), lambda p: (0, p + first))
    seg_row, seg_col = seg.reshape(1, length), seg.reshape(length, 1)
    return launch(
        functools.partial(attend_back_kernel, first),
        deps,
        onto,
        grid=(count,),
        in_specs=[whole(q), whole(k)] + [column] * 5 + [whole(seg_row), whole(seg_col)],
        out_specs=[pl.BlockSpec((length, 4 * FEAT * count), lambda p: (0, first // count)), column],
        out_shape=[jax.ShapeDtypeStruct((length, 2 * heads), low), jax.ShapeDtypeStruct((length, width), low)],
        scratch_shapes=[
            pltpu.VMEM((length, length), low),
            pltpu.VMEM((length, heads), wide),
            pltpu.VMEM((length, heads), wide),
        ],
        compiler_params=params(48),
        cost_estimate=cost(40 * count * 128 / width, 18),
        name="attention_backward",
    )(q, k, v, gm, att, recip, gconv, seg_row, seg_col)


def conv_back_kernel(v_ref, gm_ref, gate_ref, vec_ref, segc_ref, ggate_ref, gconv_ref, gfilt_ref):
    v_wide = v_ref[...].astype(wide)
    gm = gm_ref[...].astype(wide)
    seg = segc_ref[...]
    taps = [vec_ref[2 + j : 3 + j, :] for j in range(KW)]
    grad = gm * gate_ref[...].astype(wide)
    conv = taps[0] * v_wide
    gv_conv = taps[0] * grad
    lines = [jnp.sum(grad * v_wide, 0, keepdims=True)]
    for j in range(1, KW):
        moved = shift_rows(v_wide, seg, j, False)
        conv = conv + taps[j] * moved
        lines.append(jnp.sum(grad * moved, 0, keepdims=True))
        gv_conv = gv_conv + taps[j] * shift_rows(grad, seg, j, True)
    lines.append(jnp.zeros((LANES - KW, 128), wide))
    gfilt_ref[...] = jnp.concatenate(lines, 0).T.astype(low)
    ggate_ref[...] = (gm * conv).astype(low)
    gconv_ref[...] = gv_conv.astype(low)


def conv_back(v, gm, gate, vec, seg, deps=()):
    length, width = v.shape
    column = pl.BlockSpec((length, 128), lambda p: (0, p))
    small = pl.BlockSpec((8, 128), lambda p: (0, p))
    seg_col = seg.reshape(length, 1)
    return launch(
        conv_back_kernel,
        deps,
        grid=(width // 128,),
        in_specs=[column, column, column, small, whole(seg_col)],
        out_specs=[column, column, pl.BlockSpec((128, LANES), lambda p: (p, 0))],
        out_shape=[jax.ShapeDtypeStruct((length, width), low)] * 2 + [jax.ShapeDtypeStruct((width, LANES), low)],
        compiler_params=params(48),
        cost_estimate=cost(1, 10),
        name="convolution_backward",
    )(v, gm, gate, vec, seg_col)


def mix_kernel(x_ref, mixed_ref, vec_ref, weight_ref, middle_ref, hidden_ref):
    middle = x_ref[...].astype(wide) + dot(mixed_ref[...], weight_ref[...])
    inverse = lax.rsqrt(jnp.mean(middle * middle, axis=-1, keepdims=True) + EPS)
    middle_ref[...] = middle
    hidden_ref[...] = (middle * inverse * vec_ref[1:2, :]).astype(low)


def mix(x, mixed, vec, full, deps=()):
    length, width = x.shape
    return launch(
        mix_kernel,
        deps,
        grid=(length // TILE,),
        in_specs=[rows(TILE, width), rows(TILE, width), fixed(vec.shape), fixed((width, width))],
        out_specs=[rows(TILE, width), rows(TILE, width)],
        out_shape=[jax.ShapeDtypeStruct((length, width), wide), jax.ShapeDtypeStruct((length, width), low)],
        compiler_params=params(32),
        cost_estimate=cost(3, 16),
        name="mix",
    )(x, mixed, vec, full)


def first_half(n):
    return lambda i, *_: (jnp.minimum(i, n - 1), 0)


def second_half(n):
    return lambda i, *_: (jnp.maximum(i - n, 0), 0)


def feed_kernel(n, offs_ref, ha_ref, hb_ref, ca_ref, cb_ref, *refs):
    pieces, downs = refs[:4], refs[4:6]
    act_ref, both_ref, full_out_ref, down_out_ref, full_ref, down_ref, sems = refs[6:]
    copies = [
        pltpu.make_async_copy(full_ref, full_out_ref, sems.at[0]),
        pltpu.make_async_copy(down_ref, down_out_ref, sems.at[1]),
    ]
    step = pl.program_id(0)
    half = full_ref.shape[1] // 2

    @pl.when(step == 0)
    def _():
        place(offs_ref, FEED_AT, pieces, full_ref)
        place(offs_ref, DOWN_AT, downs, down_ref)
        for copy in copies:
            copy.start()

    def work(hidden, cotangent):
        for at in range(0, half, 256):
            gate = dot(hidden, full_ref[:, at : at + 256])
            up = dot(hidden, full_ref[:, half + at : half + at + 256])
            gact = dot_nt(cotangent, down_ref[at : at + 256, :])
            sig = jax.nn.sigmoid(gate)
            silu = gate * sig
            act_ref[:, at : at + 256] = (silu * up).astype(low)
            both_ref[:, at : at + 256] = (gact * up * (sig + silu * (1.0 - sig))).astype(low)
            both_ref[:, half + at : half + at + 256] = (gact * silu).astype(low)

    @pl.when(step < n)
    def _():
        work(ha_ref[...], ca_ref[...])

    @pl.when(step >= n)
    def _():
        work(hb_ref[...], cb_ref[...])

    @pl.when(step == 2 * n - 1)
    def _():
        for copy in copies:
            copy.wait()


def feed(offs, hidden, cotangent, j, w_down, pieces, down_pieces, deps=()):
    length, width = hidden[0].shape
    n = length // TILE
    half = w_down.shape[0]
    first = pl.BlockSpec((TILE, width), first_half(n))
    second = pl.BlockSpec((TILE, width), second_half(n))
    own_down = pl.BlockSpec((half // 2, width), lambda *_: (j, 0), pipeline_mode=pl.Buffered(1))
    given_rows = pl.BlockSpec(pieces[0].shape, lambda *_: (j, 0), pipeline_mode=pl.Buffered(1))
    return launch(
        functools.partial(feed_kernel, n),
        deps,
        scalars=1,
        grid=(2 * n,),
        in_specs=[first, second, first, second]
        + [fixed(pieces[0].shape), given_rows]
        + [fixed(p.shape) for p in pieces[2:]]
        + [own_down]
        + [fixed(p.shape) for p in down_pieces],
        out_specs=[rows(TILE, half), rows(TILE, 2 * half)] + [pl.BlockSpec(memory_space=pl.ANY)] * 2,
        scratch_shapes=[
            pltpu.VMEM((width, 2 * half), low),
            pltpu.VMEM((half, width), low),
            pltpu.SemaphoreType.DMA((2,)),
        ],
        out_shape=[
            jax.ShapeDtypeStruct((2 * length, half), low),
            jax.ShapeDtypeStruct((2 * length, 2 * half), low),
            jax.ShapeDtypeStruct((width, 2 * half), low),
            jax.ShapeDtypeStruct((half, width), low),
        ],
        compiler_params=params(48),
        cost_estimate=cost(16, 34),
        name="feed_in",
    )(offs, *hidden, *cotangent, *pieces, w_down, *down_pieces)


def weight_grad_kernel(shape_of, counts, outs, length, offs_ref, *refs):
    targets = [(ref, row * TILE) for ref, height in zip(refs[-len(outs) :], outs) for row in range(height)]
    step = pl.program_id(0)

    def work(lefts, rights):
        terms = max(len(lefts[0]), len(rights))

        def part_of(group, t):
            return group[t][...] if len(group) == terms else group[0][t * length : (t + 1) * length, :]

        for b, (ref, row) in enumerate(targets):
            value = None
            for t in range(terms):
                product = dot_tn(part_of(lefts[b], t), part_of(rights, t))
                value = product if value is None else value + product
            ref[row : row + TILE, :] = value.astype(low)

    start = 0
    for (left_at, right_at), count in zip(shape_of, counts):
        lefts = [[refs[n] for n in block] for block in left_at]
        rights = [refs[n] for n in right_at]
        if len(counts) == 1:
            work(lefts, rights)
        else:
            pl.when((step >= start) & (step < start + count))(functools.partial(work, lefts, rights))
        start += count


def weight_grad(offs, base, groups, outs, name, tile=512, deps=()):
    blocks = sum(outs)
    counts = [rights[0].shape[1] // tile for _, rights in groups]
    columns = sum(counts) * tile
    in_specs, operands, shape_of, known = [], [], [], {}
    start = 0
    for (lefts, rights), count in zip(groups, counts):
        key = tuple(id(a) for a in lefts)
        if key not in known:
            known[key] = []
            for b in range(blocks):
                known[key].append([len(operands) + n for n in range(len(lefts))])
                for a in lefts:
                    in_specs.append(pl.BlockSpec((a.shape[0], TILE), lambda j, offs, b=b: (0, offs[base + b])))
                    operands.append(a)
        shape_of.append((known[key], [len(operands) + n for n in range(len(rights))]))
        for a in rights:

            def where_to(j, offs, start=start, count=count):
                return (0, jnp.clip(j - start, 0, count - 1))

            in_specs.append(pl.BlockSpec((a.shape[0], tile), where_to))
            operands.append(a)
        start += count
    tokens = sum(a.shape[0] for a in groups[0][0])
    terms = max(len(groups[0][0]), len(groups[0][1]))
    return launch(
        functools.partial(weight_grad_kernel, shape_of, counts, outs, tokens // terms),
        deps,
        scalars=1,
        grid=(sum(counts),),
        in_specs=in_specs,
        out_specs=[pl.BlockSpec((height * TILE, tile), lambda j, offs: (0, j)) for height in outs],
        out_shape=[jax.ShapeDtypeStruct((height * TILE, columns), low) for height in outs],
        compiler_params=params(48),
        cost_estimate=cost(2.5e-9 * tokens * 1024 * columns, (tokens * (1024 + columns) * 2 + 2048 * columns) / 2**20),
        name=name,
    )(offs, *operands)


def feed_back_kernel(a_ref, b_ref, wa_ref, wb_ref, out_ref):
    out_ref[...] = (dot_nt(a_ref[...], wa_ref[...]) + dot_nt(b_ref[...], wb_ref[...])).astype(low)


def feed_back(first, second, full_first, full_second, deps=()):
    length = first.shape[0] // 2
    width = full_first.shape[0]
    n = length // TILE
    tile = pl.BlockSpec((TILE, first.shape[1]), lambda i: (i + n, 0))
    return launch(
        feed_back_kernel,
        deps,
        grid=(n,),
        in_specs=[tile, tile, fixed(full_first.shape), fixed(full_second.shape)],
        out_specs=rows(TILE, width),
        out_shape=jax.ShapeDtypeStruct((length, width), low),
        compiler_params=params(32),
        cost_estimate=cost(10, 18),
        name="feed_back_partner",
    )(first, second, full_first, full_second)


def middle_back_kernel(
    a_ref, b_ref, other_ref, middle_ref, cot_ref, vec_ref, wa_ref, wb_ref, wo_ref,
    gmiddle_ref, gbranch_ref, gmixed_ref, ggain_ref,
):
    ghidden = dot_nt(a_ref[...], wa_ref[...]) + dot_nt(b_ref[...], wb_ref[...]) + other_ref[...].astype(wide)
    middle = middle_ref[...]
    inverse = lax.rsqrt(jnp.mean(middle * middle, axis=-1, keepdims=True) + EPS)
    normed = middle * inverse
    gain = jnp.sum(ghidden * normed, axis=0, keepdims=True)

    @pl.when(pl.program_id(0) == 0)
    def _():
        ggain_ref[...] = jnp.zeros_like(ggain_ref)

    ggain_ref[0:1, :] += gain
    scaled = ghidden * vec_ref[1:2, :]
    gmiddle = cot_ref[...].astype(wide) + inverse * (
        scaled - normed * jnp.mean(scaled * normed, axis=-1, keepdims=True)
    )
    gmiddle_ref[...] = gmiddle
    gbranch = gmiddle.astype(low)
    gbranch_ref[...] = gbranch
    gmixed_ref[...] = dot_nt(gbranch, wo_ref[...]).astype(low)


def middle_back(first, second, other, middle, cotangent, vec, full_first, full_second, w_output, deps=()):
    length, width = middle.shape
    tile = rows(TILE, first.shape[1])
    line = rows(TILE, width)
    return launch(
        middle_back_kernel,
        deps,
        grid=(length // TILE,),
        in_specs=[
            tile, tile, line, line, line, fixed(vec.shape), fixed(full_first.shape), fixed(full_second.shape), fixed((width, width))
        ],
        out_specs=[line, line, line, fixed((8, width))],
        out_shape=[
            jax.ShapeDtypeStruct((length, width), wide),
            jax.ShapeDtypeStruct((length, width), low),
            jax.ShapeDtypeStruct((length, width), low),
            jax.ShapeDtypeStruct((8, width), wide),
        ],
        compiler_params=params(48),
        cost_estimate=cost(13, 40),
        name="middle_back",
    )(first, second, other, middle, cotangent, vec, full_first, full_second, w_output)


def feed_out_kernel(add, *refs):
    out_ref = refs[-1]
    value = dot(refs[0][...], refs[2][...]) + dot(refs[1][...], refs[3][...])
    for ref in refs[4:-1]:
        value = value + ref[...].astype(wide)
    out_ref[...] = value.astype(low)


def feed_out(first, second, down_first, down_second, shift, extras, name, deps=()):
    length = first.shape[0] // 2
    width = down_first.shape[1]
    n = length // TILE
    tile = pl.BlockSpec((TILE, first.shape[1]), lambda i: (i + shift * n, 0))
    return launch(
        functools.partial(feed_out_kernel, len(extras)),
        deps,
        grid=(n,),
        in_specs=[tile, tile, fixed(down_first.shape), fixed(down_second.shape)] + [rows(TILE, width)] * len(extras),
        out_specs=rows(TILE, width),
        out_shape=jax.ShapeDtypeStruct((length, width), low),
        compiler_params=params(32),
        cost_estimate=cost(5, 16),
        name=name,
    )(first, second, down_first, down_second, *extras)


def tokens_back_kernel(gqk_ref, gv_ref, ggate_ref, x_ref, gmiddle_ref, vec_ref, full_ref, gtokens_ref, ggain_ref):
    two = gqk_ref.shape[1]
    width = x_ref.shape[1]
    quarter = two // 4
    ghidden = None
    for n, col in enumerate((0, 2, 1, 3)):
        at = width + col * quarter
        term = dot_nt(gqk_ref[:, n * quarter : (n + 1) * quarter], full_ref[:, at : at + quarter])
        ghidden = term if ghidden is None else ghidden + term
    ghidden = (
        ghidden
        + dot_nt(gv_ref[...], full_ref[:, width + two : 2 * width + two])
        + dot_nt(ggate_ref[...], full_ref[:, two + 2 * width : two + 3 * width])
    )
    x = x_ref[...].astype(wide)
    inverse = lax.rsqrt(jnp.mean(x * x, axis=-1, keepdims=True) + EPS)
    normed = x * inverse

    @pl.when(pl.program_id(0) == 0)
    def _():
        ggain_ref[...] = jnp.zeros_like(ggain_ref)

    ggain_ref[0:1, :] += jnp.sum(ghidden * normed, axis=0, keepdims=True)
    scaled = ghidden * vec_ref[0:1, :]
    gtokens_ref[...] = gmiddle_ref[...] + inverse * (
        scaled - normed * jnp.mean(scaled * normed, axis=-1, keepdims=True)
    )


def tokens_back(gqk, gv, ggate, x, gmiddle, vec, full, deps=()):
    length, width = x.shape
    line = rows(TILE, width)
    return launch(
        tokens_back_kernel,
        deps,
        grid=(length // TILE,),
        in_specs=[rows(TILE, gqk.shape[1]), line, line, line, line, fixed(vec.shape), fixed(full.shape)],
        out_specs=[line, fixed((8, width))],
        out_shape=[jax.ShapeDtypeStruct((length, width), wide), jax.ShapeDtypeStruct((8, width), wide)],
        compiler_params=params(40),
        cost_estimate=cost(7, 24),
        name="tokens_back",
    )(gqk, gv, ggate, x, gmiddle, vec, full)


def as_line(column):
    return jnp.broadcast_to(column, (column.shape[0], LANES)).T[0]


def spread_kernel(cols_ref, gain_ref, wg_ref, wu_ref, a_ref, b_ref, c_ref, d_ref, gate_ref, up_ref, ggain_ref):
    total = None
    for n, ref in enumerate((a_ref, b_ref, c_ref, d_ref)):
        quarter = ref.shape[1] // 4
        for part_y in range(2):
            at = pl.ds(pl.multiple_of(cols_ref[COLS_AT + 2 * n + part_y], 512), quarter)
            gate = ref[:, part_y * quarter : (part_y + 1) * quarter].astype(wide)
            up = ref[:, (2 + part_y) * quarter : (3 + part_y) * quarter].astype(wide)
            gate_ref[:, at] = gate
            up_ref[:, at] = up
            term = gate * wg_ref[:, at].astype(wide) + up * wu_ref[:, at].astype(wide)
            line = jnp.sum(term, axis=1, keepdims=True)
            total = line if total is None else total + line
    ggain_ref[...] = as_line(total / gain_ref[...])


def spread(cols, gain, w_gate, w_up, blocks, deps=()):
    height, width = blocks[0].shape
    shape = jax.ShapeDtypeStruct((height, 2 * width), wide)
    return launch(
        spread_kernel,
        deps,
        scalars=1,
        grid=(1,),
        in_specs=[fixed(gain.shape), fixed(w_gate.shape), fixed(w_up.shape)] + [fixed(b.shape) for b in blocks],
        out_specs=[fixed(shape.shape)] * 2 + [fixed(gain.shape[:1])],
        out_shape=[shape, shape, jax.ShapeDtypeStruct(gain.shape[:1], wide)],
        compiler_params=params(24),
        cost_estimate=cost(0.001, 16),
        name="spread",
    )(cols, gain, w_gate, w_up, *blocks)


def pack_kernel(at_ref, g1_ref, g2_ref, taps_ref, q_ref, k_ref, v_ref, c_ref, o_ref, pack_ref, half_ref):
    height = q_ref.shape[0]
    col = 0
    for ref in (o_ref, q_ref, k_ref, v_ref, c_ref):
        pack_ref[:, col : col + ref.shape[1]] = ref[...]
        col += ref.shape[1]
    small = jnp.concatenate([g1_ref[...].astype(wide)[None], g2_ref[...].astype(wide)[None], taps_ref[...].astype(wide)], 0)
    small = jnp.concatenate([small, jnp.zeros((LANES - small.shape[0], height), wide)], 0)
    pack_ref[:, col : col + LANES] = small.T.astype(low)
    at = pl.multiple_of(at_ref[X_AT] * (height // 2), 128)
    half_ref[...] = pack_ref[pl.ds(at, height // 2), :]


def pack_mixer(at, gain_one, gain_two, taps, w_query, w_key, w_value, w_convgate, w_output):
    operands = (gain_one, gain_two, taps, w_query, w_key, w_value, w_convgate, w_output)
    height = w_query.shape[0]
    columns = sum(a.shape[1] for a in operands[3:]) + LANES
    shapes = [(height, columns), (height // 2, columns)]
    return launch(
        pack_kernel,
        scalars=1,
        grid=(1,),
        in_specs=[fixed(a.shape) for a in operands],
        out_specs=[fixed(a) for a in shapes],
        out_shape=[jax.ShapeDtypeStruct(a, low) for a in shapes],
        compiler_params=params(24),
        cost_estimate=cost(0.001, 4),
        name="pack_mixer",
    )(at, *operands)


def pack_feed_kernel(offs_ref, gate_ref, up_ref, down_ref, first_ref, second_ref, give_ref, *refs):
    send_refs, (low_ref, high_ref) = refs[:2], refs[2:]
    height = gate_ref.shape[0]
    sent = PACK_AT + 4 * offs_ref[X_AT]
    targets = (
        (first_ref, 0, PACK_AT),
        (second_ref, 0, PACK_AT + 2),
        (give_ref, 0, PACK_AT + 4),
        (give_ref, height, PACK_AT + 6),
        (send_refs[0], 0, sent),
        (send_refs[1], 0, sent + 2),
    )
    for ref, row, place_at in targets:
        quarter = ref.shape[1] // 4
        for part_y in range(2):
            at = pl.ds(pl.multiple_of(offs_ref[place_at + part_y], 512), quarter)
            ref[row : row + height, part_y * quarter : (part_y + 1) * quarter] = gate_ref[:, at]
            ref[row : row + height, (2 + part_y) * quarter : (3 + part_y) * quarter] = up_ref[:, at]
    size = low_ref.shape[0]
    low_ref[...] = down_ref[:size, :]
    high_ref[...] = down_ref[size:, :]


def pack_feed(offs, w_gate, w_up, w_down, deps=()):
    height, columns = w_gate.shape
    half = (height, columns // 2)
    shapes = [half, half, (2 * height, columns // 2), half, half] + [(w_down.shape[0] // 2, w_down.shape[1])] * 2
    return launch(
        pack_feed_kernel,
        deps,
        scalars=1,
        grid=(1,),
        in_specs=[fixed(w_gate.shape), fixed(w_up.shape), fixed(w_down.shape)],
        out_specs=[fixed(a) for a in shapes],
        out_shape=[jax.ShapeDtypeStruct(a, low) for a in shapes],
        compiler_params=params(24),
        cost_estimate=cost(0.001, 8),
        name="pack_feed",
    )(offs, w_gate, w_up, w_down)


STRIPS = 1


def operand_parts(operand):
    if not isinstance(operand, tuple):
        return operand, None, 1
    return operand if len(operand) == 3 else (*operand, 2)


def step(kernel, offs, operands, shapes, name, deps=(), giga=0.001):
    in_specs, arrays = [], []
    for operand in operands:
        array, half, parts = operand_parts(operand)
        height = array.shape[0] // parts

        def where_to(i, offs, half=half):
            if half is None:
                return (i, 0)
            return ((half(offs) if callable(half) else half) * STRIPS + i, 0)

        in_specs.append(pl.BlockSpec((height // STRIPS, array.shape[1]), where_to))
        arrays.append(array)
    return launch(
        kernel,
        deps,
        scalars=1,
        grid=(STRIPS,),
        in_specs=in_specs,
        out_specs=[rows(shape[0] // STRIPS, shape[1]) for shape in shapes],
        out_shape=[jax.ShapeDtypeStruct(shape, low) for shape in shapes],
        compiler_params=params(24),
        cost_estimate=cost(giga, 8),
        name=name,
    )(offs, *arrays)


def add(*refs):
    total = refs[0].astype(wide)
    for other in refs[1:]:
        total = total + other.astype(wide)
    return total.astype(low)


def sum_kernel(terms, offs_ref, *refs):
    for out_ref, groups in zip(refs[-len(terms) :], terms):
        col = 0
        for group in groups:
            width = refs[group[0]].shape[1]
            out_ref[:, col : col + width] = add(*(refs[n][...] for n in group))
            col += width


def strip_sum(offs, outputs, name, deps=()):
    operands, terms, shapes = [], [], []
    for groups in outputs:
        terms.append([])
        width = 0
        for group in groups:
            terms[-1].append(list(range(len(operands), len(operands) + len(group))))
            operands += group
            first, _, parts = operand_parts(group[0])
            height = first.shape[0] // parts
            width += first.shape[1]
        shapes.append((height, width))
    return step(functools.partial(sum_kernel, terms), offs, operands, shapes, name, deps)


def top_sum(offs, keep, came, deps=()):
    came = came if came.shape[0] * 2 == keep.shape[0] else (came, 0)
    return strip_sum(offs, [[[(keep, 0), came]]], "top_sum", deps)[0]


def rest_sum(offs, triples, deps=()):
    groups = []
    for keep, came, passed in triples:
        came = came if came.shape[0] * 2 == keep.shape[0] else (came, 1)
        groups.append([(keep, 1), came, passed])
    return strip_sum(offs, [groups], "rest_sum", deps)[0]


def halves_sum(offs, pairs, filters=None, deps=()):
    outputs = []
    for half in range(2):
        groups = [[(keep, half), (came, half)] for keep, came in pairs]
        if filters is not None:

            def quarter(offs_ref, half=half):
                return offs_ref[OWNER_AT + 2 + half]

            groups.append([(a, quarter, 4) for a in filters])
        outputs.append(groups)
    return strip_sum(offs, outputs, "halves_sum", deps)


def near_split(offs, keep, came, deps=()):
    def own(offs_ref):
        return offs_ref[X_AT]

    def other(offs_ref):
        return 1 - offs_ref[X_AT]

    return strip_sum(offs, [[[(keep, own), (came, own)]], [[(keep, other), (came, other)]]], "near_split", deps)


def pairs_sum(offs, pairs, deps=()):
    return strip_sum(offs, [[list(pair) for pair in pairs]], "pairs_sum", deps)[0]


def sort_kernel(offs_ref, total_ref, other_ref, own_ref, give_ref):
    skip = total_ref.shape[1] - own_ref.shape[1]

    @pl.when(offs_ref[X_AT + 1] == 0)
    def _():
        own_ref[...] = total_ref[:, skip:]
        give_ref[...] = other_ref[:, skip:]

    @pl.when(offs_ref[X_AT + 1] != 0)
    def _():
        own_ref[...] = other_ref[:, skip:]
        give_ref[...] = total_ref[:, skip:]


def sort_rows(offs, total, other, skip, deps=()):
    shape = (total.shape[0], total.shape[1] - skip)
    return step(sort_kernel, offs, [total, other], [shape, shape], "sort_rows", deps)


def settle_down_kernel(offs_ref, *refs):
    out_ref = refs[-1]
    size = out_ref.shape[0] // 4
    width = out_ref.shape[1]
    for n in range(4):
        side = offs_ref[X_AT] if n % 2 == 0 else 1 - offs_ref[X_AT]
        at = pl.ds(pl.multiple_of((n // 2) * 2 * size + side * size, 128), size)
        out_ref[at, :] = refs[n][:, :width].astype(wide)


def settle_down(offs, pairs, width, deps=()):
    operands = [a for pair in pairs for a in pair]
    size = operands[0].shape[0]
    column = pl.BlockSpec((size, width), lambda *_: (0, 0), pipeline_mode=pl.Buffered(1))
    return launch(
        settle_down_kernel,
        deps,
        scalars=1,
        grid=(1,),
        in_specs=[column] * 4,
        out_specs=fixed((4 * size, width)),
        out_shape=jax.ShapeDtypeStruct((4 * size, width), wide),
        compiler_params=params(24),
        cost_estimate=cost(0.001, 6),
        name="settle_down",
    )(offs, *operands)


def settle_mixer_kernel(
    offs_ref, gain_ref, mine_ref, other_ref, wq_ref, wk_ref, wv_ref, wc_ref,
    gq_ref, gk_ref, gv_ref, gc_ref, go_ref, gf_ref, ggain_ref, all_ref,
):
    size = mine_ref.shape[0]
    for ref, side in ((mine_ref, offs_ref[X_AT]), (other_ref, 1 - offs_ref[X_AT])):
        all_ref[pl.ds(pl.multiple_of(side * size, 128), size), :] = ref[...].astype(wide)
    width = wv_ref.shape[1]
    half = wq_ref.shape[1] // 2
    go_ref[...] = all_ref[:, :width]
    gc = all_ref[:, width : 2 * width]
    gc_ref[...] = gc
    gf_ref[...] = all_ref[:, 2 * width : 2 * width + LANES].T[:KW, :]
    at = 2 * width + LANES
    gv = all_ref[:, at + 4 * half :]
    gv_ref[...] = gv
    total = jnp.sum(gc * wc_ref[...].astype(wide), axis=1, keepdims=True)
    total = total + jnp.sum(gv * wv_ref[...].astype(wide), axis=1, keepdims=True)
    for n, (ref, weight_ref, cols) in enumerate(
        (
            (gq_ref, wq_ref, slice(0, half)),
            (gk_ref, wk_ref, slice(0, half)),
            (gq_ref, wq_ref, slice(half, 2 * half)),
            (gk_ref, wk_ref, slice(half, 2 * half)),
        )
    ):
        value = all_ref[:, at + n * half : at + (n + 1) * half]
        ref[:, cols] = value
        total = total + jnp.sum(value * weight_ref[:, cols].astype(wide), axis=1, keepdims=True)
    ggain_ref[...] = as_line(total / gain_ref[...])


def settle_mixer(offs, gain, mine, other, w_query, w_key, w_value, w_convgate, deps=()):
    operands = (gain, mine, other, w_query, w_key, w_value, w_convgate)
    height, width = w_value.shape
    shapes = [w_query.shape, w_key.shape, w_value.shape, w_convgate.shape, (height, width), (KW, height), gain.shape[:1]]
    return launch(
        settle_mixer_kernel,
        deps,
        scalars=1,
        grid=(1,),
        in_specs=[fixed(a.shape) for a in operands],
        out_specs=[fixed(a) for a in shapes],
        out_shape=[jax.ShapeDtypeStruct(a, wide) for a in shapes],
        scratch_shapes=[pltpu.VMEM((height, mine.shape[1]), wide)],
        compiler_params=params(24),
        cost_estimate=cost(0.001, 8),
        name="settle_mixer",
    )(offs, *operands)


def tick_kernel(offs_ref, out_ref):
    out_ref[...] = jnp.zeros_like(out_ref)


def tick(offs, deps=()):
    return launch(
        tick_kernel,
        deps,
        scalars=1,
        grid=(1,),
        in_specs=[],
        out_specs=fixed((16, LANES)),
        out_shape=jax.ShapeDtypeStruct((16, LANES), low),
        compiler_params=params(24),
        cost_estimate=cost(TICK, 8),
        name="arrived",
    )(offs)


def swap(value, axis):
    return lax.ppermute(value, axis, [(0, 1), (1, 0)])


def later(value, other):
    return lax.optimization_barrier((value, other))[0]


def part(value, index, count, axis=0):
    size = value.shape[axis] // count
    return lax.dynamic_slice_in_dim(value, index * size, size, axis)


def in_order(index, mine, other):
    return jnp.where(
        index == 0, jnp.concatenate([mine, other], 0), jnp.concatenate([other, mine], 0)
    )


def per_device(
    tokens, segment_ids, gain_one, w_query, w_key, w_value, w_convgate, w_output, conv_filter,
    gain_two, w_gate, w_up, w_down, cotangent,
):
    Order.last = None
    Order.scale = 0.05
    x = lax.axis_index("near")
    y = lax.axis_index("row")
    c = lax.axis_index("core")
    s = 2 * y + c
    width = tokens.shape[1]
    seg = segment_ids[0]
    block = w_down.shape[0]

    def flip(bits):
        return jnp.bitwise_xor(s, bits)

    small_block = block // 2
    half = SHARD_ROWS // 2

    def feed_cols(core, j):
        return [((2 * row + core) * 2 + j) * small_block for row in range(2)]

    feed_rows = [s, flip(1), jnp.bitwise_xor(flip(2), x), jnp.bitwise_xor(flip(3), x)]
    offs = [
        x,
        jnp.bitwise_xor(x, c),
        s * SHARD_ROWS,
        flip(1) * SHARD_ROWS,
        flip(2) * SHARD_ROWS + x * half,
        flip(2) * SHARD_ROWS + (1 - x) * half,
        flip(3) * SHARD_ROWS + x * half,
        flip(3) * SHARD_ROWS + (1 - x) * half,
        *(a * SHARD_ROWS for a in feed_rows),
        y * small_block,
        (1 - y) * small_block,
        0,
        0,
        *feed_cols(c, 0), *feed_cols(c, 1), *feed_cols(1 - c, 0), *feed_cols(1 - c, 1),
        *feed_cols(c, 0), *feed_cols(1 - c, 0), *feed_cols(c, 1), *feed_cols(1 - c, 1),
        2 * (1 - y) + 1 - x, 2 * (1 - y) + x, 2 * y + 1 - x, 2 * y + x,
        flip(3), flip(1), flip(2), s,
        2 * (1 - y) + 1 - x, 2 * y + 1 - x, 2 * (1 - y) + x, 2 * y + x,
    ]
    offs = jnp.stack([jnp.asarray(a, jnp.int32) for a in offs])

    pack, pack_half = pack_mixer(
        offs, gain_one, gain_two, conv_filter, w_query, w_key, w_value, w_convgate, w_output
    )
    direct = swap(pack_half, "row")
    near_core = swap(pack, "core")
    relayed = swap(direct, "near")
    pack_pieces = [pack, near_core, direct, relayed, swap(direct, "core"), swap(relayed, "core")]
    cot_other = swap(later(cotangent, direct), "core")

    mine_first, mine_second, give, *sends, down_first, down_second = pack_feed(offs, w_gate, w_up, w_down)
    given = swap(later(give, direct), "core")

    def across(value):
        pairs = []
        for side, row, core in np.ndindex(2, 2, 2):
            pairs.append((4 * side + 2 * row + core, 4 * side + 2 * (1 - row) + (core ^ side)))
        return lax.ppermute(value, ("near", "row", "core"), pairs)

    feed_pieces = [[own, given] for own in (mine_first, mine_second)]
    feed_pieces[0].append(across(later(sends[0], direct)))

    hidden_one, queries, keys, values, gates, vec, full_one = project(offs, tokens, pack_pieces, deps=[cot_other])
    feed_pieces[0].append(swap(later(feed_pieces[0][2], queries), "near"))
    down_pieces = [[swap(later(down_first, queries), "row")]]
    feed_pieces[1].append(across(later(sends[1], queries)))
    pairs = width // 256
    attended = attend(queries, keys, values, gates, vec, seg, 0, pairs)
    mixed, attention, recips = attend(queries, keys, values, gates, vec, seg, pairs, pairs, onto=attended)
    middle, hidden_two = mix(tokens, mixed, vec, full_one, deps=[down_pieces[0][0]])
    down_pieces.append([swap(later(down_second, middle), "row")])
    tick(offs, [feed_pieces[0][3]])
    hiddens = [hidden_two, swap(hidden_two, "core")]
    cots = [cotangent, cot_other]

    Order.scale = 20.0

    def down_grad(act, deps=()):
        return weight_grad(offs, ACT_AT, [([act], cots)], (2, 2), "grad_down", deps=deps)

    def gate_grad(both):
        return weight_grad(offs, GRAD_AT, [(hiddens, [both])], (1, 1, 2), "grad_gate_up")

    first_feed = feed(offs, hiddens, cots, 0, w_down, feed_pieces[0], down_pieces[0])
    feed_pieces[1].append(swap(later(feed_pieces[1][2], first_feed[0]), "near"))
    down_send, down_keep = down_grad(first_feed[0], deps=[feed_pieces[1][2]])
    down_came = swap(down_send, "near")
    gate_send, gate_send_own, gate_keep = gate_grad(first_feed[1])
    gate_came, gate_came_own = swap(gate_send, "row"), swap(gate_send_own, "row")
    second_feed = feed(offs, hiddens, cots, 1, w_down, feed_pieces[1], down_pieces[1])
    acts, boths, fulls, downs = zip(first_feed, second_feed)
    down_passed = swap(top_sum(offs, down_keep, down_came), "row")
    gate_passed = swap(top_sum(offs, gate_keep, gate_came), "near")
    ghidden_part = feed_back(boths[0], boths[1], fulls[0], fulls[1])
    ghidden_other = swap(ghidden_part, "core")
    down_send_2, down_keep_2 = down_grad(second_feed[0])
    down_came_2 = swap(down_send_2, "near")
    gate_send_2, gate_send_own_2, gate_keep_2 = gate_grad(second_feed[1])
    gate_came_2, gate_came_own_2 = swap(gate_send_2, "row"), swap(gate_send_own_2, "row")
    feed_sum = lax.psum(
        rest_sum(offs, [(down_keep, down_came, down_passed), (gate_keep, gate_came_own, gate_passed)]), "far"
    )
    tick(offs)
    gmiddle, gbranch, gmixed, _ = middle_back(
        boths[0], boths[1], ghidden_other, middle, cotangent, vec, fulls[0], fulls[1], full_one
    )
    down_passed_2 = swap(top_sum(offs, down_keep_2, down_came_2), "row")
    gate_passed_2 = swap(top_sum(offs, gate_keep_2, gate_came_2), "near")

    ggate, gconv, gfilter = conv_back(values, gmixed, gates, vec, seg)
    filter_came = swap(gfilter, "core")
    early_send, early_keep = weight_grad(
        offs, OWNER_AT, [([mixed], [gbranch]), ([hidden_one], [ggate])], (2, 2), "grad_output_convgate"
    )
    early_came = swap(early_send, "core")
    attended = attend_back(queries, keys, values, gmixed, attention, recips, gconv, seg, 0, pairs)
    early_give, early_held = halves_sum(offs, [(early_keep, early_came)], [gfilter, filter_came])
    early_came = swap(early_give, "row")
    tick(offs, [feed_sum])
    feed_near = rest_sum(
        offs, [(down_keep_2, down_came_2, down_passed_2), (gate_keep_2, gate_came_own_2, gate_passed_2)]
    )
    feed_other = swap(later(feed_sum, feed_near), "near")
    feed_part = lax.psum_scatter(feed_near, "far", scatter_dimension=0, tiled=True)
    tick(offs)
    gqk, gv = attend_back(
        queries, keys, values, gmixed, attention, recips, gconv, seg, pairs, pairs, onto=attended
    )
    early_own, early_other = near_split(offs, early_held, early_came)
    early_passed = swap(early_other, "near")
    late_send, late_keep = weight_grad(
        offs, OWNER_AT, [([hidden_one], [gqk]), ([hidden_one], [gv])], (2, 2), "grad_query_key_value"
    )
    late_came = swap(late_send, "core")
    own_rows, theirs = sort_rows(offs, feed_sum, feed_other, width)
    spreads = [own_rows, swap(theirs, "core")]
    Order.scale = 0.05
    feed_sum_2 = lax.all_gather(later(feed_part, tick(offs, [feed_part])), "far", axis=0, tiled=True)
    late_give, late_held = halves_sum(offs, [(late_keep, late_came)])
    late_came = swap(late_give, "row")
    grad_tokens, _ = tokens_back(gqk, gv, ggate, tokens, gmiddle, vec, full_one)
    late_own, late_other = near_split(offs, late_held, late_came)
    late_passed = swap(late_other, "near")
    out_part = feed_out(acts[0], acts[1], downs[0], downs[1], 1, [], "feed_out_partner")
    tick(offs, [feed_sum_2])
    mixer_near = pairs_sum(offs, [(early_own, early_passed), (late_own, late_passed)])
    feed_other_2 = swap(later(feed_sum_2, mixer_near), "near")
    Order.scale = 20.0
    mixer_sum = lax.psum(mixer_near, "far")
    out_came = swap(later(out_part, mixer_near), "core")
    tick(offs)
    result = feed_out(acts[0], acts[1], downs[0], downs[1], 0, [middle, out_came], "feed_out")
    own_rows, theirs = sort_rows(offs, feed_sum_2, feed_other_2, width)
    spreads += [own_rows, swap(theirs, "core")]
    grad_down = settle_down(offs, [(feed_sum, feed_other), (feed_sum_2, feed_other_2)], width)
    grad_gate, grad_up, ggain_two = spread(offs, gain_two[:, None].astype(wide), w_gate, w_up, spreads)
    mixer_other = swap(mixer_sum, "near")
    *grads, grad_output, grad_filter, ggain_one = settle_mixer(
        offs, gain_one[:, None].astype(wide), mixer_sum, mixer_other, w_query, w_key, w_value, w_convgate
    )
    return (
        result,
        grad_tokens,
        ggain_one,
        *grads,
        grad_output,
        grad_filter,
        ggain_two,
        grad_gate,
        grad_up,
        grad_down,
    )


def solution(mesh):
    replicas, shards = mesh.shape["rep"], mesh.shape["shard"]
    devices = np.asarray(mesh.devices).reshape(replicas // 2, 2, shards // 2, 2)
    fine = Mesh(devices, ("far", "near", "row", "core"))
    token = P(("far", "near", "row", "core"), None)
    line = P(("row", "core"))
    weight = P(("row", "core"), None)
    taps = P(None, ("row", "core"))
    return jax.shard_map(
        per_device,
        mesh=fine,
        in_specs=(
            token, token, line, weight, weight, weight, weight, weight, taps, line, weight, weight, weight, token
        ),
        out_specs=(
            token, token, line, weight, weight, weight, weight, weight, taps, line, weight, weight, weight
        ),
        check_vma=False,
    )
```

```python
import functools

import jax
import jax.numpy as jnp
import numpy as np
from jax import lax
from jax.experimental import pallas as pl
from jax.experimental.pallas import tpu as pltpu
from jax.sharding import Mesh
from jax.sharding import PartitionSpec as P

HEADS = 16
FEAT = 16
KW = 3
EPS = 1e-06
TILE = 256
SHARD_ROWS = 256
LANES = 128
TICK = 1e5
X_AT, MIXER_AT, FEED_AT, DOWN_AT, PACK_AT, COLS_AT, GRAD_AT, OWNER_AT, ACT_AT, QUARTER_AT = 0, 2, 12, 16, 20, 28, 36, 40, 44, 48

low = jnp.bfloat16
wide = jnp.float32


def dot(a, b):
    return jnp.dot(a, b, preferred_element_type=wide)


def dot_nt(a, b):
    return lax.dot_general(a, b, (((1,), (1,)), ((), ())), preferred_element_type=wide)


def dot_tn(a, b):
    return lax.dot_general(a, b, (((0,), (0,)), ((), ())), preferred_element_type=wide)


class Order:
    last = None
    scale = 1.0


def launch(kernel, deps=(), onto=(), *, scalars=0, grid, in_specs, out_specs, out_shape, scratch_shapes=(), **rest):
    taken = scalars + len(in_specs)
    deps = list(onto) + [d for d in deps if d is not None] + ([] if Order.last is None or any(Order.last is a for a in onto) else [Order.last])

    def body(*refs):
        kernel(*refs[:taken], *refs[taken + len(deps) :])

    spec = pltpu.PrefetchScalarGridSpec(
        num_scalar_prefetch=scalars,
        grid=grid,
        in_specs=list(in_specs) + [pl.BlockSpec(memory_space=pl.ANY)] * len(deps),
        out_specs=out_specs,
        scratch_shapes=list(scratch_shapes),
    )
    aliases = {taken + n: n for n in range(len(onto))}
    run = pl.pallas_call(body, grid_spec=spec, out_shape=out_shape, input_output_aliases=aliases, **rest)

    def call(*operands):
        result = run(*operands, *deps)
        Order.last = result[0] if isinstance(result, (list, tuple)) else result
        return result

    return call


def params(mib, least=60):
    return pltpu.CompilerParams(vmem_limit_bytes=max(mib, least) << 20)


def cost(gigaflops, mebibytes):
    return pl.CostEstimate(
        flops=int(gigaflops * Order.scale * 1e9), bytes_accessed=int(mebibytes * Order.scale * (1 << 20)), transcendentals=0
    )


def fixed(shape):
    return pl.BlockSpec(shape, lambda *_: (0,) * len(shape), pipeline_mode=pl.Buffered(1))


def rows(height, width):
    return pl.BlockSpec((height, width), lambda i, *_: (i, 0))


def place(offs_ref, base, pieces, full_ref):
    for n, piece in enumerate(pieces):
        at = pl.multiple_of(offs_ref[base + n], 64)
        full_ref[pl.ds(at, piece.shape[0]), :] = piece[...]


def project_kernel(offs_ref, x_ref, *refs):
    pieces, (hidden_ref, q_ref, k_ref, v_ref, gate_ref, vec_ref, out_ref, full_ref, sem) = refs[:10], refs[10:]
    copy = pltpu.make_async_copy(full_ref, out_ref, sem)
    heads = HEADS * FEAT
    width = x_ref.shape[1]

    @pl.when(pl.program_id(0) == 0)
    def _():
        place(offs_ref, MIXER_AT, pieces, full_ref)
        copy.start()
        small = full_ref[:, 2 * heads + 3 * width :].astype(wide)
        vec_ref[...] = small.T[:8, :]

    x = x_ref[...].astype(wide)
    inverse = lax.rsqrt(jnp.mean(x * x, axis=-1, keepdims=True) + EPS)
    hidden = (x * inverse * vec_ref[0:1, :]).astype(low)
    hidden_ref[...] = hidden
    at = width
    q_ref[...] = (dot(hidden, full_ref[:, at : at + heads]) * FEAT ** (-0.5)).astype(low)
    k_ref[...] = dot(hidden, full_ref[:, at + heads : at + 2 * heads]).astype(low)
    at = at + 2 * heads
    v_ref[...] = dot(hidden, full_ref[:, at : at + width]).astype(low)
    gate_ref[...] = dot(hidden, full_ref[:, at + width : at + 2 * width]).astype(low)

    @pl.when(pl.program_id(0) == pl.num_programs(0) - 1)
    def _():
        copy.wait()


def project(offs, x, pieces, deps=()):
    length, width = x.shape
    heads = HEADS * FEAT
    columns = pieces[0].shape[1]
    shapes = [
        jax.ShapeDtypeStruct((length, width), low),
        jax.ShapeDtypeStruct((length, heads), low),
        jax.ShapeDtypeStruct((length, heads), low),
        jax.ShapeDtypeStruct((length, width), low),
        jax.ShapeDtypeStruct((length, width), low),
        jax.ShapeDtypeStruct((8, width), wide),
        jax.ShapeDtypeStruct((width, columns), low),
    ]
    return launch(
        project_kernel,
        deps,
        scalars=1,
        grid=(length // TILE,),
        in_specs=[rows(TILE, width)] + [fixed(p.shape) for p in pieces],
        out_specs=[
            rows(TILE, width),
            rows(TILE, heads),
            rows(TILE, heads),
            rows(TILE, width),
            rows(TILE, width),
            fixed((8, width)),
            pl.BlockSpec(memory_space=pl.ANY),
        ],
        scratch_shapes=[pltpu.VMEM((width, columns), low), pltpu.SemaphoreType.DMA],
        out_shape=shapes,
        compiler_params=params(40),
        cost_estimate=cost(7, 22),
        name="project",
    )(offs, x, *pieces)


def shift_rows(v, seg, by, up):
    zeros = jnp.zeros((by, v.shape[1]), v.dtype)
    none = jnp.full((by, 1), -1, seg.dtype)
    if up:
        moved, moved_seg = jnp.concatenate([v[by:], zeros], 0), jnp.concatenate([seg[by:], none], 0)
    else:
        moved = jnp.concatenate([zeros, v[:-by]], 0)
        moved_seg = jnp.concatenate([none, seg[:-by]], 0)
    return jnp.where(moved_seg == seg, moved, 0.0)


def lane_pick(width, start, stop):
    i = lax.broadcasted_iota(jnp.int32, (1, width), 1)
    return (i >= start) & (i < stop)


def attend_kernel(
    first, q_ref, k_ref, v_ref, gate_ref, vec_ref, segr_ref, segc_ref, mixed_ref, att_ref, recip_ref, mask_ref
):
    length = q_ref.shape[0]
    pair = pl.program_id(0) + first
    zero = jnp.zeros((), low)

    @pl.when(pair == first)
    def _():
        for tb in range(0, length, TILE):
            t = lax.broadcasted_iota(jnp.int32, (TILE, length), 0) + tb
            s = lax.broadcasted_iota(jnp.int32, (TILE, length), 1)
            seen = (s <= t) & (segc_ref[tb : tb + TILE, :] == segr_ref[...])
            mask_ref[tb : tb + TILE, :] = jnp.where(seen, 1.0, 0.0).astype(low)

    v = v_ref[...]
    keys, sides = [], []
    for i in range(2):
        head = 2 * pair + i
        keys.append(jnp.where(lane_pick(HEADS * FEAT, head * FEAT, (head + 1) * FEAT), k_ref[...], zero))
        lanes = lane_pick(128, 64 * i, 64 * i + 64)
        ones = jnp.broadcast_to(jnp.where(lanes, 1.0, 0.0).astype(low), (length, 128))
        sides.append(jnp.concatenate([jnp.where(lanes, v, zero), ones], 1))
    for tb in range(0, length, TILE):
        n = tb + TILE
        total = None
        for i in range(2):
            one_plus = dot_nt(q_ref[tb:n, :], keys[i][:n]) + 1.0
            kernel = (one_plus * one_plus + 1.0).astype(low) * mask_ref[tb:n, :n]
            part = dot(kernel, sides[i][:n])
            total = part if total is None else total + part
        recip = 1.0 / total[:, 128:]
        att_ref[tb:n, :] = (total[:, :128] * recip).astype(low)
        recip_ref[tb:n, :] = (2.0 * recip).astype(low)
    v_wide = v.astype(wide)
    seg = segc_ref[...]
    conv = vec_ref[2:3, :] * v_wide
    for j in range(1, KW):
        conv = conv + vec_ref[2 + j : 3 + j, :] * shift_rows(v_wide, seg, j, False)
    mixed_ref[...] = (att_ref[...].astype(wide) + gate_ref[...].astype(wide) * conv).astype(low)


def whole(a):
    return pl.BlockSpec(a.shape, lambda p: (0, 0))


def attend(q, k, v, gate, vec, seg, first, count, onto=(), deps=()):
    length, width = v.shape
    column = pl.BlockSpec((length, 128), lambda p: (0, p + first))
    seg_row, seg_col = seg.reshape(1, length), seg.reshape(length, 1)
    return launch(
        functools.partial(attend_kernel, first),
        deps,
        onto,
        grid=(count,),
        in_specs=[
            whole(q), whole(k), column, column, pl.BlockSpec((8, 128), lambda p: (0, p + first)), whole(seg_row), whole(seg_col)
        ],
        out_specs=[column] * 3,
        out_shape=[jax.ShapeDtypeStruct((length, width), low)] * 3,
        scratch_shapes=[pltpu.VMEM((length, length), low)],
        compiler_params=params(40),
        cost_estimate=cost(18 * count * 128 / width, 14),
        name="attention_forward",
    )(q, k, v, gate, vec, seg_row, seg_col)


def attend_back_kernel(
    first, q_ref, k_ref, v_ref, gm_ref, att_ref, recip_ref, gconv_ref, segr_ref, segc_ref,
    gqk_ref, gv_ref, mask_ref, gq_acc, gk_acc,
):
    length, heads = q_ref.shape
    pair = pl.program_id(0) + first
    zero = jnp.zeros((), low)

    @pl.when(pair == first)
    def _():
        for sb in range(0, length, TILE):
            s = lax.broadcasted_iota(jnp.int32, (TILE, length), 0) + sb
            t = lax.broadcasted_iota(jnp.int32, (TILE, length), 1)
            seen = (s <= t) & (segc_ref[sb : sb + TILE, :] == segr_ref[...])
            mask_ref[sb : sb + TILE, :] = jnp.where(seen, 1.0, 0.0).astype(low)
        gk_acc[...] = jnp.zeros_like(gk_acc)
        gq_acc[...] = jnp.zeros_like(gq_acc)

    v = v_ref[...]
    gm = gm_ref[...].astype(wide)
    gnum_wide = gm * recip_ref[...].astype(wide)
    gnum = gnum_wide.astype(low)
    product = gnum_wide * att_ref[...].astype(wide)
    high = product.astype(low)
    rest = (product - high.astype(wide)).astype(low)
    r = lax.broadcasted_iota(jnp.int32, (256, 128), 0)
    c = lax.broadcasted_iota(jnp.int32, (256, 128), 1)
    same_head = jnp.where(((r % 128) // 64) == (c // 64), 1.0, 0.0).astype(low)
    gtot = -dot(jnp.concatenate([high, rest], 1), same_head)
    gtot_high = gtot.astype(low)
    gtot_rest = (gtot - gtot_high.astype(wide)).astype(low)
    lane = lax.broadcasted_iota(jnp.int32, (1, 128), 1)
    left = jnp.concatenate([gnum, jnp.where(lane % 64 == 0, gtot_high, gtot_rest)], 1)
    gnum_half = gnum * jnp.asarray(0.5, low)
    queries, sides, gnums, keys = [], [], [], []
    for i in range(2):
        head = 2 * pair + i
        mine = lane_pick(heads, head * FEAT, (head + 1) * FEAT)
        queries.append(jnp.where(mine, q_ref[...], zero))
        keys.append(jnp.where(mine, k_ref[...], zero))
        lanes = lane_pick(128, 64 * i, 64 * i + 64)
        ones = jnp.where(lane_pick(128, 64 * i, 64 * i + 2), 1.0, 0.0).astype(low)
        sides.append(jnp.concatenate([jnp.where(lanes, v, zero), jnp.broadcast_to(ones, (length, 128))], 1))
        gnums.append(jnp.where(lanes, gnum_half, zero))
    for sb in range(0, length, TILE):
        n = sb + TILE
        gv = gconv_ref[sb:n, :].astype(wide)
        gk = None
        for i in range(2):
            one_plus = dot_nt(k_ref[sb:n, :], queries[i][sb:]) + 1.0
            mask = mask_ref[sb:n, sb:]
            kernel = (one_plus * one_plus + 1.0).astype(low) * mask
            gv = gv + dot(kernel, gnums[i][sb:])
            gkernel = dot_nt(sides[i][sb:n], left[sb:])
            gscores = (gkernel * one_plus).astype(low) * mask
            part = dot(gscores, queries[i][sb:])
            gk = part if gk is None else gk + part
            gq_acc[sb:, :] += dot_tn(gscores, keys[i][sb:n])
        gv_ref[sb:n, :] = gv.astype(low)
        gk_acc[sb:n, :] += gk

    @pl.when(pl.program_id(0) == pl.num_programs(0) - 1)
    def _():
        mine = slice(2 * FEAT * first, 2 * FEAT * first + gqk_ref.shape[1] // 2)
        gqk_ref[:, : gqk_ref.shape[1] // 2] = (gq_acc[:, mine] * FEAT ** (-0.5)).astype(low)
        gqk_ref[:, gqk_ref.shape[1] // 2 :] = gk_acc[:, mine].astype(low)


def attend_back(q, k, v, gm, att, recip, gconv, seg, first, count, onto=(), deps=()):
    length, width = v.shape
    heads = q.shape[1]
    column = pl.BlockSpec((length, 128), lambda p: (0, p + first))
    seg_row, seg_col = seg.reshape(1, length), seg.reshape(length, 1)
    return launch(
        functools.partial(attend_back_kernel, first),
        deps,
        onto,
        grid=(count,),
        in_specs=[whole(q), whole(k)] + [column] * 5 + [whole(seg_row), whole(seg_col)],
        out_specs=[pl.BlockSpec((length, 4 * FEAT * count), lambda p: (0, first // count)), column],
        out_shape=[jax.ShapeDtypeStruct((length, 2 * heads), low), jax.ShapeDtypeStruct((length, width), low)],
        scratch_shapes=[
            pltpu.VMEM((length, length), low),
            pltpu.VMEM((length, heads), wide),
            pltpu.VMEM((length, heads), wide),
        ],
        compiler_params=params(48),
        cost_estimate=cost(40 * count * 128 / width, 18),
        name="attention_backward",
    )(q, k, v, gm, att, recip, gconv, seg_row, seg_col)


def conv_back_kernel(v_ref, gm_ref, gate_ref, vec_ref, segc_ref, ggate_ref, gconv_ref, gfilt_ref):
    v_wide = v_ref[...].astype(wide)
    gm = gm_ref[...].astype(wide)
    seg = segc_ref[...]
    taps = [vec_ref[2 + j : 3 + j, :] for j in range(KW)]
    grad = gm * gate_ref[...].astype(wide)
    conv = taps[0] * v_wide
    gv_conv = taps[0] * grad
    lines = [jnp.sum(grad * v_wide, 0, keepdims=True)]
    for j in range(1, KW):
        moved = shift_rows(v_wide, seg, j, False)
        conv = conv + taps[j] * moved
        lines.append(jnp.sum(grad * moved, 0, keepdims=True))
        gv_conv = gv_conv + taps[j] * shift_rows(grad, seg, j, True)
    lines.append(jnp.zeros((LANES - KW, 128), wide))
    gfilt_ref[...] = jnp.concatenate(lines, 0).T.astype(low)
    ggate_ref[...] = (gm * conv).astype(low)
    gconv_ref[...] = gv_conv.astype(low)


def conv_back(v, gm, gate, vec, seg, deps=()):
    length, width = v.shape
    column = pl.BlockSpec((length, 128), lambda p: (0, p))
    small = pl.BlockSpec((8, 128), lambda p: (0, p))
    seg_col = seg.reshape(length, 1)
    return launch(
        conv_back_kernel,
        deps,
        grid=(width // 128,),
        in_specs=[column, column, column, small, whole(seg_col)],
        out_specs=[column, column, pl.BlockSpec((128, LANES), lambda p: (p, 0))],
        out_shape=[jax.ShapeDtypeStruct((length, width), low)] * 2 + [jax.ShapeDtypeStruct((width, LANES), low)],
        compiler_params=params(48),
        cost_estimate=cost(1, 10),
        name="convolution_backward",
    )(v, gm, gate, vec, seg_col)


def mix_kernel(x_ref, mixed_ref, vec_ref, weight_ref, middle_ref, hidden_ref):
    middle = x_ref[...].astype(wide) + dot(mixed_ref[...], weight_ref[...])
    inverse = lax.rsqrt(jnp.mean(middle * middle, axis=-1, keepdims=True) + EPS)
    middle_ref[...] = middle
    hidden_ref[...] = (middle * inverse * vec_ref[1:2, :]).astype(low)


def mix(x, mixed, vec, full, deps=()):
    length, width = x.shape
    return launch(
        mix_kernel,
        deps,
        grid=(length // TILE,),
        in_specs=[rows(TILE, width), rows(TILE, width), fixed(vec.shape), fixed((width, width))],
        out_specs=[rows(TILE, width), rows(TILE, width)],
        out_shape=[jax.ShapeDtypeStruct((length, width), wide), jax.ShapeDtypeStruct((length, width), low)],
        compiler_params=params(32),
        cost_estimate=cost(3, 16),
        name="mix",
    )(x, mixed, vec, full)


def first_half(n):
    return lambda i, *_: (jnp.minimum(i, n - 1), 0)


def second_half(n):
    return lambda i, *_: (jnp.maximum(i - n, 0), 0)


def feed_kernel(n, offs_ref, ha_ref, hb_ref, ca_ref, cb_ref, *refs):
    pieces, downs = refs[:4], refs[4:6]
    act_ref, both_ref, full_out_ref, down_out_ref, full_ref, down_ref, sems = refs[6:]
    copies = [
        pltpu.make_async_copy(full_ref, full_out_ref, sems.at[0]),
        pltpu.make_async_copy(down_ref, down_out_ref, sems.at[1]),
    ]
    step = pl.program_id(0)
    half = full_ref.shape[1] // 2

    @pl.when(step == 0)
    def _():
        place(offs_ref, FEED_AT, pieces, full_ref)
        place(offs_ref, DOWN_AT, downs, down_ref)
        for copy in copies:
            copy.start()

    def work(hidden, cotangent):
        for at in range(0, half, 256):
            gate = dot(hidden, full_ref[:, at : at + 256])
            up = dot(hidden, full_ref[:, half + at : half + at + 256])
            gact = dot_nt(cotangent, down_ref[at : at + 256, :])
            sig = jax.nn.sigmoid(gate)
            silu = gate * sig
            act_ref[:, at : at + 256] = (silu * up).astype(low)
            both_ref[:, at : at + 256] = (gact * up * (sig + silu * (1.0 - sig))).astype(low)
            both_ref[:, half + at : half + at + 256] = (gact * silu).astype(low)

    @pl.when(step < n)
    def _():
        work(ha_ref[...], ca_ref[...])

    @pl.when(step >= n)
    def _():
        work(hb_ref[...], cb_ref[...])

    @pl.when(step == 2 * n - 1)
    def _():
        for copy in copies:
            copy.wait()


def feed(offs, hidden, cotangent, j, w_down, pieces, down_pieces, deps=()):
    length, width = hidden[0].shape
    n = length // TILE
    half = w_down.shape[0]
    first = pl.BlockSpec((TILE, width), first_half(n))
    second = pl.BlockSpec((TILE, width), second_half(n))
    own_down = pl.BlockSpec((half // 2, width), lambda *_: (j, 0), pipeline_mode=pl.Buffered(1))
    given_rows = pl.BlockSpec(pieces[0].shape, lambda *_: (j, 0), pipeline_mode=pl.Buffered(1))
    return launch(
        functools.partial(feed_kernel, n),
        deps,
        scalars=1,
        grid=(2 * n,),
        in_specs=[first, second, first, second]
        + [fixed(pieces[0].shape), given_rows]
        + [fixed(p.shape) for p in pieces[2:]]
        + [own_down]
        + [fixed(p.shape) for p in down_pieces],
        out_specs=[rows(TILE, half), rows(TILE, 2 * half)] + [pl.BlockSpec(memory_space=pl.ANY)] * 2,
        scratch_shapes=[
            pltpu.VMEM((width, 2 * half), low),
            pltpu.VMEM((half, width), low),
            pltpu.SemaphoreType.DMA((2,)),
        ],
        out_shape=[
            jax.ShapeDtypeStruct((2 * length, half), low),
            jax.ShapeDtypeStruct((2 * length, 2 * half), low),
            jax.ShapeDtypeStruct((width, 2 * half), low),
            jax.ShapeDtypeStruct((half, width), low),
        ],
        compiler_params=params(48),
        cost_estimate=cost(16, 34),
        name="feed_in",
    )(offs, *hidden, *cotangent, *pieces, w_down, *down_pieces)


def weight_grad_kernel(shape_of, counts, outs, length, offs_ref, *refs):
    targets = [(ref, row * TILE) for ref, height in zip(refs[-len(outs) :], outs) for row in range(height)]
    step = pl.program_id(0)

    def work(lefts, rights):
        terms = max(len(lefts[0]), len(rights))

        def part_of(group, t):
            return group[t][...] if len(group) == terms else group[0][t * length : (t + 1) * length, :]

        for b, (ref, row) in enumerate(targets):
            value = None
            for t in range(terms):
                product = dot_tn(part_of(lefts[b], t), part_of(rights, t))
                value = product if value is None else value + product
            ref[row : row + TILE, :] = value.astype(low)

    start = 0
    for (left_at, right_at), count in zip(shape_of, counts):
        lefts = [[refs[n] for n in block] for block in left_at]
        rights = [refs[n] for n in right_at]
        if len(counts) == 1:
            work(lefts, rights)
        else:
            pl.when((step >= start) & (step < start + count))(functools.partial(work, lefts, rights))
        start += count


def weight_grad(offs, base, groups, outs, name, tile=512, deps=()):
    blocks = sum(outs)
    counts = [rights[0].shape[1] // tile for _, rights in groups]
    columns = sum(counts) * tile
    in_specs, operands, shape_of, known = [], [], [], {}
    start = 0
    for (lefts, rights), count in zip(groups, counts):
        key = tuple(id(a) for a in lefts)
        if key not in known:
            known[key] = []
            for b in range(blocks):
                known[key].append([len(operands) + n for n in range(len(lefts))])
                for a in lefts:
                    in_specs.append(pl.BlockSpec((a.shape[0], TILE), lambda j, offs, b=b: (0, offs[base + b])))
                    operands.append(a)
        shape_of.append((known[key], [len(operands) + n for n in range(len(rights))]))
        for a in rights:

            def where_to(j, offs, start=start, count=count):
                return (0, jnp.clip(j - start, 0, count - 1))

            in_specs.append(pl.BlockSpec((a.shape[0], tile), where_to))
            operands.append(a)
        start += count
    tokens = sum(a.shape[0] for a in groups[0][0])
    terms = max(len(groups[0][0]), len(groups[0][1]))
    return launch(
        functools.partial(weight_grad_kernel, shape_of, counts, outs, tokens // terms),
        deps,
        scalars=1,
        grid=(sum(counts),),
        in_specs=in_specs,
        out_specs=[pl.BlockSpec((height * TILE, tile), lambda j, offs: (0, j)) for height in outs],
        out_shape=[jax.ShapeDtypeStruct((height * TILE, columns), low) for height in outs],
        compiler_params=params(48, 48),
        cost_estimate=cost(2.5e-9 * tokens * 1024 * columns, (tokens * (1024 + columns) * 2 + 2048 * columns) / 2**20),
        name=name,
    )(offs, *operands)


def feed_back_kernel(a_ref, b_ref, wa_ref, wb_ref, out_ref):
    out_ref[...] = (dot_nt(a_ref[...], wa_ref[...]) + dot_nt(b_ref[...], wb_ref[...])).astype(low)


def feed_back(first, second, full_first, full_second, deps=()):
    length = first.shape[0] // 2
    width = full_first.shape[0]
    n = length // TILE
    tile = pl.BlockSpec((TILE, first.shape[1]), lambda i: (i + n, 0))
    return launch(
        feed_back_kernel,
        deps,
        grid=(n,),
        in_specs=[tile, tile, fixed(full_first.shape), fixed(full_second.shape)],
        out_specs=rows(TILE, width),
        out_shape=jax.ShapeDtypeStruct((length, width), low),
        compiler_params=params(32),
        cost_estimate=cost(10, 18),
        name="feed_back_partner",
    )(first, second, full_first, full_second)


def middle_back_kernel(
    a_ref, b_ref, other_ref, middle_ref, cot_ref, vec_ref, wa_ref, wb_ref, wo_ref,
    gmiddle_ref, gbranch_ref, gmixed_ref, ggain_ref,
):
    ghidden = dot_nt(a_ref[...], wa_ref[...]) + dot_nt(b_ref[...], wb_ref[...]) + other_ref[...].astype(wide)
    middle = middle_ref[...]
    inverse = lax.rsqrt(jnp.mean(middle * middle, axis=-1, keepdims=True) + EPS)
    normed = middle * inverse
    gain = jnp.sum(ghidden * normed, axis=0, keepdims=True)

    @pl.when(pl.program_id(0) == 0)
    def _():
        ggain_ref[...] = jnp.zeros_like(ggain_ref)

    ggain_ref[0:1, :] += gain
    scaled = ghidden * vec_ref[1:2, :]
    gmiddle = cot_ref[...].astype(wide) + inverse * (
        scaled - normed * jnp.mean(scaled * normed, axis=-1, keepdims=True)
    )
    gmiddle_ref[...] = gmiddle
    gbranch = gmiddle.astype(low)
    gbranch_ref[...] = gbranch
    gmixed_ref[...] = dot_nt(gbranch, wo_ref[...]).astype(low)


def middle_back(first, second, other, middle, cotangent, vec, full_first, full_second, w_output, deps=()):
    length, width = middle.shape
    tile = rows(TILE, first.shape[1])
    line = rows(TILE, width)
    return launch(
        middle_back_kernel,
        deps,
        grid=(length // TILE,),
        in_specs=[
            tile, tile, line, line, line, fixed(vec.shape), fixed(full_first.shape), fixed(full_second.shape), fixed((width, width))
        ],
        out_specs=[line, line, line, fixed((8, width))],
        out_shape=[
            jax.ShapeDtypeStruct((length, width), wide),
            jax.ShapeDtypeStruct((length, width), low),
            jax.ShapeDtypeStruct((length, width), low),
            jax.ShapeDtypeStruct((8, width), wide),
        ],
        compiler_params=params(48),
        cost_estimate=cost(13, 40),
        name="middle_back",
    )(first, second, other, middle, cotangent, vec, full_first, full_second, w_output)


def feed_out_kernel(add, *refs):
    out_ref = refs[-1]
    value = dot(refs[0][...], refs[2][...]) + dot(refs[1][...], refs[3][...])
    for ref in refs[4:-1]:
        value = value + ref[...].astype(wide)
    out_ref[...] = value.astype(low)


def feed_out(first, second, down_first, down_second, shift, extras, name, deps=()):
    length = first.shape[0] // 2
    width = down_first.shape[1]
    n = length // TILE
    tile = pl.BlockSpec((TILE, first.shape[1]), lambda i: (i + shift * n, 0))
    return launch(
        functools.partial(feed_out_kernel, len(extras)),
        deps,
        grid=(n,),
        in_specs=[tile, tile, fixed(down_first.shape), fixed(down_second.shape)] + [rows(TILE, width)] * len(extras),
        out_specs=rows(TILE, width),
        out_shape=jax.ShapeDtypeStruct((length, width), low),
        compiler_params=params(32),
        cost_estimate=cost(5, 16),
        name=name,
    )(first, second, down_first, down_second, *extras)


def tokens_back_kernel(gqk_ref, gv_ref, ggate_ref, x_ref, gmiddle_ref, vec_ref, full_ref, gtokens_ref, ggain_ref):
    two = gqk_ref.shape[1]
    width = x_ref.shape[1]
    quarter = two // 4
    ghidden = None
    for n, col in enumerate((0, 2, 1, 3)):
        at = width + col * quarter
        term = dot_nt(gqk_ref[:, n * quarter : (n + 1) * quarter], full_ref[:, at : at + quarter])
        ghidden = term if ghidden is None else ghidden + term
    ghidden = (
        ghidden
        + dot_nt(gv_ref[...], full_ref[:, width + two : 2 * width + two])
        + dot_nt(ggate_ref[...], full_ref[:, two + 2 * width : two + 3 * width])
    )
    x = x_ref[...].astype(wide)
    inverse = lax.rsqrt(jnp.mean(x * x, axis=-1, keepdims=True) + EPS)
    normed = x * inverse

    @pl.when(pl.program_id(0) == 0)
    def _():
        ggain_ref[...] = jnp.zeros_like(ggain_ref)

    ggain_ref[0:1, :] += jnp.sum(ghidden * normed, axis=0, keepdims=True)
    scaled = ghidden * vec_ref[0:1, :]
    gtokens_ref[...] = gmiddle_ref[...] + inverse * (
        scaled - normed * jnp.mean(scaled * normed, axis=-1, keepdims=True)
    )


def tokens_back(gqk, gv, ggate, x, gmiddle, vec, full, deps=()):
    length, width = x.shape
    line = rows(TILE, width)
    return launch(
        tokens_back_kernel,
        deps,
        grid=(length // TILE,),
        in_specs=[rows(TILE, gqk.shape[1]), line, line, line, line, fixed(vec.shape), fixed(full.shape)],
        out_specs=[line, fixed((8, width))],
        out_shape=[jax.ShapeDtypeStruct((length, width), wide), jax.ShapeDtypeStruct((8, width), wide)],
        compiler_params=params(40),
        cost_estimate=cost(7, 24),
        name="tokens_back",
    )(gqk, gv, ggate, x, gmiddle, vec, full)


def as_line(column):
    return jnp.broadcast_to(column, (column.shape[0], LANES)).T[0]


def spread_kernel(cols_ref, gain_ref, wg_ref, wu_ref, a_ref, b_ref, c_ref, d_ref, gate_ref, up_ref, ggain_ref):
    total = None
    for n, ref in enumerate((a_ref, b_ref, c_ref, d_ref)):
        quarter = ref.shape[1] // 4
        for part_y in range(2):
            at = pl.ds(pl.multiple_of(cols_ref[COLS_AT + 2 * n + part_y], 512), quarter)
            gate = ref[:, part_y * quarter : (part_y + 1) * quarter].astype(wide)
            up = ref[:, (2 + part_y) * quarter : (3 + part_y) * quarter].astype(wide)
            gate_ref[:, at] = gate
            up_ref[:, at] = up
            term = gate * wg_ref[:, at].astype(wide) + up * wu_ref[:, at].astype(wide)
            line = jnp.sum(term, axis=1, keepdims=True)
            total = line if total is None else total + line
    ggain_ref[...] = as_line(total / gain_ref[...])


def spread(cols, gain, w_gate, w_up, blocks, deps=()):
    height, width = blocks[0].shape
    shape = jax.ShapeDtypeStruct((height, 2 * width), wide)
    return launch(
        spread_kernel,
        deps,
        scalars=1,
        grid=(1,),
        in_specs=[fixed(gain.shape), fixed(w_gate.shape), fixed(w_up.shape)] + [fixed(b.shape) for b in blocks],
        out_specs=[fixed(shape.shape)] * 2 + [fixed(gain.shape[:1])],
        out_shape=[shape, shape, jax.ShapeDtypeStruct(gain.shape[:1], wide)],
        compiler_params=params(24),
        cost_estimate=cost(0.001, 16),
        name="spread",
    )(cols, gain, w_gate, w_up, *blocks)


def pack_kernel(at_ref, g1_ref, g2_ref, taps_ref, q_ref, k_ref, v_ref, c_ref, o_ref, pack_ref, part_ref):
    height = q_ref.shape[0]
    col = 0
    for ref in (o_ref, q_ref, k_ref, v_ref, c_ref):
        pack_ref[:, col : col + ref.shape[1]] = ref[...]
        col += ref.shape[1]
    small = jnp.concatenate([g1_ref[...].astype(wide)[None], g2_ref[...].astype(wide)[None], taps_ref[...].astype(wide)], 0)
    small = jnp.concatenate([small, jnp.zeros((LANES - small.shape[0], height), wide)], 0)
    pack_ref[:, col : col + LANES] = small.T.astype(low)
    size = part_ref.shape[0]
    part_ref[...] = pack_ref[pl.ds(pl.multiple_of(at_ref[QUARTER_AT] * size, 64), size), :]


def pack_mixer(at, gain_one, gain_two, taps, w_query, w_key, w_value, w_convgate, w_output):
    operands = (gain_one, gain_two, taps, w_query, w_key, w_value, w_convgate, w_output)
    height = w_query.shape[0]
    columns = sum(a.shape[1] for a in operands[3:]) + LANES
    shapes = [(height, columns), (height // 4, columns)]
    return launch(
        pack_kernel,
        scalars=1,
        grid=(1,),
        in_specs=[fixed(a.shape) for a in operands],
        out_specs=[fixed(a) for a in shapes],
        out_shape=[jax.ShapeDtypeStruct(a, low) for a in shapes],
        compiler_params=params(24),
        cost_estimate=cost(0.001, 4),
        name="pack_mixer",
    )(at, *operands)


def pack_feed_kernel(offs_ref, gate_ref, up_ref, down_ref, first_ref, second_ref, give_ref, *refs):
    send_refs, (low_ref, high_ref) = refs[:2], refs[2:]
    height = gate_ref.shape[0]
    sent = PACK_AT + 4 * offs_ref[X_AT]
    targets = (
        (first_ref, 0, PACK_AT),
        (second_ref, 0, PACK_AT + 2),
        (give_ref, 0, PACK_AT + 4),
        (give_ref, height, PACK_AT + 6),
        (send_refs[0], 0, sent),
        (send_refs[1], 0, sent + 2),
    )
    for ref, row, place_at in targets:
        quarter = ref.shape[1] // 4
        for part_y in range(2):
            at = pl.ds(pl.multiple_of(offs_ref[place_at + part_y], 512), quarter)
            ref[row : row + height, part_y * quarter : (part_y + 1) * quarter] = gate_ref[:, at]
            ref[row : row + height, (2 + part_y) * quarter : (3 + part_y) * quarter] = up_ref[:, at]
    size = low_ref.shape[0]
    low_ref[...] = down_ref[:size, :]
    high_ref[...] = down_ref[size:, :]


def pack_feed(offs, w_gate, w_up, w_down, deps=()):
    height, columns = w_gate.shape
    half = (height, columns // 2)
    shapes = [half, half, (2 * height, columns // 2), half, half] + [(w_down.shape[0] // 2, w_down.shape[1])] * 2
    return launch(
        pack_feed_kernel,
        deps,
        scalars=1,
        grid=(1,),
        in_specs=[fixed(w_gate.shape), fixed(w_up.shape), fixed(w_down.shape)],
        out_specs=[fixed(a) for a in shapes],
        out_shape=[jax.ShapeDtypeStruct(a, low) for a in shapes],
        compiler_params=params(24),
        cost_estimate=cost(0.001, 8),
        name="pack_feed",
    )(offs, w_gate, w_up, w_down)


STRIPS = 1


def operand_parts(operand):
    if not isinstance(operand, tuple):
        return operand, None, 1
    return operand if len(operand) == 3 else (*operand, 2)


def step(kernel, offs, operands, shapes, name, deps=(), giga=0.001):
    in_specs, arrays = [], []
    for operand in operands:
        array, half, parts = operand_parts(operand)
        height = array.shape[0] // parts

        def where_to(i, offs, half=half):
            if half is None:
                return (i, 0)
            return ((half(offs) if callable(half) else half) * STRIPS + i, 0)

        in_specs.append(pl.BlockSpec((height // STRIPS, array.shape[1]), where_to))
        arrays.append(array)
    return launch(
        kernel,
        deps,
        scalars=1,
        grid=(STRIPS,),
        in_specs=in_specs,
        out_specs=[rows(shape[0] // STRIPS, shape[1]) for shape in shapes],
        out_shape=[jax.ShapeDtypeStruct(shape, low) for shape in shapes],
        compiler_params=params(24),
        cost_estimate=cost(giga, 8),
        name=name,
    )(offs, *arrays)


def add(*refs):
    total = refs[0].astype(wide)
    for other in refs[1:]:
        total = total + other.astype(wide)
    return total.astype(low)


def sum_kernel(terms, offs_ref, *refs):
    for out_ref, groups in zip(refs[-len(terms) :], terms):
        col = 0
        for group in groups:
            width = refs[group[0]].shape[1]
            out_ref[:, col : col + width] = add(*(refs[n][...] for n in group))
            col += width


def strip_sum(offs, outputs, name, deps=()):
    operands, terms, shapes = [], [], []
    for groups in outputs:
        terms.append([])
        width = 0
        for group in groups:
            terms[-1].append(list(range(len(operands), len(operands) + len(group))))
            operands += group
            first, _, parts = operand_parts(group[0])
            height = first.shape[0] // parts
            width += first.shape[1]
        shapes.append((height, width))
    return step(functools.partial(sum_kernel, terms), offs, operands, shapes, name, deps)


def top_sum(offs, keep, came, deps=()):
    came = came if came.shape[0] * 2 == keep.shape[0] else (came, 0)
    return strip_sum(offs, [[[(keep, 0), came]]], "top_sum", deps)[0]


def rest_sum(offs, triples, deps=()):
    groups = []
    for keep, came, passed in triples:
        came = came if came.shape[0] * 2 == keep.shape[0] else (came, 1)
        groups.append([(keep, 1), came, passed])
    return strip_sum(offs, [groups], "rest_sum", deps)[0]


def halves_sum(offs, pairs, filters=None, deps=()):
    outputs = []
    for half in range(2):
        groups = [[(keep, half), (came, half)] for keep, came in pairs]
        if filters is not None:

            def quarter(offs_ref, half=half):
                return offs_ref[OWNER_AT + 2 + half]

            groups.append([(a, quarter, 4) for a in filters])
        outputs.append(groups)
    return strip_sum(offs, outputs, "halves_sum", deps)


def near_split(offs, keep, came, deps=()):
    def own(offs_ref):
        return offs_ref[X_AT]

    def other(offs_ref):
        return 1 - offs_ref[X_AT]

    return strip_sum(offs, [[[(keep, own), (came, own)]], [[(keep, other), (came, other)]]], "near_split", deps)


def pairs_sum(offs, pairs, deps=()):
    return strip_sum(offs, [[list(pair) for pair in pairs]], "pairs_sum", deps)[0]


def sort_kernel(offs_ref, total_ref, other_ref, own_ref, give_ref):
    skip = total_ref.shape[1] - own_ref.shape[1]

    @pl.when(offs_ref[X_AT + 1] == 0)
    def _():
        own_ref[...] = total_ref[:, skip:]
        give_ref[...] = other_ref[:, skip:]

    @pl.when(offs_ref[X_AT + 1] != 0)
    def _():
        own_ref[...] = other_ref[:, skip:]
        give_ref[...] = total_ref[:, skip:]


def sort_rows(offs, total, other, skip, deps=()):
    shape = (total.shape[0], total.shape[1] - skip)
    return step(sort_kernel, offs, [total, other], [shape, shape], "sort_rows", deps)


def settle_down_kernel(offs_ref, *refs):
    out_ref = refs[-1]
    size = out_ref.shape[0] // 4
    width = out_ref.shape[1]
    for n in range(4):
        side = offs_ref[X_AT] if n % 2 == 0 else 1 - offs_ref[X_AT]
        at = pl.ds(pl.multiple_of((n // 2) * 2 * size + side * size, 128), size)
        out_ref[at, :] = refs[n][:, :width].astype(wide)


def settle_down(offs, pairs, width, deps=()):
    operands = [a for pair in pairs for a in pair]
    size = operands[0].shape[0]
    column = pl.BlockSpec((size, width), lambda *_: (0, 0), pipeline_mode=pl.Buffered(1))
    return launch(
        settle_down_kernel,
        deps,
        scalars=1,
        grid=(1,),
        in_specs=[column] * 4,
        out_specs=fixed((4 * size, width)),
        out_shape=jax.ShapeDtypeStruct((4 * size, width), wide),
        compiler_params=params(24),
        cost_estimate=cost(0.001, 6),
        name="settle_down",
    )(offs, *operands)


def settle_mixer_kernel(
    offs_ref, gain_ref, mine_ref, other_ref, wq_ref, wk_ref, wv_ref, wc_ref,
    gq_ref, gk_ref, gv_ref, gc_ref, go_ref, gf_ref, ggain_ref, all_ref,
):
    size = mine_ref.shape[0]
    for ref, side in ((mine_ref, offs_ref[X_AT]), (other_ref, 1 - offs_ref[X_AT])):
        all_ref[pl.ds(pl.multiple_of(side * size, 128), size), :] = ref[...].astype(wide)
    width = wv_ref.shape[1]
    half = wq_ref.shape[1] // 2
    go_ref[...] = all_ref[:, :width]
    gc = all_ref[:, width : 2 * width]
    gc_ref[...] = gc
    gf_ref[...] = all_ref[:, 2 * width : 2 * width + LANES].T[:KW, :]
    at = 2 * width + LANES
    gv = all_ref[:, at + 4 * half :]
    gv_ref[...] = gv
    total = jnp.sum(gc * wc_ref[...].astype(wide), axis=1, keepdims=True)
    total = total + jnp.sum(gv * wv_ref[...].astype(wide), axis=1, keepdims=True)
    for n, (ref, weight_ref, cols) in enumerate(
        (
            (gq_ref, wq_ref, slice(0, half)),
            (gk_ref, wk_ref, slice(0, half)),
            (gq_ref, wq_ref, slice(half, 2 * half)),
            (gk_ref, wk_ref, slice(half, 2 * half)),
        )
    ):
        value = all_ref[:, at + n * half : at + (n + 1) * half]
        ref[:, cols] = value
        total = total + jnp.sum(value * weight_ref[:, cols].astype(wide), axis=1, keepdims=True)
    ggain_ref[...] = as_line(total / gain_ref[...])


def settle_mixer(offs, gain, mine, other, w_query, w_key, w_value, w_convgate, deps=()):
    operands = (gain, mine, other, w_query, w_key, w_value, w_convgate)
    height, width = w_value.shape
    shapes = [w_query.shape, w_key.shape, w_value.shape, w_convgate.shape, (height, width), (KW, height), gain.shape[:1]]
    return launch(
        settle_mixer_kernel,
        deps,
        scalars=1,
        grid=(1,),
        in_specs=[fixed(a.shape) for a in operands],
        out_specs=[fixed(a) for a in shapes],
        out_shape=[jax.ShapeDtypeStruct(a, wide) for a in shapes],
        scratch_shapes=[pltpu.VMEM((height, mine.shape[1]), wide)],
        compiler_params=params(24),
        cost_estimate=cost(0.001, 8),
        name="settle_mixer",
    )(offs, *operands)


def tick_kernel(offs_ref, out_ref):
    out_ref[...] = jnp.zeros_like(out_ref)


def tick(offs, deps=()):
    return launch(
        tick_kernel,
        deps,
        scalars=1,
        grid=(1,),
        in_specs=[],
        out_specs=fixed((16, LANES)),
        out_shape=jax.ShapeDtypeStruct((16, LANES), low),
        compiler_params=params(24),
        cost_estimate=cost(TICK, 8),
        name="arrived",
    )(offs)


def swap(value, axis):
    return lax.ppermute(value, axis, [(0, 1), (1, 0)])


def later(value, other):
    return lax.optimization_barrier((value, other))[0]


def part(value, index, count, axis=0):
    size = value.shape[axis] // count
    return lax.dynamic_slice_in_dim(value, index * size, size, axis)


def in_order(index, mine, other):
    return jnp.where(
        index == 0, jnp.concatenate([mine, other], 0), jnp.concatenate([other, mine], 0)
    )


def per_device(
    tokens, segment_ids, gain_one, w_query, w_key, w_value, w_convgate, w_output, conv_filter,
    gain_two, w_gate, w_up, w_down, cotangent,
):
    Order.last = None
    Order.scale = 0.05
    x = lax.axis_index("near")
    y = lax.axis_index("row")
    c = lax.axis_index("core")
    s = 2 * y + c
    width = tokens.shape[1]
    seg = segment_ids[0]
    block = w_down.shape[0]

    def flip(bits):
        return jnp.bitwise_xor(s, bits)

    small_block = block // 2
    z = lax.axis_index("far") % 2
    quarters = [(2 * a + b) * (SHARD_ROWS // 4) for a, b in ((x, z), (1 - x, z), (x, 1 - z), (1 - x, 1 - z))]

    def feed_cols(core, j):
        return [((2 * row + core) * 2 + j) * small_block for row in range(2)]

    feed_rows = [s, flip(1), jnp.bitwise_xor(flip(2), x), jnp.bitwise_xor(flip(3), x)]
    offs = [
        x,
        jnp.bitwise_xor(x, c),
        s * SHARD_ROWS,
        flip(1) * SHARD_ROWS,
        *(flip(2) * SHARD_ROWS + a for a in quarters),
        *(flip(3) * SHARD_ROWS + a for a in quarters),
        *(a * SHARD_ROWS for a in feed_rows),
        y * small_block,
        (1 - y) * small_block,
        0,
        0,
        *feed_cols(c, 0), *feed_cols(c, 1), *feed_cols(1 - c, 0), *feed_cols(1 - c, 1),
        *feed_cols(c, 0), *feed_cols(1 - c, 0), *feed_cols(c, 1), *feed_cols(1 - c, 1),
        2 * (1 - y) + 1 - x, 2 * (1 - y) + x, 2 * y + 1 - x, 2 * y + x,
        flip(3), flip(1), flip(2), s,
        2 * (1 - y) + 1 - x, 2 * y + 1 - x, 2 * (1 - y) + x, 2 * y + x,
        2 * x + z,
    ]
    offs = jnp.stack([jnp.asarray(a, jnp.int32) for a in offs])

    pack, pack_part = pack_mixer(
        offs, gain_one, gain_two, conv_filter, w_query, w_key, w_value, w_convgate, w_output
    )
    direct = swap(pack_part, "row")
    count = lax.axis_size("far")
    over_z = lax.ppermute(direct, "far", [(i, i ^ 1) for i in range(count)])
    came = [direct, swap(direct, "near"), over_z, swap(over_z, "near")]
    pack_pieces = [pack, swap(pack, "core"), *came, *(swap(a, "core") for a in came)]
    cot_other = swap(later(cotangent, direct), "core")

    mine_first, mine_second, give, *sends, down_first, down_second = pack_feed(offs, w_gate, w_up, w_down)
    given = swap(later(give, direct), "core")

    def across(value):
        pairs = []
        for side, row, core in np.ndindex(2, 2, 2):
            pairs.append((4 * side + 2 * row + core, 4 * side + 2 * (1 - row) + (core ^ side)))
        return lax.ppermute(value, ("near", "row", "core"), pairs)

    feed_pieces = [[own, given] for own in (mine_first, mine_second)]
    feed_pieces[0].append(across(later(sends[0], direct)))

    hidden_one, queries, keys, values, gates, vec, full_one = project(offs, tokens, pack_pieces, deps=[cot_other])
    feed_pieces[0].append(swap(later(feed_pieces[0][2], queries), "near"))
    down_pieces = [[swap(later(down_first, queries), "row")]]
    feed_pieces[1].append(across(later(sends[1], queries)))
    pairs = width // 256
    mixed, attention, recips = attend(queries, keys, values, gates, vec, seg, 0, 2 * pairs)
    middle, hidden_two = mix(tokens, mixed, vec, full_one, deps=[down_pieces[0][0]])
    down_pieces.append([swap(later(down_second, middle), "row")])
    tick(offs, [feed_pieces[0][3]])
    hiddens = [hidden_two, swap(hidden_two, "core")]
    cots = [cotangent, cot_other]

    Order.scale = 20.0

    def scatter_far(value):
        return lax.psum_scatter(value, "far", scatter_dimension=0, tiled=True)

    def gather_far(value):
        return lax.all_gather(later(value, tick(offs, [value])), "far", axis=0, tiled=True)

    def down_grad(act, deps=()):
        return weight_grad(offs, ACT_AT, [([act], cots)], (2, 2), "grad_down", deps=deps)

    def gate_grad(both):
        return weight_grad(offs, GRAD_AT, [(hiddens, [both])], (1, 1, 2), "grad_gate_up")

    first_feed = feed(offs, hiddens, cots, 0, w_down, feed_pieces[0], down_pieces[0])
    feed_pieces[1].append(swap(later(feed_pieces[1][2], first_feed[0]), "near"))
    down_send, down_keep = down_grad(first_feed[0], deps=[feed_pieces[1][2]])
    down_came = swap(down_send, "near")
    gate_send, gate_send_own, gate_keep = gate_grad(first_feed[1])
    gate_came, gate_came_own = swap(gate_send, "row"), swap(gate_send_own, "row")
    second_feed = feed(offs, hiddens, cots, 1, w_down, feed_pieces[1], down_pieces[1])
    acts, boths, fulls, downs = zip(first_feed, second_feed)
    down_passed = swap(top_sum(offs, down_keep, down_came), "row")
    gate_passed = swap(top_sum(offs, gate_keep, gate_came), "near")
    ghidden_part = feed_back(boths[0], boths[1], fulls[0], fulls[1])
    ghidden_other = swap(ghidden_part, "core")
    down_send_2, down_keep_2 = down_grad(second_feed[0])
    down_came_2 = swap(down_send_2, "near")
    gate_send_2, gate_send_own_2, gate_keep_2 = gate_grad(second_feed[1])
    gate_came_2, gate_came_own_2 = swap(gate_send_2, "row"), swap(gate_send_own_2, "row")
    feed_part = scatter_far(
        rest_sum(offs, [(down_keep, down_came, down_passed), (gate_keep, gate_came_own, gate_passed)])
    )
    tick(offs)
    gmiddle, gbranch, gmixed, _ = middle_back(
        boths[0], boths[1], ghidden_other, middle, cotangent, vec, fulls[0], fulls[1], full_one
    )
    down_passed_2 = swap(top_sum(offs, down_keep_2, down_came_2), "row")
    gate_passed_2 = swap(top_sum(offs, gate_keep_2, gate_came_2), "near")

    ggate, gconv, gfilter = conv_back(values, gmixed, gates, vec, seg)
    filter_came = swap(gfilter, "core")
    feed_sum = gather_far(feed_part)
    early_send, early_keep = weight_grad(
        offs, OWNER_AT, [([mixed], [gbranch]), ([hidden_one], [ggate])], (2, 2), "grad_output_convgate"
    )
    early_came = swap(early_send, "core")
    feed_part = scatter_far(
        rest_sum(
            offs, [(down_keep_2, down_came_2, down_passed_2), (gate_keep_2, gate_came_own_2, gate_passed_2)]
        )
    )
    tick(offs)
    attended = attend_back(queries, keys, values, gmixed, attention, recips, gconv, seg, 0, pairs)
    feed_other = swap(later(feed_sum, tick(offs, [feed_sum])), "near")
    early_give, early_held = halves_sum(offs, [(early_keep, early_came)], [gfilter, filter_came])
    early_came = swap(early_give, "row")
    gqk, gv = attend_back(
        queries, keys, values, gmixed, attention, recips, gconv, seg, pairs, pairs, onto=attended
    )
    late_send, late_keep = weight_grad(
        offs, OWNER_AT, [([hidden_one], [gqk]), ([hidden_one], [gv])], (2, 2), "grad_query_key_value"
    )
    late_came = swap(late_send, "core")
    early_own, early_other = near_split(offs, early_held, early_came)
    early_passed = swap(early_other, "near")
    feed_sum_2 = gather_far(feed_part)
    Order.scale = 0.05
    late_give, late_held = halves_sum(offs, [(late_keep, late_came)])
    late_came = swap(late_give, "row")
    own_rows, theirs = sort_rows(offs, feed_sum, feed_other, width)
    spreads = [own_rows, swap(theirs, "core")]
    out_part = feed_out(acts[0], acts[1], downs[0], downs[1], 1, [], "feed_out_partner")
    late_own, late_other = near_split(offs, late_held, late_came)
    late_passed = swap(late_other, "near")
    tick(offs, [feed_sum_2])
    mixer_near = pairs_sum(offs, [(early_own, early_passed), (late_own, late_passed)])
    feed_other_2 = swap(later(feed_sum_2, mixer_near), "near")
    Order.scale = 20.0
    mixer_sum = lax.psum(mixer_near, "far")
    out_came = swap(later(out_part, mixer_near), "core")
    tick(offs)
    result = feed_out(acts[0], acts[1], downs[0], downs[1], 0, [middle, out_came], "feed_out")
    grad_tokens, _ = tokens_back(gqk, gv, ggate, tokens, gmiddle, vec, full_one)
    own_rows, theirs = sort_rows(offs, feed_sum_2, feed_other_2, width)
    spreads += [own_rows, swap(theirs, "core")]
    grad_down = settle_down(offs, [(feed_sum, feed_other), (feed_sum_2, feed_other_2)], width)
    grad_gate, grad_up, ggain_two = spread(offs, gain_two[:, None].astype(wide), w_gate, w_up, spreads)
    mixer_other = swap(mixer_sum, "near")
    *grads, grad_output, grad_filter, ggain_one = settle_mixer(
        offs, gain_one[:, None].astype(wide), mixer_sum, mixer_other, w_query, w_key, w_value, w_convgate
    )
    return (
        result,
        grad_tokens,
        ggain_one,
        *grads,
        grad_output,
        grad_filter,
        ggain_two,
        grad_gate,
        grad_up,
        grad_down,
    )


def solution(mesh):
    replicas, shards = mesh.shape["rep"], mesh.shape["shard"]
    devices = np.asarray(mesh.devices).reshape(replicas // 2, 2, shards // 2, 2)
    fine = Mesh(devices, ("far", "near", "row", "core"))
    token = P(("far", "near", "row", "core"), None)
    line = P(("row", "core"))
    weight = P(("row", "core"), None)
    taps = P(None, ("row", "core"))
    return jax.shard_map(
        per_device,
        mesh=fine,
        in_specs=(
            token, token, line, weight, weight, weight, weight, weight, taps, line, weight, weight, weight, token
        ),
        out_specs=(
            token, token, line, weight, weight, weight, weight, weight, taps, line, weight, weight, weight
        ),
        check_vma=False,
    )
```

```python
import functools

import jax
import jax.numpy as jnp
import numpy as np
from jax import lax
from jax.experimental import pallas as pl
from jax.experimental.pallas import tpu as pltpu
from jax.sharding import Mesh
from jax.sharding import PartitionSpec as P

HEADS = 16
FEAT = 16
KW = 3
EPS = 1e-06
TILE = 256
SHARD_ROWS = 256
LANES = 128
TICK = 1e5
X_AT, MIXER_AT, FEED_AT, DOWN_AT, PACK_AT, COLS_AT, GRAD_AT, OWNER_AT, ACT_AT, QUARTER_AT = 0, 2, 12, 16, 20, 28, 36, 40, 44, 48

low = jnp.bfloat16
wide = jnp.float32


def dot(a, b):
    return jnp.dot(a, b, preferred_element_type=wide)


def dot_nt(a, b):
    return lax.dot_general(a, b, (((1,), (1,)), ((), ())), preferred_element_type=wide)


def dot_tn(a, b):
    return lax.dot_general(a, b, (((0,), (0,)), ((), ())), preferred_element_type=wide)


class Order:
    last = None
    scale = 1.0


def launch(kernel, deps=(), onto=(), *, scalars=0, grid, in_specs, out_specs, out_shape, scratch_shapes=(), **rest):
    taken = scalars + len(in_specs)
    deps = list(onto) + [d for d in deps if d is not None] + ([] if Order.last is None or any(Order.last is a for a in onto) else [Order.last])

    def body(*refs):
        kernel(*refs[:taken], *refs[taken + len(deps) :])

    spec = pltpu.PrefetchScalarGridSpec(
        num_scalar_prefetch=scalars,
        grid=grid,
        in_specs=list(in_specs) + [pl.BlockSpec(memory_space=pl.ANY)] * len(deps),
        out_specs=out_specs,
        scratch_shapes=list(scratch_shapes),
    )
    aliases = {taken + n: n for n in range(len(onto))}
    run = pl.pallas_call(body, grid_spec=spec, out_shape=out_shape, input_output_aliases=aliases, **rest)

    def call(*operands):
        result = run(*operands, *deps)
        Order.last = result[0] if isinstance(result, (list, tuple)) else result
        return result

    return call


def params(mib, least=60):
    return pltpu.CompilerParams(vmem_limit_bytes=max(mib, least) << 20)


def cost(gigaflops, mebibytes):
    return pl.CostEstimate(
        flops=int(gigaflops * Order.scale * 1e9), bytes_accessed=int(mebibytes * Order.scale * (1 << 20)), transcendentals=0
    )


def fixed(shape):
    return pl.BlockSpec(shape, lambda *_: (0,) * len(shape), pipeline_mode=pl.Buffered(1))


def rows(height, width):
    return pl.BlockSpec((height, width), lambda i, *_: (i, 0))


def place(offs_ref, base, pieces, full_ref):
    for n, piece in enumerate(pieces):
        at = pl.multiple_of(offs_ref[base + n], 64)
        full_ref[pl.ds(at, piece.shape[0]), :] = piece[...]


def project_kernel(offs_ref, x_ref, *refs):
    pieces, (hidden_ref, q_ref, k_ref, v_ref, gate_ref, vec_ref, out_ref, full_ref, sem) = refs[:10], refs[10:]
    copy = pltpu.make_async_copy(full_ref, out_ref, sem)
    heads = HEADS * FEAT
    width = x_ref.shape[1]

    @pl.when(pl.program_id(0) == 0)
    def _():
        place(offs_ref, MIXER_AT, pieces, full_ref)
        copy.start()
        small = full_ref[:, 2 * heads + 3 * width :].astype(wide)
        vec_ref[...] = small.T[:8, :]

    x = x_ref[...].astype(wide)
    inverse = lax.rsqrt(jnp.mean(x * x, axis=-1, keepdims=True) + EPS)
    hidden = (x * inverse * vec_ref[0:1, :]).astype(low)
    hidden_ref[...] = hidden
    at = width
    q_ref[...] = (dot(hidden, full_ref[:, at : at + heads]) * FEAT ** (-0.5)).astype(low)
    k_ref[...] = dot(hidden, full_ref[:, at + heads : at + 2 * heads]).astype(low)
    at = at + 2 * heads
    v_ref[...] = dot(hidden, full_ref[:, at : at + width]).astype(low)
    gate_ref[...] = dot(hidden, full_ref[:, at + width : at + 2 * width]).astype(low)

    @pl.when(pl.program_id(0) == pl.num_programs(0) - 1)
    def _():
        copy.wait()


def project(offs, x, pieces, deps=()):
    length, width = x.shape
    heads = HEADS * FEAT
    columns = pieces[0].shape[1]
    shapes = [
        jax.ShapeDtypeStruct((length, width), low),
        jax.ShapeDtypeStruct((length, heads), low),
        jax.ShapeDtypeStruct((length, heads), low),
        jax.ShapeDtypeStruct((length, width), low),
        jax.ShapeDtypeStruct((length, width), low),
        jax.ShapeDtypeStruct((8, width), wide),
        jax.ShapeDtypeStruct((width, columns), low),
    ]
    return launch(
        project_kernel,
        deps,
        scalars=1,
        grid=(length // TILE,),
        in_specs=[rows(TILE, width)] + [fixed(p.shape) for p in pieces],
        out_specs=[
            rows(TILE, width),
            rows(TILE, heads),
            rows(TILE, heads),
            rows(TILE, width),
            rows(TILE, width),
            fixed((8, width)),
            pl.BlockSpec(memory_space=pl.ANY),
        ],
        scratch_shapes=[pltpu.VMEM((width, columns), low), pltpu.SemaphoreType.DMA],
        out_shape=shapes,
        compiler_params=params(40),
        cost_estimate=cost(7, 22),
        name="project",
    )(offs, x, *pieces)


def shift_rows(v, seg, by, up):
    zeros = jnp.zeros((by, v.shape[1]), v.dtype)
    none = jnp.full((by, 1), -1, seg.dtype)
    if up:
        moved, moved_seg = jnp.concatenate([v[by:], zeros], 0), jnp.concatenate([seg[by:], none], 0)
    else:
        moved = jnp.concatenate([zeros, v[:-by]], 0)
        moved_seg = jnp.concatenate([none, seg[:-by]], 0)
    return jnp.where(moved_seg == seg, moved, 0.0)


def lane_pick(width, start, stop):
    i = lax.broadcasted_iota(jnp.int32, (1, width), 1)
    return (i >= start) & (i < stop)


def attend_kernel(
    first, q_ref, k_ref, v_ref, gate_ref, vec_ref, segr_ref, segc_ref, mixed_ref, att_ref, recip_ref, mask_ref
):
    length = q_ref.shape[0]
    pair = pl.program_id(0) + first
    zero = jnp.zeros((), low)

    @pl.when(pair == first)
    def _():
        for tb in range(0, length, TILE):
            t = lax.broadcasted_iota(jnp.int32, (TILE, length), 0) + tb
            s = lax.broadcasted_iota(jnp.int32, (TILE, length), 1)
            seen = (s <= t) & (segc_ref[tb : tb + TILE, :] == segr_ref[...])
            mask_ref[tb : tb + TILE, :] = jnp.where(seen, 1.0, 0.0).astype(low)

    v = v_ref[...]
    keys, sides = [], []
    for i in range(2):
        head = 2 * pair + i
        keys.append(jnp.where(lane_pick(HEADS * FEAT, head * FEAT, (head + 1) * FEAT), k_ref[...], zero))
        lanes = lane_pick(128, 64 * i, 64 * i + 64)
        ones = jnp.broadcast_to(jnp.where(lanes, 1.0, 0.0).astype(low), (length, 128))
        sides.append(jnp.concatenate([jnp.where(lanes, v, zero), ones], 1))
    for tb in range(0, length, TILE):
        n = tb + TILE
        total = None
        for i in range(2):
            one_plus = dot_nt(q_ref[tb:n, :], keys[i][:n]) + 1.0
            kernel = (one_plus * one_plus + 1.0).astype(low) * mask_ref[tb:n, :n]
            part = dot(kernel, sides[i][:n])
            total = part if total is None else total + part
        recip = 1.0 / total[:, 128:]
        att_ref[tb:n, :] = (total[:, :128] * recip).astype(low)
        recip_ref[tb:n, :] = (2.0 * recip).astype(low)
    v_wide = v.astype(wide)
    seg = segc_ref[...]
    conv = vec_ref[2:3, :] * v_wide
    for j in range(1, KW):
        conv = conv + vec_ref[2 + j : 3 + j, :] * shift_rows(v_wide, seg, j, False)
    mixed_ref[...] = (att_ref[...].astype(wide) + gate_ref[...].astype(wide) * conv).astype(low)


def whole(a):
    return pl.BlockSpec(a.shape, lambda p: (0, 0))


def attend(q, k, v, gate, vec, seg, first, count, onto=(), deps=()):
    length, width = v.shape
    column = pl.BlockSpec((length, 128), lambda p: (0, p + first))
    seg_row, seg_col = seg.reshape(1, length), seg.reshape(length, 1)
    return launch(
        functools.partial(attend_kernel, first),
        deps,
        onto,
        grid=(count,),
        in_specs=[
            whole(q), whole(k), column, column, pl.BlockSpec((8, 128), lambda p: (0, p + first)), whole(seg_row), whole(seg_col)
        ],
        out_specs=[column] * 3,
        out_shape=[jax.ShapeDtypeStruct((length, width), low)] * 3,
        scratch_shapes=[pltpu.VMEM((length, length), low)],
        compiler_params=params(40),
        cost_estimate=cost(18 * count * 128 / width, 14),
        name="attention_forward",
    )(q, k, v, gate, vec, seg_row, seg_col)


def attend_back_kernel(
    first, q_ref, k_ref, v_ref, gm_ref, att_ref, recip_ref, gconv_ref, segr_ref, segc_ref,
    gqk_ref, gv_ref, mask_ref, gq_acc, gk_acc,
):
    length, heads = q_ref.shape
    pair = pl.program_id(0) + first
    zero = jnp.zeros((), low)

    @pl.when(pair == first)
    def _():
        for sb in range(0, length, TILE):
            s = lax.broadcasted_iota(jnp.int32, (TILE, length), 0) + sb
            t = lax.broadcasted_iota(jnp.int32, (TILE, length), 1)
            seen = (s <= t) & (segc_ref[sb : sb + TILE, :] == segr_ref[...])
            mask_ref[sb : sb + TILE, :] = jnp.where(seen, 1.0, 0.0).astype(low)
        gk_acc[...] = jnp.zeros_like(gk_acc)
        gq_acc[...] = jnp.zeros_like(gq_acc)

    v = v_ref[...]
    gm = gm_ref[...].astype(wide)
    gnum_wide = gm * recip_ref[...].astype(wide)
    gnum = gnum_wide.astype(low)
    product = gnum_wide * att_ref[...].astype(wide)
    high = product.astype(low)
    rest = (product - high.astype(wide)).astype(low)
    r = lax.broadcasted_iota(jnp.int32, (256, 128), 0)
    c = lax.broadcasted_iota(jnp.int32, (256, 128), 1)
    same_head = jnp.where(((r % 128) // 64) == (c // 64), 1.0, 0.0).astype(low)
    gtot = -dot(jnp.concatenate([high, rest], 1), same_head)
    gtot_high = gtot.astype(low)
    gtot_rest = (gtot - gtot_high.astype(wide)).astype(low)
    lane = lax.broadcasted_iota(jnp.int32, (1, 128), 1)
    left = jnp.concatenate([gnum, jnp.where(lane % 64 == 0, gtot_high, gtot_rest)], 1)
    gnum_half = gnum * jnp.asarray(0.5, low)
    queries, sides, gnums, keys = [], [], [], []
    for i in range(2):
        head = 2 * pair + i
        mine = lane_pick(heads, head * FEAT, (head + 1) * FEAT)
        queries.append(jnp.where(mine, q_ref[...], zero))
        keys.append(jnp.where(mine, k_ref[...], zero))
        lanes = lane_pick(128, 64 * i, 64 * i + 64)
        ones = jnp.where(lane_pick(128, 64 * i, 64 * i + 2), 1.0, 0.0).astype(low)
        sides.append(jnp.concatenate([jnp.where(lanes, v, zero), jnp.broadcast_to(ones, (length, 128))], 1))
        gnums.append(jnp.where(lanes, gnum_half, zero))
    for sb in range(0, length, TILE):
        n = sb + TILE
        gv = gconv_ref[sb:n, :].astype(wide)
        gk = None
        for i in range(2):
            one_plus = dot_nt(k_ref[sb:n, :], queries[i][sb:]) + 1.0
            mask = mask_ref[sb:n, sb:]
            kernel = (one_plus * one_plus + 1.0).astype(low) * mask
            gv = gv + dot(kernel, gnums[i][sb:])
            gkernel = dot_nt(sides[i][sb:n], left[sb:])
            gscores = (gkernel * one_plus).astype(low) * mask
            part = dot(gscores, queries[i][sb:])
            gk = part if gk is None else gk + part
            gq_acc[sb:, :] += dot_tn(gscores, keys[i][sb:n])
        gv_ref[sb:n, :] = gv.astype(low)
        gk_acc[sb:n, :] += gk

    @pl.when(pl.program_id(0) == pl.num_programs(0) - 1)
    def _():
        mine = slice(2 * FEAT * first, 2 * FEAT * first + gqk_ref.shape[1] // 2)
        gqk_ref[:, : gqk_ref.shape[1] // 2] = (gq_acc[:, mine] * FEAT ** (-0.5)).astype(low)
        gqk_ref[:, gqk_ref.shape[1] // 2 :] = gk_acc[:, mine].astype(low)


def attend_back(q, k, v, gm, att, recip, gconv, seg, first, count, onto=(), deps=()):
    length, width = v.shape
    heads = q.shape[1]
    column = pl.BlockSpec((length, 128), lambda p: (0, p + first))
    seg_row, seg_col = seg.reshape(1, length), seg.reshape(length, 1)
    return launch(
        functools.partial(attend_back_kernel, first),
        deps,
        onto,
        grid=(count,),
        in_specs=[whole(q), whole(k)] + [column] * 5 + [whole(seg_row), whole(seg_col)],
        out_specs=[pl.BlockSpec((length, 4 * FEAT * count), lambda p: (0, first // count)), column],
        out_shape=[jax.ShapeDtypeStruct((length, 2 * heads), low), jax.ShapeDtypeStruct((length, width), low)],
        scratch_shapes=[
            pltpu.VMEM((length, length), low),
            pltpu.VMEM((length, heads), wide),
            pltpu.VMEM((length, heads), wide),
        ],
        compiler_params=params(48),
        cost_estimate=cost(40 * count * 128 / width, 18),
        name="attention_backward",
    )(q, k, v, gm, att, recip, gconv, seg_row, seg_col)


def conv_back_kernel(v_ref, gm_ref, gate_ref, vec_ref, segc_ref, ggate_ref, gconv_ref, gfilt_ref):
    v_wide = v_ref[...].astype(wide)
    gm = gm_ref[...].astype(wide)
    seg = segc_ref[...]
    taps = [vec_ref[2 + j : 3 + j, :] for j in range(KW)]
    grad = gm * gate_ref[...].astype(wide)
    conv = taps[0] * v_wide
    gv_conv = taps[0] * grad
    lines = [jnp.sum(grad * v_wide, 0, keepdims=True)]
    for j in range(1, KW):
        moved = shift_rows(v_wide, seg, j, False)
        conv = conv + taps[j] * moved
        lines.append(jnp.sum(grad * moved, 0, keepdims=True))
        gv_conv = gv_conv + taps[j] * shift_rows(grad, seg, j, True)
    lines.append(jnp.zeros((LANES - KW, 128), wide))
    gfilt_ref[...] = jnp.concatenate(lines, 0).T.astype(low)
    ggate_ref[...] = (gm * conv).astype(low)
    gconv_ref[...] = gv_conv.astype(low)


def conv_back(v, gm, gate, vec, seg, deps=()):
    length, width = v.shape
    column = pl.BlockSpec((length, 128), lambda p: (0, p))
    small = pl.BlockSpec((8, 128), lambda p: (0, p))
    seg_col = seg.reshape(length, 1)
    return launch(
        conv_back_kernel,
        deps,
        grid=(width // 128,),
        in_specs=[column, column, column, small, whole(seg_col)],
        out_specs=[column, column, pl.BlockSpec((128, LANES), lambda p: (p, 0))],
        out_shape=[jax.ShapeDtypeStruct((length, width), low)] * 2 + [jax.ShapeDtypeStruct((width, LANES), low)],
        compiler_params=params(48),
        cost_estimate=cost(1, 10),
        name="convolution_backward",
    )(v, gm, gate, vec, seg_col)


def mix_kernel(x_ref, mixed_ref, vec_ref, weight_ref, middle_ref, hidden_ref):
    middle = x_ref[...].astype(wide) + dot(mixed_ref[...], weight_ref[...])
    inverse = lax.rsqrt(jnp.mean(middle * middle, axis=-1, keepdims=True) + EPS)
    middle_ref[...] = middle
    hidden_ref[...] = (middle * inverse * vec_ref[1:2, :]).astype(low)


def mix(x, mixed, vec, full, deps=()):
    length, width = x.shape
    return launch(
        mix_kernel,
        deps,
        grid=(length // TILE,),
        in_specs=[rows(TILE, width), rows(TILE, width), fixed(vec.shape), fixed((width, width))],
        out_specs=[rows(TILE, width), rows(TILE, width)],
        out_shape=[jax.ShapeDtypeStruct((length, width), wide), jax.ShapeDtypeStruct((length, width), low)],
        compiler_params=params(32),
        cost_estimate=cost(3, 16),
        name="mix",
    )(x, mixed, vec, full)


def first_half(n):
    return lambda i, *_: (jnp.minimum(i, n - 1), 0)


def second_half(n):
    return lambda i, *_: (jnp.maximum(i - n, 0), 0)


def feed_kernel(n, offs_ref, ha_ref, hb_ref, ca_ref, cb_ref, *refs):
    pieces, downs = refs[:4], refs[4:6]
    act_ref, both_ref, full_out_ref, down_out_ref, full_ref, down_ref, sems = refs[6:]
    copies = [
        pltpu.make_async_copy(full_ref, full_out_ref, sems.at[0]),
        pltpu.make_async_copy(down_ref, down_out_ref, sems.at[1]),
    ]
    step = pl.program_id(0)
    half = full_ref.shape[1] // 2

    @pl.when(step == 0)
    def _():
        place(offs_ref, FEED_AT, pieces, full_ref)
        place(offs_ref, DOWN_AT, downs, down_ref)
        for copy in copies:
            copy.start()

    def work(hidden, cotangent):
        for at in range(0, half, 256):
            gate = dot(hidden, full_ref[:, at : at + 256])
            up = dot(hidden, full_ref[:, half + at : half + at + 256])
            gact = dot_nt(cotangent, down_ref[at : at + 256, :])
            sig = jax.nn.sigmoid(gate)
            silu = gate * sig
            act_ref[:, at : at + 256] = (silu * up).astype(low)
            both_ref[:, at : at + 256] = (gact * up * (sig + silu * (1.0 - sig))).astype(low)
            both_ref[:, half + at : half + at + 256] = (gact * silu).astype(low)

    @pl.when(step < n)
    def _():
        work(ha_ref[...], ca_ref[...])

    @pl.when(step >= n)
    def _():
        work(hb_ref[...], cb_ref[...])

    @pl.when(step == 2 * n - 1)
    def _():
        for copy in copies:
            copy.wait()


def feed(offs, hidden, cotangent, j, w_down, pieces, down_pieces, deps=()):
    length, width = hidden[0].shape
    n = length // TILE
    half = w_down.shape[0]
    first = pl.BlockSpec((TILE, width), first_half(n))
    second = pl.BlockSpec((TILE, width), second_half(n))
    own_down = pl.BlockSpec((half // 2, width), lambda *_: (j, 0), pipeline_mode=pl.Buffered(1))
    given_rows = pl.BlockSpec(pieces[0].shape, lambda *_: (j, 0), pipeline_mode=pl.Buffered(1))
    return launch(
        functools.partial(feed_kernel, n),
        deps,
        scalars=1,
        grid=(2 * n,),
        in_specs=[first, second, first, second]
        + [fixed(pieces[0].shape), given_rows]
        + [fixed(p.shape) for p in pieces[2:]]
        + [own_down]
        + [fixed(p.shape) for p in down_pieces],
        out_specs=[rows(TILE, half), rows(TILE, 2 * half)] + [pl.BlockSpec(memory_space=pl.ANY)] * 2,
        scratch_shapes=[
            pltpu.VMEM((width, 2 * half), low),
            pltpu.VMEM((half, width), low),
            pltpu.SemaphoreType.DMA((2,)),
        ],
        out_shape=[
            jax.ShapeDtypeStruct((2 * length, half), low),
            jax.ShapeDtypeStruct((2 * length, 2 * half), low),
            jax.ShapeDtypeStruct((width, 2 * half), low),
            jax.ShapeDtypeStruct((half, width), low),
        ],
        compiler_params=params(48),
        cost_estimate=cost(16, 34),
        name="feed_in",
    )(offs, *hidden, *cotangent, *pieces, w_down, *down_pieces)


def weight_grad_kernel(shape_of, counts, outs, length, offs_ref, *refs):
    targets = [(ref, row * TILE) for ref, height in zip(refs[-len(outs) :], outs) for row in range(height)]
    step = pl.program_id(0)

    def work(lefts, rights):
        terms = max(len(lefts[0]), len(rights))

        def part_of(group, t):
            return group[t][...] if len(group) == terms else group[0][t * length : (t + 1) * length, :]

        for b, (ref, row) in enumerate(targets):
            value = None
            for t in range(terms):
                product = dot_tn(part_of(lefts[b], t), part_of(rights, t))
                value = product if value is None else value + product
            ref[row : row + TILE, :] = value.astype(low)

    start = 0
    for (left_at, right_at), count in zip(shape_of, counts):
        lefts = [[refs[n] for n in block] for block in left_at]
        rights = [refs[n] for n in right_at]
        if len(counts) == 1:
            work(lefts, rights)
        else:
            pl.when((step >= start) & (step < start + count))(functools.partial(work, lefts, rights))
        start += count


def weight_grad(offs, base, groups, outs, name, tile=512, deps=()):
    blocks = sum(outs)
    counts = [rights[0].shape[1] // tile for _, rights in groups]
    columns = sum(counts) * tile
    in_specs, operands, shape_of, known = [], [], [], {}
    start = 0
    for (lefts, rights), count in zip(groups, counts):
        key = tuple(id(a) for a in lefts)
        if key not in known:
            known[key] = []
            for b in range(blocks):
                known[key].append([len(operands) + n for n in range(len(lefts))])
                for a in lefts:
                    in_specs.append(pl.BlockSpec((a.shape[0], TILE), lambda j, offs, b=b: (0, offs[base + b])))
                    operands.append(a)
        shape_of.append((known[key], [len(operands) + n for n in range(len(rights))]))
        for a in rights:

            def where_to(j, offs, start=start, count=count):
                return (0, jnp.clip(j - start, 0, count - 1))

            in_specs.append(pl.BlockSpec((a.shape[0], tile), where_to))
            operands.append(a)
        start += count
    tokens = sum(a.shape[0] for a in groups[0][0])
    terms = max(len(groups[0][0]), len(groups[0][1]))
    return launch(
        functools.partial(weight_grad_kernel, shape_of, counts, outs, tokens // terms),
        deps,
        scalars=1,
        grid=(sum(counts),),
        in_specs=in_specs,
        out_specs=[pl.BlockSpec((height * TILE, tile), lambda j, offs: (0, j)) for height in outs],
        out_shape=[jax.ShapeDtypeStruct((height * TILE, columns), low) for height in outs],
        compiler_params=params(48, 48),
        cost_estimate=cost(2.5e-9 * tokens * 1024 * columns, (tokens * (1024 + columns) * 2 + 2048 * columns) / 2**20),
        name=name,
    )(offs, *operands)


def feed_back_kernel(a_ref, b_ref, wa_ref, wb_ref, out_ref):
    out_ref[...] = (dot_nt(a_ref[...], wa_ref[...]) + dot_nt(b_ref[...], wb_ref[...])).astype(low)


def feed_back(first, second, full_first, full_second, deps=()):
    length = first.shape[0] // 2
    width = full_first.shape[0]
    n = length // TILE
    tile = pl.BlockSpec((TILE, first.shape[1]), lambda i: (i + n, 0))
    return launch(
        feed_back_kernel,
        deps,
        grid=(n,),
        in_specs=[tile, tile, fixed(full_first.shape), fixed(full_second.shape)],
        out_specs=rows(TILE, width),
        out_shape=jax.ShapeDtypeStruct((length, width), low),
        compiler_params=params(32),
        cost_estimate=cost(10, 18),
        name="feed_back_partner",
    )(first, second, full_first, full_second)


def middle_back_kernel(
    a_ref, b_ref, other_ref, middle_ref, cot_ref, vec_ref, wa_ref, wb_ref, wo_ref,
    gmiddle_ref, gbranch_ref, gmixed_ref, ggain_ref,
):
    ghidden = dot_nt(a_ref[...], wa_ref[...]) + dot_nt(b_ref[...], wb_ref[...]) + other_ref[...].astype(wide)
    middle = middle_ref[...]
    inverse = lax.rsqrt(jnp.mean(middle * middle, axis=-1, keepdims=True) + EPS)
    normed = middle * inverse
    gain = jnp.sum(ghidden * normed, axis=0, keepdims=True)

    @pl.when(pl.program_id(0) == 0)
    def _():
        ggain_ref[...] = jnp.zeros_like(ggain_ref)

    ggain_ref[0:1, :] += gain
    scaled = ghidden * vec_ref[1:2, :]
    gmiddle = cot_ref[...].astype(wide) + inverse * (
        scaled - normed * jnp.mean(scaled * normed, axis=-1, keepdims=True)
    )
    gmiddle_ref[...] = gmiddle
    gbranch = gmiddle.astype(low)
    gbranch_ref[...] = gbranch
    gmixed_ref[...] = dot_nt(gbranch, wo_ref[...]).astype(low)


def middle_back(first, second, other, middle, cotangent, vec, full_first, full_second, w_output, deps=()):
    length, width = middle.shape
    tile = rows(TILE, first.shape[1])
    line = rows(TILE, width)
    return launch(
        middle_back_kernel,
        deps,
        grid=(length // TILE,),
        in_specs=[
            tile, tile, line, line, line, fixed(vec.shape), fixed(full_first.shape), fixed(full_second.shape), fixed((width, width))
        ],
        out_specs=[line, line, line, fixed((8, width))],
        out_shape=[
            jax.ShapeDtypeStruct((length, width), wide),
            jax.ShapeDtypeStruct((length, width), low),
            jax.ShapeDtypeStruct((length, width), low),
            jax.ShapeDtypeStruct((8, width), wide),
        ],
        compiler_params=params(48),
        cost_estimate=cost(13, 40),
        name="middle_back",
    )(first, second, other, middle, cotangent, vec, full_first, full_second, w_output)


def feed_out_kernel(add, *refs):
    out_ref = refs[-1]
    value = dot(refs[0][...], refs[2][...]) + dot(refs[1][...], refs[3][...])
    for ref in refs[4:-1]:
        value = value + ref[...].astype(wide)
    out_ref[...] = value.astype(low)


def feed_out(first, second, down_first, down_second, shift, extras, name, deps=()):
    length = first.shape[0] // 2
    width = down_first.shape[1]
    n = length // TILE
    tile = pl.BlockSpec((TILE, first.shape[1]), lambda i: (i + shift * n, 0))
    return launch(
        functools.partial(feed_out_kernel, len(extras)),
        deps,
        grid=(n,),
        in_specs=[tile, tile, fixed(down_first.shape), fixed(down_second.shape)] + [rows(TILE, width)] * len(extras),
        out_specs=rows(TILE, width),
        out_shape=jax.ShapeDtypeStruct((length, width), low),
        compiler_params=params(32),
        cost_estimate=cost(5, 16),
        name=name,
    )(first, second, down_first, down_second, *extras)


def tokens_back_kernel(gqk_ref, gv_ref, ggate_ref, x_ref, gmiddle_ref, vec_ref, full_ref, gtokens_ref, ggain_ref):
    two = gqk_ref.shape[1]
    width = x_ref.shape[1]
    quarter = two // 4
    ghidden = None
    for n, col in enumerate((0, 2, 1, 3)):
        at = width + col * quarter
        term = dot_nt(gqk_ref[:, n * quarter : (n + 1) * quarter], full_ref[:, at : at + quarter])
        ghidden = term if ghidden is None else ghidden + term
    ghidden = (
        ghidden
        + dot_nt(gv_ref[...], full_ref[:, width + two : 2 * width + two])
        + dot_nt(ggate_ref[...], full_ref[:, two + 2 * width : two + 3 * width])
    )
    x = x_ref[...].astype(wide)
    inverse = lax.rsqrt(jnp.mean(x * x, axis=-1, keepdims=True) + EPS)
    normed = x * inverse

    @pl.when(pl.program_id(0) == 0)
    def _():
        ggain_ref[...] = jnp.zeros_like(ggain_ref)

    ggain_ref[0:1, :] += jnp.sum(ghidden * normed, axis=0, keepdims=True)
    scaled = ghidden * vec_ref[0:1, :]
    gtokens_ref[...] = gmiddle_ref[...] + inverse * (
        scaled - normed * jnp.mean(scaled * normed, axis=-1, keepdims=True)
    )


def tokens_back(gqk, gv, ggate, x, gmiddle, vec, full, deps=()):
    length, width = x.shape
    line = rows(TILE, width)
    return launch(
        tokens_back_kernel,
        deps,
        grid=(length // TILE,),
        in_specs=[rows(TILE, gqk.shape[1]), line, line, line, line, fixed(vec.shape), fixed(full.shape)],
        out_specs=[line, fixed((8, width))],
        out_shape=[jax.ShapeDtypeStruct((length, width), wide), jax.ShapeDtypeStruct((8, width), wide)],
        compiler_params=params(40),
        cost_estimate=cost(7, 24),
        name="tokens_back",
    )(gqk, gv, ggate, x, gmiddle, vec, full)


def as_line(column):
    return jnp.broadcast_to(column, (column.shape[0], LANES)).T[0]


def spread_kernel(cols_ref, gain_ref, wg_ref, wu_ref, a_ref, b_ref, c_ref, d_ref, gate_ref, up_ref, ggain_ref):
    total = None
    for n, ref in enumerate((a_ref, b_ref, c_ref, d_ref)):
        quarter = ref.shape[1] // 4
        for part_y in range(2):
            at = pl.ds(pl.multiple_of(cols_ref[COLS_AT + 2 * n + part_y], 512), quarter)
            gate = ref[:, part_y * quarter : (part_y + 1) * quarter].astype(wide)
            up = ref[:, (2 + part_y) * quarter : (3 + part_y) * quarter].astype(wide)
            gate_ref[:, at] = gate
            up_ref[:, at] = up
            term = gate * wg_ref[:, at].astype(wide) + up * wu_ref[:, at].astype(wide)
            line = jnp.sum(term, axis=1, keepdims=True)
            total = line if total is None else total + line
    ggain_ref[...] = as_line(total / gain_ref[...])


def spread(cols, gain, w_gate, w_up, blocks, deps=()):
    height, width = blocks[0].shape
    shape = jax.ShapeDtypeStruct((height, 2 * width), wide)
    return launch(
        spread_kernel,
        deps,
        scalars=1,
        grid=(1,),
        in_specs=[fixed(gain.shape), fixed(w_gate.shape), fixed(w_up.shape)] + [fixed(b.shape) for b in blocks],
        out_specs=[fixed(shape.shape)] * 2 + [fixed(gain.shape[:1])],
        out_shape=[shape, shape, jax.ShapeDtypeStruct(gain.shape[:1], wide)],
        compiler_params=params(24),
        cost_estimate=cost(0.001, 16),
        name="spread",
    )(cols, gain, w_gate, w_up, *blocks)


def pack_kernel(at_ref, g1_ref, g2_ref, taps_ref, q_ref, k_ref, v_ref, c_ref, o_ref, pack_ref, part_ref):
    height = q_ref.shape[0]
    col = 0
    for ref in (o_ref, q_ref, k_ref, v_ref, c_ref):
        pack_ref[:, col : col + ref.shape[1]] = ref[...]
        col += ref.shape[1]
    small = jnp.concatenate([g1_ref[...].astype(wide)[None], g2_ref[...].astype(wide)[None], taps_ref[...].astype(wide)], 0)
    small = jnp.concatenate([small, jnp.zeros((LANES - small.shape[0], height), wide)], 0)
    pack_ref[:, col : col + LANES] = small.T.astype(low)
    size = part_ref.shape[0]
    part_ref[...] = pack_ref[pl.ds(pl.multiple_of(at_ref[QUARTER_AT] * size, 64), size), :]


def pack_mixer(at, gain_one, gain_two, taps, w_query, w_key, w_value, w_convgate, w_output):
    operands = (gain_one, gain_two, taps, w_query, w_key, w_value, w_convgate, w_output)
    height = w_query.shape[0]
    columns = sum(a.shape[1] for a in operands[3:]) + LANES
    shapes = [(height, columns), (height // 4, columns)]
    return launch(
        pack_kernel,
        scalars=1,
        grid=(1,),
        in_specs=[fixed(a.shape) for a in operands],
        out_specs=[fixed(a) for a in shapes],
        out_shape=[jax.ShapeDtypeStruct(a, low) for a in shapes],
        compiler_params=params(24),
        cost_estimate=cost(0.001, 4),
        name="pack_mixer",
    )(at, *operands)


def pack_feed_kernel(offs_ref, gate_ref, up_ref, down_ref, first_ref, second_ref, give_ref, *refs):
    send_refs, (low_ref, high_ref) = refs[:2], refs[2:]
    height = gate_ref.shape[0]
    sent = PACK_AT + 4 * offs_ref[X_AT]
    targets = (
        (first_ref, 0, PACK_AT),
        (second_ref, 0, PACK_AT + 2),
        (give_ref, 0, PACK_AT + 4),
        (give_ref, height, PACK_AT + 6),
        (send_refs[0], 0, sent),
        (send_refs[1], 0, sent + 2),
    )
    for ref, row, place_at in targets:
        quarter = ref.shape[1] // 4
        for part_y in range(2):
            at = pl.ds(pl.multiple_of(offs_ref[place_at + part_y], 512), quarter)
            ref[row : row + height, part_y * quarter : (part_y + 1) * quarter] = gate_ref[:, at]
            ref[row : row + height, (2 + part_y) * quarter : (3 + part_y) * quarter] = up_ref[:, at]
    size = low_ref.shape[0]
    low_ref[...] = down_ref[:size, :]
    high_ref[...] = down_ref[size:, :]


def pack_feed(offs, w_gate, w_up, w_down, deps=()):
    height, columns = w_gate.shape
    half = (height, columns // 2)
    shapes = [half, half, (2 * height, columns // 2), half, half] + [(w_down.shape[0] // 2, w_down.shape[1])] * 2
    return launch(
        pack_feed_kernel,
        deps,
        scalars=1,
        grid=(1,),
        in_specs=[fixed(w_gate.shape), fixed(w_up.shape), fixed(w_down.shape)],
        out_specs=[fixed(a) for a in shapes],
        out_shape=[jax.ShapeDtypeStruct(a, low) for a in shapes],
        compiler_params=params(24),
        cost_estimate=cost(0.001, 8),
        name="pack_feed",
    )(offs, w_gate, w_up, w_down)


STRIPS = 1


def operand_parts(operand):
    if not isinstance(operand, tuple):
        return operand, None, 1
    return operand if len(operand) == 3 else (*operand, 2)


def step(kernel, offs, operands, shapes, name, deps=(), giga=0.001):
    in_specs, arrays = [], []
    for operand in operands:
        array, half, parts = operand_parts(operand)
        height = array.shape[0] // parts

        def where_to(i, offs, half=half):
            if half is None:
                return (i, 0)
            return ((half(offs) if callable(half) else half) * STRIPS + i, 0)

        in_specs.append(pl.BlockSpec((height // STRIPS, array.shape[1]), where_to))
        arrays.append(array)
    return launch(
        kernel,
        deps,
        scalars=1,
        grid=(STRIPS,),
        in_specs=in_specs,
        out_specs=[rows(shape[0] // STRIPS, shape[1]) for shape in shapes],
        out_shape=[jax.ShapeDtypeStruct(shape, low) for shape in shapes],
        compiler_params=params(24),
        cost_estimate=cost(giga, 8),
        name=name,
    )(offs, *arrays)


def add(*refs):
    total = refs[0].astype(wide)
    for other in refs[1:]:
        total = total + other.astype(wide)
    return total.astype(low)


def sum_kernel(terms, offs_ref, *refs):
    for out_ref, groups in zip(refs[-len(terms) :], terms):
        col = 0
        for group in groups:
            width = refs[group[0]].shape[1]
            out_ref[:, col : col + width] = add(*(refs[n][...] for n in group))
            col += width


def strip_sum(offs, outputs, name, deps=()):
    operands, terms, shapes = [], [], []
    for groups in outputs:
        terms.append([])
        width = 0
        for group in groups:
            terms[-1].append(list(range(len(operands), len(operands) + len(group))))
            operands += group
            first, _, parts = operand_parts(group[0])
            height = first.shape[0] // parts
            width += first.shape[1]
        shapes.append((height, width))
    return step(functools.partial(sum_kernel, terms), offs, operands, shapes, name, deps)


def top_sum(offs, keep, came, deps=()):
    came = came if came.shape[0] * 2 == keep.shape[0] else (came, 0)
    return strip_sum(offs, [[[(keep, 0), came]]], "top_sum", deps)[0]


def rest_sum(offs, triples, deps=()):
    groups = []
    for keep, came, passed in triples:
        came = came if came.shape[0] * 2 == keep.shape[0] else (came, 1)
        groups.append([(keep, 1), came, passed])
    return strip_sum(offs, [groups], "rest_sum", deps)[0]


def halves_sum(offs, pairs, filters=None, deps=()):
    outputs = []
    for half in range(2):
        groups = [[(keep, half), (came, half)] for keep, came in pairs]
        if filters is not None:

            def quarter(offs_ref, half=half):
                return offs_ref[OWNER_AT + 2 + half]

            groups.append([(a, quarter, 4) for a in filters])
        outputs.append(groups)
    return strip_sum(offs, outputs, "halves_sum", deps)


def near_split(offs, keep, came, deps=()):
    def own(offs_ref):
        return offs_ref[X_AT]

    def other(offs_ref):
        return 1 - offs_ref[X_AT]

    return strip_sum(offs, [[[(keep, own), (came, own)]], [[(keep, other), (came, other)]]], "near_split", deps)


def pairs_sum(offs, pairs, deps=()):
    return strip_sum(offs, [[list(pair) for pair in pairs]], "pairs_sum", deps)[0]


def sort_kernel(offs_ref, total_ref, other_ref, own_ref, give_ref):
    skip = total_ref.shape[1] - own_ref.shape[1]

    @pl.when(offs_ref[X_AT + 1] == 0)
    def _():
        own_ref[...] = total_ref[:, skip:]
        give_ref[...] = other_ref[:, skip:]

    @pl.when(offs_ref[X_AT + 1] != 0)
    def _():
        own_ref[...] = other_ref[:, skip:]
        give_ref[...] = total_ref[:, skip:]


def sort_rows(offs, total, other, skip, deps=()):
    shape = (total.shape[0], total.shape[1] - skip)
    return step(sort_kernel, offs, [total, other], [shape, shape], "sort_rows", deps)


def settle_down_kernel(offs_ref, *refs):
    out_ref = refs[-1]
    size = out_ref.shape[0] // 4
    width = out_ref.shape[1]
    for n in range(4):
        side = offs_ref[X_AT] if n % 2 == 0 else 1 - offs_ref[X_AT]
        at = pl.ds(pl.multiple_of((n // 2) * 2 * size + side * size, 128), size)
        out_ref[at, :] = refs[n][:, :width].astype(wide)


def settle_down(offs, pairs, width, deps=()):
    operands = [a for pair in pairs for a in pair]
    size = operands[0].shape[0]
    column = pl.BlockSpec((size, width), lambda *_: (0, 0), pipeline_mode=pl.Buffered(1))
    return launch(
        settle_down_kernel,
        deps,
        scalars=1,
        grid=(1,),
        in_specs=[column] * 4,
        out_specs=fixed((4 * size, width)),
        out_shape=jax.ShapeDtypeStruct((4 * size, width), wide),
        compiler_params=params(24),
        cost_estimate=cost(0.001, 6),
        name="settle_down",
    )(offs, *operands)


def settle_mixer_kernel(
    offs_ref, gain_ref, mine_ref, other_ref, wq_ref, wk_ref, wv_ref, wc_ref,
    gq_ref, gk_ref, gv_ref, gc_ref, go_ref, gf_ref, ggain_ref, all_ref,
):
    size = mine_ref.shape[0]
    for ref, side in ((mine_ref, offs_ref[X_AT]), (other_ref, 1 - offs_ref[X_AT])):
        all_ref[pl.ds(pl.multiple_of(side * size, 128), size), :] = ref[...].astype(wide)
    width = wv_ref.shape[1]
    half = wq_ref.shape[1] // 2
    go_ref[...] = all_ref[:, :width]
    gc = all_ref[:, width : 2 * width]
    gc_ref[...] = gc
    gf_ref[...] = all_ref[:, 2 * width : 2 * width + LANES].T[:KW, :]
    at = 2 * width + LANES
    gv = all_ref[:, at + 4 * half :]
    gv_ref[...] = gv
    total = jnp.sum(gc * wc_ref[...].astype(wide), axis=1, keepdims=True)
    total = total + jnp.sum(gv * wv_ref[...].astype(wide), axis=1, keepdims=True)
    for n, (ref, weight_ref, cols) in enumerate(
        (
            (gq_ref, wq_ref, slice(0, half)),
            (gk_ref, wk_ref, slice(0, half)),
            (gq_ref, wq_ref, slice(half, 2 * half)),
            (gk_ref, wk_ref, slice(half, 2 * half)),
        )
    ):
        value = all_ref[:, at + n * half : at + (n + 1) * half]
        ref[:, cols] = value
        total = total + jnp.sum(value * weight_ref[:, cols].astype(wide), axis=1, keepdims=True)
    ggain_ref[...] = as_line(total / gain_ref[...])


def settle_mixer(offs, gain, mine, other, w_query, w_key, w_value, w_convgate, deps=()):
    operands = (gain, mine, other, w_query, w_key, w_value, w_convgate)
    height, width = w_value.shape
    shapes = [w_query.shape, w_key.shape, w_value.shape, w_convgate.shape, (height, width), (KW, height), gain.shape[:1]]
    return launch(
        settle_mixer_kernel,
        deps,
        scalars=1,
        grid=(1,),
        in_specs=[fixed(a.shape) for a in operands],
        out_specs=[fixed(a) for a in shapes],
        out_shape=[jax.ShapeDtypeStruct(a, wide) for a in shapes],
        scratch_shapes=[pltpu.VMEM((height, mine.shape[1]), wide)],
        compiler_params=params(24),
        cost_estimate=cost(0.001, 8),
        name="settle_mixer",
    )(offs, *operands)


def tick_kernel(offs_ref, out_ref):
    out_ref[...] = jnp.zeros_like(out_ref)


def tick(offs, deps=()):
    return launch(
        tick_kernel,
        deps,
        scalars=1,
        grid=(1,),
        in_specs=[],
        out_specs=fixed((16, LANES)),
        out_shape=jax.ShapeDtypeStruct((16, LANES), low),
        compiler_params=params(24),
        cost_estimate=cost(TICK, 8),
        name="arrived",
    )(offs)


def swap(value, axis):
    return lax.ppermute(value, axis, [(0, 1), (1, 0)])


def later(value, other):
    return lax.optimization_barrier((value, other))[0]


def part(value, index, count, axis=0):
    size = value.shape[axis] // count
    return lax.dynamic_slice_in_dim(value, index * size, size, axis)


def in_order(index, mine, other):
    return jnp.where(
        index == 0, jnp.concatenate([mine, other], 0), jnp.concatenate([other, mine], 0)
    )


def per_device(
    tokens, segment_ids, gain_one, w_query, w_key, w_value, w_convgate, w_output, conv_filter,
    gain_two, w_gate, w_up, w_down, cotangent,
):
    Order.last = None
    Order.scale = 0.05
    x = lax.axis_index("near")
    y = lax.axis_index("row")
    c = lax.axis_index("core")
    s = 2 * y + c
    width = tokens.shape[1]
    seg = segment_ids[0]
    block = w_down.shape[0]

    def flip(bits):
        return jnp.bitwise_xor(s, bits)

    small_block = block // 2
    z = lax.axis_index("far") % 2
    quarters = [(2 * a + b) * (SHARD_ROWS // 4) for a, b in ((x, z), (1 - x, z), (x, 1 - z), (1 - x, 1 - z))]

    def feed_cols(core, j):
        return [((2 * row + core) * 2 + j) * small_block for row in range(2)]

    feed_rows = [s, flip(1), jnp.bitwise_xor(flip(2), x), jnp.bitwise_xor(flip(3), x)]
    offs = [
        x,
        jnp.bitwise_xor(x, c),
        s * SHARD_ROWS,
        flip(1) * SHARD_ROWS,
        *(flip(2) * SHARD_ROWS + a for a in quarters),
        *(flip(3) * SHARD_ROWS + a for a in quarters),
        *(a * SHARD_ROWS for a in feed_rows),
        y * small_block,
        (1 - y) * small_block,
        0,
        0,
        *feed_cols(c, 0), *feed_cols(c, 1), *feed_cols(1 - c, 0), *feed_cols(1 - c, 1),
        *feed_cols(c, 0), *feed_cols(1 - c, 0), *feed_cols(c, 1), *feed_cols(1 - c, 1),
        2 * (1 - y) + 1 - x, 2 * (1 - y) + x, 2 * y + 1 - x, 2 * y + x,
        flip(3), flip(1), flip(2), s,
        2 * (1 - y) + 1 - x, 2 * y + 1 - x, 2 * (1 - y) + x, 2 * y + x,
        2 * x + z,
    ]
    offs = jnp.stack([jnp.asarray(a, jnp.int32) for a in offs])

    pack, pack_part = pack_mixer(
        offs, gain_one, gain_two, conv_filter, w_query, w_key, w_value, w_convgate, w_output
    )
    direct = swap(pack_part, "row")
    count = lax.axis_size("far")
    over_z = lax.ppermute(direct, "far", [(i, i ^ 1) for i in range(count)])
    came = [direct, swap(direct, "near"), over_z, swap(over_z, "near")]
    pack_pieces = [pack, swap(pack, "core"), *came, *(swap(a, "core") for a in came)]
    cot_other = swap(later(cotangent, direct), "core")

    mine_first, mine_second, give, *sends, down_first, down_second = pack_feed(offs, w_gate, w_up, w_down)
    given = swap(later(give, direct), "core")

    def across(value):
        pairs = []
        for side, row, core in np.ndindex(2, 2, 2):
            pairs.append((4 * side + 2 * row + core, 4 * side + 2 * (1 - row) + (core ^ side)))
        return lax.ppermute(value, ("near", "row", "core"), pairs)

    feed_pieces = [[own, given] for own in (mine_first, mine_second)]
    feed_pieces[0].append(across(later(sends[0], direct)))

    hidden_one, queries, keys, values, gates, vec, full_one = project(offs, tokens, pack_pieces, deps=[cot_other])
    feed_pieces[0].append(swap(later(feed_pieces[0][2], queries), "near"))
    down_pieces = [[swap(later(down_first, queries), "row")]]
    feed_pieces[1].append(across(later(sends[1], queries)))
    pairs = width // 256
    mixed, attention, recips = attend(queries, keys, values, gates, vec, seg, 0, 2 * pairs)
    middle, hidden_two = mix(tokens, mixed, vec, full_one, deps=[down_pieces[0][0]])
    down_pieces.append([swap(later(down_second, middle), "row")])
    tick(offs, [feed_pieces[0][3]])
    hiddens = [hidden_two, swap(hidden_two, "core")]
    cots = [cotangent, cot_other]

    Order.scale = 20.0

    def scatter_far(value):
        return lax.psum_scatter(value, "far", scatter_dimension=0, tiled=True)

    def gather_far(value):
        return lax.all_gather(later(value, tick(offs, [value])), "far", axis=0, tiled=True)

    def down_grad(act, deps=()):
        return weight_grad(offs, ACT_AT, [([act], cots)], (2, 2), "grad_down", deps=deps)

    def gate_grad(both):
        return weight_grad(offs, GRAD_AT, [(hiddens, [both])], (1, 1, 2), "grad_gate_up")

    first_feed = feed(offs, hiddens, cots, 0, w_down, feed_pieces[0], down_pieces[0])
    feed_pieces[1].append(swap(later(feed_pieces[1][2], first_feed[0]), "near"))
    down_send, down_keep = down_grad(first_feed[0], deps=[feed_pieces[1][2]])
    down_came = swap(down_send, "near")
    gate_send, gate_send_own, gate_keep = gate_grad(first_feed[1])
    gate_came = swap(gate_send, "row")
    second_feed = feed(offs, hiddens, cots, 1, w_down, feed_pieces[1], down_pieces[1])
    gate_came_own = swap(later(gate_send_own, second_feed[0]), "row")
    acts, boths, fulls, downs = zip(first_feed, second_feed)
    down_passed = swap(top_sum(offs, down_keep, down_came), "row")
    gate_passed = swap(top_sum(offs, gate_keep, gate_came), "near")
    ghidden_part = feed_back(boths[0], boths[1], fulls[0], fulls[1])
    ghidden_other = swap(ghidden_part, "core")
    down_send_2, down_keep_2 = down_grad(second_feed[0])
    down_came_2 = swap(down_send_2, "near")
    gate_send_2, gate_send_own_2, gate_keep_2 = gate_grad(second_feed[1])
    gate_came_2 = swap(gate_send_2, "row")
    feed_part = scatter_far(
        rest_sum(offs, [(down_keep, down_came, down_passed), (gate_keep, gate_came_own, gate_passed)])
    )
    gate_came_own_2 = swap(later(gate_send_own_2, tick(offs)), "row")
    gmiddle, gbranch, gmixed, _ = middle_back(
        boths[0], boths[1], ghidden_other, middle, cotangent, vec, fulls[0], fulls[1], full_one
    )
    down_passed_2 = swap(top_sum(offs, down_keep_2, down_came_2), "row")
    gate_passed_2 = swap(top_sum(offs, gate_keep_2, gate_came_2), "near")

    ggate, gconv, gfilter = conv_back(values, gmixed, gates, vec, seg)
    filter_came = swap(gfilter, "core")
    feed_sum = gather_far(feed_part)
    early_send, early_keep = weight_grad(
        offs, OWNER_AT, [([mixed], [gbranch]), ([hidden_one], [ggate])], (2, 2), "grad_output_convgate"
    )
    early_came = swap(early_send, "core")
    feed_part = scatter_far(
        rest_sum(
            offs, [(down_keep_2, down_came_2, down_passed_2), (gate_keep_2, gate_came_own_2, gate_passed_2)]
        )
    )
    tick(offs)
    attended = attend_back(queries, keys, values, gmixed, attention, recips, gconv, seg, 0, pairs)
    feed_other = swap(later(feed_sum, tick(offs, [feed_sum])), "near")
    early_give, early_held = halves_sum(offs, [(early_keep, early_came)], [gfilter, filter_came])
    early_came = swap(early_give, "row")
    gqk, gv = attend_back(
        queries, keys, values, gmixed, attention, recips, gconv, seg, pairs, pairs, onto=attended
    )
    late_send, late_keep = weight_grad(
        offs, OWNER_AT, [([hidden_one], [gqk]), ([hidden_one], [gv])], (2, 2), "grad_query_key_value"
    )
    late_came = swap(late_send, "core")
    own_rows, theirs = sort_rows(offs, feed_sum, feed_other, width)
    spreads = [own_rows, swap(theirs, "core")]
    early_own, early_other = near_split(offs, early_held, early_came)
    early_passed = swap(early_other, "near")
    feed_sum_2 = gather_far(feed_part)
    Order.scale = 0.05
    late_give, late_held = halves_sum(offs, [(late_keep, late_came)])
    late_came = swap(late_give, "row")
    out_part = feed_out(acts[0], acts[1], downs[0], downs[1], 1, [], "feed_out_partner")
    late_own, late_other = near_split(offs, late_held, late_came)
    late_passed = swap(late_other, "near")
    tick(offs, [feed_sum_2])
    mixer_near = pairs_sum(offs, [(early_own, early_passed), (late_own, late_passed)])
    feed_other_2 = swap(later(feed_sum_2, mixer_near), "near")
    Order.scale = 20.0
    mixer_sum = lax.psum(mixer_near, "far")
    out_came = swap(later(out_part, mixer_near), "core")
    tick(offs)
    result = feed_out(acts[0], acts[1], downs[0], downs[1], 0, [middle, out_came], "feed_out")
    grad_tokens, _ = tokens_back(gqk, gv, ggate, tokens, gmiddle, vec, full_one)
    own_rows, theirs = sort_rows(offs, feed_sum_2, feed_other_2, width)
    spreads += [own_rows, swap(theirs, "core")]
    grad_down = settle_down(offs, [(feed_sum, feed_other), (feed_sum_2, feed_other_2)], width)
    grad_gate, grad_up, ggain_two = spread(offs, gain_two[:, None].astype(wide), w_gate, w_up, spreads)
    mixer_other = swap(mixer_sum, "near")
    *grads, grad_output, grad_filter, ggain_one = settle_mixer(
        offs, gain_one[:, None].astype(wide), mixer_sum, mixer_other, w_query, w_key, w_value, w_convgate
    )
    return (
        result,
        grad_tokens,
        ggain_one,
        *grads,
        grad_output,
        grad_filter,
        ggain_two,
        grad_gate,
        grad_up,
        grad_down,
    )


def solution(mesh):
    replicas, shards = mesh.shape["rep"], mesh.shape["shard"]
    devices = np.asarray(mesh.devices).reshape(replicas // 2, 2, shards // 2, 2)
    fine = Mesh(devices, ("far", "near", "row", "core"))
    token = P(("far", "near", "row", "core"), None)
    line = P(("row", "core"))
    weight = P(("row", "core"), None)
    taps = P(None, ("row", "core"))
    return jax.shard_map(
        per_device,
        mesh=fine,
        in_specs=(
            token, token, line, weight, weight, weight, weight, weight, taps, line, weight, weight, weight, token
        ),
        out_specs=(
            token, token, line, weight, weight, weight, weight, weight, taps, line, weight, weight, weight
        ),
        check_vma=False,
    )
```

```python
import functools

import jax
import jax.numpy as jnp
import numpy as np
from jax import lax
from jax.experimental import pallas as pl
from jax.experimental.pallas import tpu as pltpu
from jax.sharding import Mesh
from jax.sharding import PartitionSpec as P

HEADS = 16
FEAT = 16
KW = 3
EPS = 1e-06
TILE = 256
SHARD_ROWS = 256
LANES = 128
TICK = 1e5
X_AT, MIXER_AT, FEED_AT, DOWN_AT, PACK_AT, COLS_AT, GRAD_AT, OWNER_AT, ACT_AT, QUARTER_AT = 0, 2, 12, 16, 20, 28, 36, 40, 44, 48

low = jnp.bfloat16
wide = jnp.float32


def dot(a, b):
    return jnp.dot(a, b, preferred_element_type=wide)


def dot_nt(a, b):
    return lax.dot_general(a, b, (((1,), (1,)), ((), ())), preferred_element_type=wide)


def dot_tn(a, b):
    return lax.dot_general(a, b, (((0,), (0,)), ((), ())), preferred_element_type=wide)


class Order:
    last = None
    scale = 1.0


def launch(kernel, deps=(), onto=(), *, scalars=0, grid, in_specs, out_specs, out_shape, scratch_shapes=(), **rest):
    taken = scalars + len(in_specs)
    deps = list(onto) + [d for d in deps if d is not None] + ([] if Order.last is None or any(Order.last is a for a in onto) else [Order.last])

    def body(*refs):
        kernel(*refs[:taken], *refs[taken + len(deps) :])

    spec = pltpu.PrefetchScalarGridSpec(
        num_scalar_prefetch=scalars,
        grid=grid,
        in_specs=list(in_specs) + [pl.BlockSpec(memory_space=pl.ANY)] * len(deps),
        out_specs=out_specs,
        scratch_shapes=list(scratch_shapes),
    )
    aliases = {taken + n: n for n in range(len(onto))}
    run = pl.pallas_call(body, grid_spec=spec, out_shape=out_shape, input_output_aliases=aliases, **rest)

    def call(*operands):
        result = run(*operands, *deps)
        Order.last = result[0] if isinstance(result, (list, tuple)) else result
        return result

    return call


def params(mib, least=60):
    return pltpu.CompilerParams(vmem_limit_bytes=max(mib, least) << 20)


def cost(gigaflops, mebibytes):
    return pl.CostEstimate(
        flops=int(gigaflops * Order.scale * 1e9), bytes_accessed=int(mebibytes * Order.scale * (1 << 20)), transcendentals=0
    )


def fixed(shape):
    return pl.BlockSpec(shape, lambda *_: (0,) * len(shape), pipeline_mode=pl.Buffered(1))


def rows(height, width):
    return pl.BlockSpec((height, width), lambda i, *_: (i, 0))


def place(offs_ref, base, pieces, full_ref):
    for n, piece in enumerate(pieces):
        at = pl.multiple_of(offs_ref[base + n], 64)
        full_ref[pl.ds(at, piece.shape[0]), :] = piece[...]


def project_kernel(offs_ref, x_ref, *refs):
    pieces, (hidden_ref, q_ref, k_ref, v_ref, gate_ref, vec_ref, out_ref, full_ref, sem) = refs[:10], refs[10:]
    copy = pltpu.make_async_copy(full_ref, out_ref, sem)
    heads = HEADS * FEAT
    width = x_ref.shape[1]

    @pl.when(pl.program_id(0) == 0)
    def _():
        place(offs_ref, MIXER_AT, pieces, full_ref)
        copy.start()
        small = full_ref[:, 2 * heads + 3 * width :].astype(wide)
        vec_ref[...] = small.T[:8, :]

    x = x_ref[...].astype(wide)
    inverse = lax.rsqrt(jnp.mean(x * x, axis=-1, keepdims=True) + EPS)
    hidden = (x * inverse * vec_ref[0:1, :]).astype(low)
    hidden_ref[...] = hidden
    at = width
    q_ref[...] = (dot(hidden, full_ref[:, at : at + heads]) * FEAT ** (-0.5)).astype(low)
    k_ref[...] = dot(hidden, full_ref[:, at + heads : at + 2 * heads]).astype(low)
    at = at + 2 * heads
    v_ref[...] = dot(hidden, full_ref[:, at : at + width]).astype(low)
    gate_ref[...] = dot(hidden, full_ref[:, at + width : at + 2 * width]).astype(low)

    @pl.when(pl.program_id(0) == pl.num_programs(0) - 1)
    def _():
        copy.wait()


def project(offs, x, pieces, deps=()):
    length, width = x.shape
    heads = HEADS * FEAT
    columns = pieces[0].shape[1]
    shapes = [
        jax.ShapeDtypeStruct((length, width), low),
        jax.ShapeDtypeStruct((length, heads), low),
        jax.ShapeDtypeStruct((length, heads), low),
        jax.ShapeDtypeStruct((length, width), low),
        jax.ShapeDtypeStruct((length, width), low),
        jax.ShapeDtypeStruct((8, width), wide),
        jax.ShapeDtypeStruct((width, columns), low),
    ]
    return launch(
        project_kernel,
        deps,
        scalars=1,
        grid=(length // TILE,),
        in_specs=[rows(TILE, width)] + [fixed(p.shape) for p in pieces],
        out_specs=[
            rows(TILE, width),
            rows(TILE, heads),
            rows(TILE, heads),
            rows(TILE, width),
            rows(TILE, width),
            fixed((8, width)),
            pl.BlockSpec(memory_space=pl.ANY),
        ],
        scratch_shapes=[pltpu.VMEM((width, columns), low), pltpu.SemaphoreType.DMA],
        out_shape=shapes,
        compiler_params=params(40),
        cost_estimate=cost(7, 22),
        name="project",
    )(offs, x, *pieces)


def shift_rows(v, seg, by, up):
    zeros = jnp.zeros((by, v.shape[1]), v.dtype)
    none = jnp.full((by, 1), -1, seg.dtype)
    if up:
        moved, moved_seg = jnp.concatenate([v[by:], zeros], 0), jnp.concatenate([seg[by:], none], 0)
    else:
        moved = jnp.concatenate([zeros, v[:-by]], 0)
        moved_seg = jnp.concatenate([none, seg[:-by]], 0)
    return jnp.where(moved_seg == seg, moved, 0.0)


def lane_pick(width, start, stop):
    i = lax.broadcasted_iota(jnp.int32, (1, width), 1)
    return (i >= start) & (i < stop)


def attend_kernel(
    first, q_ref, k_ref, v_ref, gate_ref, vec_ref, segr_ref, segc_ref, mixed_ref, att_ref, recip_ref, mask_ref
):
    length = q_ref.shape[0]
    pair = pl.program_id(0) + first
    zero = jnp.zeros((), low)

    @pl.when(pair == first)
    def _():
        for tb in range(0, length, TILE):
            t = lax.broadcasted_iota(jnp.int32, (TILE, length), 0) + tb
            s = lax.broadcasted_iota(jnp.int32, (TILE, length), 1)
            seen = (s <= t) & (segc_ref[tb : tb + TILE, :] == segr_ref[...])
            mask_ref[tb : tb + TILE, :] = jnp.where(seen, 1.0, 0.0).astype(low)

    v = v_ref[...]
    keys, sides = [], []
    for i in range(2):
        head = 2 * pair + i
        keys.append(jnp.where(lane_pick(HEADS * FEAT, head * FEAT, (head + 1) * FEAT), k_ref[...], zero))
        lanes = lane_pick(128, 64 * i, 64 * i + 64)
        ones = jnp.broadcast_to(jnp.where(lanes, 1.0, 0.0).astype(low), (length, 128))
        sides.append(jnp.concatenate([jnp.where(lanes, v, zero), ones], 1))
    for tb in range(0, length, TILE):
        n = tb + TILE
        total = None
        for i in range(2):
            one_plus = dot_nt(q_ref[tb:n, :], keys[i][:n]) + 1.0
            kernel = (one_plus * one_plus + 1.0).astype(low) * mask_ref[tb:n, :n]
            part = dot(kernel, sides[i][:n])
            total = part if total is None else total + part
        recip = 1.0 / total[:, 128:]
        att_ref[tb:n, :] = (total[:, :128] * recip).astype(low)
        recip_ref[tb:n, :] = (2.0 * recip).astype(low)
    v_wide = v.astype(wide)
    seg = segc_ref[...]
    conv = vec_ref[2:3, :] * v_wide
    for j in range(1, KW):
        conv = conv + vec_ref[2 + j : 3 + j, :] * shift_rows(v_wide, seg, j, False)
    mixed_ref[...] = (att_ref[...].astype(wide) + gate_ref[...].astype(wide) * conv).astype(low)


def whole(a):
    return pl.BlockSpec(a.shape, lambda p: (0, 0))


def attend(q, k, v, gate, vec, seg, first, count, onto=(), deps=()):
    length, width = v.shape
    column = pl.BlockSpec((length, 128), lambda p: (0, p + first))
    seg_row, seg_col = seg.reshape(1, length), seg.reshape(length, 1)
    return launch(
        functools.partial(attend_kernel, first),
        deps,
        onto,
        grid=(count,),
        in_specs=[
            whole(q), whole(k), column, column, pl.BlockSpec((8, 128), lambda p: (0, p + first)), whole(seg_row), whole(seg_col)
        ],
        out_specs=[column] * 3,
        out_shape=[jax.ShapeDtypeStruct((length, width), low)] * 3,
        scratch_shapes=[pltpu.VMEM((length, length), low)],
        compiler_params=params(40),
        cost_estimate=cost(18 * count * 128 / width, 14),
        name="attention_forward",
    )(q, k, v, gate, vec, seg_row, seg_col)


def attend_back_kernel(
    first, q_ref, k_ref, v_ref, gm_ref, att_ref, recip_ref, gconv_ref, segr_ref, segc_ref,
    gqk_ref, gv_ref, mask_ref, gq_acc, gk_acc,
):
    length, heads = q_ref.shape
    pair = pl.program_id(0) + first
    zero = jnp.zeros((), low)

    @pl.when(pair == first)
    def _():
        for sb in range(0, length, TILE):
            s = lax.broadcasted_iota(jnp.int32, (TILE, length), 0) + sb
            t = lax.broadcasted_iota(jnp.int32, (TILE, length), 1)
            seen = (s <= t) & (segc_ref[sb : sb + TILE, :] == segr_ref[...])
            mask_ref[sb : sb + TILE, :] = jnp.where(seen, 1.0, 0.0).astype(low)
        gk_acc[...] = jnp.zeros_like(gk_acc)
        gq_acc[...] = jnp.zeros_like(gq_acc)

    v = v_ref[...]
    gm = gm_ref[...].astype(wide)
    gnum_wide = gm * recip_ref[...].astype(wide)
    gnum = gnum_wide.astype(low)
    product = gnum_wide * att_ref[...].astype(wide)
    high = product.astype(low)
    rest = (product - high.astype(wide)).astype(low)
    r = lax.broadcasted_iota(jnp.int32, (256, 128), 0)
    c = lax.broadcasted_iota(jnp.int32, (256, 128), 1)
    same_head = jnp.where(((r % 128) // 64) == (c // 64), 1.0, 0.0).astype(low)
    gtot = -dot(jnp.concatenate([high, rest], 1), same_head)
    gtot_high = gtot.astype(low)
    gtot_rest = (gtot - gtot_high.astype(wide)).astype(low)
    lane = lax.broadcasted_iota(jnp.int32, (1, 128), 1)
    left = jnp.concatenate([gnum, jnp.where(lane % 64 == 0, gtot_high, gtot_rest)], 1)
    gnum_half = gnum * jnp.asarray(0.5, low)
    queries, sides, gnums, keys = [], [], [], []
    for i in range(2):
        head = 2 * pair + i
        mine = lane_pick(heads, head * FEAT, (head + 1) * FEAT)
        queries.append(jnp.where(mine, q_ref[...], zero))
        keys.append(jnp.where(mine, k_ref[...], zero))
        lanes = lane_pick(128, 64 * i, 64 * i + 64)
        ones = jnp.where(lane_pick(128, 64 * i, 64 * i + 2), 1.0, 0.0).astype(low)
        sides.append(jnp.concatenate([jnp.where(lanes, v, zero), jnp.broadcast_to(ones, (length, 128))], 1))
        gnums.append(jnp.where(lanes, gnum_half, zero))
    for sb in range(0, length, TILE):
        n = sb + TILE
        gv = gconv_ref[sb:n, :].astype(wide)
        gk = None
        for i in range(2):
            one_plus = dot_nt(k_ref[sb:n, :], queries[i][sb:]) + 1.0
            mask = mask_ref[sb:n, sb:]
            kernel = (one_plus * one_plus + 1.0).astype(low) * mask
            gv = gv + dot(kernel, gnums[i][sb:])
            gkernel = dot_nt(sides[i][sb:n], left[sb:])
            gscores = (gkernel * one_plus).astype(low) * mask
            part = dot(gscores, queries[i][sb:])
            gk = part if gk is None else gk + part
            gq_acc[sb:, :] += dot_tn(gscores, keys[i][sb:n])
        gv_ref[sb:n, :] = gv.astype(low)
        gk_acc[sb:n, :] += gk

    @pl.when(pl.program_id(0) == pl.num_programs(0) - 1)
    def _():
        mine = slice(2 * FEAT * first, 2 * FEAT * first + gqk_ref.shape[1] // 2)
        gqk_ref[:, : gqk_ref.shape[1] // 2] = (gq_acc[:, mine] * FEAT ** (-0.5)).astype(low)
        gqk_ref[:, gqk_ref.shape[1] // 2 :] = gk_acc[:, mine].astype(low)


def attend_back(q, k, v, gm, att, recip, gconv, seg, first, count, onto=(), deps=()):
    length, width = v.shape
    heads = q.shape[1]
    column = pl.BlockSpec((length, 128), lambda p: (0, p + first))
    seg_row, seg_col = seg.reshape(1, length), seg.reshape(length, 1)
    return launch(
        functools.partial(attend_back_kernel, first),
        deps,
        onto,
        grid=(count,),
        in_specs=[whole(q), whole(k)] + [column] * 5 + [whole(seg_row), whole(seg_col)],
        out_specs=[pl.BlockSpec((length, 4 * FEAT * count), lambda p: (0, first // count)), column],
        out_shape=[jax.ShapeDtypeStruct((length, 2 * heads), low), jax.ShapeDtypeStruct((length, width), low)],
        scratch_shapes=[
            pltpu.VMEM((length, length), low),
            pltpu.VMEM((length, heads), wide),
            pltpu.VMEM((length, heads), wide),
        ],
        compiler_params=params(48),
        cost_estimate=cost(40 * count * 128 / width, 18),
        name="attention_backward",
    )(q, k, v, gm, att, recip, gconv, seg_row, seg_col)


def conv_back_kernel(v_ref, gm_ref, gate_ref, vec_ref, segc_ref, ggate_ref, gconv_ref, gfilt_ref):
    v_wide = v_ref[...].astype(wide)
    gm = gm_ref[...].astype(wide)
    seg = segc_ref[...]
    taps = [vec_ref[2 + j : 3 + j, :] for j in range(KW)]
    grad = gm * gate_ref[...].astype(wide)
    conv = taps[0] * v_wide
    gv_conv = taps[0] * grad
    lines = [jnp.sum(grad * v_wide, 0, keepdims=True)]
    for j in range(1, KW):
        moved = shift_rows(v_wide, seg, j, False)
        conv = conv + taps[j] * moved
        lines.append(jnp.sum(grad * moved, 0, keepdims=True))
        gv_conv = gv_conv + taps[j] * shift_rows(grad, seg, j, True)
    lines.append(jnp.zeros((LANES - KW, 128), wide))
    gfilt_ref[...] = jnp.concatenate(lines, 0).T.astype(low)
    ggate_ref[...] = (gm * conv).astype(low)
    gconv_ref[...] = gv_conv.astype(low)


def conv_back(v, gm, gate, vec, seg, deps=()):
    length, width = v.shape
    column = pl.BlockSpec((length, 128), lambda p: (0, p))
    small = pl.BlockSpec((8, 128), lambda p: (0, p))
    seg_col = seg.reshape(length, 1)
    return launch(
        conv_back_kernel,
        deps,
        grid=(width // 128,),
        in_specs=[column, column, column, small, whole(seg_col)],
        out_specs=[column, column, pl.BlockSpec((128, LANES), lambda p: (p, 0))],
        out_shape=[jax.ShapeDtypeStruct((length, width), low)] * 2 + [jax.ShapeDtypeStruct((width, LANES), low)],
        compiler_params=params(48),
        cost_estimate=cost(1, 10),
        name="convolution_backward",
    )(v, gm, gate, vec, seg_col)


def mix_kernel(x_ref, mixed_ref, vec_ref, weight_ref, middle_ref, hidden_ref):
    middle = x_ref[...].astype(wide) + dot(mixed_ref[...], weight_ref[...])
    inverse = lax.rsqrt(jnp.mean(middle * middle, axis=-1, keepdims=True) + EPS)
    middle_ref[...] = middle
    hidden_ref[...] = (middle * inverse * vec_ref[1:2, :]).astype(low)


def mix(x, mixed, vec, full, deps=()):
    length, width = x.shape
    return launch(
        mix_kernel,
        deps,
        grid=(length // TILE,),
        in_specs=[rows(TILE, width), rows(TILE, width), fixed(vec.shape), fixed((width, width))],
        out_specs=[rows(TILE, width), rows(TILE, width)],
        out_shape=[jax.ShapeDtypeStruct((length, width), wide), jax.ShapeDtypeStruct((length, width), low)],
        compiler_params=params(32),
        cost_estimate=cost(3, 16),
        name="mix",
    )(x, mixed, vec, full)


def first_half(n):
    return lambda i, *_: (jnp.minimum(i, n - 1), 0)


def second_half(n):
    return lambda i, *_: (jnp.maximum(i - n, 0), 0)


def feed_kernel(n, offs_ref, ha_ref, hb_ref, ca_ref, cb_ref, *refs):
    pieces, downs = refs[:4], refs[4:6]
    act_ref, both_ref, full_out_ref, down_out_ref, full_ref, down_ref, sems = refs[6:]
    copies = [
        pltpu.make_async_copy(full_ref, full_out_ref, sems.at[0]),
        pltpu.make_async_copy(down_ref, down_out_ref, sems.at[1]),
    ]
    step = pl.program_id(0)
    half = full_ref.shape[1] // 2

    @pl.when(step == 0)
    def _():
        place(offs_ref, FEED_AT, pieces, full_ref)
        place(offs_ref, DOWN_AT, downs, down_ref)
        for copy in copies:
            copy.start()

    def work(hidden, cotangent):
        for at in range(0, half, 256):
            gate = dot(hidden, full_ref[:, at : at + 256])
            up = dot(hidden, full_ref[:, half + at : half + at + 256])
            gact = dot_nt(cotangent, down_ref[at : at + 256, :])
            sig = jax.nn.sigmoid(gate)
            silu = gate * sig
            act_ref[:, at : at + 256] = (silu * up).astype(low)
            both_ref[:, at : at + 256] = (gact * up * (sig + silu * (1.0 - sig))).astype(low)
            both_ref[:, half + at : half + at + 256] = (gact * silu).astype(low)

    @pl.when(step < n)
    def _():
        work(ha_ref[...], ca_ref[...])

    @pl.when(step >= n)
    def _():
        work(hb_ref[...], cb_ref[...])

    @pl.when(step == 2 * n - 1)
    def _():
        for copy in copies:
            copy.wait()


def feed(offs, hidden, cotangent, j, w_down, pieces, down_pieces, deps=()):
    length, width = hidden[0].shape
    n = length // TILE
    half = w_down.shape[0]
    first = pl.BlockSpec((TILE, width), first_half(n))
    second = pl.BlockSpec((TILE, width), second_half(n))
    own_down = pl.BlockSpec((half // 2, width), lambda *_: (j, 0), pipeline_mode=pl.Buffered(1))
    given_rows = pl.BlockSpec(pieces[0].shape, lambda *_: (j, 0), pipeline_mode=pl.Buffered(1))
    return launch(
        functools.partial(feed_kernel, n),
        deps,
        scalars=1,
        grid=(2 * n,),
        in_specs=[first, second, first, second]
        + [fixed(pieces[0].shape), given_rows]
        + [fixed(p.shape) for p in pieces[2:]]
        + [own_down]
        + [fixed(p.shape) for p in down_pieces],
        out_specs=[rows(TILE, half), rows(TILE, 2 * half)] + [pl.BlockSpec(memory_space=pl.ANY)] * 2,
        scratch_shapes=[
            pltpu.VMEM((width, 2 * half), low),
            pltpu.VMEM((half, width), low),
            pltpu.SemaphoreType.DMA((2,)),
        ],
        out_shape=[
            jax.ShapeDtypeStruct((2 * length, half), low),
            jax.ShapeDtypeStruct((2 * length, 2 * half), low),
            jax.ShapeDtypeStruct((width, 2 * half), low),
            jax.ShapeDtypeStruct((half, width), low),
        ],
        compiler_params=params(48),
        cost_estimate=cost(16, 34),
        name="feed_in",
    )(offs, *hidden, *cotangent, *pieces, w_down, *down_pieces)


def weight_grad_kernel(shape_of, counts, outs, length, offs_ref, *refs):
    targets = [(ref, row * TILE) for ref, height in zip(refs[-len(outs) :], outs) for row in range(height)]
    step = pl.program_id(0)

    def work(lefts, rights):
        terms = max(len(lefts[0]), len(rights))

        def part_of(group, t):
            return group[t][...] if len(group) == terms else group[0][t * length : (t + 1) * length, :]

        for b, (ref, row) in enumerate(targets):
            value = None
            for t in range(terms):
                product = dot_tn(part_of(lefts[b], t), part_of(rights, t))
                value = product if value is None else value + product
            ref[row : row + TILE, :] = value.astype(low)

    start = 0
    for (left_at, right_at), count in zip(shape_of, counts):
        lefts = [[refs[n] for n in block] for block in left_at]
        rights = [refs[n] for n in right_at]
        if len(counts) == 1:
            work(lefts, rights)
        else:
            pl.when((step >= start) & (step < start + count))(functools.partial(work, lefts, rights))
        start += count


def weight_grad(offs, base, groups, outs, name, tile=512, deps=()):
    blocks = sum(outs)
    counts = [rights[0].shape[1] // tile for _, rights in groups]
    columns = sum(counts) * tile
    in_specs, operands, shape_of, known = [], [], [], {}
    start = 0
    for (lefts, rights), count in zip(groups, counts):
        key = tuple(id(a) for a in lefts)
        if key not in known:
            known[key] = []
            for b in range(blocks):
                known[key].append([len(operands) + n for n in range(len(lefts))])
                for a in lefts:
                    in_specs.append(pl.BlockSpec((a.shape[0], TILE), lambda j, offs, b=b: (0, offs[base + b])))
                    operands.append(a)
        shape_of.append((known[key], [len(operands) + n for n in range(len(rights))]))
        for a in rights:

            def where_to(j, offs, start=start, count=count):
                return (0, jnp.clip(j - start, 0, count - 1))

            in_specs.append(pl.BlockSpec((a.shape[0], tile), where_to))
            operands.append(a)
        start += count
    tokens = sum(a.shape[0] for a in groups[0][0])
    terms = max(len(groups[0][0]), len(groups[0][1]))
    return launch(
        functools.partial(weight_grad_kernel, shape_of, counts, outs, tokens // terms),
        deps,
        scalars=1,
        grid=(sum(counts),),
        in_specs=in_specs,
        out_specs=[pl.BlockSpec((height * TILE, tile), lambda j, offs: (0, j)) for height in outs],
        out_shape=[jax.ShapeDtypeStruct((height * TILE, columns), low) for height in outs],
        compiler_params=params(48, 48),
        cost_estimate=cost(2.5e-9 * tokens * 1024 * columns, (tokens * (1024 + columns) * 2 + 2048 * columns) / 2**20),
        name=name,
    )(offs, *operands)


def feed_back_kernel(a_ref, b_ref, wa_ref, wb_ref, out_ref):
    out_ref[...] = (dot_nt(a_ref[...], wa_ref[...]) + dot_nt(b_ref[...], wb_ref[...])).astype(low)


def feed_back(first, second, full_first, full_second, deps=()):
    length = first.shape[0] // 2
    width = full_first.shape[0]
    n = length // TILE
    tile = pl.BlockSpec((TILE, first.shape[1]), lambda i: (i + n, 0))
    return launch(
        feed_back_kernel,
        deps,
        grid=(n,),
        in_specs=[tile, tile, fixed(full_first.shape), fixed(full_second.shape)],
        out_specs=rows(TILE, width),
        out_shape=jax.ShapeDtypeStruct((length, width), low),
        compiler_params=params(32),
        cost_estimate=cost(10, 18),
        name="feed_back_partner",
    )(first, second, full_first, full_second)


def middle_back_kernel(
    a_ref, b_ref, other_ref, middle_ref, cot_ref, vec_ref, wa_ref, wb_ref, wo_ref,
    gmiddle_ref, gbranch_ref, gmixed_ref, ggain_ref,
):
    ghidden = dot_nt(a_ref[...], wa_ref[...]) + dot_nt(b_ref[...], wb_ref[...]) + other_ref[...].astype(wide)
    middle = middle_ref[...]
    inverse = lax.rsqrt(jnp.mean(middle * middle, axis=-1, keepdims=True) + EPS)
    normed = middle * inverse
    gain = jnp.sum(ghidden * normed, axis=0, keepdims=True)

    @pl.when(pl.program_id(0) == 0)
    def _():
        ggain_ref[...] = jnp.zeros_like(ggain_ref)

    ggain_ref[0:1, :] += gain
    scaled = ghidden * vec_ref[1:2, :]
    gmiddle = cot_ref[...].astype(wide) + inverse * (
        scaled - normed * jnp.mean(scaled * normed, axis=-1, keepdims=True)
    )
    gmiddle_ref[...] = gmiddle
    gbranch = gmiddle.astype(low)
    gbranch_ref[...] = gbranch
    gmixed_ref[...] = dot_nt(gbranch, wo_ref[...]).astype(low)


def middle_back(first, second, other, middle, cotangent, vec, full_first, full_second, w_output, deps=()):
    length, width = middle.shape
    tile = rows(TILE, first.shape[1])
    line = rows(TILE, width)
    return launch(
        middle_back_kernel,
        deps,
        grid=(length // TILE,),
        in_specs=[
            tile, tile, line, line, line, fixed(vec.shape), fixed(full_first.shape), fixed(full_second.shape), fixed((width, width))
        ],
        out_specs=[line, line, line, fixed((8, width))],
        out_shape=[
            jax.ShapeDtypeStruct((length, width), wide),
            jax.ShapeDtypeStruct((length, width), low),
            jax.ShapeDtypeStruct((length, width), low),
            jax.ShapeDtypeStruct((8, width), wide),
        ],
        compiler_params=params(48),
        cost_estimate=cost(13, 40),
        name="middle_back",
    )(first, second, other, middle, cotangent, vec, full_first, full_second, w_output)


def feed_out_kernel(add, *refs):
    out_ref = refs[-1]
    value = dot(refs[0][...], refs[2][...]) + dot(refs[1][...], refs[3][...])
    for ref in refs[4:-1]:
        value = value + ref[...].astype(wide)
    out_ref[...] = value.astype(low)


def feed_out(first, second, down_first, down_second, shift, extras, name, deps=()):
    length = first.shape[0] // 2
    width = down_first.shape[1]
    n = length // TILE
    tile = pl.BlockSpec((TILE, first.shape[1]), lambda i: (i + shift * n, 0))
    return launch(
        functools.partial(feed_out_kernel, len(extras)),
        deps,
        grid=(n,),
        in_specs=[tile, tile, fixed(down_first.shape), fixed(down_second.shape)] + [rows(TILE, width)] * len(extras),
        out_specs=rows(TILE, width),
        out_shape=jax.ShapeDtypeStruct((length, width), low),
        compiler_params=params(32),
        cost_estimate=cost(5, 16),
        name=name,
    )(first, second, down_first, down_second, *extras)


def tokens_back_kernel(gqk_ref, gv_ref, ggate_ref, x_ref, gmiddle_ref, vec_ref, full_ref, gtokens_ref, ggain_ref):
    two = gqk_ref.shape[1]
    width = x_ref.shape[1]
    quarter = two // 4
    ghidden = None
    for n, col in enumerate((0, 2, 1, 3)):
        at = width + col * quarter
        term = dot_nt(gqk_ref[:, n * quarter : (n + 1) * quarter], full_ref[:, at : at + quarter])
        ghidden = term if ghidden is None else ghidden + term
    ghidden = (
        ghidden
        + dot_nt(gv_ref[...], full_ref[:, width + two : 2 * width + two])
        + dot_nt(ggate_ref[...], full_ref[:, two + 2 * width : two + 3 * width])
    )
    x = x_ref[...].astype(wide)
    inverse = lax.rsqrt(jnp.mean(x * x, axis=-1, keepdims=True) + EPS)
    normed = x * inverse

    @pl.when(pl.program_id(0) == 0)
    def _():
        ggain_ref[...] = jnp.zeros_like(ggain_ref)

    ggain_ref[0:1, :] += jnp.sum(ghidden * normed, axis=0, keepdims=True)
    scaled = ghidden * vec_ref[0:1, :]
    gtokens_ref[...] = gmiddle_ref[...] + inverse * (
        scaled - normed * jnp.mean(scaled * normed, axis=-1, keepdims=True)
    )


def tokens_back(gqk, gv, ggate, x, gmiddle, vec, full, deps=()):
    length, width = x.shape
    line = rows(TILE, width)
    return launch(
        tokens_back_kernel,
        deps,
        grid=(length // TILE,),
        in_specs=[rows(TILE, gqk.shape[1]), line, line, line, line, fixed(vec.shape), fixed(full.shape)],
        out_specs=[line, fixed((8, width))],
        out_shape=[jax.ShapeDtypeStruct((length, width), wide), jax.ShapeDtypeStruct((8, width), wide)],
        compiler_params=params(40),
        cost_estimate=cost(7, 24),
        name="tokens_back",
    )(gqk, gv, ggate, x, gmiddle, vec, full)


def as_line(column):
    return jnp.broadcast_to(column, (column.shape[0], LANES)).T[0]


def spread_kernel(cols_ref, gain_ref, wg_ref, wu_ref, a_ref, b_ref, c_ref, d_ref, gate_ref, up_ref, ggain_ref):
    total = None
    for n, ref in enumerate((a_ref, b_ref, c_ref, d_ref)):
        quarter = ref.shape[1] // 4
        for part_y in range(2):
            at = pl.ds(pl.multiple_of(cols_ref[COLS_AT + 2 * n + part_y], 512), quarter)
            gate = ref[:, part_y * quarter : (part_y + 1) * quarter].astype(wide)
            up = ref[:, (2 + part_y) * quarter : (3 + part_y) * quarter].astype(wide)
            gate_ref[:, at] = gate
            up_ref[:, at] = up
            term = gate * wg_ref[:, at].astype(wide) + up * wu_ref[:, at].astype(wide)
            line = jnp.sum(term, axis=1, keepdims=True)
            total = line if total is None else total + line
    ggain_ref[...] = as_line(total / gain_ref[...])


def spread(cols, gain, w_gate, w_up, blocks, deps=()):
    height, width = blocks[0].shape
    shape = jax.ShapeDtypeStruct((height, 2 * width), wide)
    return launch(
        spread_kernel,
        deps,
        scalars=1,
        grid=(1,),
        in_specs=[fixed(gain.shape), fixed(w_gate.shape), fixed(w_up.shape)] + [fixed(b.shape) for b in blocks],
        out_specs=[fixed(shape.shape)] * 2 + [fixed(gain.shape[:1])],
        out_shape=[shape, shape, jax.ShapeDtypeStruct(gain.shape[:1], wide)],
        compiler_params=params(24),
        cost_estimate=cost(0.001, 16),
        name="spread",
    )(cols, gain, w_gate, w_up, *blocks)


def pack_kernel(at_ref, g1_ref, g2_ref, taps_ref, q_ref, k_ref, v_ref, c_ref, o_ref, pack_ref, part_ref):
    height = q_ref.shape[0]
    col = 0
    for ref in (o_ref, q_ref, k_ref, v_ref, c_ref):
        pack_ref[:, col : col + ref.shape[1]] = ref[...]
        col += ref.shape[1]
    small = jnp.concatenate([g1_ref[...].astype(wide)[None], g2_ref[...].astype(wide)[None], taps_ref[...].astype(wide)], 0)
    small = jnp.concatenate([small, jnp.zeros((LANES - small.shape[0], height), wide)], 0)
    pack_ref[:, col : col + LANES] = small.T.astype(low)
    size = part_ref.shape[0]
    part_ref[...] = pack_ref[pl.ds(pl.multiple_of(at_ref[QUARTER_AT] * size, 64), size), :]


def pack_mixer(at, gain_one, gain_two, taps, w_query, w_key, w_value, w_convgate, w_output):
    operands = (gain_one, gain_two, taps, w_query, w_key, w_value, w_convgate, w_output)
    height = w_query.shape[0]
    columns = sum(a.shape[1] for a in operands[3:]) + LANES
    shapes = [(height, columns), (height // 4, columns)]
    return launch(
        pack_kernel,
        scalars=1,
        grid=(1,),
        in_specs=[fixed(a.shape) for a in operands],
        out_specs=[fixed(a) for a in shapes],
        out_shape=[jax.ShapeDtypeStruct(a, low) for a in shapes],
        compiler_params=params(24),
        cost_estimate=cost(0.001, 4),
        name="pack_mixer",
    )(at, *operands)


def pack_feed_kernel(offs_ref, gate_ref, up_ref, down_ref, first_ref, second_ref, give_ref, *refs):
    send_refs, (low_ref, high_ref) = refs[:2], refs[2:]
    height = gate_ref.shape[0]
    sent = PACK_AT + 4 * offs_ref[X_AT]
    targets = (
        (first_ref, 0, PACK_AT),
        (second_ref, 0, PACK_AT + 2),
        (give_ref, 0, PACK_AT + 4),
        (give_ref, height, PACK_AT + 6),
        (send_refs[0], 0, sent),
        (send_refs[1], 0, sent + 2),
    )
    for ref, row, place_at in targets:
        quarter = ref.shape[1] // 4
        for part_y in range(2):
            at = pl.ds(pl.multiple_of(offs_ref[place_at + part_y], 512), quarter)
            ref[row : row + height, part_y * quarter : (part_y + 1) * quarter] = gate_ref[:, at]
            ref[row : row + height, (2 + part_y) * quarter : (3 + part_y) * quarter] = up_ref[:, at]
    size = low_ref.shape[0]
    low_ref[...] = down_ref[:size, :]
    high_ref[...] = down_ref[size:, :]


def pack_feed(offs, w_gate, w_up, w_down, deps=()):
    height, columns = w_gate.shape
    half = (height, columns // 2)
    shapes = [half, half, (2 * height, columns // 2), half, half] + [(w_down.shape[0] // 2, w_down.shape[1])] * 2
    return launch(
        pack_feed_kernel,
        deps,
        scalars=1,
        grid=(1,),
        in_specs=[fixed(w_gate.shape), fixed(w_up.shape), fixed(w_down.shape)],
        out_specs=[fixed(a) for a in shapes],
        out_shape=[jax.ShapeDtypeStruct(a, low) for a in shapes],
        compiler_params=params(24),
        cost_estimate=cost(0.001, 8),
        name="pack_feed",
    )(offs, w_gate, w_up, w_down)


STRIPS = 1


def operand_parts(operand):
    if not isinstance(operand, tuple):
        return operand, None, 1
    return operand if len(operand) == 3 else (*operand, 2)


def step(kernel, offs, operands, shapes, name, deps=(), giga=0.001):
    in_specs, arrays = [], []
    for operand in operands:
        array, half, parts = operand_parts(operand)
        height = array.shape[0] // parts

        def where_to(i, offs, half=half):
            if half is None:
                return (i, 0)
            return ((half(offs) if callable(half) else half) * STRIPS + i, 0)

        in_specs.append(pl.BlockSpec((height // STRIPS, array.shape[1]), where_to))
        arrays.append(array)
    return launch(
        kernel,
        deps,
        scalars=1,
        grid=(STRIPS,),
        in_specs=in_specs,
        out_specs=[rows(shape[0] // STRIPS, shape[1]) for shape in shapes],
        out_shape=[jax.ShapeDtypeStruct(shape, low) for shape in shapes],
        compiler_params=params(24),
        cost_estimate=cost(giga, 8),
        name=name,
    )(offs, *arrays)


def add(*refs):
    total = refs[0].astype(wide)
    for other in refs[1:]:
        total = total + other.astype(wide)
    return total.astype(low)


def sum_kernel(terms, offs_ref, *refs):
    for out_ref, groups in zip(refs[-len(terms) :], terms):
        col = 0
        for group in groups:
            width = refs[group[0]].shape[1]
            out_ref[:, col : col + width] = add(*(refs[n][...] for n in group))
            col += width


def strip_sum(offs, outputs, name, deps=()):
    operands, terms, shapes = [], [], []
    for groups in outputs:
        terms.append([])
        width = 0
        for group in groups:
            terms[-1].append(list(range(len(operands), len(operands) + len(group))))
            operands += group
            first, _, parts = operand_parts(group[0])
            height = first.shape[0] // parts
            width += first.shape[1]
        shapes.append((height, width))
    return step(functools.partial(sum_kernel, terms), offs, operands, shapes, name, deps)


def top_sum(offs, keep, came, deps=()):
    came = came if came.shape[0] * 2 == keep.shape[0] else (came, 0)
    return strip_sum(offs, [[[(keep, 0), came]]], "top_sum", deps)[0]


def rest_sum(offs, triples, deps=()):
    groups = []
    for keep, came, passed in triples:
        came = came if came.shape[0] * 2 == keep.shape[0] else (came, 1)
        groups.append([(keep, 1), came, passed])
    return strip_sum(offs, [groups], "rest_sum", deps)[0]


def halves_sum(offs, pairs, filters=None, deps=()):
    outputs = []
    for half in range(2):
        groups = [[(keep, half), (came, half)] for keep, came in pairs]
        if filters is not None:

            def quarter(offs_ref, half=half):
                return offs_ref[OWNER_AT + 2 + half]

            groups.append([(a, quarter, 4) for a in filters])
        outputs.append(groups)
    return strip_sum(offs, outputs, "halves_sum", deps)


def near_split(offs, keep, came, deps=()):
    def own(offs_ref):
        return offs_ref[X_AT]

    def other(offs_ref):
        return 1 - offs_ref[X_AT]

    return strip_sum(offs, [[[(keep, own), (came, own)]], [[(keep, other), (came, other)]]], "near_split", deps)


def pairs_sum(offs, pairs, deps=()):
    return strip_sum(offs, [[list(pair) for pair in pairs]], "pairs_sum", deps)[0]


def sort_kernel(offs_ref, total_ref, other_ref, own_ref, give_ref):
    skip = total_ref.shape[1] - own_ref.shape[1]

    @pl.when(offs_ref[X_AT + 1] == 0)
    def _():
        own_ref[...] = total_ref[:, skip:]
        give_ref[...] = other_ref[:, skip:]

    @pl.when(offs_ref[X_AT + 1] != 0)
    def _():
        own_ref[...] = other_ref[:, skip:]
        give_ref[...] = total_ref[:, skip:]


def sort_rows(offs, total, other, skip, deps=()):
    shape = (total.shape[0], total.shape[1] - skip)
    return step(sort_kernel, offs, [total, other], [shape, shape], "sort_rows", deps)


def settle_down_kernel(offs_ref, *refs):
    out_ref = refs[-1]
    size = out_ref.shape[0] // 4
    width = out_ref.shape[1]
    for n in range(4):
        side = offs_ref[X_AT] if n % 2 == 0 else 1 - offs_ref[X_AT]
        at = pl.ds(pl.multiple_of((n // 2) * 2 * size + side * size, 128), size)
        out_ref[at, :] = refs[n][:, :width].astype(wide)


def settle_down(offs, pairs, width, deps=()):
    operands = [a for pair in pairs for a in pair]
    size = operands[0].shape[0]
    column = pl.BlockSpec((size, width), lambda *_: (0, 0), pipeline_mode=pl.Buffered(1))
    return launch(
        settle_down_kernel,
        deps,
        scalars=1,
        grid=(1,),
        in_specs=[column] * 4,
        out_specs=fixed((4 * size, width)),
        out_shape=jax.ShapeDtypeStruct((4 * size, width), wide),
        compiler_params=params(24),
        cost_estimate=cost(0.001, 6),
        name="settle_down",
    )(offs, *operands)


def settle_mixer_kernel(
    offs_ref, gain_ref, mine_ref, other_ref, wq_ref, wk_ref, wv_ref, wc_ref,
    gq_ref, gk_ref, gv_ref, gc_ref, go_ref, gf_ref, ggain_ref, all_ref,
):
    size = mine_ref.shape[0]
    for ref, side in ((mine_ref, offs_ref[X_AT]), (other_ref, 1 - offs_ref[X_AT])):
        all_ref[pl.ds(pl.multiple_of(side * size, 128), size), :] = ref[...].astype(wide)
    width = wv_ref.shape[1]
    half = wq_ref.shape[1] // 2
    go_ref[...] = all_ref[:, :width]
    gc = all_ref[:, width : 2 * width]
    gc_ref[...] = gc
    gf_ref[...] = all_ref[:, 2 * width : 2 * width + LANES].T[:KW, :]
    at = 2 * width + LANES
    gv = all_ref[:, at + 4 * half :]
    gv_ref[...] = gv
    total = jnp.sum(gc * wc_ref[...].astype(wide), axis=1, keepdims=True)
    total = total + jnp.sum(gv * wv_ref[...].astype(wide), axis=1, keepdims=True)
    for n, (ref, weight_ref, cols) in enumerate(
        (
            (gq_ref, wq_ref, slice(0, half)),
            (gk_ref, wk_ref, slice(0, half)),
            (gq_ref, wq_ref, slice(half, 2 * half)),
            (gk_ref, wk_ref, slice(half, 2 * half)),
        )
    ):
        value = all_ref[:, at + n * half : at + (n + 1) * half]
        ref[:, cols] = value
        total = total + jnp.sum(value * weight_ref[:, cols].astype(wide), axis=1, keepdims=True)
    ggain_ref[...] = as_line(total / gain_ref[...])


def settle_mixer(offs, gain, mine, other, w_query, w_key, w_value, w_convgate, deps=()):
    operands = (gain, mine, other, w_query, w_key, w_value, w_convgate)
    height, width = w_value.shape
    shapes = [w_query.shape, w_key.shape, w_value.shape, w_convgate.shape, (height, width), (KW, height), gain.shape[:1]]
    return launch(
        settle_mixer_kernel,
        deps,
        scalars=1,
        grid=(1,),
        in_specs=[fixed(a.shape) for a in operands],
        out_specs=[fixed(a) for a in shapes],
        out_shape=[jax.ShapeDtypeStruct(a, wide) for a in shapes],
        scratch_shapes=[pltpu.VMEM((height, mine.shape[1]), wide)],
        compiler_params=params(24),
        cost_estimate=cost(0.001, 8),
        name="settle_mixer",
    )(offs, *operands)


def tick_kernel(offs_ref, out_ref):
    out_ref[...] = jnp.zeros_like(out_ref)


def tick(offs, deps=()):
    return launch(
        tick_kernel,
        deps,
        scalars=1,
        grid=(1,),
        in_specs=[],
        out_specs=fixed((16, LANES)),
        out_shape=jax.ShapeDtypeStruct((16, LANES), low),
        compiler_params=params(24),
        cost_estimate=cost(TICK, 8),
        name="arrived",
    )(offs)


def swap(value, axis):
    return lax.ppermute(value, axis, [(0, 1), (1, 0)])


def later(value, other):
    return lax.optimization_barrier((value, other))[0]


def part(value, index, count, axis=0):
    size = value.shape[axis] // count
    return lax.dynamic_slice_in_dim(value, index * size, size, axis)


def in_order(index, mine, other):
    return jnp.where(
        index == 0, jnp.concatenate([mine, other], 0), jnp.concatenate([other, mine], 0)
    )


def per_device(
    tokens, segment_ids, gain_one, w_query, w_key, w_value, w_convgate, w_output, conv_filter,
    gain_two, w_gate, w_up, w_down, cotangent,
):
    Order.last = None
    Order.scale = 0.05
    x = lax.axis_index("near")
    y = lax.axis_index("row")
    c = lax.axis_index("core")
    s = 2 * y + c
    width = tokens.shape[1]
    seg = segment_ids[0]
    block = w_down.shape[0]

    def flip(bits):
        return jnp.bitwise_xor(s, bits)

    small_block = block // 2
    z = lax.axis_index("far") % 2
    quarters = [(2 * a + b) * (SHARD_ROWS // 4) for a, b in ((x, z), (1 - x, z), (x, 1 - z), (1 - x, 1 - z))]

    def feed_cols(core, j):
        return [((2 * row + core) * 2 + j) * small_block for row in range(2)]

    feed_rows = [s, flip(1), jnp.bitwise_xor(flip(2), x), jnp.bitwise_xor(flip(3), x)]
    offs = [
        x,
        jnp.bitwise_xor(x, c),
        s * SHARD_ROWS,
        flip(1) * SHARD_ROWS,
        *(flip(2) * SHARD_ROWS + a for a in quarters),
        *(flip(3) * SHARD_ROWS + a for a in quarters),
        *(a * SHARD_ROWS for a in feed_rows),
        y * small_block,
        (1 - y) * small_block,
        0,
        0,
        *feed_cols(c, 0), *feed_cols(c, 1), *feed_cols(1 - c, 0), *feed_cols(1 - c, 1),
        *feed_cols(c, 0), *feed_cols(1 - c, 0), *feed_cols(c, 1), *feed_cols(1 - c, 1),
        2 * (1 - y) + 1 - x, 2 * (1 - y) + x, 2 * y + 1 - x, 2 * y + x,
        flip(3), flip(1), flip(2), s,
        2 * (1 - y) + 1 - x, 2 * y + 1 - x, 2 * (1 - y) + x, 2 * y + x,
        2 * x + z,
    ]
    offs = jnp.stack([jnp.asarray(a, jnp.int32) for a in offs])

    pack, pack_part = pack_mixer(
        offs, gain_one, gain_two, conv_filter, w_query, w_key, w_value, w_convgate, w_output
    )
    direct = swap(pack_part, "row")
    count = lax.axis_size("far")
    over_z = lax.ppermute(direct, "far", [(i, i ^ 1) for i in range(count)])
    came = [direct, swap(direct, "near"), over_z, swap(over_z, "near")]
    pack_pieces = [pack, swap(pack, "core"), *came, *(swap(a, "core") for a in came)]
    cot_other = swap(later(cotangent, direct), "core")

    mine_first, mine_second, give, *sends, down_first, down_second = pack_feed(offs, w_gate, w_up, w_down)
    given = swap(later(give, direct), "core")

    def across(value):
        pairs = []
        for side, row, core in np.ndindex(2, 2, 2):
            pairs.append((4 * side + 2 * row + core, 4 * side + 2 * (1 - row) + (core ^ side)))
        return lax.ppermute(value, ("near", "row", "core"), pairs)

    feed_pieces = [[own, given] for own in (mine_first, mine_second)]
    feed_pieces[0].append(across(later(sends[0], direct)))

    hidden_one, queries, keys, values, gates, vec, full_one = project(offs, tokens, pack_pieces, deps=[cot_other])
    feed_pieces[0].append(swap(later(feed_pieces[0][2], queries), "near"))
    down_pieces = [[swap(later(down_first, queries), "row")]]
    feed_pieces[1].append(across(later(sends[1], queries)))
    pairs = width // 256
    mixed, attention, recips = attend(queries, keys, values, gates, vec, seg, 0, 2 * pairs)
    middle, hidden_two = mix(tokens, mixed, vec, full_one, deps=[down_pieces[0][0]])
    down_pieces.append([swap(later(down_second, middle), "row")])
    tick(offs, [feed_pieces[0][3]])
    hiddens = [hidden_two, swap(hidden_two, "core")]
    cots = [cotangent, cot_other]

    Order.scale = 20.0

    def down_grad(act, deps=()):
        return weight_grad(offs, ACT_AT, [([act], cots)], (2, 2), "grad_down", deps=deps)

    def gate_grad(both):
        return weight_grad(offs, GRAD_AT, [(hiddens, [both])], (1, 1, 2), "grad_gate_up")

    first_feed = feed(offs, hiddens, cots, 0, w_down, feed_pieces[0], down_pieces[0])
    feed_pieces[1].append(swap(later(feed_pieces[1][2], first_feed[0]), "near"))
    down_send, down_keep = down_grad(first_feed[0], deps=[feed_pieces[1][2]])
    down_came = swap(down_send, "near")
    gate_send, gate_send_own, gate_keep = gate_grad(first_feed[1])
    gate_came, gate_came_own = swap(gate_send, "row"), swap(gate_send_own, "row")
    second_feed = feed(offs, hiddens, cots, 1, w_down, feed_pieces[1], down_pieces[1])
    acts, boths, fulls, downs = zip(first_feed, second_feed)
    down_passed = swap(top_sum(offs, down_keep, down_came), "row")
    gate_passed = swap(top_sum(offs, gate_keep, gate_came), "near")
    ghidden_part = feed_back(boths[0], boths[1], fulls[0], fulls[1])
    ghidden_other = swap(ghidden_part, "core")
    down_send_2, down_keep_2 = down_grad(second_feed[0])
    down_came_2 = swap(down_send_2, "near")
    gate_send_2, gate_send_own_2, gate_keep_2 = gate_grad(second_feed[1])
    gate_came_2, gate_came_own_2 = swap(gate_send_2, "row"), swap(gate_send_own_2, "row")
    feed_sum = lax.psum(
        rest_sum(offs, [(down_keep, down_came, down_passed), (gate_keep, gate_came_own, gate_passed)]), "far"
    )
    tick(offs)
    gmiddle, gbranch, gmixed, _ = middle_back(
        boths[0], boths[1], ghidden_other, middle, cotangent, vec, fulls[0], fulls[1], full_one
    )
    down_passed_2 = swap(top_sum(offs, down_keep_2, down_came_2), "row")
    gate_passed_2 = swap(top_sum(offs, gate_keep_2, gate_came_2), "near")

    ggate, gconv, gfilter = conv_back(values, gmixed, gates, vec, seg)
    filter_came = swap(gfilter, "core")
    early_send, early_keep = weight_grad(
        offs, OWNER_AT, [([mixed], [gbranch]), ([hidden_one], [ggate])], (2, 2), "grad_output_convgate"
    )
    early_came = swap(early_send, "core")
    attended = attend_back(queries, keys, values, gmixed, attention, recips, gconv, seg, 0, pairs)
    early_give, early_held = halves_sum(offs, [(early_keep, early_came)], [gfilter, filter_came])
    early_came = swap(early_give, "row")
    tick(offs, [feed_sum])
    feed_near = rest_sum(
        offs, [(down_keep_2, down_came_2, down_passed_2), (gate_keep_2, gate_came_own_2, gate_passed_2)]
    )
    feed_other = swap(later(feed_sum, feed_near), "near")
    feed_part = lax.psum_scatter(feed_near, "far", scatter_dimension=0, tiled=True)
    tick(offs)
    gqk, gv = attend_back(
        queries, keys, values, gmixed, attention, recips, gconv, seg, pairs, pairs, onto=attended
    )
    early_own, early_other = near_split(offs, early_held, early_came)
    early_passed = swap(early_other, "near")
    late_send, late_keep = weight_grad(
        offs, OWNER_AT, [([hidden_one], [gqk]), ([hidden_one], [gv])], (2, 2), "grad_query_key_value"
    )
    late_came = swap(late_send, "core")
    Order.scale = 0.05
    feed_sum_2 = lax.all_gather(later(feed_part, tick(offs, [feed_part])), "far", axis=0, tiled=True)
    own_rows, theirs = sort_rows(offs, feed_sum, feed_other, width)
    spreads = [own_rows, swap(theirs, "core")]
    late_give, late_held = halves_sum(offs, [(late_keep, late_came)])
    late_came = swap(late_give, "row")
    grad_tokens, _ = tokens_back(gqk, gv, ggate, tokens, gmiddle, vec, full_one)
    late_own, late_other = near_split(offs, late_held, late_came)
    late_passed = swap(late_other, "near")
    out_part = feed_out(acts[0], acts[1], downs[0], downs[1], 1, [], "feed_out_partner")
    tick(offs, [feed_sum_2])
    mixer_near = pairs_sum(offs, [(early_own, early_passed), (late_own, late_passed)])
    feed_other_2 = swap(later(feed_sum_2, mixer_near), "near")
    Order.scale = 20.0
    mixer_sum = lax.psum(mixer_near, "far")
    out_came = swap(later(out_part, mixer_near), "core")
    tick(offs)
    result = feed_out(acts[0], acts[1], downs[0], downs[1], 0, [middle, out_came], "feed_out")
    own_rows, theirs = sort_rows(offs, feed_sum_2, feed_other_2, width)
    spreads += [own_rows, swap(theirs, "core")]
    grad_down = settle_down(offs, [(feed_sum, feed_other), (feed_sum_2, feed_other_2)], width)
    grad_gate, grad_up, ggain_two = spread(offs, gain_two[:, None].astype(wide), w_gate, w_up, spreads)
    mixer_other = swap(mixer_sum, "near")
    *grads, grad_output, grad_filter, ggain_one = settle_mixer(
        offs, gain_one[:, None].astype(wide), mixer_sum, mixer_other, w_query, w_key, w_value, w_convgate
    )
    return (
        result,
        grad_tokens,
        ggain_one,
        *grads,
        grad_output,
        grad_filter,
        ggain_two,
        grad_gate,
        grad_up,
        grad_down,
    )


def solution(mesh):
    replicas, shards = mesh.shape["rep"], mesh.shape["shard"]
    devices = np.asarray(mesh.devices).reshape(replicas // 2, 2, shards // 2, 2)
    fine = Mesh(devices, ("far", "near", "row", "core"))
    token = P(("far", "near", "row", "core"), None)
    line = P(("row", "core"))
    weight = P(("row", "core"), None)
    taps = P(None, ("row", "core"))
    return jax.shard_map(
        per_device,
        mesh=fine,
        in_specs=(
            token, token, line, weight, weight, weight, weight, weight, taps, line, weight, weight, weight, token
        ),
        out_specs=(
            token, token, line, weight, weight, weight, weight, weight, taps, line, weight, weight, weight
        ),
        check_vma=False,
    )
```

```python
import functools

import jax
import jax.numpy as jnp
import numpy as np
from jax import lax
from jax.experimental import pallas as pl
from jax.experimental.pallas import tpu as pltpu
from jax.sharding import Mesh
from jax.sharding import PartitionSpec as P

HEADS = 16
FEAT = 16
KW = 3
EPS = 1e-06
TILE = 256
FEED_TILE = 512
SHARD_ROWS = 256
LANES = 128
TICK = 1e5
X_AT, MIXER_AT, FEED_AT, DOWN_AT, PACK_AT, COLS_AT, GRAD_AT, OWNER_AT, ACT_AT, QUARTER_AT = 0, 2, 12, 16, 20, 28, 36, 40, 44, 48

low = jnp.bfloat16
wide = jnp.float32


def dot(a, b):
    return jnp.dot(a, b, preferred_element_type=wide)


def dot_nt(a, b):
    return lax.dot_general(a, b, (((1,), (1,)), ((), ())), preferred_element_type=wide)


def dot_tn(a, b):
    return lax.dot_general(a, b, (((0,), (0,)), ((), ())), preferred_element_type=wide)


class Order:
    last = None
    scale = 1.0


def launch(kernel, deps=(), onto=(), *, scalars=0, grid, in_specs, out_specs, out_shape, scratch_shapes=(), **rest):
    taken = scalars + len(in_specs)
    deps = list(onto) + [d for d in deps if d is not None] + ([] if Order.last is None or any(Order.last is a for a in onto) else [Order.last])

    def body(*refs):
        kernel(*refs[:taken], *refs[taken + len(deps) :])

    spec = pltpu.PrefetchScalarGridSpec(
        num_scalar_prefetch=scalars,
        grid=grid,
        in_specs=list(in_specs) + [pl.BlockSpec(memory_space=pl.ANY)] * len(deps),
        out_specs=out_specs,
        scratch_shapes=list(scratch_shapes),
    )
    aliases = {taken + n: n for n in range(len(onto))}
    run = pl.pallas_call(body, grid_spec=spec, out_shape=out_shape, input_output_aliases=aliases, **rest)

    def call(*operands):
        result = run(*operands, *deps)
        Order.last = result[0] if isinstance(result, (list, tuple)) else result
        return result

    return call


def params(mib, least=60):
    return pltpu.CompilerParams(vmem_limit_bytes=max(mib, least) << 20)


def cost(gigaflops, mebibytes):
    return pl.CostEstimate(
        flops=int(gigaflops * Order.scale * 1e9), bytes_accessed=int(mebibytes * Order.scale * (1 << 20)), transcendentals=0
    )


def fixed(shape):
    return pl.BlockSpec(shape, lambda *_: (0,) * len(shape), pipeline_mode=pl.Buffered(1))


def rows(height, width):
    return pl.BlockSpec((height, width), lambda i, *_: (i, 0))


def place(offs_ref, base, pieces, full_ref):
    for n, piece in enumerate(pieces):
        at = pl.multiple_of(offs_ref[base + n], 64)
        full_ref[pl.ds(at, piece.shape[0]), :] = piece[...]


def project_kernel(offs_ref, x_ref, *refs):
    pieces, (hidden_ref, q_ref, k_ref, v_ref, gate_ref, vec_ref, out_ref, full_ref, sem) = refs[:10], refs[10:]
    copy = pltpu.make_async_copy(full_ref, out_ref, sem)
    heads = HEADS * FEAT
    width = x_ref.shape[1]

    @pl.when(pl.program_id(0) == 0)
    def _():
        place(offs_ref, MIXER_AT, pieces, full_ref)
        copy.start()
        small = full_ref[:, 2 * heads + 3 * width :].astype(wide)
        vec_ref[...] = small.T[:8, :]

    x = x_ref[...].astype(wide)
    inverse = lax.rsqrt(jnp.mean(x * x, axis=-1, keepdims=True) + EPS)
    hidden = (x * inverse * vec_ref[0:1, :]).astype(low)
    hidden_ref[...] = hidden
    at = width
    q_ref[...] = (dot(hidden, full_ref[:, at : at + heads]) * FEAT ** (-0.5)).astype(low)
    k_ref[...] = dot(hidden, full_ref[:, at + heads : at + 2 * heads]).astype(low)
    at = at + 2 * heads
    v_ref[...] = dot(hidden, full_ref[:, at : at + width]).astype(low)
    gate_ref[...] = dot(hidden, full_ref[:, at + width : at + 2 * width]).astype(low)

    @pl.when(pl.program_id(0) == pl.num_programs(0) - 1)
    def _():
        copy.wait()


def project(offs, x, pieces, deps=()):
    length, width = x.shape
    heads = HEADS * FEAT
    columns = pieces[0].shape[1]
    shapes = [
        jax.ShapeDtypeStruct((length, width), low),
        jax.ShapeDtypeStruct((length, heads), low),
        jax.ShapeDtypeStruct((length, heads), low),
        jax.ShapeDtypeStruct((length, width), low),
        jax.ShapeDtypeStruct((length, width), low),
        jax.ShapeDtypeStruct((8, width), wide),
        jax.ShapeDtypeStruct((width, columns), low),
    ]
    return launch(
        project_kernel,
        deps,
        scalars=1,
        grid=(length // TILE,),
        in_specs=[rows(TILE, width)] + [fixed(p.shape) for p in pieces],
        out_specs=[
            rows(TILE, width),
            rows(TILE, heads),
            rows(TILE, heads),
            rows(TILE, width),
            rows(TILE, width),
            fixed((8, width)),
            pl.BlockSpec(memory_space=pl.ANY),
        ],
        scratch_shapes=[pltpu.VMEM((width, columns), low), pltpu.SemaphoreType.DMA],
        out_shape=shapes,
        compiler_params=params(40),
        cost_estimate=cost(7, 22),
        name="project",
    )(offs, x, *pieces)


def shift_rows(v, seg, by, up):
    zeros = jnp.zeros((by, v.shape[1]), v.dtype)
    none = jnp.full((by, 1), -1, seg.dtype)
    if up:
        moved, moved_seg = jnp.concatenate([v[by:], zeros], 0), jnp.concatenate([seg[by:], none], 0)
    else:
        moved = jnp.concatenate([zeros, v[:-by]], 0)
        moved_seg = jnp.concatenate([none, seg[:-by]], 0)
    return jnp.where(moved_seg == seg, moved, 0.0)


def lane_pick(width, start, stop):
    i = lax.broadcasted_iota(jnp.int32, (1, width), 1)
    return (i >= start) & (i < stop)


def attend_kernel(
    first, q_ref, k_ref, v_ref, gate_ref, vec_ref, segr_ref, segc_ref, mixed_ref, att_ref, recip_ref, mask_ref
):
    length = q_ref.shape[0]
    pair = pl.program_id(0) + first
    zero = jnp.zeros((), low)

    @pl.when(pair == first)
    def _():
        for tb in range(0, length, TILE):
            t = lax.broadcasted_iota(jnp.int32, (TILE, length), 0) + tb
            s = lax.broadcasted_iota(jnp.int32, (TILE, length), 1)
            seen = (s <= t) & (segc_ref[tb : tb + TILE, :] == segr_ref[...])
            mask_ref[tb : tb + TILE, :] = jnp.where(seen, 1.0, 0.0).astype(low)

    v = v_ref[...]
    keys, sides = [], []
    for i in range(2):
        head = 2 * pair + i
        keys.append(jnp.where(lane_pick(HEADS * FEAT, head * FEAT, (head + 1) * FEAT), k_ref[...], zero))
        lanes = lane_pick(128, 64 * i, 64 * i + 64)
        ones = jnp.broadcast_to(jnp.where(lanes, 1.0, 0.0).astype(low), (length, 128))
        sides.append(jnp.concatenate([jnp.where(lanes, v, zero), ones], 1))
    for tb in range(0, length, TILE):
        n = tb + TILE
        total = None
        for i in range(2):
            one_plus = dot_nt(q_ref[tb:n, :], keys[i][:n]) + 1.0
            kernel = (one_plus * one_plus + 1.0).astype(low) * mask_ref[tb:n, :n]
            part = dot(kernel, sides[i][:n])
            total = part if total is None else total + part
        recip = 1.0 / total[:, 128:]
        att_ref[tb:n, :] = (total[:, :128] * recip).astype(low)
        recip_ref[tb:n, :] = (2.0 * recip).astype(low)
    v_wide = v.astype(wide)
    seg = segc_ref[...]
    conv = vec_ref[2:3, :] * v_wide
    for j in range(1, KW):
        conv = conv + vec_ref[2 + j : 3 + j, :] * shift_rows(v_wide, seg, j, False)
    mixed_ref[...] = (att_ref[...].astype(wide) + gate_ref[...].astype(wide) * conv).astype(low)


def whole(a):
    return pl.BlockSpec(a.shape, lambda p: (0, 0))


def attend(q, k, v, gate, vec, seg, first, count, onto=(), deps=()):
    length, width = v.shape
    column = pl.BlockSpec((length, 128), lambda p: (0, p + first))
    seg_row, seg_col = seg.reshape(1, length), seg.reshape(length, 1)
    return launch(
        functools.partial(attend_kernel, first),
        deps,
        onto,
        grid=(count,),
        in_specs=[
            whole(q), whole(k), column, column, pl.BlockSpec((8, 128), lambda p: (0, p + first)), whole(seg_row), whole(seg_col)
        ],
        out_specs=[column] * 3,
        out_shape=[jax.ShapeDtypeStruct((length, width), low)] * 3,
        scratch_shapes=[pltpu.VMEM((length, length), low)],
        compiler_params=params(40),
        cost_estimate=cost(18 * count * 128 / width, 14),
        name="attention_forward",
    )(q, k, v, gate, vec, seg_row, seg_col)


def attend_back_kernel(
    first, q_ref, k_ref, v_ref, gm_ref, att_ref, recip_ref, gconv_ref, segr_ref, segc_ref,
    gqk_ref, gv_ref, mask_ref, gq_acc, gk_acc,
):
    length, heads = q_ref.shape
    pair = pl.program_id(0) + first
    zero = jnp.zeros((), low)

    @pl.when(pair == first)
    def _():
        for sb in range(0, length, TILE):
            s = lax.broadcasted_iota(jnp.int32, (TILE, length), 0) + sb
            t = lax.broadcasted_iota(jnp.int32, (TILE, length), 1)
            seen = (s <= t) & (segc_ref[sb : sb + TILE, :] == segr_ref[...])
            mask_ref[sb : sb + TILE, :] = jnp.where(seen, 1.0, 0.0).astype(low)
        gk_acc[...] = jnp.zeros_like(gk_acc)
        gq_acc[...] = jnp.zeros_like(gq_acc)

    v = v_ref[...]
    gm = gm_ref[...].astype(wide)
    gnum_wide = gm * recip_ref[...].astype(wide)
    gnum = gnum_wide.astype(low)
    product = gnum_wide * att_ref[...].astype(wide)
    high = product.astype(low)
    rest = (product - high.astype(wide)).astype(low)
    r = lax.broadcasted_iota(jnp.int32, (256, 128), 0)
    c = lax.broadcasted_iota(jnp.int32, (256, 128), 1)
    same_head = jnp.where(((r % 128) // 64) == (c // 64), 1.0, 0.0).astype(low)
    gtot = -dot(jnp.concatenate([high, rest], 1), same_head)
    gtot_high = gtot.astype(low)
    gtot_rest = (gtot - gtot_high.astype(wide)).astype(low)
    lane = lax.broadcasted_iota(jnp.int32, (1, 128), 1)
    left = jnp.concatenate([gnum, jnp.where(lane % 64 == 0, gtot_high, gtot_rest)], 1)
    gnum_half = gnum * jnp.asarray(0.5, low)
    queries, sides, gnums, keys = [], [], [], []
    for i in range(2):
        head = 2 * pair + i
        mine = lane_pick(heads, head * FEAT, (head + 1) * FEAT)
        queries.append(jnp.where(mine, q_ref[...], zero))
        keys.append(jnp.where(mine, k_ref[...], zero))
        lanes = lane_pick(128, 64 * i, 64 * i + 64)
        ones = jnp.where(lane_pick(128, 64 * i, 64 * i + 2), 1.0, 0.0).astype(low)
        sides.append(jnp.concatenate([jnp.where(lanes, v, zero), jnp.broadcast_to(ones, (length, 128))], 1))
        gnums.append(jnp.where(lanes, gnum_half, zero))
    for sb in range(0, length, TILE):
        n = sb + TILE
        gv = gconv_ref[sb:n, :].astype(wide)
        gk = None
        for i in range(2):
            one_plus = dot_nt(k_ref[sb:n, :], queries[i][sb:]) + 1.0
            mask = mask_ref[sb:n, sb:]
            kernel = (one_plus * one_plus + 1.0).astype(low) * mask
            gv = gv + dot(kernel, gnums[i][sb:])
            gkernel = dot_nt(sides[i][sb:n], left[sb:])
            gscores = (gkernel * one_plus).astype(low) * mask
            part = dot(gscores, queries[i][sb:])
            gk = part if gk is None else gk + part
            gq_acc[sb:, :] += dot_tn(gscores, keys[i][sb:n])
        gv_ref[sb:n, :] = gv.astype(low)
        gk_acc[sb:n, :] += gk

    @pl.when(pl.program_id(0) == pl.num_programs(0) - 1)
    def _():
        mine = slice(2 * FEAT * first, 2 * FEAT * first + gqk_ref.shape[1] // 2)
        gqk_ref[:, : gqk_ref.shape[1] // 2] = (gq_acc[:, mine] * FEAT ** (-0.5)).astype(low)
        gqk_ref[:, gqk_ref.shape[1] // 2 :] = gk_acc[:, mine].astype(low)


def attend_back(q, k, v, gm, att, recip, gconv, seg, first, count, onto=(), deps=()):
    length, width = v.shape
    heads = q.shape[1]
    column = pl.BlockSpec((length, 128), lambda p: (0, p + first))
    seg_row, seg_col = seg.reshape(1, length), seg.reshape(length, 1)
    return launch(
        functools.partial(attend_back_kernel, first),
        deps,
        onto,
        grid=(count,),
        in_specs=[whole(q), whole(k)] + [column] * 5 + [whole(seg_row), whole(seg_col)],
        out_specs=[pl.BlockSpec((length, 4 * FEAT * count), lambda p: (0, first // count)), column],
        out_shape=[jax.ShapeDtypeStruct((length, 2 * heads), low), jax.ShapeDtypeStruct((length, width), low)],
        scratch_shapes=[
            pltpu.VMEM((length, length), low),
            pltpu.VMEM((length, heads), wide),
            pltpu.VMEM((length, heads), wide),
        ],
        compiler_params=params(48),
        cost_estimate=cost(40 * count * 128 / width, 18),
        name="attention_backward",
    )(q, k, v, gm, att, recip, gconv, seg_row, seg_col)


def conv_back_kernel(v_ref, gm_ref, gate_ref, vec_ref, segc_ref, ggate_ref, gconv_ref, gfilt_ref):
    v_wide = v_ref[...].astype(wide)
    gm = gm_ref[...].astype(wide)
    seg = segc_ref[...]
    taps = [vec_ref[2 + j : 3 + j, :] for j in range(KW)]
    grad = gm * gate_ref[...].astype(wide)
    conv = taps[0] * v_wide
    gv_conv = taps[0] * grad
    lines = [jnp.sum(grad * v_wide, 0, keepdims=True)]
    for j in range(1, KW):
        moved = shift_rows(v_wide, seg, j, False)
        conv = conv + taps[j] * moved
        lines.append(jnp.sum(grad * moved, 0, keepdims=True))
        gv_conv = gv_conv + taps[j] * shift_rows(grad, seg, j, True)
    lines.append(jnp.zeros((LANES - KW, 128), wide))
    gfilt_ref[...] = jnp.concatenate(lines, 0).T.astype(low)
    ggate_ref[...] = (gm * conv).astype(low)
    gconv_ref[...] = gv_conv.astype(low)


def conv_back(v, gm, gate, vec, seg, deps=()):
    length, width = v.shape
    column = pl.BlockSpec((length, 128), lambda p: (0, p))
    small = pl.BlockSpec((8, 128), lambda p: (0, p))
    seg_col = seg.reshape(length, 1)
    return launch(
        conv_back_kernel,
        deps,
        grid=(width // 128,),
        in_specs=[column, column, column, small, whole(seg_col)],
        out_specs=[column, column, pl.BlockSpec((128, LANES), lambda p: (p, 0))],
        out_shape=[jax.ShapeDtypeStruct((length, width), low)] * 2 + [jax.ShapeDtypeStruct((width, LANES), low)],
        compiler_params=params(48),
        cost_estimate=cost(1, 10),
        name="convolution_backward",
    )(v, gm, gate, vec, seg_col)


def mix_kernel(x_ref, mixed_ref, vec_ref, weight_ref, middle_ref, hidden_ref):
    middle = x_ref[...].astype(wide) + dot(mixed_ref[...], weight_ref[...])
    inverse = lax.rsqrt(jnp.mean(middle * middle, axis=-1, keepdims=True) + EPS)
    middle_ref[...] = middle
    hidden_ref[...] = (middle * inverse * vec_ref[1:2, :]).astype(low)


def mix(x, mixed, vec, full, deps=()):
    length, width = x.shape
    return launch(
        mix_kernel,
        deps,
        grid=(length // TILE,),
        in_specs=[rows(TILE, width), rows(TILE, width), fixed(vec.shape), fixed((width, width))],
        out_specs=[rows(TILE, width), rows(TILE, width)],
        out_shape=[jax.ShapeDtypeStruct((length, width), wide), jax.ShapeDtypeStruct((length, width), low)],
        compiler_params=params(32),
        cost_estimate=cost(3, 16),
        name="mix",
    )(x, mixed, vec, full)


def first_half(n):
    return lambda i, *_: (jnp.minimum(i, n - 1), 0)


def second_half(n):
    return lambda i, *_: (jnp.maximum(i - n, 0), 0)


def feed_kernel(n, offs_ref, ha_ref, hb_ref, ca_ref, cb_ref, *refs):
    pieces, downs = refs[:4], refs[4:6]
    act_ref, both_ref, full_out_ref, down_out_ref, full_ref, down_ref, sems = refs[6:]
    copies = [
        pltpu.make_async_copy(full_ref, full_out_ref, sems.at[0]),
        pltpu.make_async_copy(down_ref, down_out_ref, sems.at[1]),
    ]
    step = pl.program_id(0)
    half = full_ref.shape[1] // 2

    @pl.when(step == 0)
    def _():
        place(offs_ref, FEED_AT, pieces, full_ref)
        place(offs_ref, DOWN_AT, downs, down_ref)
        for copy in copies:
            copy.start()

    def work(hidden, cotangent):
        for at in range(0, half, 256):
            gate = dot(hidden, full_ref[:, at : at + 256])
            up = dot(hidden, full_ref[:, half + at : half + at + 256])
            gact = dot_nt(cotangent, down_ref[at : at + 256, :])
            sig = jax.nn.sigmoid(gate)
            silu = gate * sig
            act_ref[:, at : at + 256] = (silu * up).astype(low)
            both_ref[:, at : at + 256] = (gact * up * (sig + silu * (1.0 - sig))).astype(low)
            both_ref[:, half + at : half + at + 256] = (gact * silu).astype(low)

    @pl.when(step < n)
    def _():
        work(ha_ref[...], ca_ref[...])

    @pl.when(step >= n)
    def _():
        work(hb_ref[...], cb_ref[...])

    @pl.when(step == 2 * n - 1)
    def _():
        for copy in copies:
            copy.wait()


def feed(offs, hidden, cotangent, j, w_down, pieces, down_pieces, deps=()):
    length, width = hidden[0].shape
    n = length // FEED_TILE
    half = w_down.shape[0]
    first = pl.BlockSpec((FEED_TILE, width), first_half(n))
    second = pl.BlockSpec((FEED_TILE, width), second_half(n))
    own_down = pl.BlockSpec((half // 2, width), lambda *_: (j, 0), pipeline_mode=pl.Buffered(1))
    given_rows = pl.BlockSpec(pieces[0].shape, lambda *_: (j, 0), pipeline_mode=pl.Buffered(1))
    return launch(
        functools.partial(feed_kernel, n),
        deps,
        scalars=1,
        grid=(2 * n,),
        in_specs=[first, second, first, second]
        + [fixed(pieces[0].shape), given_rows]
        + [fixed(p.shape) for p in pieces[2:]]
        + [own_down]
        + [fixed(p.shape) for p in down_pieces],
        out_specs=[rows(FEED_TILE, half), rows(FEED_TILE, 2 * half)] + [pl.BlockSpec(memory_space=pl.ANY)] * 2,
        scratch_shapes=[
            pltpu.VMEM((width, 2 * half), low),
            pltpu.VMEM((half, width), low),
            pltpu.SemaphoreType.DMA((2,)),
        ],
        out_shape=[
            jax.ShapeDtypeStruct((2 * length, half), low),
            jax.ShapeDtypeStruct((2 * length, 2 * half), low),
            jax.ShapeDtypeStruct((width, 2 * half), low),
            jax.ShapeDtypeStruct((half, width), low),
        ],
        compiler_params=params(48),
        cost_estimate=cost(16, 34),
        name="feed_in",
    )(offs, *hidden, *cotangent, *pieces, w_down, *down_pieces)


def weight_grad_kernel(shape_of, counts, outs, length, offs_ref, *refs):
    targets = [(ref, row * TILE) for ref, height in zip(refs[-len(outs) :], outs) for row in range(height)]
    step = pl.program_id(0)

    def work(lefts, rights):
        terms = max(len(lefts[0]), len(rights))

        def part_of(group, t):
            return group[t][...] if len(group) == terms else group[0][t * length : (t + 1) * length, :]

        for b, (ref, row) in enumerate(targets):
            value = None
            for t in range(terms):
                product = dot_tn(part_of(lefts[b], t), part_of(rights, t))
                value = product if value is None else value + product
            ref[row : row + TILE, :] = value.astype(low)

    start = 0
    for (left_at, right_at), count in zip(shape_of, counts):
        lefts = [[refs[n] for n in block] for block in left_at]
        rights = [refs[n] for n in right_at]
        if len(counts) == 1:
            work(lefts, rights)
        else:
            pl.when((step >= start) & (step < start + count))(functools.partial(work, lefts, rights))
        start += count


def weight_grad(offs, base, groups, outs, name, tile=512, deps=()):
    blocks = sum(outs)
    counts = [rights[0].shape[1] // tile for _, rights in groups]
    columns = sum(counts) * tile
    in_specs, operands, shape_of, known = [], [], [], {}
    start = 0
    for (lefts, rights), count in zip(groups, counts):
        key = tuple(id(a) for a in lefts)
        if key not in known:
            known[key] = []
            for b in range(blocks):
                known[key].append([len(operands) + n for n in range(len(lefts))])
                for a in lefts:
                    in_specs.append(pl.BlockSpec((a.shape[0], TILE), lambda j, offs, b=b: (0, offs[base + b])))
                    operands.append(a)
        shape_of.append((known[key], [len(operands) + n for n in range(len(rights))]))
        for a in rights:

            def where_to(j, offs, start=start, count=count):
                return (0, jnp.clip(j - start, 0, count - 1))

            in_specs.append(pl.BlockSpec((a.shape[0], tile), where_to))
            operands.append(a)
        start += count
    tokens = sum(a.shape[0] for a in groups[0][0])
    terms = max(len(groups[0][0]), len(groups[0][1]))
    return launch(
        functools.partial(weight_grad_kernel, shape_of, counts, outs, tokens // terms),
        deps,
        scalars=1,
        grid=(sum(counts),),
        in_specs=in_specs,
        out_specs=[pl.BlockSpec((height * TILE, tile), lambda j, offs: (0, j)) for height in outs],
        out_shape=[jax.ShapeDtypeStruct((height * TILE, columns), low) for height in outs],
        compiler_params=params(48, 48),
        cost_estimate=cost(2.5e-9 * tokens * 1024 * columns, (tokens * (1024 + columns) * 2 + 2048 * columns) / 2**20),
        name=name,
    )(offs, *operands)


def feed_back_kernel(a_ref, b_ref, wa_ref, wb_ref, out_ref):
    out_ref[...] = (dot_nt(a_ref[...], wa_ref[...]) + dot_nt(b_ref[...], wb_ref[...])).astype(low)


def feed_back(first, second, full_first, full_second, deps=()):
    length = first.shape[0] // 2
    width = full_first.shape[0]
    n = length // TILE
    tile = pl.BlockSpec((TILE, first.shape[1]), lambda i: (i + n, 0))
    return launch(
        feed_back_kernel,
        deps,
        grid=(n,),
        in_specs=[tile, tile, fixed(full_first.shape), fixed(full_second.shape)],
        out_specs=rows(TILE, width),
        out_shape=jax.ShapeDtypeStruct((length, width), low),
        compiler_params=params(32),
        cost_estimate=cost(10, 18),
        name="feed_back_partner",
    )(first, second, full_first, full_second)


def middle_back_kernel(
    a_ref, b_ref, other_ref, middle_ref, cot_ref, vec_ref, wa_ref, wb_ref, wo_ref,
    gmiddle_ref, gbranch_ref, gmixed_ref, ggain_ref,
):
    ghidden = dot_nt(a_ref[...], wa_ref[...]) + dot_nt(b_ref[...], wb_ref[...]) + other_ref[...].astype(wide)
    middle = middle_ref[...]
    inverse = lax.rsqrt(jnp.mean(middle * middle, axis=-1, keepdims=True) + EPS)
    normed = middle * inverse
    gain = jnp.sum(ghidden * normed, axis=0, keepdims=True)

    @pl.when(pl.program_id(0) == 0)
    def _():
        ggain_ref[...] = jnp.zeros_like(ggain_ref)

    ggain_ref[0:1, :] += gain
    scaled = ghidden * vec_ref[1:2, :]
    gmiddle = cot_ref[...].astype(wide) + inverse * (
        scaled - normed * jnp.mean(scaled * normed, axis=-1, keepdims=True)
    )
    gmiddle_ref[...] = gmiddle
    gbranch = gmiddle.astype(low)
    gbranch_ref[...] = gbranch
    gmixed_ref[...] = dot_nt(gbranch, wo_ref[...]).astype(low)


def middle_back(first, second, other, middle, cotangent, vec, full_first, full_second, w_output, deps=()):
    length, width = middle.shape
    tile = rows(TILE, first.shape[1])
    line = rows(TILE, width)
    return launch(
        middle_back_kernel,
        deps,
        grid=(length // TILE,),
        in_specs=[
            tile, tile, line, line, line, fixed(vec.shape), fixed(full_first.shape), fixed(full_second.shape), fixed((width, width))
        ],
        out_specs=[line, line, line, fixed((8, width))],
        out_shape=[
            jax.ShapeDtypeStruct((length, width), wide),
            jax.ShapeDtypeStruct((length, width), low),
            jax.ShapeDtypeStruct((length, width), low),
            jax.ShapeDtypeStruct((8, width), wide),
        ],
        compiler_params=params(48),
        cost_estimate=cost(13, 40),
        name="middle_back",
    )(first, second, other, middle, cotangent, vec, full_first, full_second, w_output)


def feed_out_kernel(add, *refs):
    out_ref = refs[-1]
    value = dot(refs[0][...], refs[2][...]) + dot(refs[1][...], refs[3][...])
    for ref in refs[4:-1]:
        value = value + ref[...].astype(wide)
    out_ref[...] = value.astype(low)


def feed_out(first, second, down_first, down_second, shift, extras, name, deps=()):
    length = first.shape[0] // 2
    width = down_first.shape[1]
    n = length // TILE
    tile = pl.BlockSpec((TILE, first.shape[1]), lambda i: (i + shift * n, 0))
    return launch(
        functools.partial(feed_out_kernel, len(extras)),
        deps,
        grid=(n,),
        in_specs=[tile, tile, fixed(down_first.shape), fixed(down_second.shape)] + [rows(TILE, width)] * len(extras),
        out_specs=rows(TILE, width),
        out_shape=jax.ShapeDtypeStruct((length, width), low),
        compiler_params=params(32),
        cost_estimate=cost(5, 16),
        name=name,
    )(first, second, down_first, down_second, *extras)


def tokens_back_kernel(gqk_ref, gv_ref, ggate_ref, x_ref, gmiddle_ref, vec_ref, full_ref, gtokens_ref, ggain_ref):
    two = gqk_ref.shape[1]
    width = x_ref.shape[1]
    quarter = two // 4
    ghidden = None
    for n, col in enumerate((0, 2, 1, 3)):
        at = width + col * quarter
        term = dot_nt(gqk_ref[:, n * quarter : (n + 1) * quarter], full_ref[:, at : at + quarter])
        ghidden = term if ghidden is None else ghidden + term
    ghidden = (
        ghidden
        + dot_nt(gv_ref[...], full_ref[:, width + two : 2 * width + two])
        + dot_nt(ggate_ref[...], full_ref[:, two + 2 * width : two + 3 * width])
    )
    x = x_ref[...].astype(wide)
    inverse = lax.rsqrt(jnp.mean(x * x, axis=-1, keepdims=True) + EPS)
    normed = x * inverse

    @pl.when(pl.program_id(0) == 0)
    def _():
        ggain_ref[...] = jnp.zeros_like(ggain_ref)

    ggain_ref[0:1, :] += jnp.sum(ghidden * normed, axis=0, keepdims=True)
    scaled = ghidden * vec_ref[0:1, :]
    gtokens_ref[...] = gmiddle_ref[...] + inverse * (
        scaled - normed * jnp.mean(scaled * normed, axis=-1, keepdims=True)
    )


def tokens_back(gqk, gv, ggate, x, gmiddle, vec, full, deps=()):
    length, width = x.shape
    line = rows(TILE, width)
    return launch(
        tokens_back_kernel,
        deps,
        grid=(length // TILE,),
        in_specs=[rows(TILE, gqk.shape[1]), line, line, line, line, fixed(vec.shape), fixed(full.shape)],
        out_specs=[line, fixed((8, width))],
        out_shape=[jax.ShapeDtypeStruct((length, width), wide), jax.ShapeDtypeStruct((8, width), wide)],
        compiler_params=params(40),
        cost_estimate=cost(7, 24),
        name="tokens_back",
    )(gqk, gv, ggate, x, gmiddle, vec, full)


def as_line(column):
    return jnp.broadcast_to(column, (column.shape[0], LANES)).T[0]


def spread_kernel(cols_ref, gain_ref, wg_ref, wu_ref, a_ref, b_ref, c_ref, d_ref, gate_ref, up_ref, ggain_ref):
    total = None
    for n, ref in enumerate((a_ref, b_ref, c_ref, d_ref)):
        quarter = ref.shape[1] // 4
        for part_y in range(2):
            at = pl.ds(pl.multiple_of(cols_ref[COLS_AT + 2 * n + part_y], 512), quarter)
            gate = ref[:, part_y * quarter : (part_y + 1) * quarter].astype(wide)
            up = ref[:, (2 + part_y) * quarter : (3 + part_y) * quarter].astype(wide)
            gate_ref[:, at] = gate
            up_ref[:, at] = up
            term = gate * wg_ref[:, at].astype(wide) + up * wu_ref[:, at].astype(wide)
            line = jnp.sum(term, axis=1, keepdims=True)
            total = line if total is None else total + line
    ggain_ref[...] = as_line(total / gain_ref[...])


def spread(cols, gain, w_gate, w_up, blocks, deps=()):
    height, width = blocks[0].shape
    shape = jax.ShapeDtypeStruct((height, 2 * width), wide)
    return launch(
        spread_kernel,
        deps,
        scalars=1,
        grid=(1,),
        in_specs=[fixed(gain.shape), fixed(w_gate.shape), fixed(w_up.shape)] + [fixed(b.shape) for b in blocks],
        out_specs=[fixed(shape.shape)] * 2 + [fixed(gain.shape[:1])],
        out_shape=[shape, shape, jax.ShapeDtypeStruct(gain.shape[:1], wide)],
        compiler_params=params(24),
        cost_estimate=cost(0.001, 16),
        name="spread",
    )(cols, gain, w_gate, w_up, *blocks)


def pack_kernel(at_ref, g1_ref, g2_ref, taps_ref, q_ref, k_ref, v_ref, c_ref, o_ref, pack_ref, part_ref):
    height = q_ref.shape[0]
    col = 0
    for ref in (o_ref, q_ref, k_ref, v_ref, c_ref):
        pack_ref[:, col : col + ref.shape[1]] = ref[...]
        col += ref.shape[1]
    small = jnp.concatenate([g1_ref[...].astype(wide)[None], g2_ref[...].astype(wide)[None], taps_ref[...].astype(wide)], 0)
    small = jnp.concatenate([small, jnp.zeros((LANES - small.shape[0], height), wide)], 0)
    pack_ref[:, col : col + LANES] = small.T.astype(low)
    size = part_ref.shape[0]
    part_ref[...] = pack_ref[pl.ds(pl.multiple_of(at_ref[QUARTER_AT] * size, 64), size), :]


def pack_mixer(at, gain_one, gain_two, taps, w_query, w_key, w_value, w_convgate, w_output):
    operands = (gain_one, gain_two, taps, w_query, w_key, w_value, w_convgate, w_output)
    height = w_query.shape[0]
    columns = sum(a.shape[1] for a in operands[3:]) + LANES
    shapes = [(height, columns), (height // 4, columns)]
    return launch(
        pack_kernel,
        scalars=1,
        grid=(1,),
        in_specs=[fixed(a.shape) for a in operands],
        out_specs=[fixed(a) for a in shapes],
        out_shape=[jax.ShapeDtypeStruct(a, low) for a in shapes],
        compiler_params=params(24),
        cost_estimate=cost(0.001, 4),
        name="pack_mixer",
    )(at, *operands)


def pack_feed_kernel(offs_ref, gate_ref, up_ref, down_ref, first_ref, second_ref, give_ref, *refs):
    send_refs, (low_ref, high_ref) = refs[:2], refs[2:]
    height = gate_ref.shape[0]
    sent = PACK_AT + 4 * offs_ref[X_AT]
    targets = (
        (first_ref, 0, PACK_AT),
        (second_ref, 0, PACK_AT + 2),
        (give_ref, 0, PACK_AT + 4),
        (give_ref, height, PACK_AT + 6),
        (send_refs[0], 0, sent),
        (send_refs[1], 0, sent + 2),
    )
    for ref, row, place_at in targets:
        quarter = ref.shape[1] // 4
        for part_y in range(2):
            at = pl.ds(pl.multiple_of(offs_ref[place_at + part_y], 512), quarter)
            ref[row : row + height, part_y * quarter : (part_y + 1) * quarter] = gate_ref[:, at]
            ref[row : row + height, (2 + part_y) * quarter : (3 + part_y) * quarter] = up_ref[:, at]
    size = low_ref.shape[0]
    low_ref[...] = down_ref[:size, :]
    high_ref[...] = down_ref[size:, :]


def pack_feed(offs, w_gate, w_up, w_down, deps=()):
    height, columns = w_gate.shape
    half = (height, columns // 2)
    shapes = [half, half, (2 * height, columns // 2), half, half] + [(w_down.shape[0] // 2, w_down.shape[1])] * 2
    return launch(
        pack_feed_kernel,
        deps,
        scalars=1,
        grid=(1,),
        in_specs=[fixed(w_gate.shape), fixed(w_up.shape), fixed(w_down.shape)],
        out_specs=[fixed(a) for a in shapes],
        out_shape=[jax.ShapeDtypeStruct(a, low) for a in shapes],
        compiler_params=params(24),
        cost_estimate=cost(0.001, 8),
        name="pack_feed",
    )(offs, w_gate, w_up, w_down)


STRIPS = 1


def operand_parts(operand):
    if not isinstance(operand, tuple):
        return operand, None, 1
    return operand if len(operand) == 3 else (*operand, 2)


def step(kernel, offs, operands, shapes, name, deps=(), giga=0.001):
    in_specs, arrays = [], []
    for operand in operands:
        array, half, parts = operand_parts(operand)
        height = array.shape[0] // parts

        def where_to(i, offs, half=half):
            if half is None:
                return (i, 0)
            return ((half(offs) if callable(half) else half) * STRIPS + i, 0)

        in_specs.append(pl.BlockSpec((height // STRIPS, array.shape[1]), where_to))
        arrays.append(array)
    return launch(
        kernel,
        deps,
        scalars=1,
        grid=(STRIPS,),
        in_specs=in_specs,
        out_specs=[rows(shape[0] // STRIPS, shape[1]) for shape in shapes],
        out_shape=[jax.ShapeDtypeStruct(shape, low) for shape in shapes],
        compiler_params=params(24),
        cost_estimate=cost(giga, 8),
        name=name,
    )(offs, *arrays)


def add(*refs):
    total = refs[0].astype(wide)
    for other in refs[1:]:
        total = total + other.astype(wide)
    return total.astype(low)


def sum_kernel(terms, offs_ref, *refs):
    for out_ref, groups in zip(refs[-len(terms) :], terms):
        col = 0
        for group in groups:
            width = refs[group[0]].shape[1]
            out_ref[:, col : col + width] = add(*(refs[n][...] for n in group))
            col += width


def strip_sum(offs, outputs, name, deps=()):
    operands, terms, shapes = [], [], []
    for groups in outputs:
        terms.append([])
        width = 0
        for group in groups:
            terms[-1].append(list(range(len(operands), len(operands) + len(group))))
            operands += group
            first, _, parts = operand_parts(group[0])
            height = first.shape[0] // parts
            width += first.shape[1]
        shapes.append((height, width))
    return step(functools.partial(sum_kernel, terms), offs, operands, shapes, name, deps)


def top_sum(offs, keep, came, deps=()):
    came = came if came.shape[0] * 2 == keep.shape[0] else (came, 0)
    return strip_sum(offs, [[[(keep, 0), came]]], "top_sum", deps)[0]


def rest_sum(offs, triples, deps=()):
    groups = []
    for keep, came, passed in triples:
        came = came if came.shape[0] * 2 == keep.shape[0] else (came, 1)
        groups.append([(keep, 1), came, passed])
    return strip_sum(offs, [groups], "rest_sum", deps)[0]


def halves_sum(offs, pairs, filters=None, deps=()):
    outputs = []
    for half in range(2):
        groups = [[(keep, half), (came, half)] for keep, came in pairs]
        if filters is not None:

            def quarter(offs_ref, half=half):
                return offs_ref[OWNER_AT + 2 + half]

            groups.append([(a, quarter, 4) for a in filters])
        outputs.append(groups)
    return strip_sum(offs, outputs, "halves_sum", deps)


def near_split(offs, keep, came, deps=()):
    def own(offs_ref):
        return offs_ref[X_AT]

    def other(offs_ref):
        return 1 - offs_ref[X_AT]

    return strip_sum(offs, [[[(keep, own), (came, own)]], [[(keep, other), (came, other)]]], "near_split", deps)


def pairs_sum(offs, pairs, deps=()):
    return strip_sum(offs, [[list(pair) for pair in pairs]], "pairs_sum", deps)[0]


def sort_kernel(offs_ref, total_ref, other_ref, own_ref, give_ref):
    skip = total_ref.shape[1] - own_ref.shape[1]

    @pl.when(offs_ref[X_AT + 1] == 0)
    def _():
        own_ref[...] = total_ref[:, skip:]
        give_ref[...] = other_ref[:, skip:]

    @pl.when(offs_ref[X_AT + 1] != 0)
    def _():
        own_ref[...] = other_ref[:, skip:]
        give_ref[...] = total_ref[:, skip:]


def sort_rows(offs, total, other, skip, deps=()):
    shape = (total.shape[0], total.shape[1] - skip)
    return step(sort_kernel, offs, [total, other], [shape, shape], "sort_rows", deps)


def settle_down_kernel(offs_ref, *refs):
    out_ref = refs[-1]
    size = out_ref.shape[0] // 4
    width = out_ref.shape[1]
    for n in range(4):
        side = offs_ref[X_AT] if n % 2 == 0 else 1 - offs_ref[X_AT]
        at = pl.ds(pl.multiple_of((n // 2) * 2 * size + side * size, 128), size)
        out_ref[at, :] = refs[n][:, :width].astype(wide)


def settle_down(offs, pairs, width, deps=()):
    operands = [a for pair in pairs for a in pair]
    size = operands[0].shape[0]
    column = pl.BlockSpec((size, width), lambda *_: (0, 0), pipeline_mode=pl.Buffered(1))
    return launch(
        settle_down_kernel,
        deps,
        scalars=1,
        grid=(1,),
        in_specs=[column] * 4,
        out_specs=fixed((4 * size, width)),
        out_shape=jax.ShapeDtypeStruct((4 * size, width), wide),
        compiler_params=params(24),
        cost_estimate=cost(0.001, 6),
        name="settle_down",
    )(offs, *operands)


def settle_mixer_kernel(
    offs_ref, gain_ref, mine_ref, other_ref, wq_ref, wk_ref, wv_ref, wc_ref,
    gq_ref, gk_ref, gv_ref, gc_ref, go_ref, gf_ref, ggain_ref, all_ref,
):
    size = mine_ref.shape[0]
    for ref, side in ((mine_ref, offs_ref[X_AT]), (other_ref, 1 - offs_ref[X_AT])):
        all_ref[pl.ds(pl.multiple_of(side * size, 128), size), :] = ref[...].astype(wide)
    width = wv_ref.shape[1]
    half = wq_ref.shape[1] // 2
    go_ref[...] = all_ref[:, :width]
    gc = all_ref[:, width : 2 * width]
    gc_ref[...] = gc
    gf_ref[...] = all_ref[:, 2 * width : 2 * width + LANES].T[:KW, :]
    at = 2 * width + LANES
    gv = all_ref[:, at + 4 * half :]
    gv_ref[...] = gv
    total = jnp.sum(gc * wc_ref[...].astype(wide), axis=1, keepdims=True)
    total = total + jnp.sum(gv * wv_ref[...].astype(wide), axis=1, keepdims=True)
    for n, (ref, weight_ref, cols) in enumerate(
        (
            (gq_ref, wq_ref, slice(0, half)),
            (gk_ref, wk_ref, slice(0, half)),
            (gq_ref, wq_ref, slice(half, 2 * half)),
            (gk_ref, wk_ref, slice(half, 2 * half)),
        )
    ):
        value = all_ref[:, at + n * half : at + (n + 1) * half]
        ref[:, cols] = value
        total = total + jnp.sum(value * weight_ref[:, cols].astype(wide), axis=1, keepdims=True)
    ggain_ref[...] = as_line(total / gain_ref[...])


def settle_mixer(offs, gain, mine, other, w_query, w_key, w_value, w_convgate, deps=()):
    operands = (gain, mine, other, w_query, w_key, w_value, w_convgate)
    height, width = w_value.shape
    shapes = [w_query.shape, w_key.shape, w_value.shape, w_convgate.shape, (height, width), (KW, height), gain.shape[:1]]
    return launch(
        settle_mixer_kernel,
        deps,
        scalars=1,
        grid=(1,),
        in_specs=[fixed(a.shape) for a in operands],
        out_specs=[fixed(a) for a in shapes],
        out_shape=[jax.ShapeDtypeStruct(a, wide) for a in shapes],
        scratch_shapes=[pltpu.VMEM((height, mine.shape[1]), wide)],
        compiler_params=params(24),
        cost_estimate=cost(0.001, 8),
        name="settle_mixer",
    )(offs, *operands)


def tick_kernel(offs_ref, out_ref):
    out_ref[...] = jnp.zeros_like(out_ref)


def tick(offs, deps=()):
    return launch(
        tick_kernel,
        deps,
        scalars=1,
        grid=(1,),
        in_specs=[],
        out_specs=fixed((16, LANES)),
        out_shape=jax.ShapeDtypeStruct((16, LANES), low),
        compiler_params=params(24),
        cost_estimate=cost(TICK, 8),
        name="arrived",
    )(offs)


def swap(value, axis):
    return lax.ppermute(value, axis, [(0, 1), (1, 0)])


def later(value, other):
    return lax.optimization_barrier((value, other))[0]


def part(value, index, count, axis=0):
    size = value.shape[axis] // count
    return lax.dynamic_slice_in_dim(value, index * size, size, axis)


def in_order(index, mine, other):
    return jnp.where(
        index == 0, jnp.concatenate([mine, other], 0), jnp.concatenate([other, mine], 0)
    )


def per_device(
    tokens, segment_ids, gain_one, w_query, w_key, w_value, w_convgate, w_output, conv_filter,
    gain_two, w_gate, w_up, w_down, cotangent,
):
    Order.last = None
    Order.scale = 0.05
    x = lax.axis_index("near")
    y = lax.axis_index("row")
    c = lax.axis_index("core")
    s = 2 * y + c
    width = tokens.shape[1]
    seg = segment_ids[0]
    block = w_down.shape[0]

    def flip(bits):
        return jnp.bitwise_xor(s, bits)

    small_block = block // 2
    z = lax.axis_index("far") % 2
    quarters = [(2 * a + b) * (SHARD_ROWS // 4) for a, b in ((x, z), (1 - x, z), (x, 1 - z), (1 - x, 1 - z))]

    def feed_cols(core, j):
        return [((2 * row + core) * 2 + j) * small_block for row in range(2)]

    feed_rows = [s, flip(1), jnp.bitwise_xor(flip(2), x), jnp.bitwise_xor(flip(3), x)]
    offs = [
        x,
        jnp.bitwise_xor(x, c),
        s * SHARD_ROWS,
        flip(1) * SHARD_ROWS,
        *(flip(2) * SHARD_ROWS + a for a in quarters),
        *(flip(3) * SHARD_ROWS + a for a in quarters),
        *(a * SHARD_ROWS for a in feed_rows),
        y * small_block,
        (1 - y) * small_block,
        0,
        0,
        *feed_cols(c, 0), *feed_cols(c, 1), *feed_cols(1 - c, 0), *feed_cols(1 - c, 1),
        *feed_cols(c, 0), *feed_cols(1 - c, 0), *feed_cols(c, 1), *feed_cols(1 - c, 1),
        2 * (1 - y) + 1 - x, 2 * (1 - y) + x, 2 * y + 1 - x, 2 * y + x,
        flip(3), flip(1), flip(2), s,
        2 * (1 - y) + 1 - x, 2 * y + 1 - x, 2 * (1 - y) + x, 2 * y + x,
        2 * x + z,
    ]
    offs = jnp.stack([jnp.asarray(a, jnp.int32) for a in offs])

    pack, pack_part = pack_mixer(
        offs, gain_one, gain_two, conv_filter, w_query, w_key, w_value, w_convgate, w_output
    )
    direct = swap(pack_part, "row")
    count = lax.axis_size("far")
    over_z = lax.ppermute(direct, "far", [(i, i ^ 1) for i in range(count)])
    came = [direct, swap(direct, "near"), over_z, swap(over_z, "near")]
    pack_pieces = [pack, swap(pack, "core"), *came, *(swap(a, "core") for a in came)]
    cot_other = swap(later(cotangent, direct), "core")

    mine_first, mine_second, give, *sends, down_first, down_second = pack_feed(offs, w_gate, w_up, w_down)
    given = swap(later(give, direct), "core")

    def across(value):
        pairs = []
        for side, row, core in np.ndindex(2, 2, 2):
            pairs.append((4 * side + 2 * row + core, 4 * side + 2 * (1 - row) + (core ^ side)))
        return lax.ppermute(value, ("near", "row", "core"), pairs)

    feed_pieces = [[own, given] for own in (mine_first, mine_second)]
    feed_pieces[0].append(across(later(sends[0], direct)))

    hidden_one, queries, keys, values, gates, vec, full_one = project(offs, tokens, pack_pieces, deps=[cot_other])
    feed_pieces[0].append(swap(later(feed_pieces[0][2], queries), "near"))
    down_pieces = [[swap(later(down_first, queries), "row")]]
    feed_pieces[1].append(across(later(sends[1], queries)))
    pairs = width // 256
    mixed, attention, recips = attend(queries, keys, values, gates, vec, seg, 0, 2 * pairs)
    middle, hidden_two = mix(tokens, mixed, vec, full_one, deps=[down_pieces[0][0]])
    down_pieces.append([swap(later(down_second, middle), "row")])
    tick(offs, [feed_pieces[0][3]])
    hiddens = [hidden_two, swap(hidden_two, "core")]
    cots = [cotangent, cot_other]

    Order.scale = 20.0

    def down_grad(act, deps=()):
        return weight_grad(offs, ACT_AT, [([act], cots)], (2, 2), "grad_down", deps=deps)

    def gate_grad(both):
        return weight_grad(offs, GRAD_AT, [(hiddens, [both])], (1, 1, 2), "grad_gate_up")

    first_feed = feed(offs, hiddens, cots, 0, w_down, feed_pieces[0], down_pieces[0])
    feed_pieces[1].append(swap(later(feed_pieces[1][2], first_feed[0]), "near"))
    down_send, down_keep = down_grad(first_feed[0], deps=[feed_pieces[1][2]])
    down_came = swap(down_send, "near")
    gate_send, gate_send_own, gate_keep = gate_grad(first_feed[1])
    gate_came, gate_came_own = swap(gate_send, "row"), swap(gate_send_own, "row")
    second_feed = feed(offs, hiddens, cots, 1, w_down, feed_pieces[1], down_pieces[1])
    acts, boths, fulls, downs = zip(first_feed, second_feed)
    down_passed = swap(top_sum(offs, down_keep, down_came), "row")
    gate_passed = swap(top_sum(offs, gate_keep, gate_came), "near")
    ghidden_part = feed_back(boths[0], boths[1], fulls[0], fulls[1])
    ghidden_other = swap(ghidden_part, "core")
    down_send_2, down_keep_2 = down_grad(second_feed[0])
    down_came_2 = swap(down_send_2, "near")
    gate_send_2, gate_send_own_2, gate_keep_2 = gate_grad(second_feed[1])
    gate_came_2, gate_came_own_2 = swap(gate_send_2, "row"), swap(gate_send_own_2, "row")
    feed_sum = lax.psum(
        rest_sum(offs, [(down_keep, down_came, down_passed), (gate_keep, gate_came_own, gate_passed)]), "far"
    )
    tick(offs)
    gmiddle, gbranch, gmixed, _ = middle_back(
        boths[0], boths[1], ghidden_other, middle, cotangent, vec, fulls[0], fulls[1], full_one
    )
    down_passed_2 = swap(top_sum(offs, down_keep_2, down_came_2), "row")
    gate_passed_2 = swap(top_sum(offs, gate_keep_2, gate_came_2), "near")

    ggate, gconv, gfilter = conv_back(values, gmixed, gates, vec, seg)
    filter_came = swap(gfilter, "core")
    early_send, early_keep = weight_grad(
        offs, OWNER_AT, [([mixed], [gbranch]), ([hidden_one], [ggate])], (2, 2), "grad_output_convgate"
    )
    early_came = swap(early_send, "core")
    attended = attend_back(queries, keys, values, gmixed, attention, recips, gconv, seg, 0, pairs)
    early_give, early_held = halves_sum(offs, [(early_keep, early_came)], [gfilter, filter_came])
    early_came = swap(early_give, "row")
    tick(offs, [feed_sum])
    feed_near = rest_sum(
        offs, [(down_keep_2, down_came_2, down_passed_2), (gate_keep_2, gate_came_own_2, gate_passed_2)]
    )
    feed_other = swap(later(feed_sum, feed_near), "near")
    feed_part = lax.psum_scatter(feed_near, "far", scatter_dimension=0, tiled=True)
    tick(offs)
    gqk, gv = attend_back(
        queries, keys, values, gmixed, attention, recips, gconv, seg, pairs, pairs, onto=attended
    )
    early_own, early_other = near_split(offs, early_held, early_came)
    early_passed = swap(early_other, "near")
    late_send, late_keep = weight_grad(
        offs, OWNER_AT, [([hidden_one], [gqk]), ([hidden_one], [gv])], (2, 2), "grad_query_key_value"
    )
    late_came = swap(late_send, "core")
    Order.scale = 0.05
    feed_sum_2 = lax.all_gather(later(feed_part, tick(offs, [feed_part])), "far", axis=0, tiled=True)
    own_rows, theirs = sort_rows(offs, feed_sum, feed_other, width)
    spreads = [own_rows, swap(theirs, "core")]
    late_give, late_held = halves_sum(offs, [(late_keep, late_came)])
    late_came = swap(late_give, "row")
    out_part = feed_out(acts[0], acts[1], downs[0], downs[1], 1, [], "feed_out_partner")
    late_own, late_other = near_split(offs, late_held, late_came)
    late_passed = swap(late_other, "near")
    tick(offs, [feed_sum_2])
    mixer_near = pairs_sum(offs, [(early_own, early_passed), (late_own, late_passed)])
    feed_other_2 = swap(later(feed_sum_2, mixer_near), "near")
    Order.scale = 20.0
    mixer_sum = lax.psum(mixer_near, "far")
    out_came = swap(later(out_part, mixer_near), "core")
    tick(offs)
    result = feed_out(acts[0], acts[1], downs[0], downs[1], 0, [middle, out_came], "feed_out")
    grad_tokens, _ = tokens_back(gqk, gv, ggate, tokens, gmiddle, vec, full_one)
    own_rows, theirs = sort_rows(offs, feed_sum_2, feed_other_2, width)
    spreads += [own_rows, swap(theirs, "core")]
    grad_down = settle_down(offs, [(feed_sum, feed_other), (feed_sum_2, feed_other_2)], width)
    grad_gate, grad_up, ggain_two = spread(offs, gain_two[:, None].astype(wide), w_gate, w_up, spreads)
    mixer_other = swap(mixer_sum, "near")
    *grads, grad_output, grad_filter, ggain_one = settle_mixer(
        offs, gain_one[:, None].astype(wide), mixer_sum, mixer_other, w_query, w_key, w_value, w_convgate
    )
    return (
        result,
        grad_tokens,
        ggain_one,
        *grads,
        grad_output,
        grad_filter,
        ggain_two,
        grad_gate,
        grad_up,
        grad_down,
    )


def solution(mesh):
    replicas, shards = mesh.shape["rep"], mesh.shape["shard"]
    devices = np.asarray(mesh.devices).reshape(replicas // 2, 2, shards // 2, 2)
    fine = Mesh(devices, ("far", "near", "row", "core"))
    token = P(("far", "near", "row", "core"), None)
    line = P(("row", "core"))
    weight = P(("row", "core"), None)
    taps = P(None, ("row", "core"))
    return jax.shard_map(
        per_device,
        mesh=fine,
        in_specs=(
            token, token, line, weight, weight, weight, weight, weight, taps, line, weight, weight, weight, token
        ),
        out_specs=(
            token, token, line, weight, weight, weight, weight, weight, taps, line, weight, weight, weight
        ),
        check_vma=False,
    )
```

```python
import functools

import jax
import jax.numpy as jnp
import numpy as np
from jax import lax
from jax.experimental import pallas as pl
from jax.experimental.pallas import tpu as pltpu
from jax.sharding import Mesh
from jax.sharding import PartitionSpec as P

HEADS = 16
FEAT = 16
KW = 3
EPS = 1e-06
TILE = 256
FEED_TILE = 512
FEED_COLUMNS = 512
SHARD_ROWS = 256
LANES = 128
TICK = 1e5
X_AT, MIXER_AT, FEED_AT, DOWN_AT, PACK_AT, COLS_AT, GRAD_AT, OWNER_AT, ACT_AT, QUARTER_AT = 0, 2, 12, 16, 20, 28, 36, 40, 44, 48

low = jnp.bfloat16
wide = jnp.float32


def dot(a, b):
    return jnp.dot(a, b, preferred_element_type=wide)


def dot_nt(a, b):
    return lax.dot_general(a, b, (((1,), (1,)), ((), ())), preferred_element_type=wide)


def dot_tn(a, b):
    return lax.dot_general(a, b, (((0,), (0,)), ((), ())), preferred_element_type=wide)


class Order:
    last = None
    scale = 1.0


def launch(kernel, deps=(), onto=(), *, scalars=0, grid, in_specs, out_specs, out_shape, scratch_shapes=(), **rest):
    taken = scalars + len(in_specs)
    deps = list(onto) + [d for d in deps if d is not None] + ([] if Order.last is None or any(Order.last is a for a in onto) else [Order.last])

    def body(*refs):
        kernel(*refs[:taken], *refs[taken + len(deps) :])

    spec = pltpu.PrefetchScalarGridSpec(
        num_scalar_prefetch=scalars,
        grid=grid,
        in_specs=list(in_specs) + [pl.BlockSpec(memory_space=pl.ANY)] * len(deps),
        out_specs=out_specs,
        scratch_shapes=list(scratch_shapes),
    )
    aliases = {taken + n: n for n in range(len(onto))}
    run = pl.pallas_call(body, grid_spec=spec, out_shape=out_shape, input_output_aliases=aliases, **rest)

    def call(*operands):
        result = run(*operands, *deps)
        Order.last = result[0] if isinstance(result, (list, tuple)) else result
        return result

    return call


def params(mib, least=60):
    return pltpu.CompilerParams(vmem_limit_bytes=max(mib, least) << 20)


def cost(gigaflops, mebibytes):
    return pl.CostEstimate(
        flops=int(gigaflops * Order.scale * 1e9), bytes_accessed=int(mebibytes * Order.scale * (1 << 20)), transcendentals=0
    )


def fixed(shape):
    return pl.BlockSpec(shape, lambda *_: (0,) * len(shape), pipeline_mode=pl.Buffered(1))


def rows(height, width):
    return pl.BlockSpec((height, width), lambda i, *_: (i, 0))


def place(offs_ref, base, pieces, full_ref):
    for n, piece in enumerate(pieces):
        at = pl.multiple_of(offs_ref[base + n], 64)
        full_ref[pl.ds(at, piece.shape[0]), :] = piece[...]


def project_kernel(offs_ref, x_ref, *refs):
    pieces, (hidden_ref, q_ref, k_ref, v_ref, gate_ref, vec_ref, out_ref, full_ref, sem) = refs[:10], refs[10:]
    copy = pltpu.make_async_copy(full_ref, out_ref, sem)
    heads = HEADS * FEAT
    width = x_ref.shape[1]

    @pl.when(pl.program_id(0) == 0)
    def _():
        place(offs_ref, MIXER_AT, pieces, full_ref)
        copy.start()
        small = full_ref[:, 2 * heads + 3 * width :].astype(wide)
        vec_ref[...] = small.T[:8, :]

    x = x_ref[...].astype(wide)
    inverse = lax.rsqrt(jnp.mean(x * x, axis=-1, keepdims=True) + EPS)
    hidden = (x * inverse * vec_ref[0:1, :]).astype(low)
    hidden_ref[...] = hidden
    at = width
    q_ref[...] = (dot(hidden, full_ref[:, at : at + heads]) * FEAT ** (-0.5)).astype(low)
    k_ref[...] = dot(hidden, full_ref[:, at + heads : at + 2 * heads]).astype(low)
    at = at + 2 * heads
    v_ref[...] = dot(hidden, full_ref[:, at : at + width]).astype(low)
    gate_ref[...] = dot(hidden, full_ref[:, at + width : at + 2 * width]).astype(low)

    @pl.when(pl.program_id(0) == pl.num_programs(0) - 1)
    def _():
        copy.wait()


def project(offs, x, pieces, deps=()):
    length, width = x.shape
    heads = HEADS * FEAT
    columns = pieces[0].shape[1]
    shapes = [
        jax.ShapeDtypeStruct((length, width), low),
        jax.ShapeDtypeStruct((length, heads), low),
        jax.ShapeDtypeStruct((length, heads), low),
        jax.ShapeDtypeStruct((length, width), low),
        jax.ShapeDtypeStruct((length, width), low),
        jax.ShapeDtypeStruct((8, width), wide),
        jax.ShapeDtypeStruct((width, columns), low),
    ]
    return launch(
        project_kernel,
        deps,
        scalars=1,
        grid=(length // TILE,),
        in_specs=[rows(TILE, width)] + [fixed(p.shape) for p in pieces],
        out_specs=[
            rows(TILE, width),
            rows(TILE, heads),
            rows(TILE, heads),
            rows(TILE, width),
            rows(TILE, width),
            fixed((8, width)),
            pl.BlockSpec(memory_space=pl.ANY),
        ],
        scratch_shapes=[pltpu.VMEM((width, columns), low), pltpu.SemaphoreType.DMA],
        out_shape=shapes,
        compiler_params=params(40),
        cost_estimate=cost(7, 22),
        name="project",
    )(offs, x, *pieces)


def shift_rows(v, seg, by, up):
    zeros = jnp.zeros((by, v.shape[1]), v.dtype)
    none = jnp.full((by, 1), -1, seg.dtype)
    if up:
        moved, moved_seg = jnp.concatenate([v[by:], zeros], 0), jnp.concatenate([seg[by:], none], 0)
    else:
        moved = jnp.concatenate([zeros, v[:-by]], 0)
        moved_seg = jnp.concatenate([none, seg[:-by]], 0)
    return jnp.where(moved_seg == seg, moved, 0.0)


def lane_pick(width, start, stop):
    i = lax.broadcasted_iota(jnp.int32, (1, width), 1)
    return (i >= start) & (i < stop)


def attend_kernel(
    first, q_ref, k_ref, v_ref, gate_ref, vec_ref, segr_ref, segc_ref, mixed_ref, att_ref, recip_ref, mask_ref
):
    length = q_ref.shape[0]
    pair = pl.program_id(0) + first
    zero = jnp.zeros((), low)

    @pl.when(pair == first)
    def _():
        for tb in range(0, length, TILE):
            t = lax.broadcasted_iota(jnp.int32, (TILE, length), 0) + tb
            s = lax.broadcasted_iota(jnp.int32, (TILE, length), 1)
            seen = (s <= t) & (segc_ref[tb : tb + TILE, :] == segr_ref[...])
            mask_ref[tb : tb + TILE, :] = jnp.where(seen, 1.0, 0.0).astype(low)

    v = v_ref[...]
    keys, sides = [], []
    for i in range(2):
        head = 2 * pair + i
        keys.append(jnp.where(lane_pick(HEADS * FEAT, head * FEAT, (head + 1) * FEAT), k_ref[...], zero))
        lanes = lane_pick(128, 64 * i, 64 * i + 64)
        ones = jnp.broadcast_to(jnp.where(lanes, 1.0, 0.0).astype(low), (length, 128))
        sides.append(jnp.concatenate([jnp.where(lanes, v, zero), ones], 1))
    for tb in range(0, length, TILE):
        n = tb + TILE
        total = None
        for i in range(2):
            one_plus = dot_nt(q_ref[tb:n, :], keys[i][:n]) + 1.0
            kernel = (one_plus * one_plus + 1.0).astype(low) * mask_ref[tb:n, :n]
            part = dot(kernel, sides[i][:n])
            total = part if total is None else total + part
        recip = 1.0 / total[:, 128:]
        att_ref[tb:n, :] = (total[:, :128] * recip).astype(low)
        recip_ref[tb:n, :] = (2.0 * recip).astype(low)
    v_wide = v.astype(wide)
    seg = segc_ref[...]
    conv = vec_ref[2:3, :] * v_wide
    for j in range(1, KW):
        conv = conv + vec_ref[2 + j : 3 + j, :] * shift_rows(v_wide, seg, j, False)
    mixed_ref[...] = (att_ref[...].astype(wide) + gate_ref[...].astype(wide) * conv).astype(low)


def whole(a):
    return pl.BlockSpec(a.shape, lambda p: (0, 0))


def attend(q, k, v, gate, vec, seg, first, count, onto=(), deps=()):
    length, width = v.shape
    column = pl.BlockSpec((length, 128), lambda p: (0, p + first))
    seg_row, seg_col = seg.reshape(1, length), seg.reshape(length, 1)
    return launch(
        functools.partial(attend_kernel, first),
        deps,
        onto,
        grid=(count,),
        in_specs=[
            whole(q), whole(k), column, column, pl.BlockSpec((8, 128), lambda p: (0, p + first)), whole(seg_row), whole(seg_col)
        ],
        out_specs=[column] * 3,
        out_shape=[jax.ShapeDtypeStruct((length, width), low)] * 3,
        scratch_shapes=[pltpu.VMEM((length, length), low)],
        compiler_params=params(40),
        cost_estimate=cost(18 * count * 128 / width, 14),
        name="attention_forward",
    )(q, k, v, gate, vec, seg_row, seg_col)


def attend_back_kernel(
    first, q_ref, k_ref, v_ref, gm_ref, att_ref, recip_ref, gconv_ref, segr_ref, segc_ref,
    gqk_ref, gv_ref, mask_ref, gq_acc, gk_acc,
):
    length, heads = q_ref.shape
    pair = pl.program_id(0) + first
    zero = jnp.zeros((), low)

    @pl.when(pair == first)
    def _():
        for sb in range(0, length, TILE):
            s = lax.broadcasted_iota(jnp.int32, (TILE, length), 0) + sb
            t = lax.broadcasted_iota(jnp.int32, (TILE, length), 1)
            seen = (s <= t) & (segc_ref[sb : sb + TILE, :] == segr_ref[...])
            mask_ref[sb : sb + TILE, :] = jnp.where(seen, 1.0, 0.0).astype(low)
        gk_acc[...] = jnp.zeros_like(gk_acc)
        gq_acc[...] = jnp.zeros_like(gq_acc)

    v = v_ref[...]
    gm = gm_ref[...].astype(wide)
    gnum_wide = gm * recip_ref[...].astype(wide)
    gnum = gnum_wide.astype(low)
    product = gnum_wide * att_ref[...].astype(wide)
    high = product.astype(low)
    rest = (product - high.astype(wide)).astype(low)
    r = lax.broadcasted_iota(jnp.int32, (256, 128), 0)
    c = lax.broadcasted_iota(jnp.int32, (256, 128), 1)
    same_head = jnp.where(((r % 128) // 64) == (c // 64), 1.0, 0.0).astype(low)
    gtot = -dot(jnp.concatenate([high, rest], 1), same_head)
    gtot_high = gtot.astype(low)
    gtot_rest = (gtot - gtot_high.astype(wide)).astype(low)
    lane = lax.broadcasted_iota(jnp.int32, (1, 128), 1)
    left = jnp.concatenate([gnum, jnp.where(lane % 64 == 0, gtot_high, gtot_rest)], 1)
    gnum_half = gnum * jnp.asarray(0.5, low)
    queries, sides, gnums, keys = [], [], [], []
    for i in range(2):
        head = 2 * pair + i
        mine = lane_pick(heads, head * FEAT, (head + 1) * FEAT)
        queries.append(jnp.where(mine, q_ref[...], zero))
        keys.append(jnp.where(mine, k_ref[...], zero))
        lanes = lane_pick(128, 64 * i, 64 * i + 64)
        ones = jnp.where(lane_pick(128, 64 * i, 64 * i + 2), 1.0, 0.0).astype(low)
        sides.append(jnp.concatenate([jnp.where(lanes, v, zero), jnp.broadcast_to(ones, (length, 128))], 1))
        gnums.append(jnp.where(lanes, gnum_half, zero))
    for sb in range(0, length, TILE):
        n = sb + TILE
        gv = gconv_ref[sb:n, :].astype(wide)
        gk = None
        for i in range(2):
            one_plus = dot_nt(k_ref[sb:n, :], queries[i][sb:]) + 1.0
            mask = mask_ref[sb:n, sb:]
            kernel = (one_plus * one_plus + 1.0).astype(low) * mask
            gv = gv + dot(kernel, gnums[i][sb:])
            gkernel = dot_nt(sides[i][sb:n], left[sb:])
            gscores = (gkernel * one_plus).astype(low) * mask
            part = dot(gscores, queries[i][sb:])
            gk = part if gk is None else gk + part
            gq_acc[sb:, :] += dot_tn(gscores, keys[i][sb:n])
        gv_ref[sb:n, :] = gv.astype(low)
        gk_acc[sb:n, :] += gk

    @pl.when(pl.program_id(0) == pl.num_programs(0) - 1)
    def _():
        mine = slice(2 * FEAT * first, 2 * FEAT * first + gqk_ref.shape[1] // 2)
        gqk_ref[:, : gqk_ref.shape[1] // 2] = (gq_acc[:, mine] * FEAT ** (-0.5)).astype(low)
        gqk_ref[:, gqk_ref.shape[1] // 2 :] = gk_acc[:, mine].astype(low)


def attend_back(q, k, v, gm, att, recip, gconv, seg, first, count, onto=(), deps=()):
    length, width = v.shape
    heads = q.shape[1]
    column = pl.BlockSpec((length, 128), lambda p: (0, p + first))
    seg_row, seg_col = seg.reshape(1, length), seg.reshape(length, 1)
    return launch(
        functools.partial(attend_back_kernel, first),
        deps,
        onto,
        grid=(count,),
        in_specs=[whole(q), whole(k)] + [column] * 5 + [whole(seg_row), whole(seg_col)],
        out_specs=[pl.BlockSpec((length, 4 * FEAT * count), lambda p: (0, first // count)), column],
        out_shape=[jax.ShapeDtypeStruct((length, 2 * heads), low), jax.ShapeDtypeStruct((length, width), low)],
        scratch_shapes=[
            pltpu.VMEM((length, length), low),
            pltpu.VMEM((length, heads), wide),
            pltpu.VMEM((length, heads), wide),
        ],
        compiler_params=params(48),
        cost_estimate=cost(40 * count * 128 / width, 18),
        name="attention_backward",
    )(q, k, v, gm, att, recip, gconv, seg_row, seg_col)


def conv_back_kernel(v_ref, gm_ref, gate_ref, vec_ref, segc_ref, ggate_ref, gconv_ref, gfilt_ref):
    v_wide = v_ref[...].astype(wide)
    gm = gm_ref[...].astype(wide)
    seg = segc_ref[...]
    taps = [vec_ref[2 + j : 3 + j, :] for j in range(KW)]
    grad = gm * gate_ref[...].astype(wide)
    conv = taps[0] * v_wide
    gv_conv = taps[0] * grad
    lines = [jnp.sum(grad * v_wide, 0, keepdims=True)]
    for j in range(1, KW):
        moved = shift_rows(v_wide, seg, j, False)
        conv = conv + taps[j] * moved
        lines.append(jnp.sum(grad * moved, 0, keepdims=True))
        gv_conv = gv_conv + taps[j] * shift_rows(grad, seg, j, True)
    lines.append(jnp.zeros((LANES - KW, 128), wide))
    gfilt_ref[...] = jnp.concatenate(lines, 0).T.astype(low)
    ggate_ref[...] = (gm * conv).astype(low)
    gconv_ref[...] = gv_conv.astype(low)


def conv_back(v, gm, gate, vec, seg, deps=()):
    length, width = v.shape
    column = pl.BlockSpec((length, 128), lambda p: (0, p))
    small = pl.BlockSpec((8, 128), lambda p: (0, p))
    seg_col = seg.reshape(length, 1)
    return launch(
        conv_back_kernel,
        deps,
        grid=(width // 128,),
        in_specs=[column, column, column, small, whole(seg_col)],
        out_specs=[column, column, pl.BlockSpec((128, LANES), lambda p: (p, 0))],
        out_shape=[jax.ShapeDtypeStruct((length, width), low)] * 2 + [jax.ShapeDtypeStruct((width, LANES), low)],
        compiler_params=params(48),
        cost_estimate=cost(1, 10),
        name="convolution_backward",
    )(v, gm, gate, vec, seg_col)


def mix_kernel(x_ref, mixed_ref, vec_ref, weight_ref, middle_ref, hidden_ref):
    middle = x_ref[...].astype(wide) + dot(mixed_ref[...], weight_ref[...])
    inverse = lax.rsqrt(jnp.mean(middle * middle, axis=-1, keepdims=True) + EPS)
    middle_ref[...] = middle
    hidden_ref[...] = (middle * inverse * vec_ref[1:2, :]).astype(low)


def mix(x, mixed, vec, full, deps=()):
    length, width = x.shape
    return launch(
        mix_kernel,
        deps,
        grid=(length // TILE,),
        in_specs=[rows(TILE, width), rows(TILE, width), fixed(vec.shape), fixed((width, width))],
        out_specs=[rows(TILE, width), rows(TILE, width)],
        out_shape=[jax.ShapeDtypeStruct((length, width), wide), jax.ShapeDtypeStruct((length, width), low)],
        compiler_params=params(32),
        cost_estimate=cost(3, 16),
        name="mix",
    )(x, mixed, vec, full)


def first_half(n):
    return lambda i, *_: (jnp.minimum(i, n - 1), 0)


def second_half(n):
    return lambda i, *_: (jnp.maximum(i - n, 0), 0)


def feed_kernel(n, offs_ref, ha_ref, hb_ref, ca_ref, cb_ref, *refs):
    pieces, downs = refs[:4], refs[4:6]
    act_ref, both_ref, full_out_ref, down_out_ref, full_ref, down_ref, sems = refs[6:]
    copies = [
        pltpu.make_async_copy(full_ref, full_out_ref, sems.at[0]),
        pltpu.make_async_copy(down_ref, down_out_ref, sems.at[1]),
    ]
    step = pl.program_id(0)
    half = full_ref.shape[1] // 2

    @pl.when(step == 0)
    def _():
        place(offs_ref, FEED_AT, pieces, full_ref)
        place(offs_ref, DOWN_AT, downs, down_ref)
        for copy in copies:
            copy.start()

    def work(hidden, cotangent):
        for at in range(0, half, FEED_COLUMNS):
            gate = dot(hidden, full_ref[:, at : at + FEED_COLUMNS])
            up = dot(hidden, full_ref[:, half + at : half + at + FEED_COLUMNS])
            gact = dot_nt(cotangent, down_ref[at : at + FEED_COLUMNS, :])
            sig = jax.nn.sigmoid(gate)
            silu = gate * sig
            act_ref[:, at : at + FEED_COLUMNS] = (silu * up).astype(low)
            both_ref[:, at : at + FEED_COLUMNS] = (gact * up * (sig + silu * (1.0 - sig))).astype(low)
            both_ref[:, half + at : half + at + FEED_COLUMNS] = (gact * silu).astype(low)

    @pl.when(step < n)
    def _():
        work(ha_ref[...], ca_ref[...])

    @pl.when(step >= n)
    def _():
        work(hb_ref[...], cb_ref[...])

    @pl.when(step == 2 * n - 1)
    def _():
        for copy in copies:
            copy.wait()


def feed(offs, hidden, cotangent, j, w_down, pieces, down_pieces, deps=()):
    length, width = hidden[0].shape
    n = length // FEED_TILE
    half = w_down.shape[0]
    first = pl.BlockSpec((FEED_TILE, width), first_half(n))
    second = pl.BlockSpec((FEED_TILE, width), second_half(n))
    own_down = pl.BlockSpec((half // 2, width), lambda *_: (j, 0), pipeline_mode=pl.Buffered(1))
    given_rows = pl.BlockSpec(pieces[0].shape, lambda *_: (j, 0), pipeline_mode=pl.Buffered(1))
    return launch(
        functools.partial(feed_kernel, n),
        deps,
        scalars=1,
        grid=(2 * n,),
        in_specs=[first, second, first, second]
        + [fixed(pieces[0].shape), given_rows]
        + [fixed(p.shape) for p in pieces[2:]]
        + [own_down]
        + [fixed(p.shape) for p in down_pieces],
        out_specs=[rows(FEED_TILE, half), rows(FEED_TILE, 2 * half)] + [pl.BlockSpec(memory_space=pl.ANY)] * 2,
        scratch_shapes=[
            pltpu.VMEM((width, 2 * half), low),
            pltpu.VMEM((half, width), low),
            pltpu.SemaphoreType.DMA((2,)),
        ],
        out_shape=[
            jax.ShapeDtypeStruct((2 * length, half), low),
            jax.ShapeDtypeStruct((2 * length, 2 * half), low),
            jax.ShapeDtypeStruct((width, 2 * half), low),
            jax.ShapeDtypeStruct((half, width), low),
        ],
        compiler_params=params(48),
        cost_estimate=cost(16, 34),
        name="feed_in",
    )(offs, *hidden, *cotangent, *pieces, w_down, *down_pieces)


def weight_grad_kernel(shape_of, counts, outs, length, offs_ref, *refs):
    targets = [(ref, row * TILE) for ref, height in zip(refs[-len(outs) :], outs) for row in range(height)]
    step = pl.program_id(0)

    def work(lefts, rights):
        terms = max(len(lefts[0]), len(rights))

        def part_of(group, t):
            return group[t][...] if len(group) == terms else group[0][t * length : (t + 1) * length, :]

        for b, (ref, row) in enumerate(targets):
            value = None
            for t in range(terms):
                product = dot_tn(part_of(lefts[b], t), part_of(rights, t))
                value = product if value is None else value + product
            ref[row : row + TILE, :] = value.astype(low)

    start = 0
    for (left_at, right_at), count in zip(shape_of, counts):
        lefts = [[refs[n] for n in block] for block in left_at]
        rights = [refs[n] for n in right_at]
        if len(counts) == 1:
            work(lefts, rights)
        else:
            pl.when((step >= start) & (step < start + count))(functools.partial(work, lefts, rights))
        start += count


def weight_grad(offs, base, groups, outs, name, tile=512, deps=()):
    blocks = sum(outs)
    counts = [rights[0].shape[1] // tile for _, rights in groups]
    columns = sum(counts) * tile
    in_specs, operands, shape_of, known = [], [], [], {}
    start = 0
    for (lefts, rights), count in zip(groups, counts):
        key = tuple(id(a) for a in lefts)
        if key not in known:
            known[key] = []
            for b in range(blocks):
                known[key].append([len(operands) + n for n in range(len(lefts))])
                for a in lefts:
                    in_specs.append(pl.BlockSpec((a.shape[0], TILE), lambda j, offs, b=b: (0, offs[base + b])))
                    operands.append(a)
        shape_of.append((known[key], [len(operands) + n for n in range(len(rights))]))
        for a in rights:

            def where_to(j, offs, start=start, count=count):
                return (0, jnp.clip(j - start, 0, count - 1))

            in_specs.append(pl.BlockSpec((a.shape[0], tile), where_to))
            operands.append(a)
        start += count
    tokens = sum(a.shape[0] for a in groups[0][0])
    terms = max(len(groups[0][0]), len(groups[0][1]))
    return launch(
        functools.partial(weight_grad_kernel, shape_of, counts, outs, tokens // terms),
        deps,
        scalars=1,
        grid=(sum(counts),),
        in_specs=in_specs,
        out_specs=[pl.BlockSpec((height * TILE, tile), lambda j, offs: (0, j)) for height in outs],
        out_shape=[jax.ShapeDtypeStruct((height * TILE, columns), low) for height in outs],
        compiler_params=params(48, 48),
        cost_estimate=cost(2.5e-9 * tokens * 1024 * columns, (tokens * (1024 + columns) * 2 + 2048 * columns) / 2**20),
        name=name,
    )(offs, *operands)


def feed_back_kernel(a_ref, b_ref, wa_ref, wb_ref, out_ref):
    out_ref[...] = (dot_nt(a_ref[...], wa_ref[...]) + dot_nt(b_ref[...], wb_ref[...])).astype(low)


def feed_back(first, second, full_first, full_second, deps=()):
    length = first.shape[0] // 2
    width = full_first.shape[0]
    n = length // TILE
    tile = pl.BlockSpec((TILE, first.shape[1]), lambda i: (i + n, 0))
    return launch(
        feed_back_kernel,
        deps,
        grid=(n,),
        in_specs=[tile, tile, fixed(full_first.shape), fixed(full_second.shape)],
        out_specs=rows(TILE, width),
        out_shape=jax.ShapeDtypeStruct((length, width), low),
        compiler_params=params(32),
        cost_estimate=cost(10, 18),
        name="feed_back_partner",
    )(first, second, full_first, full_second)


def middle_back_kernel(
    a_ref, b_ref, other_ref, middle_ref, cot_ref, vec_ref, wa_ref, wb_ref, wo_ref,
    gmiddle_ref, gbranch_ref, gmixed_ref, ggain_ref,
):
    ghidden = dot_nt(a_ref[...], wa_ref[...]) + dot_nt(b_ref[...], wb_ref[...]) + other_ref[...].astype(wide)
    middle = middle_ref[...]
    inverse = lax.rsqrt(jnp.mean(middle * middle, axis=-1, keepdims=True) + EPS)
    normed = middle * inverse
    gain = jnp.sum(ghidden * normed, axis=0, keepdims=True)

    @pl.when(pl.program_id(0) == 0)
    def _():
        ggain_ref[...] = jnp.zeros_like(ggain_ref)

    ggain_ref[0:1, :] += gain
    scaled = ghidden * vec_ref[1:2, :]
    gmiddle = cot_ref[...].astype(wide) + inverse * (
        scaled - normed * jnp.mean(scaled * normed, axis=-1, keepdims=True)
    )
    gmiddle_ref[...] = gmiddle
    gbranch = gmiddle.astype(low)
    gbranch_ref[...] = gbranch
    gmixed_ref[...] = dot_nt(gbranch, wo_ref[...]).astype(low)


def middle_back(first, second, other, middle, cotangent, vec, full_first, full_second, w_output, deps=()):
    length, width = middle.shape
    tile = rows(TILE, first.shape[1])
    line = rows(TILE, width)
    return launch(
        middle_back_kernel,
        deps,
        grid=(length // TILE,),
        in_specs=[
            tile, tile, line, line, line, fixed(vec.shape), fixed(full_first.shape), fixed(full_second.shape), fixed((width, width))
        ],
        out_specs=[line, line, line, fixed((8, width))],
        out_shape=[
            jax.ShapeDtypeStruct((length, width), wide),
            jax.ShapeDtypeStruct((length, width), low),
            jax.ShapeDtypeStruct((length, width), low),
            jax.ShapeDtypeStruct((8, width), wide),
        ],
        compiler_params=params(48),
        cost_estimate=cost(13, 40),
        name="middle_back",
    )(first, second, other, middle, cotangent, vec, full_first, full_second, w_output)


def feed_out_kernel(add, *refs):
    out_ref = refs[-1]
    value = dot(refs[0][...], refs[2][...]) + dot(refs[1][...], refs[3][...])
    for ref in refs[4:-1]:
        value = value + ref[...].astype(wide)
    out_ref[...] = value.astype(low)


def feed_out(first, second, down_first, down_second, shift, extras, name, deps=()):
    length = first.shape[0] // 2
    width = down_first.shape[1]
    n = length // TILE
    tile = pl.BlockSpec((TILE, first.shape[1]), lambda i: (i + shift * n, 0))
    return launch(
        functools.partial(feed_out_kernel, len(extras)),
        deps,
        grid=(n,),
        in_specs=[tile, tile, fixed(down_first.shape), fixed(down_second.shape)] + [rows(TILE, width)] * len(extras),
        out_specs=rows(TILE, width),
        out_shape=jax.ShapeDtypeStruct((length, width), low),
        compiler_params=params(32),
        cost_estimate=cost(5, 16),
        name=name,
    )(first, second, down_first, down_second, *extras)


def tokens_back_kernel(gqk_ref, gv_ref, ggate_ref, x_ref, gmiddle_ref, vec_ref, full_ref, gtokens_ref, ggain_ref):
    two = gqk_ref.shape[1]
    width = x_ref.shape[1]
    quarter = two // 4
    ghidden = None
    for n, col in enumerate((0, 2, 1, 3)):
        at = width + col * quarter
        term = dot_nt(gqk_ref[:, n * quarter : (n + 1) * quarter], full_ref[:, at : at + quarter])
        ghidden = term if ghidden is None else ghidden + term
    ghidden = (
        ghidden
        + dot_nt(gv_ref[...], full_ref[:, width + two : 2 * width + two])
        + dot_nt(ggate_ref[...], full_ref[:, two + 2 * width : two + 3 * width])
    )
    x = x_ref[...].astype(wide)
    inverse = lax.rsqrt(jnp.mean(x * x, axis=-1, keepdims=True) + EPS)
    normed = x * inverse

    @pl.when(pl.program_id(0) == 0)
    def _():
        ggain_ref[...] = jnp.zeros_like(ggain_ref)

    ggain_ref[0:1, :] += jnp.sum(ghidden * normed, axis=0, keepdims=True)
    scaled = ghidden * vec_ref[0:1, :]
    gtokens_ref[...] = gmiddle_ref[...] + inverse * (
        scaled - normed * jnp.mean(scaled * normed, axis=-1, keepdims=True)
    )


def tokens_back(gqk, gv, ggate, x, gmiddle, vec, full, deps=()):
    length, width = x.shape
    line = rows(TILE, width)
    return launch(
        tokens_back_kernel,
        deps,
        grid=(length // TILE,),
        in_specs=[rows(TILE, gqk.shape[1]), line, line, line, line, fixed(vec.shape), fixed(full.shape)],
        out_specs=[line, fixed((8, width))],
        out_shape=[jax.ShapeDtypeStruct((length, width), wide), jax.ShapeDtypeStruct((8, width), wide)],
        compiler_params=params(40),
        cost_estimate=cost(7, 24),
        name="tokens_back",
    )(gqk, gv, ggate, x, gmiddle, vec, full)


def as_line(column):
    return jnp.broadcast_to(column, (column.shape[0], LANES)).T[0]


def spread_kernel(cols_ref, gain_ref, wg_ref, wu_ref, a_ref, b_ref, c_ref, d_ref, gate_ref, up_ref, ggain_ref):
    total = None
    for n, ref in enumerate((a_ref, b_ref, c_ref, d_ref)):
        quarter = ref.shape[1] // 4
        for part_y in range(2):
            at = pl.ds(pl.multiple_of(cols_ref[COLS_AT + 2 * n + part_y], 512), quarter)
            gate = ref[:, part_y * quarter : (part_y + 1) * quarter].astype(wide)
            up = ref[:, (2 + part_y) * quarter : (3 + part_y) * quarter].astype(wide)
            gate_ref[:, at] = gate
            up_ref[:, at] = up
            term = gate * wg_ref[:, at].astype(wide) + up * wu_ref[:, at].astype(wide)
            line = jnp.sum(term, axis=1, keepdims=True)
            total = line if total is None else total + line
    ggain_ref[...] = as_line(total / gain_ref[...])


def spread(cols, gain, w_gate, w_up, blocks, deps=()):
    height, width = blocks[0].shape
    shape = jax.ShapeDtypeStruct((height, 2 * width), wide)
    return launch(
        spread_kernel,
        deps,
        scalars=1,
        grid=(1,),
        in_specs=[fixed(gain.shape), fixed(w_gate.shape), fixed(w_up.shape)] + [fixed(b.shape) for b in blocks],
        out_specs=[fixed(shape.shape)] * 2 + [fixed(gain.shape[:1])],
        out_shape=[shape, shape, jax.ShapeDtypeStruct(gain.shape[:1], wide)],
        compiler_params=params(24),
        cost_estimate=cost(0.001, 16),
        name="spread",
    )(cols, gain, w_gate, w_up, *blocks)


def pack_kernel(at_ref, g1_ref, g2_ref, taps_ref, q_ref, k_ref, v_ref, c_ref, o_ref, pack_ref, part_ref):
    height = q_ref.shape[0]
    col = 0
    for ref in (o_ref, q_ref, k_ref, v_ref, c_ref):
        pack_ref[:, col : col + ref.shape[1]] = ref[...]
        col += ref.shape[1]
    small = jnp.concatenate([g1_ref[...].astype(wide)[None], g2_ref[...].astype(wide)[None], taps_ref[...].astype(wide)], 0)
    small = jnp.concatenate([small, jnp.zeros((LANES - small.shape[0], height), wide)], 0)
    pack_ref[:, col : col + LANES] = small.T.astype(low)
    size = part_ref.shape[0]
    part_ref[...] = pack_ref[pl.ds(pl.multiple_of(at_ref[QUARTER_AT] * size, 64), size), :]


def pack_mixer(at, gain_one, gain_two, taps, w_query, w_key, w_value, w_convgate, w_output):
    operands = (gain_one, gain_two, taps, w_query, w_key, w_value, w_convgate, w_output)
    height = w_query.shape[0]
    columns = sum(a.shape[1] for a in operands[3:]) + LANES
    shapes = [(height, columns), (height // 4, columns)]
    return launch(
        pack_kernel,
        scalars=1,
        grid=(1,),
        in_specs=[fixed(a.shape) for a in operands],
        out_specs=[fixed(a) for a in shapes],
        out_shape=[jax.ShapeDtypeStruct(a, low) for a in shapes],
        compiler_params=params(24),
        cost_estimate=cost(0.001, 4),
        name="pack_mixer",
    )(at, *operands)


def pack_feed_kernel(offs_ref, gate_ref, up_ref, down_ref, first_ref, second_ref, give_ref, *refs):
    send_refs, (low_ref, high_ref) = refs[:2], refs[2:]
    height = gate_ref.shape[0]
    sent = PACK_AT + 4 * offs_ref[X_AT]
    targets = (
        (first_ref, 0, PACK_AT),
        (second_ref, 0, PACK_AT + 2),
        (give_ref, 0, PACK_AT + 4),
        (give_ref, height, PACK_AT + 6),
        (send_refs[0], 0, sent),
        (send_refs[1], 0, sent + 2),
    )
    for ref, row, place_at in targets:
        quarter = ref.shape[1] // 4
        for part_y in range(2):
            at = pl.ds(pl.multiple_of(offs_ref[place_at + part_y], 512), quarter)
            ref[row : row + height, part_y * quarter : (part_y + 1) * quarter] = gate_ref[:, at]
            ref[row : row + height, (2 + part_y) * quarter : (3 + part_y) * quarter] = up_ref[:, at]
    size = low_ref.shape[0]
    low_ref[...] = down_ref[:size, :]
    high_ref[...] = down_ref[size:, :]


def pack_feed(offs, w_gate, w_up, w_down, deps=()):
    height, columns = w_gate.shape
    half = (height, columns // 2)
    shapes = [half, half, (2 * height, columns // 2), half, half] + [(w_down.shape[0] // 2, w_down.shape[1])] * 2
    return launch(
        pack_feed_kernel,
        deps,
        scalars=1,
        grid=(1,),
        in_specs=[fixed(w_gate.shape), fixed(w_up.shape), fixed(w_down.shape)],
        out_specs=[fixed(a) for a in shapes],
        out_shape=[jax.ShapeDtypeStruct(a, low) for a in shapes],
        compiler_params=params(24),
        cost_estimate=cost(0.001, 8),
        name="pack_feed",
    )(offs, w_gate, w_up, w_down)


STRIPS = 1


def operand_parts(operand):
    if not isinstance(operand, tuple):
        return operand, None, 1
    return operand if len(operand) == 3 else (*operand, 2)


def step(kernel, offs, operands, shapes, name, deps=(), giga=0.001):
    in_specs, arrays = [], []
    for operand in operands:
        array, half, parts = operand_parts(operand)
        height = array.shape[0] // parts

        def where_to(i, offs, half=half):
            if half is None:
                return (i, 0)
            return ((half(offs) if callable(half) else half) * STRIPS + i, 0)

        in_specs.append(pl.BlockSpec((height // STRIPS, array.shape[1]), where_to))
        arrays.append(array)
    return launch(
        kernel,
        deps,
        scalars=1,
        grid=(STRIPS,),
        in_specs=in_specs,
        out_specs=[rows(shape[0] // STRIPS, shape[1]) for shape in shapes],
        out_shape=[jax.ShapeDtypeStruct(shape, low) for shape in shapes],
        compiler_params=params(24),
        cost_estimate=cost(giga, 8),
        name=name,
    )(offs, *arrays)


def add(*refs):
    total = refs[0].astype(wide)
    for other in refs[1:]:
        total = total + other.astype(wide)
    return total.astype(low)


def sum_kernel(terms, offs_ref, *refs):
    for out_ref, groups in zip(refs[-len(terms) :], terms):
        col = 0
        for group in groups:
            width = refs[group[0]].shape[1]
            out_ref[:, col : col + width] = add(*(refs[n][...] for n in group))
            col += width


def strip_sum(offs, outputs, name, deps=()):
    operands, terms, shapes = [], [], []
    for groups in outputs:
        terms.append([])
        width = 0
        for group in groups:
            terms[-1].append(list(range(len(operands), len(operands) + len(group))))
            operands += group
            first, _, parts = operand_parts(group[0])
            height = first.shape[0] // parts
            width += first.shape[1]
        shapes.append((height, width))
    return step(functools.partial(sum_kernel, terms), offs, operands, shapes, name, deps)


def top_sum(offs, keep, came, deps=()):
    came = came if came.shape[0] * 2 == keep.shape[0] else (came, 0)
    return strip_sum(offs, [[[(keep, 0), came]]], "top_sum", deps)[0]


def rest_sum(offs, triples, deps=()):
    groups = []
    for keep, came, passed in triples:
        came = came if came.shape[0] * 2 == keep.shape[0] else (came, 1)
        groups.append([(keep, 1), came, passed])
    return strip_sum(offs, [groups], "rest_sum", deps)[0]


def halves_sum(offs, pairs, filters=None, deps=()):
    outputs = []
    for half in range(2):
        groups = [[(keep, half), (came, half)] for keep, came in pairs]
        if filters is not None:

            def quarter(offs_ref, half=half):
                return offs_ref[OWNER_AT + 2 + half]

            groups.append([(a, quarter, 4) for a in filters])
        outputs.append(groups)
    return strip_sum(offs, outputs, "halves_sum", deps)


def near_split(offs, keep, came, deps=()):
    def own(offs_ref):
        return offs_ref[X_AT]

    def other(offs_ref):
        return 1 - offs_ref[X_AT]

    return strip_sum(offs, [[[(keep, own), (came, own)]], [[(keep, other), (came, other)]]], "near_split", deps)


def pairs_sum(offs, pairs, deps=()):
    return strip_sum(offs, [[list(pair) for pair in pairs]], "pairs_sum", deps)[0]


def sort_kernel(offs_ref, total_ref, other_ref, own_ref, give_ref):
    skip = total_ref.shape[1] - own_ref.shape[1]

    @pl.when(offs_ref[X_AT + 1] == 0)
    def _():
        own_ref[...] = total_ref[:, skip:]
        give_ref[...] = other_ref[:, skip:]

    @pl.when(offs_ref[X_AT + 1] != 0)
    def _():
        own_ref[...] = other_ref[:, skip:]
        give_ref[...] = total_ref[:, skip:]


def sort_rows(offs, total, other, skip, deps=()):
    shape = (total.shape[0], total.shape[1] - skip)
    return step(sort_kernel, offs, [total, other], [shape, shape], "sort_rows", deps)


def settle_down_kernel(offs_ref, *refs):
    out_ref = refs[-1]
    size = out_ref.shape[0] // 4
    width = out_ref.shape[1]
    for n in range(4):
        side = offs_ref[X_AT] if n % 2 == 0 else 1 - offs_ref[X_AT]
        at = pl.ds(pl.multiple_of((n // 2) * 2 * size + side * size, 128), size)
        out_ref[at, :] = refs[n][:, :width].astype(wide)


def settle_down(offs, pairs, width, deps=()):
    operands = [a for pair in pairs for a in pair]
    size = operands[0].shape[0]
    column = pl.BlockSpec((size, width), lambda *_: (0, 0), pipeline_mode=pl.Buffered(1))
    return launch(
        settle_down_kernel,
        deps,
        scalars=1,
        grid=(1,),
        in_specs=[column] * 4,
        out_specs=fixed((4 * size, width)),
        out_shape=jax.ShapeDtypeStruct((4 * size, width), wide),
        compiler_params=params(24),
        cost_estimate=cost(0.001, 6),
        name="settle_down",
    )(offs, *operands)


def settle_mixer_kernel(
    offs_ref, gain_ref, mine_ref, other_ref, wq_ref, wk_ref, wv_ref, wc_ref,
    gq_ref, gk_ref, gv_ref, gc_ref, go_ref, gf_ref, ggain_ref, all_ref,
):
    size = mine_ref.shape[0]
    for ref, side in ((mine_ref, offs_ref[X_AT]), (other_ref, 1 - offs_ref[X_AT])):
        all_ref[pl.ds(pl.multiple_of(side * size, 128), size), :] = ref[...].astype(wide)
    width = wv_ref.shape[1]
    half = wq_ref.shape[1] // 2
    go_ref[...] = all_ref[:, :width]
    gc = all_ref[:, width : 2 * width]
    gc_ref[...] = gc
    gf_ref[...] = all_ref[:, 2 * width : 2 * width + LANES].T[:KW, :]
    at = 2 * width + LANES
    gv = all_ref[:, at + 4 * half :]
    gv_ref[...] = gv
    total = jnp.sum(gc * wc_ref[...].astype(wide), axis=1, keepdims=True)
    total = total + jnp.sum(gv * wv_ref[...].astype(wide), axis=1, keepdims=True)
    for n, (ref, weight_ref, cols) in enumerate(
        (
            (gq_ref, wq_ref, slice(0, half)),
            (gk_ref, wk_ref, slice(0, half)),
            (gq_ref, wq_ref, slice(half, 2 * half)),
            (gk_ref, wk_ref, slice(half, 2 * half)),
        )
    ):
        value = all_ref[:, at + n * half : at + (n + 1) * half]
        ref[:, cols] = value
        total = total + jnp.sum(value * weight_ref[:, cols].astype(wide), axis=1, keepdims=True)
    ggain_ref[...] = as_line(total / gain_ref[...])


def settle_mixer(offs, gain, mine, other, w_query, w_key, w_value, w_convgate, deps=()):
    operands = (gain, mine, other, w_query, w_key, w_value, w_convgate)
    height, width = w_value.shape
    shapes = [w_query.shape, w_key.shape, w_value.shape, w_convgate.shape, (height, width), (KW, height), gain.shape[:1]]
    return launch(
        settle_mixer_kernel,
        deps,
        scalars=1,
        grid=(1,),
        in_specs=[fixed(a.shape) for a in operands],
        out_specs=[fixed(a) for a in shapes],
        out_shape=[jax.ShapeDtypeStruct(a, wide) for a in shapes],
        scratch_shapes=[pltpu.VMEM((height, mine.shape[1]), wide)],
        compiler_params=params(24),
        cost_estimate=cost(0.001, 8),
        name="settle_mixer",
    )(offs, *operands)


def tick_kernel(offs_ref, out_ref):
    out_ref[...] = jnp.zeros_like(out_ref)


def tick(offs, deps=()):
    return launch(
        tick_kernel,
        deps,
        scalars=1,
        grid=(1,),
        in_specs=[],
        out_specs=fixed((16, LANES)),
        out_shape=jax.ShapeDtypeStruct((16, LANES), low),
        compiler_params=params(24),
        cost_estimate=cost(TICK, 8),
        name="arrived",
    )(offs)


def swap(value, axis):
    return lax.ppermute(value, axis, [(0, 1), (1, 0)])


def later(value, other):
    return lax.optimization_barrier((value, other))[0]


def part(value, index, count, axis=0):
    size = value.shape[axis] // count
    return lax.dynamic_slice_in_dim(value, index * size, size, axis)


def in_order(index, mine, other):
    return jnp.where(
        index == 0, jnp.concatenate([mine, other], 0), jnp.concatenate([other, mine], 0)
    )


def per_device(
    tokens, segment_ids, gain_one, w_query, w_key, w_value, w_convgate, w_output, conv_filter,
    gain_two, w_gate, w_up, w_down, cotangent,
):
    Order.last = None
    Order.scale = 0.05
    x = lax.axis_index("near")
    y = lax.axis_index("row")
    c = lax.axis_index("core")
    s = 2 * y + c
    width = tokens.shape[1]
    seg = segment_ids[0]
    block = w_down.shape[0]

    def flip(bits):
        return jnp.bitwise_xor(s, bits)

    small_block = block // 2
    z = lax.axis_index("far") % 2
    quarters = [(2 * a + b) * (SHARD_ROWS // 4) for a, b in ((x, z), (1 - x, z), (x, 1 - z), (1 - x, 1 - z))]

    def feed_cols(core, j):
        return [((2 * row + core) * 2 + j) * small_block for row in range(2)]

    feed_rows = [s, flip(1), jnp.bitwise_xor(flip(2), x), jnp.bitwise_xor(flip(3), x)]
    offs = [
        x,
        jnp.bitwise_xor(x, c),
        s * SHARD_ROWS,
        flip(1) * SHARD_ROWS,
        *(flip(2) * SHARD_ROWS + a for a in quarters),
        *(flip(3) * SHARD_ROWS + a for a in quarters),
        *(a * SHARD_ROWS for a in feed_rows),
        y * small_block,
        (1 - y) * small_block,
        0,
        0,
        *feed_cols(c, 0), *feed_cols(c, 1), *feed_cols(1 - c, 0), *feed_cols(1 - c, 1),
        *feed_cols(c, 0), *feed_cols(1 - c, 0), *feed_cols(c, 1), *feed_cols(1 - c, 1),
        2 * (1 - y) + 1 - x, 2 * (1 - y) + x, 2 * y + 1 - x, 2 * y + x,
        flip(3), flip(1), flip(2), s,
        2 * (1 - y) + 1 - x, 2 * y + 1 - x, 2 * (1 - y) + x, 2 * y + x,
        2 * x + z,
    ]
    offs = jnp.stack([jnp.asarray(a, jnp.int32) for a in offs])

    pack, pack_part = pack_mixer(
        offs, gain_one, gain_two, conv_filter, w_query, w_key, w_value, w_convgate, w_output
    )
    direct = swap(pack_part, "row")
    count = lax.axis_size("far")
    over_z = lax.ppermute(direct, "far", [(i, i ^ 1) for i in range(count)])
    came = [direct, swap(direct, "near"), over_z, swap(over_z, "near")]
    pack_pieces = [pack, swap(pack, "core"), *came, *(swap(a, "core") for a in came)]
    cot_other = swap(later(cotangent, direct), "core")

    mine_first, mine_second, give, *sends, down_first, down_second = pack_feed(offs, w_gate, w_up, w_down)
    given = swap(later(give, direct), "core")

    def across(value):
        pairs = []
        for side, row, core in np.ndindex(2, 2, 2):
            pairs.append((4 * side + 2 * row + core, 4 * side + 2 * (1 - row) + (core ^ side)))
        return lax.ppermute(value, ("near", "row", "core"), pairs)

    feed_pieces = [[own, given] for own in (mine_first, mine_second)]
    feed_pieces[0].append(across(later(sends[0], direct)))

    hidden_one, queries, keys, values, gates, vec, full_one = project(offs, tokens, pack_pieces, deps=[cot_other])
    feed_pieces[0].append(swap(later(feed_pieces[0][2], queries), "near"))
    down_pieces = [[swap(later(down_first, queries), "row")]]
    feed_pieces[1].append(across(later(sends[1], queries)))
    pairs = width // 256
    mixed, attention, recips = attend(queries, keys, values, gates, vec, seg, 0, 2 * pairs)
    middle, hidden_two = mix(tokens, mixed, vec, full_one, deps=[down_pieces[0][0]])
    down_pieces.append([swap(later(down_second, middle), "row")])
    tick(offs, [feed_pieces[0][3]])
    hiddens = [hidden_two, swap(hidden_two, "core")]
    cots = [cotangent, cot_other]

    Order.scale = 20.0

    def down_grad(act, deps=()):
        return weight_grad(offs, ACT_AT, [([act], cots)], (2, 2), "grad_down", deps=deps)

    def gate_grad(both):
        return weight_grad(offs, GRAD_AT, [(hiddens, [both])], (1, 1, 2), "grad_gate_up")

    first_feed = feed(offs, hiddens, cots, 0, w_down, feed_pieces[0], down_pieces[0])
    feed_pieces[1].append(swap(later(feed_pieces[1][2], first_feed[0]), "near"))
    down_send, down_keep = down_grad(first_feed[0], deps=[feed_pieces[1][2]])
    down_came = swap(down_send, "near")
    gate_send, gate_send_own, gate_keep = gate_grad(first_feed[1])
    gate_came, gate_came_own = swap(gate_send, "row"), swap(gate_send_own, "row")
    second_feed = feed(offs, hiddens, cots, 1, w_down, feed_pieces[1], down_pieces[1])
    acts, boths, fulls, downs = zip(first_feed, second_feed)
    down_passed = swap(top_sum(offs, down_keep, down_came), "row")
    gate_passed = swap(top_sum(offs, gate_keep, gate_came), "near")
    ghidden_part = feed_back(boths[0], boths[1], fulls[0], fulls[1])
    ghidden_other = swap(ghidden_part, "core")
    down_send_2, down_keep_2 = down_grad(second_feed[0])
    down_came_2 = swap(down_send_2, "near")
    gate_send_2, gate_send_own_2, gate_keep_2 = gate_grad(second_feed[1])
    gate_came_2, gate_came_own_2 = swap(gate_send_2, "row"), swap(gate_send_own_2, "row")
    feed_sum = lax.psum(
        rest_sum(offs, [(down_keep, down_came, down_passed), (gate_keep, gate_came_own, gate_passed)]), "far"
    )
    tick(offs)
    gmiddle, gbranch, gmixed, _ = middle_back(
        boths[0], boths[1], ghidden_other, middle, cotangent, vec, fulls[0], fulls[1], full_one
    )
    down_passed_2 = swap(top_sum(offs, down_keep_2, down_came_2), "row")
    gate_passed_2 = swap(top_sum(offs, gate_keep_2, gate_came_2), "near")

    ggate, gconv, gfilter = conv_back(values, gmixed, gates, vec, seg)
    filter_came = swap(gfilter, "core")
    early_send, early_keep = weight_grad(
        offs, OWNER_AT, [([mixed], [gbranch]), ([hidden_one], [ggate])], (2, 2), "grad_output_convgate"
    )
    early_came = swap(early_send, "core")
    attended = attend_back(queries, keys, values, gmixed, attention, recips, gconv, seg, 0, pairs)
    early_give, early_held = halves_sum(offs, [(early_keep, early_came)], [gfilter, filter_came])
    early_came = swap(early_give, "row")
    tick(offs, [feed_sum])
    feed_near = rest_sum(
        offs, [(down_keep_2, down_came_2, down_passed_2), (gate_keep_2, gate_came_own_2, gate_passed_2)]
    )
    feed_other = swap(later(feed_sum, feed_near), "near")
    feed_part = lax.psum_scatter(feed_near, "far", scatter_dimension=0, tiled=True)
    tick(offs)
    gqk, gv = attend_back(
        queries, keys, values, gmixed, attention, recips, gconv, seg, pairs, pairs, onto=attended
    )
    early_own, early_other = near_split(offs, early_held, early_came)
    early_passed = swap(early_other, "near")
    late_send, late_keep = weight_grad(
        offs, OWNER_AT, [([hidden_one], [gqk]), ([hidden_one], [gv])], (2, 2), "grad_query_key_value"
    )
    late_came = swap(late_send, "core")
    Order.scale = 0.05
    feed_sum_2 = lax.all_gather(later(feed_part, tick(offs, [feed_part])), "far", axis=0, tiled=True)
    own_rows, theirs = sort_rows(offs, feed_sum, feed_other, width)
    spreads = [own_rows, swap(theirs, "core")]
    late_give, late_held = halves_sum(offs, [(late_keep, late_came)])
    late_came = swap(late_give, "row")
    out_part = feed_out(acts[0], acts[1], downs[0], downs[1], 1, [], "feed_out_partner")
    late_own, late_other = near_split(offs, late_held, late_came)
    late_passed = swap(late_other, "near")
    tick(offs, [feed_sum_2])
    mixer_near = pairs_sum(offs, [(early_own, early_passed), (late_own, late_passed)])
    feed_other_2 = swap(later(feed_sum_2, mixer_near), "near")
    Order.scale = 20.0
    mixer_sum = lax.psum(mixer_near, "far")
    out_came = swap(later(out_part, mixer_near), "core")
    tick(offs)
    result = feed_out(acts[0], acts[1], downs[0], downs[1], 0, [middle, out_came], "feed_out")
    grad_tokens, _ = tokens_back(gqk, gv, ggate, tokens, gmiddle, vec, full_one)
    own_rows, theirs = sort_rows(offs, feed_sum_2, feed_other_2, width)
    spreads += [own_rows, swap(theirs, "core")]
    grad_down = settle_down(offs, [(feed_sum, feed_other), (feed_sum_2, feed_other_2)], width)
    grad_gate, grad_up, ggain_two = spread(offs, gain_two[:, None].astype(wide), w_gate, w_up, spreads)
    mixer_other = swap(mixer_sum, "near")
    *grads, grad_output, grad_filter, ggain_one = settle_mixer(
        offs, gain_one[:, None].astype(wide), mixer_sum, mixer_other, w_query, w_key, w_value, w_convgate
    )
    return (
        result,
        grad_tokens,
        ggain_one,
        *grads,
        grad_output,
        grad_filter,
        ggain_two,
        grad_gate,
        grad_up,
        grad_down,
    )


def solution(mesh):
    replicas, shards = mesh.shape["rep"], mesh.shape["shard"]
    devices = np.asarray(mesh.devices).reshape(replicas // 2, 2, shards // 2, 2)
    fine = Mesh(devices, ("far", "near", "row", "core"))
    token = P(("far", "near", "row", "core"), None)
    line = P(("row", "core"))
    weight = P(("row", "core"), None)
    taps = P(None, ("row", "core"))
    return jax.shard_map(
        per_device,
        mesh=fine,
        in_specs=(
            token, token, line, weight, weight, weight, weight, weight, taps, line, weight, weight, weight, token
        ),
        out_specs=(
            token, token, line, weight, weight, weight, weight, weight, taps, line, weight, weight, weight
        ),
        check_vma=False,
    )
```
